32 devices in a mesh: clu: 32 (over z, y, x, core).
Axes of the slice: x: 2, y: 2, z: 4, core: 2. Of those that a mesh axis runs over, the one named last changes fastest.
Arguments:
- charges: bfloat16 [256, 32, 256], P('clu'), may hold values from -6 to 6
- basis: bfloat16 [256, 96, 256], P('clu'), may hold values from -0.375 to 0.375
- transfer: bfloat16 [256, 96, 96], P('clu'), may hold values from -0.4375 to 0.4375
- near_field: bfloat16 [256, 3, 256, 256], P('clu'), may hold values from -0.21875 to 0.21875
- coupling: bfloat16 [4096, 96, 96], P('clu'), may hold values from -0.625 to 0.625
- ranks: int32 [384], P('clu'), may hold values from 32 to 96, as said below
- block_source: int32 [4096], P('clu'), may hold values from 0 to 383, as said below
- block_target: int32 [4096], P('clu'), may hold values from 0 to 383, as said below
Outputs:
- first: bfloat16 [256, 32, 256], P('clu')
- second: bfloat16 [256, 32, 256], P('clu')
The draws below stay inside these ranges and needn't reach their ends.
Inputs may be any that keep to these rules, and one draw needn't show every extreme that they name: `ranks`: each cluster's rank; 96 and 32 are both taken. `block_source`: global cluster numbers; a block's source and target are both leaves or both parents. Among the blocks of one device, at most 8 have their source on any one device, and exactly 8 for some device. `block_target`: global cluster numbers of the same level as the block's source. Among the blocks of one device, at most 8 have their target on any one device, and exactly 8 for some device.
All inputs are finite; a program needn't handle non-finite values.
Results may differ from the reference program's by a relative error of at most 0.025.
Values may be sent and summed in bfloat16 or wider, within the bound.
No kernel may reach another device: no remote copies, remote signals or barrier semaphores. Data moves between devices by JAX's collectives and lax.ppermute only.
A program may use at most 128 MiB of HBM per device.

```python
import jax
import jax.numpy as jnp
from jax import lax

LEAF = 256
RMAX = 96
RHS = 32
LEAF_DEV = 8
BLK_DEV = 128
DEVS = 32
CL_DEV = 12
CAP = 8
LEAVES = 256
CLUSTERS = 384
BLOCKS = 4096


def peer_lists(key):
    keys = jax.random.split(key, DEVS)

    def one_device(subkey):
        key_a, key_b, key_c = jax.random.split(subkey, 3)
        leading = jax.random.randint(key_a, (), 0, DEVS)
        others = (leading + 1 + jnp.arange((DEVS - 1) * CAP) // CAP) % DEVS
        picked = others[jax.random.permutation(key_b, (DEVS - 1) * CAP)[:BLK_DEV - CAP]]
        joined = jnp.concatenate([jnp.full((CAP,), leading, jnp.int32), picked.astype(jnp.int32)])
        return joined[jax.random.permutation(key_c, BLK_DEV)]
    return jax.vmap(one_device)(keys)


def first_match(devices, wanted):
    return jnp.argmax((devices.ravel() == wanted).astype(jnp.int32)).astype(jnp.int32)


def routing(key):
    keys = jax.random.split(key, 7)
    source_dev = peer_lists(keys[0])
    target_dev = peer_lists(keys[1])
    low_src = first_match(source_dev, 0)
    high_src = first_match(source_dev, DEVS - 1)
    low_tgt = first_match(target_dev, 0)
    high_tgt = first_match(target_dev, DEVS - 1)
    level = jax.random.randint(keys[2], (DEVS * BLK_DEV,), 0, 2)
    level = level.at[low_src].set(0).at[low_tgt].set(0).at[high_src].set(1).at[high_tgt].set(1)
    source_loc = jnp.where(level == 0, jax.random.randint(keys[3], (DEVS * BLK_DEV,), 0, LEAF_DEV), LEAF_DEV + jax.random.randint(keys[4], (DEVS * BLK_DEV,), 0, LEAF_DEV // 2))
    target_loc = jnp.where(level == 0, jax.random.randint(keys[5], (DEVS * BLK_DEV,), 0, LEAF_DEV), LEAF_DEV + jax.random.randint(keys[6], (DEVS * BLK_DEV,), 0, LEAF_DEV // 2))
    source_loc = source_loc.at[low_src].set(0).at[high_src].set(CL_DEV - 1)
    target_loc = target_loc.at[low_tgt].set(0).at[high_tgt].set(CL_DEV - 1)
    source_loc = source_loc.reshape(DEVS, BLK_DEV).astype(jnp.int32)
    target_loc = target_loc.reshape(DEVS, BLK_DEV).astype(jnp.int32)
    return (source_dev, source_loc, target_dev, target_loc)


def draw_ranks(key, part):
    key = jax.random.fold_in(key, 11)
    values = jax.random.randint(key, (CLUSTERS,), RMAX // 3, RMAX + 1)
    return values.at[0].set(RMAX).at[1].set(RMAX // 3).astype(jnp.int32)


def draw_block_source(key, part):
    source_dev, source_loc, target_dev, target_loc = routing(key)
    return (source_dev * CL_DEV + source_loc).ravel().astype(jnp.int32)


def draw_block_target(key, part):
    source_dev, source_loc, target_dev, target_loc = routing(key)
    return (target_dev * CL_DEV + target_loc).ravel().astype(jnp.int32)


def shard_levels(stream_key, dims, cuts, least, high):
    def one(position, parts):
        draws = jax.random.uniform(jax.random.fold_in(jax.random.fold_in(stream_key, 6), position), (parts,), jnp.float32, least / len(cuts), high / len(cuts))
        return jnp.repeat(jnp.exp(draws), dims[position] // parts).reshape((-1,) + (1,) * (len(dims) - position - 1))

    level = one(*cuts[0])
    for cut in cuts[1:]:
        level = level * one(*cut)
    return level


def noise(own_key, shape, spread, most, cuts=(), dtype=jnp.bfloat16):
    entries = jax.random.normal(own_key, shape, jnp.float32) * spread
    if len(cuts) > 0:
        entries = shard_levels(own_key, shape, cuts, -0.22, 0.18) * entries
    return jnp.clip(entries, min=-most, max=most).astype(dtype)


def setup_inputs(seed: int = 0) -> dict:
    key_list = jax.random.split(jax.random.key(seed), 9)
    charges = noise(key_list[0], (LEAVES, RHS, LEAF), 1.0, 6.0, ((0, 32),))
    basis = noise(key_list[1], (LEAVES, RMAX, LEAF), LEAF ** -0.5, 0.375, ((0, 32),))
    transfer = noise(key_list[2], (LEAVES, RMAX, RMAX), (2 * RMAX) ** -0.5, 0.4375, ((0, 32),))
    near_field = noise(key_list[3], (LEAVES, 3, LEAF, LEAF), (3 * LEAF) ** -0.5, 0.21875, ((0, 32),))
    coupling = noise(key_list[4], (BLOCKS, RMAX, RMAX), RMAX ** -0.5, 0.625, ((0, 32),))
    ranks = draw_ranks(jax.random.fold_in(key_list[8], 71), 0)
    block_source = draw_block_source(jax.random.fold_in(key_list[8], 71), 0)
    block_target = draw_block_target(jax.random.fold_in(key_list[8], 71), 0)
    return dict(charges=charges, basis=basis, transfer=transfer, near_field=near_field, coupling=coupling, ranks=ranks, block_source=block_source, block_target=block_target)


def rank_table(ranks):
    return (jnp.arange(RMAX)[None, :] < ranks[:, None]).astype(jnp.float32)


def apply_matrix(field_in, basis, transfer, near_field, coupling, masks, block_source, block_target):
    highest = lax.Precision.HIGHEST
    grouped = masks.reshape(DEVS, CL_DEV, RMAX)
    leaf_mask = grouped[:, :LEAF_DEV].reshape(LEAVES, RMAX)
    parent_mask = grouped[:, LEAF_DEV:].reshape(LEAVES // 2, RMAX)
    basis_wide = basis.astype(jnp.float32)
    leaf_coeff = jnp.einsum('irb,ikb->irk', field_in.astype(jnp.float32), basis_wide, precision=highest)
    leaf_coeff = (leaf_coeff * leaf_mask[:, None, :]).astype(jnp.bfloat16)
    kids = leaf_coeff.reshape(LEAVES // 2, 2, RHS, RMAX).astype(jnp.float32)
    pairs = transfer.reshape(LEAVES // 2, 2, RMAX, RMAX).astype(jnp.float32)
    parent_coeff = jnp.einsum('qcrk,qckp->qrp', kids, pairs, precision=highest)
    parent_coeff = (parent_coeff * parent_mask[:, None, :]).astype(jnp.bfloat16)
    coeffs = jnp.concatenate([leaf_coeff.reshape(DEVS, LEAF_DEV, RHS, RMAX),
                              parent_coeff.reshape(DEVS, LEAF_DEV // 2, RHS, RMAX)], axis=1)
    coeffs = coeffs.reshape(CLUSTERS, RHS, RMAX)

    def add_blocks(index, total):
        start = (index * BLK_DEV).astype(jnp.int32)
        sources = lax.dynamic_slice_in_dim(block_source, start, BLK_DEV)
        targets = lax.dynamic_slice_in_dim(block_target, start, BLK_DEV)
        mats = lax.dynamic_slice_in_dim(coupling, start, BLK_DEV).astype(jnp.float32)
        terms = jnp.einsum('jrk,jkp->jrp', coeffs[sources].astype(jnp.float32), mats, precision=highest)
        return total.at[targets].add(terms)

    field = lax.fori_loop(0, DEVS, add_blocks, jnp.zeros((CLUSTERS, RHS, RMAX), jnp.float32))
    field = (field * masks[:, None, :]).astype(jnp.bfloat16).reshape(DEVS, CL_DEV, RHS, RMAX)
    leaf_field = field[:, :LEAF_DEV].reshape(LEAVES, RHS, RMAX).astype(jnp.float32)
    parent_field = field[:, LEAF_DEV:].reshape(LEAVES // 2, RHS, RMAX).astype(jnp.float32)
    downward = jnp.einsum('qrp,qckp->qcrk', parent_field, pairs, precision=highest).reshape(LEAVES, RHS, RMAX)
    leaf_total = ((leaf_field + downward) * leaf_mask[:, None, :]).astype(jnp.bfloat16)
    result = jnp.einsum('irk,ikb->irb', leaf_total.astype(jnp.float32), basis_wide, precision=highest)
    padded = jnp.pad(field_in.astype(jnp.float32), ((1, 1), (0, 0), (0, 0)))
    for offset in range(3):
        result = result + jnp.einsum('irb,iba->ira', padded[offset:offset + LEAVES],
                                     near_field[:, offset].astype(jnp.float32), precision=highest)
    return result.astype(jnp.bfloat16)


def reference(charges, basis, transfer, near_field, coupling, ranks, block_source, block_target):
    masks = rank_table(ranks)
    first = apply_matrix(charges, basis, transfer, near_field, coupling, masks, block_source, block_target)
    second = apply_matrix(first, basis, transfer, near_field, coupling, masks, block_source, block_target)
    return (first, second)
```

```python
import functools

import jax
import jax.numpy as jnp
from jax import lax
from jax.experimental import pallas as pl
from jax.experimental.pallas import tpu as pltpu
from jax.sharding import PartitionSpec as P

LANES = 128
BF = jnp.bfloat16
F32 = jnp.float32
VMEM = pl.BlockSpec(memory_space=pltpu.VMEM)
SMEM = pl.BlockSpec(memory_space=pltpu.SMEM)


def dot(a, b):
    return lax.dot_general(a, b, (((1,), (0,)), ((), ())), preferred_element_type=F32)


def dot_t(a, b):
    return lax.dot_general(a, b, (((1,), (1,)), ((), ())), preferred_element_type=F32)


def spread(rank_top, piece):
    third = LANES - rank_top
    row = lax.broadcasted_iota(jnp.int32, (rank_top, LANES), 0)
    lane = lax.broadcasted_iota(jnp.int32, (rank_top, LANES), 1)
    hit = (lane - rank_top == row - third * piece) & (lane >= rank_top)
    return hit.astype(F32).astype(BF)


def collect(rank_top, piece):
    third = LANES - rank_top
    row = lax.broadcasted_iota(jnp.int32, (LANES, LANES), 0)
    lane = lax.broadcasted_iota(jnp.int32, (LANES, LANES), 1)
    hit = (row - rank_top == lane - third * piece) & (row >= rank_top)
    return hit.astype(F32).astype(BF)


def emit_coeffs(read_leaf, basis_ref, transfer_ref, ranks_ref, out_ref, leaves, rank_top):
    rhs = out_ref.shape[1]
    lane = lax.broadcasted_iota(jnp.int32, (rhs, rank_top), 1)
    coeffs = []
    for i in range(leaves):
        value = dot_t(read_leaf(i), basis_ref[i])
        coeffs.append(jnp.where(lane < ranks_ref[i], value, 0.0).astype(BF))
    for q in range(leaves // 2):
        value = dot(coeffs[2 * q], transfer_ref[2 * q]) + dot(coeffs[2 * q + 1], transfer_ref[2 * q + 1])
        coeffs.append(jnp.where(lane < ranks_ref[leaves + q], value, 0.0).astype(BF))
    mains = out_ref.shape[0]
    for q in range(mains // 3):
        for k in range(3):
            tile = dot(coeffs[mains + q], spread(rank_top, k)).astype(BF)
            out_ref[3 * q + k] = tile
            out_ref[3 * q + k, :, :rank_top] = coeffs[3 * q + k]


def coeff_kernel(ranks_ref, v_ref, basis_ref, transfer_ref, out_ref):
    leaves, rank_top, _ = basis_ref.shape
    emit_coeffs(lambda i: v_ref[i], basis_ref, transfer_ref, ranks_ref, out_ref, leaves, rank_top)


def slots_kernel(targets_ref, ids_ref, slots_ref, counts, *, clusters, per_peer):
    blocks = targets_ref.shape[0]
    peers = ids_ref.shape[0] // per_peer

    def reset(i, _):
        counts[i] = 0
        return 0

    def unused(i, _):
        ids_ref[i] = clusters
        return 0

    def place(j, _):
        target = targets_ref[j]
        peer = lax.div(target, jnp.int32(clusters))
        slot = peer * per_peer + counts[peer]
        counts[peer] = counts[peer] + 1
        ids_ref[slot] = target - peer * clusters
        slots_ref[j] = slot
        return 0

    lax.fori_loop(0, peers, reset, 0)
    lax.fori_loop(0, peers * per_peer, unused, 0)
    lax.fori_loop(0, blocks, place, 0)


def unpack(packed_ref, pads_ref, rank_top, step):
    groups, rhs, _ = pads_ref.shape
    pieces = [collect(rank_top, k) for k in range(3)]

    def some(s, _):
        total = None
        for k in range(3):
            tiles = jnp.concatenate([packed_ref[(s * step + g) * 3 + k] for g in range(step)], axis=0)
            part = dot(tiles, pieces[k])
            total = part if total is None else total + part
        total = total.astype(BF).reshape(step, rhs, LANES)
        for g in range(step):
            pads_ref[s * step + g] = total[g]
        return 0

    lax.fori_loop(0, groups // step, some, 0)


def couple_kernel(main_ref, pad_ref, is_pad_ref, slot_ref, gathered_ref, coupling_ref, out_ref, pads, terms, *, unroll):
    blocks, rank_top, _ = coupling_ref.shape
    rhs = out_ref.shape[1]
    slots = terms.shape[0]
    unpack(gathered_ref, pads, rank_top, 8)

    def clear(s, _):
        for u in range(8):
            terms[s * 8 + u] = jnp.zeros((rhs, LANES), BF)
        return 0

    lax.fori_loop(0, slots // 8, clear, 0)

    def some(s, _):
        for u in range(unroll):
            j = s * unroll + u
            main = gathered_ref[main_ref[j], :, :rank_top]
            pad = pads[pad_ref[j], :, :rank_top]
            source = jnp.where(is_pad_ref[j] > 0, pad, main)
            terms[slot_ref[j], :, :rank_top] = dot(source, coupling_ref[j]).astype(BF)
        return 0

    lax.fori_loop(0, blocks // unroll, some, 0)

    pieces = [spread(rank_top, k) for k in range(3)]
    step = 8
    low = lax.broadcasted_iota(jnp.int32, (rhs, LANES), 1) < rank_top

    def pack(s, _):
        fourth = jnp.concatenate([terms[(s * step + g) * 4 + 3, :, :rank_top] for g in range(step)], axis=0)
        for k in range(3):
            moved = dot(fourth, pieces[k]).astype(BF).reshape(step, rhs, LANES)
            for g in range(step):
                quad = s * step + g
                out_ref[quad * 3 + k] = jnp.where(low, terms[quad * 4 + k], moved[g])
        return 0

    lax.fori_loop(0, slots // 4 // step, pack, 0)


def near_kernel(v_ref, before_ref, after_ref, near_ref, out_ref):
    leaves = v_ref.shape[0]
    for i in range(leaves):
        left = v_ref[i - 1] if i > 0 else before_ref[0]
        right = v_ref[i + 1] if i < leaves - 1 else after_ref[0]
        out_ref[i] = dot(left, near_ref[i, 0]) + dot(v_ref[i], near_ref[i, 1]) + dot(right, near_ref[i, 2])


def field_kernel(ids_ref, ranks_ref, terms_ref, near_ref, basis_ref, transfer_ref, out_ref, *rest):
    *coeff_ref, pads, total = rest
    leaves, rank_top, _ = basis_ref.shape
    rhs = out_ref.shape[1]
    clusters = leaves + leaves // 2
    unpack(terms_ref, pads, rank_top, 8)
    for c in range(clusters + 1):
        total[c] = jnp.zeros((rhs, LANES), F32)

    def add(quad, _):
        for k in range(3):
            at = ids_ref[quad * 4 + k]
            total[at] = total[at] + terms_ref[quad * 3 + k].astype(F32)
        at = ids_ref[quad * 4 + 3]
        total[at] = total[at] + pads[quad].astype(F32)
        return 0

    lax.fori_loop(0, pads.shape[0], add, 0, unroll=4)

    lane = lax.broadcasted_iota(jnp.int32, (rhs, rank_top), 1)
    fields = [
        jnp.where(lane < ranks_ref[c], total[c, :, :rank_top], 0.0).astype(BF) for c in range(clusters)
    ]
    for i in range(leaves):
        down = fields[i].astype(F32) + dot_t(fields[leaves + i // 2], transfer_ref[i])
        leaf_total = jnp.where(lane < ranks_ref[i], down, 0.0).astype(BF)
        out_ref[i] = (near_ref[i] + dot(leaf_total, basis_ref[i])).astype(BF)
    if coeff_ref:
        emit_coeffs(
            lambda i: out_ref[i], basis_ref, transfer_ref, ranks_ref, coeff_ref[0], leaves, rank_top
        )


def params(mebibytes):
    return pltpu.CompilerParams(vmem_limit_bytes=mebibytes << 20)


def local(charges, basis, transfer, near_field, coupling, ranks, block_source, block_target):
    leaves, rank_top, width = basis.shape
    rhs = charges.shape[1]
    clusters = ranks.shape[0]
    blocks = coupling.shape[0]
    devices = lax.axis_size("clu")
    mains = clusters * 3 // 4
    per_peer = max(2, 2 * blocks // devices)
    per_peer = (per_peer + 3) // 4 * 4
    slots = per_peer * devices
    shape = jax.ShapeDtypeStruct

    cores, chips = 2, 4
    planes = devices // (cores * chips)
    plane_groups = [[p * cores * chips + r for p in range(planes)] for r in range(cores * chips)]
    chip_groups = [
        [p * cores * chips + c * cores + k for c in range(chips)] for p in range(planes) for k in range(cores)
    ]
    core_groups = [[h * cores + k for k in range(cores)] for h in range(devices // cores)]

    def gather(coeffs):
        for groups in (plane_groups, chip_groups, core_groups):
            coeffs = lax.all_gather(coeffs, "clu", axis=0, tiled=True, axis_index_groups=groups)
        return coeffs

    source_dev = block_source // clusters
    source_loc = block_source % clusters
    place = ((source_dev % cores) * chips + (source_dev // cores) % chips) * planes + source_dev // (cores * chips)
    is_pad = (source_loc >= mains).astype(jnp.int32)
    main_row = place * mains + jnp.where(source_loc >= mains, 0, source_loc)
    pad_row = place * (clusters - mains) + jnp.where(source_loc >= mains, source_loc - mains, 0)

    coeff_shape = shape((mains, rhs, LANES), BF)
    out_shape = shape((leaves, rhs, width), BF)
    first_coeffs = pl.pallas_call(
        coeff_kernel,
        out_shape=coeff_shape,
        in_specs=[SMEM, VMEM, VMEM, VMEM],
        out_specs=VMEM,
        compiler_params=params(16),
    )(ranks, charges, basis, transfer)

    wanted, slot_rows = pl.pallas_call(
        functools.partial(slots_kernel, clusters=clusters, per_peer=per_peer),
        out_shape=[shape((slots,), jnp.int32), shape((blocks,), jnp.int32)],
        in_specs=[SMEM],
        out_specs=[SMEM, SMEM],
        scratch_shapes=[pltpu.SMEM((devices,), jnp.int32)],
    )(block_target)
    owner_ids = lax.all_to_all(
        wanted.reshape(devices, per_peer), "clu", split_axis=0, concat_axis=0, tiled=True
    ).reshape(slots)

    couple = pl.pallas_call(
        functools.partial(couple_kernel, unroll=8),
        out_shape=shape((slots // 4 * 3, rhs, LANES), BF),
        in_specs=[SMEM, SMEM, SMEM, SMEM, VMEM, VMEM],
        out_specs=VMEM,
        scratch_shapes=[
            pltpu.VMEM((devices * (clusters - mains), rhs, LANES), BF),
            pltpu.VMEM((slots, rhs, LANES), BF),
        ],
        compiler_params=params(32),
        cost_estimate=pl.CostEstimate(
            flops=2 * blocks * rhs * rank_top * rank_top, bytes_accessed=10 << 20, transcendentals=0
        ),
    )

    near = pl.pallas_call(
        near_kernel,
        out_shape=shape((leaves, rhs, width), F32),
        in_specs=[VMEM] * 4,
        out_specs=VMEM,
        compiler_params=params(16),
        cost_estimate=pl.CostEstimate(
            flops=2 * leaves * 3 * rhs * width * width, bytes_accessed=4 << 20, transcendentals=0
        ),
    )

    def finish(with_coeffs):
        return pl.pallas_call(
            field_kernel,
            out_shape=[out_shape, coeff_shape] if with_coeffs else [out_shape],
            in_specs=[SMEM, SMEM, VMEM, VMEM, VMEM, VMEM],
            out_specs=[VMEM, VMEM] if with_coeffs else [VMEM],
            scratch_shapes=[
                pltpu.VMEM((slots // 4, rhs, LANES), BF),
                pltpu.VMEM((clusters + 1, rhs, LANES), F32),
            ],
            compiler_params=params(24),
        )

    ends = devices - 1

    def apply_matrix(field_in, coeffs, with_coeffs):
        gathered = gather(coeffs)
        outbound = couple(main_row, pad_row, is_pad, slot_rows, gathered, coupling)
        returned = lax.all_to_all(
            outbound.reshape(devices, per_peer * 3 // 4, rhs, LANES), "clu", split_axis=0, concat_axis=0, tiled=True
        ).reshape(slots // 4 * 3, rhs, LANES)
        before = lax.ppermute(field_in[leaves - 1 :], "clu", [(i, i + 1) for i in range(ends)])
        after = lax.ppermute(field_in[:1], "clu", [(i + 1, i) for i in range(ends)])
        near_sum = near(field_in, before, after, near_field)
        return finish(with_coeffs)(owner_ids, ranks, returned, near_sum, basis, transfer)

    first, second_coeffs = apply_matrix(charges, first_coeffs, True)
    (second,) = apply_matrix(first, second_coeffs, False)
    return (first, second)


def solution(mesh):
    in_specs = (
        P("clu", None, None),
        P("clu", None, None),
        P("clu", None, None),
        P("clu", None, None, None),
        P("clu", None, None),
        P("clu"),
        P("clu"),
        P("clu"),
    )
    out_specs = (P("clu", None, None), P("clu", None, None))
    return jax.shard_map(local, mesh=mesh, in_specs=in_specs, out_specs=out_specs, check_vma=False)
```

```python
import functools

import jax
import jax.numpy as jnp
from jax import lax
from jax.experimental import pallas as pl
from jax.experimental.pallas import tpu as pltpu
from jax.sharding import PartitionSpec as P

LANES = 128
BF = jnp.bfloat16
F32 = jnp.float32
VMEM = pl.BlockSpec(memory_space=pltpu.VMEM)
SMEM = pl.BlockSpec(memory_space=pltpu.SMEM)


def dot(a, b):
    return lax.dot_general(a, b, (((1,), (0,)), ((), ())), preferred_element_type=F32)


def dot_t(a, b):
    return lax.dot_general(a, b, (((1,), (1,)), ((), ())), preferred_element_type=F32)


def spread(rank_top, piece):
    third = LANES - rank_top
    row = lax.broadcasted_iota(jnp.int32, (rank_top, LANES), 0)
    lane = lax.broadcasted_iota(jnp.int32, (rank_top, LANES), 1)
    hit = (lane - rank_top == row - third * piece) & (lane >= rank_top)
    return hit.astype(F32).astype(BF)


def collect(rank_top, piece):
    third = LANES - rank_top
    row = lax.broadcasted_iota(jnp.int32, (LANES, LANES), 0)
    lane = lax.broadcasted_iota(jnp.int32, (LANES, LANES), 1)
    hit = (row - rank_top == lane - third * piece) & (row >= rank_top)
    return hit.astype(F32).astype(BF)


def emit_coeffs(read_leaf, basis_ref, transfer_ref, ranks_ref, out_ref, leaves, rank_top):
    copies, mains, rhs, _ = out_ref.shape
    lane = lax.broadcasted_iota(jnp.int32, (rhs, rank_top), 1)
    coeffs = []
    for i in range(leaves):
        value = dot_t(read_leaf(i), basis_ref[i])
        coeffs.append(jnp.where(lane < ranks_ref[i], value, 0.0).astype(BF))
    for q in range(leaves // 2):
        value = dot(coeffs[2 * q], transfer_ref[2 * q]) + dot(coeffs[2 * q + 1], transfer_ref[2 * q + 1])
        coeffs.append(jnp.where(lane < ranks_ref[leaves + q], value, 0.0).astype(BF))
    for q in range(mains // 3):
        for k in range(3):
            tile = dot(coeffs[mains + q], spread(rank_top, k)).astype(BF)
            for c in range(copies):
                out_ref[c, 3 * q + k] = tile
                out_ref[c, 3 * q + k, :, :rank_top] = coeffs[3 * q + k]


def coeff_kernel(ranks_ref, v_ref, basis_ref, transfer_ref, out_ref):
    leaves, rank_top, _ = basis_ref.shape
    emit_coeffs(lambda i: v_ref[i], basis_ref, transfer_ref, ranks_ref, out_ref, leaves, rank_top)


def couple_kernel(source_ref, target_ref, own_ref, other_ref, coupling_ref, keep_ref, send_ref, sources, total, *, unroll):
    blocks, rank_top, _ = coupling_ref.shape
    devices, mains, rhs, _ = own_ref.shape
    quads = mains // 3
    clusters = mains + quads
    gathers = [collect(rank_top, k) for k in range(3)]

    for half, packed_ref in enumerate((own_ref, other_ref)):

        def split(d, _):
            row = (half * devices + d) * clusters
            pads = None
            for k in range(3):
                tiles = jnp.concatenate([packed_ref[d, 3 * q + k] for q in range(quads)], axis=0)
                part = dot(tiles, gathers[k])
                pads = part if pads is None else pads + part
            pads = pads.astype(BF).reshape(quads, rhs, LANES)
            for c in range(mains):
                sources[row + c] = packed_ref[d, c]
            for q in range(quads):
                sources[row + mains + q] = pads[q]
            return 0

        lax.fori_loop(0, devices, split, 0)

    def clear(s, _):
        for u in range(clusters):
            total[s * clusters + u] = jnp.zeros((rhs, LANES), F32)
        return 0

    lax.fori_loop(0, 2 * devices, clear, 0)

    def some(s, _):
        for u in range(unroll):
            j = s * unroll + u
            term = dot(sources[source_ref[j], :, :rank_top], coupling_ref[j])
            at = target_ref[j]
            total[at, :, :rank_top] = total[at, :, :rank_top] + term
        return 0

    lax.fori_loop(0, blocks // unroll, some, 0)

    moves = [spread(rank_top, k) for k in range(3)]
    low = lax.broadcasted_iota(jnp.int32, (rhs, LANES), 1) < rank_top
    for half, packed_ref in enumerate((keep_ref, send_ref)):

        def pack(d, _):
            row = (half * devices + d) * clusters
            pads = jnp.concatenate([total[row + mains + q, :, :rank_top] for q in range(quads)], axis=0).astype(BF)
            for k in range(3):
                moved = dot(pads, moves[k]).reshape(quads, rhs, LANES)
                for q in range(quads):
                    packed_ref[d, 3 * q + k] = jnp.where(low, total[row + 3 * q + k], moved[q]).astype(BF)
            return 0

        lax.fori_loop(0, devices, pack, 0)


def near_kernel(v_ref, before_ref, after_ref, near_ref, out_ref):
    leaves = v_ref.shape[0]
    for i in range(leaves):
        left = v_ref[i - 1] if i > 0 else before_ref[0]
        right = v_ref[i + 1] if i < leaves - 1 else after_ref[0]
        out_ref[i] = dot(left, near_ref[i, 0]) + dot(v_ref[i], near_ref[i, 1]) + dot(right, near_ref[i, 2])


def field_kernel(ranks_ref, terms_ref, near_ref, basis_ref, transfer_ref, out_ref, *coeff_ref):
    leaves, rank_top, _ = basis_ref.shape
    parts, mains, rhs, _ = terms_ref.shape
    packed = []
    for t in range(mains):
        tile = terms_ref[0, t].astype(F32)
        for p in range(1, parts):
            tile = tile + terms_ref[p, t].astype(F32)
        packed.append(tile.astype(BF))
    sums = [tile[:, :rank_top] for tile in packed]
    for q in range(mains // 3):
        pad = None
        for k in range(3):
            part = dot(packed[3 * q + k], collect(rank_top, k))
            pad = part if pad is None else pad + part
        sums.append(pad[:, :rank_top].astype(BF))
    lane = lax.broadcasted_iota(jnp.int32, (rhs, rank_top), 1)
    fields = [jnp.where(lane < ranks_ref[c], total.astype(F32), 0.0) for c, total in enumerate(sums)]
    for i in range(leaves):
        down = fields[i] + dot_t(fields[leaves + i // 2].astype(BF), transfer_ref[i])
        leaf_total = jnp.where(lane < ranks_ref[i], down, 0.0).astype(BF)
        out_ref[i] = (near_ref[i] + dot(leaf_total, basis_ref[i])).astype(BF)
    if coeff_ref:
        emit_coeffs(lambda i: out_ref[i], basis_ref, transfer_ref, ranks_ref, coeff_ref[0], leaves, rank_top)


def params(mebibytes):
    return pltpu.CompilerParams(vmem_limit_bytes=mebibytes << 20)


def local(charges, basis, transfer, near_field, coupling, ranks, block_source, block_target):
    leaves, rank_top, width = basis.shape
    rhs = charges.shape[1]
    clusters = ranks.shape[0]
    blocks = coupling.shape[0]
    devices = lax.axis_size("clu")
    mains = clusters * 3 // 4
    shape = jax.ShapeDtypeStruct

    cores, chips = 2, 4
    planes = devices // (cores * chips)
    half = chips * planes
    plane_groups = [[p * cores * chips + r for p in range(planes)] for r in range(cores * chips)]
    chip_groups = [
        [p * cores * chips + c * cores + k for c in range(chips)] for p in range(planes) for k in range(cores)
    ]

    def exchange(parts, groups):
        return lax.all_to_all(
            parts, "clu", split_axis=0, concat_axis=0, tiled=True, axis_index_groups=groups
        )

    def swap_cores(part):
        return lax.ppermute(part, "clu", [(d, d ^ 1) for d in range(devices)])

    core = lax.axis_index("clu") % cores

    def rows(cluster):
        device = cluster // clusters
        chip, plane = (device // cores) % chips, device // (cores * chips)
        return (((device % cores + core) % cores * chips + chip) * planes + plane) * clusters + cluster % clusters

    source_rows, target_rows = rows(block_source), rows(block_target)

    coeff_shape = shape((planes, mains, rhs, LANES), BF)
    out_shape = shape((leaves, rhs, width), BF)
    half_shape = shape((half, mains, rhs, LANES), BF)
    first_coeffs = pl.pallas_call(
        coeff_kernel,
        out_shape=coeff_shape,
        in_specs=[SMEM, VMEM, VMEM, VMEM],
        out_specs=VMEM,
        compiler_params=params(16),
    )(ranks, charges, basis, transfer)

    couple = pl.pallas_call(
        functools.partial(couple_kernel, unroll=8),
        out_shape=[half_shape, half_shape],
        in_specs=[SMEM, SMEM, VMEM, VMEM, VMEM],
        out_specs=[VMEM, VMEM],
        scratch_shapes=[
            pltpu.VMEM((devices * clusters, rhs, LANES), BF),
            pltpu.VMEM((devices * clusters, rhs, LANES), F32),
        ],
        compiler_params=params(32 if devices <= 32 else 60),
        cost_estimate=pl.CostEstimate(
            flops=2 * blocks * rhs * rank_top * rank_top, bytes_accessed=10 << 20, transcendentals=0
        ),
    )

    near = pl.pallas_call(
        near_kernel,
        out_shape=shape((leaves, rhs, width), F32),
        in_specs=[VMEM] * 4,
        out_specs=VMEM,
        compiler_params=params(16),
        cost_estimate=pl.CostEstimate(
            flops=2 * leaves * 3 * rhs * width * width, bytes_accessed=4 << 20, transcendentals=0
        ),
    )

    def finish(with_coeffs):
        return pl.pallas_call(
            field_kernel,
            out_shape=[out_shape, coeff_shape] if with_coeffs else [out_shape],
            in_specs=[SMEM, VMEM, VMEM, VMEM, VMEM],
            out_specs=[VMEM, VMEM] if with_coeffs else [VMEM],
            compiler_params=params(16),
        )

    ends = devices - 1

    def apply_matrix(field_in, coeffs, with_coeffs):
        column = exchange(coeffs, plane_groups)
        own = exchange(jnp.broadcast_to(column[None], (chips,) + column.shape), chip_groups)
        own = own.reshape(half_shape.shape)
        other = swap_cores(own)
        keep, send = couple(source_rows, target_rows, own, other, coupling)
        chip_sum = keep.astype(F32) + swap_cores(send).astype(F32)
        parts = exchange(chip_sum.astype(BF).reshape(chips, planes, mains, rhs, LANES), chip_groups)
        column_sum = jnp.sum(parts.astype(F32), axis=0).astype(BF)
        terms = exchange(column_sum, plane_groups)
        before = lax.ppermute(field_in[leaves - 1 :], "clu", [(i, i + 1) for i in range(ends)])
        after = lax.ppermute(field_in[:1], "clu", [(i + 1, i) for i in range(ends)])
        near_sum = near(field_in, before, after, near_field)
        return finish(with_coeffs)(ranks, terms, near_sum, basis, transfer)

    first, second_coeffs = apply_matrix(charges, first_coeffs, True)
    (second,) = apply_matrix(first, second_coeffs, False)
    return (first, second)


def solution(mesh):
    in_specs = (
        P("clu", None, None),
        P("clu", None, None),
        P("clu", None, None),
        P("clu", None, None, None),
        P("clu", None, None),
        P("clu"),
        P("clu"),
        P("clu"),
    )
    out_specs = (P("clu", None, None), P("clu", None, None))
    return jax.shard_map(local, mesh=mesh, in_specs=in_specs, out_specs=out_specs, check_vma=False)
```

```python
import functools

import jax
import jax.numpy as jnp
from jax import lax
from jax.experimental import pallas as pl
from jax.experimental.pallas import tpu as pltpu
from jax.sharding import PartitionSpec as P

LANES = 128
BF = jnp.bfloat16
F32 = jnp.float32
VMEM = pl.BlockSpec(memory_space=pltpu.VMEM)
SMEM = pl.BlockSpec(memory_space=pltpu.SMEM)
HBM = pl.BlockSpec(memory_space=pltpu.HBM)


def dot(a, b):
    return lax.dot_general(a, b, (((1,), (0,)), ((), ())), preferred_element_type=F32)


def dot_t(a, b):
    return lax.dot_general(a, b, (((1,), (1,)), ((), ())), preferred_element_type=F32)


def lanes(rows):
    return lax.broadcasted_iota(jnp.int32, (rows, LANES), 1)


def fourth(tiles, rank_top):
    third = LANES - rank_top
    lane = lanes(tiles[0].shape[0])
    moved = [pltpu.roll(tile, third * (k + 1), 1) for k, tile in enumerate(tiles)]
    return jnp.where(lane < third, moved[0], jnp.where(lane < 2 * third, moved[1], moved[2]))


def packed(mains, pad, rank_top):
    lane = lanes(pad.shape[0])
    third = LANES - rank_top
    return [
        jnp.where(lane < rank_top, main, pltpu.roll(pad, rank_top - third * k, 1)) for k, main in enumerate(mains)
    ]


def widen(value):
    return jnp.concatenate([value, jnp.zeros((value.shape[0], LANES - value.shape[1]), value.dtype)], axis=1)


def emit_coeffs(read_leaf, basis_ref, transfer_ref, ranks_ref, out_ref, leaves, rank_top):
    mains, rhs, _ = out_ref.shape
    lane = lax.broadcasted_iota(jnp.int32, (rhs, rank_top), 1)
    coeffs = []
    for i in range(leaves):
        value = dot_t(read_leaf(i), basis_ref[i])
        coeffs.append(jnp.where(lane < ranks_ref[i], value, 0.0).astype(BF))
    for q in range(leaves // 2):
        value = dot(coeffs[2 * q], transfer_ref[2 * q]) + dot(coeffs[2 * q + 1], transfer_ref[2 * q + 1])
        coeffs.append(jnp.where(lane < ranks_ref[leaves + q], value, 0.0).astype(BF))
    wide = [widen(value.astype(F32)) for value in coeffs]
    for q in range(mains // 3):
        for k, tile in enumerate(packed(wide[3 * q : 3 * q + 3], wide[mains + q], rank_top)):
            out_ref[3 * q + k] = tile.astype(BF)


def fetch(pairs, sems):
    copies = [pltpu.make_async_copy(src, dst, sems.at[n]) for n, (src, dst) in enumerate(pairs)]
    for copy in copies:
        copy.start()
    return copies


def coeff_kernel(ranks_ref, v_hbm, basis_hbm, transfer_hbm, out_ref, v_ref, basis_ref, transfer_ref, sems):
    leaves, rank_top, _ = basis_ref.shape
    for copy in fetch([(v_hbm, v_ref), (basis_hbm, basis_ref), (transfer_hbm, transfer_ref)], sems):
        copy.wait()
    emit_coeffs(lambda i: v_ref[i], basis_ref, transfer_ref, ranks_ref, out_ref, leaves, rank_top)


def couple_kernel(source_ref, target_ref, own_ref, other_ref, coupling_ref, keep_ref, send_ref, sources, total, *, unroll):
    blocks, rank_top, _ = coupling_ref.shape
    devices, mains, rhs, _ = own_ref.shape
    quads = mains // 3
    clusters = mains + quads

    def split(d, _):
        for half, packed_ref in enumerate((own_ref, other_ref)):
            row = (half * devices + d) * clusters
            tiles = [packed_ref[d, c] for c in range(mains)]
            for c in range(mains):
                sources[row + c] = tiles[c]
            for q in range(quads):
                wide = [tile.astype(F32) for tile in tiles[3 * q : 3 * q + 3]]
                sources[row + mains + q] = fourth(wide, rank_top).astype(BF)
            for c in range(clusters):
                total[row + c] = jnp.zeros((rhs, LANES), F32)
        return 0

    lax.fori_loop(0, devices, split, 0, unroll=2)

    def some(s, _):
        for u in range(unroll):
            j = s * unroll + u
            term = dot(sources[source_ref[j], :, :rank_top], coupling_ref[j])
            at = target_ref[j]
            total[at, :, :rank_top] = total[at, :, :rank_top] + term
        return 0

    lax.fori_loop(0, blocks // unroll, some, 0)

    def pack(d, _):
        for half, packed_ref in enumerate((keep_ref, send_ref)):
            row = (half * devices + d) * clusters
            for q in range(quads):
                mains_now = [total[row + 3 * q + k] for k in range(3)]
                for k, tile in enumerate(packed(mains_now, total[row + mains + q], rank_top)):
                    packed_ref[d, 3 * q + k] = tile.astype(BF)
        return 0

    lax.fori_loop(0, devices, pack, 0, unroll=2)


def near_kernel(v_ref, before_ref, after_ref, near_ref, out_ref):
    leaves = v_ref.shape[0]
    for i in range(leaves):
        left = v_ref[i - 1] if i > 0 else before_ref[0]
        right = v_ref[i + 1] if i < leaves - 1 else after_ref[0]
        out_ref[i] = dot(left, near_ref[i, 0]) + dot(v_ref[i], near_ref[i, 1]) + dot(right, near_ref[i, 2])


def sum_kernel(parts_ref, keep_ref, send_ref):
    parts, far, mains, _, _ = parts_ref.shape
    for f in range(far):
        for t in range(mains):
            tile = parts_ref[0, f, t].astype(F32)
            for p in range(1, parts):
                tile = tile + parts_ref[p, f, t].astype(F32)
            if f == 0:
                keep_ref[t] = tile
            else:
                send_ref[f - 1, t] = tile.astype(BF)


def field_kernel(ranks_ref, keep_ref, terms_ref, near_hbm, basis_hbm, transfer_hbm, out_ref, *rest):
    *coeff_ref, near_ref, basis_ref, transfer_ref, sems = rest
    copies = fetch([(transfer_hbm, transfer_ref), (basis_hbm, basis_ref), (near_hbm, near_ref)], sems)
    leaves, rank_top, _ = basis_ref.shape
    parts, mains, rhs, _ = terms_ref.shape
    tiles = []
    for t in range(mains):
        tile = keep_ref[t]
        for p in range(parts):
            tile = tile + terms_ref[p, t].astype(F32)
        tiles.append(tile)
    sums = tiles + [fourth(tiles[3 * q : 3 * q + 3], rank_top) for q in range(mains // 3)]
    lane = lax.broadcasted_iota(jnp.int32, (rhs, rank_top), 1)
    fields = [
        jnp.where(lane < ranks_ref[c], total[:, :rank_top], 0.0).astype(BF) for c, total in enumerate(sums)
    ]
    for copy in copies:
        copy.wait()
    for i in range(leaves):
        down = fields[i].astype(F32) + dot_t(fields[leaves + i // 2], transfer_ref[i])
        leaf_total = jnp.where(lane < ranks_ref[i], down, 0.0).astype(BF)
        out_ref[i] = (near_ref[i] + dot(leaf_total, basis_ref[i])).astype(BF)
    if coeff_ref:
        emit_coeffs(lambda i: out_ref[i], basis_ref, transfer_ref, ranks_ref, coeff_ref[0], leaves, rank_top)


def params(mebibytes):
    return pltpu.CompilerParams(vmem_limit_bytes=mebibytes << 20)


def local(charges, basis, transfer, near_field, coupling, ranks, block_source, block_target):
    leaves, rank_top, width = basis.shape
    rhs = charges.shape[1]
    clusters = ranks.shape[0]
    blocks = coupling.shape[0]
    devices = lax.axis_size("clu")
    mains = clusters * 3 // 4
    shape = jax.ShapeDtypeStruct

    cores, chips = 2, 8
    cube = cores * chips
    far = devices // cube
    half = chips * far
    cube_groups = [[f * cube + q * cores + k for q in range(chips)] for f in range(far) for k in range(cores)]

    def exchange(parts):
        return lax.all_to_all(
            parts, "clu", split_axis=0, concat_axis=0, tiled=True, axis_index_groups=cube_groups
        )

    def swap_far(part, shift):
        return lax.ppermute(part, "clu", [(d, (d + shift * cube) % devices) for d in range(devices)])

    def swap_cores(part):
        return lax.ppermute(part, "clu", [(d, d ^ 1) for d in range(devices)])

    me = lax.axis_index("clu")

    def rows(cluster, sign):
        device = cluster // clusters
        core = (device + me) % cores
        chip = (device // cores) % chips
        away = (sign * (device // cube - me // cube)) % far
        return ((core * chips + chip) * far + away) * clusters + cluster % clusters

    source_rows, target_rows = rows(block_source, -1), rows(block_target, 1)

    tile_shape = (mains, rhs, LANES)
    out_shape = shape((leaves, rhs, width), BF)
    half_shape = shape((half,) + tile_shape, BF)
    weights = [pltpu.VMEM(basis.shape, BF), pltpu.VMEM(transfer.shape, BF), pltpu.SemaphoreType.DMA((3,))]
    first_coeffs = pl.pallas_call(
        coeff_kernel,
        out_shape=shape(tile_shape, BF),
        in_specs=[SMEM, HBM, HBM, HBM],
        out_specs=VMEM,
        scratch_shapes=[pltpu.VMEM(charges.shape, BF)] + weights,
        compiler_params=params(16),
    )(ranks, charges, basis, transfer)

    couple = pl.pallas_call(
        functools.partial(couple_kernel, unroll=8),
        out_shape=[half_shape, half_shape],
        in_specs=[SMEM, SMEM, VMEM, VMEM, VMEM],
        out_specs=[VMEM, VMEM],
        scratch_shapes=[
            pltpu.VMEM((devices * clusters, rhs, LANES), BF),
            pltpu.VMEM((devices * clusters, rhs, LANES), F32),
        ],
        compiler_params=params(32 if devices <= 32 else 60),
        cost_estimate=pl.CostEstimate(
            flops=2 * blocks * rhs * rank_top * rank_top, bytes_accessed=10 << 20, transcendentals=0
        ),
    )

    near = pl.pallas_call(
        near_kernel,
        out_shape=shape((leaves, rhs, width), F32),
        in_specs=[VMEM] * 4,
        out_specs=VMEM,
        compiler_params=params(16),
        cost_estimate=pl.CostEstimate(
            flops=2 * leaves * 3 * rhs * width * width, bytes_accessed=4 << 20, transcendentals=0
        ),
    )

    add_parts = pl.pallas_call(
        sum_kernel,
        out_shape=[shape(tile_shape, F32), shape((far - 1,) + tile_shape, BF)],
        in_specs=[VMEM],
        out_specs=[VMEM, VMEM],
        compiler_params=params(16),
    )

    def finish(with_coeffs):
        return pl.pallas_call(
            field_kernel,
            out_shape=[out_shape, shape(tile_shape, BF)] if with_coeffs else [out_shape],
            in_specs=[SMEM, VMEM, VMEM, HBM, HBM, HBM],
            out_specs=[VMEM, VMEM] if with_coeffs else [VMEM],
            scratch_shapes=[pltpu.VMEM((leaves, rhs, width), F32)] + weights,
            compiler_params=params(16),
        )

    ends = devices - 1

    def apply_matrix(field_in, coeffs, with_coeffs):
        column = jnp.stack([coeffs] + [swap_far(coeffs, s) for s in range(1, far)])
        own = exchange(jnp.broadcast_to(column[None], (chips,) + column.shape))
        before = lax.ppermute(field_in[leaves - 1 :], "clu", [(i, i + 1) for i in range(ends)])
        after = lax.ppermute(field_in[:1], "clu", [(i + 1, i) for i in range(ends)])
        near_sum = near(field_in, before, after, near_field)
        own, near_sum = lax.optimization_barrier((own, near_sum))
        own = own.reshape(half_shape.shape)
        other = swap_cores(own)
        keep, send = couple(source_rows, target_rows, own, other, coupling)
        chip_sum = keep.astype(F32) + swap_cores(send).astype(F32)
        parts = exchange(chip_sum.astype(BF).reshape((chips, far) + tile_shape))
        mine, away = add_parts(parts)
        terms = jnp.concatenate([swap_far(away[s - 1 : s], s) for s in range(1, far)])
        return finish(with_coeffs)(ranks, mine, terms, near_sum, basis, transfer)

    first, second_coeffs = apply_matrix(charges, first_coeffs, True)
    (second,) = apply_matrix(first, second_coeffs, False)
    return (first, second)


def solution(mesh):
    in_specs = (
        P("clu", None, None),
        P("clu", None, None),
        P("clu", None, None),
        P("clu", None, None, None),
        P("clu", None, None),
        P("clu"),
        P("clu"),
        P("clu"),
    )
    out_specs = (P("clu", None, None), P("clu", None, None))
    return jax.shard_map(local, mesh=mesh, in_specs=in_specs, out_specs=out_specs, check_vma=False)
```

```python
import functools

import jax
import jax.numpy as jnp
from jax import lax
from jax.experimental import pallas as pl
from jax.experimental.pallas import tpu as pltpu
from jax.sharding import PartitionSpec as P

LANES = 128
BF = jnp.bfloat16
F32 = jnp.float32
VMEM = pl.BlockSpec(memory_space=pltpu.VMEM)
SMEM = pl.BlockSpec(memory_space=pltpu.SMEM)
HBM = pl.BlockSpec(memory_space=pltpu.HBM)


def dot(a, b):
    return lax.dot_general(a, b, (((1,), (0,)), ((), ())), preferred_element_type=F32)


def dot_t(a, b):
    return lax.dot_general(a, b, (((1,), (1,)), ((), ())), preferred_element_type=F32)


def lanes(rows):
    return lax.broadcasted_iota(jnp.int32, (rows, LANES), 1)


def fourth(tiles, rank_top):
    third = LANES - rank_top
    lane = lanes(tiles[0].shape[0])
    moved = [pltpu.roll(tile, third * (k + 1), 1) for k, tile in enumerate(tiles)]
    return jnp.where(lane < third, moved[0], jnp.where(lane < 2 * third, moved[1], moved[2]))


def packed(mains, pad, rank_top):
    lane = lanes(pad.shape[0])
    third = LANES - rank_top
    return [
        jnp.where(lane < rank_top, main, pltpu.roll(pad, rank_top - third * k, 1)) for k, main in enumerate(mains)
    ]


def widen(value):
    return jnp.concatenate([value, jnp.zeros((value.shape[0], LANES - value.shape[1]), value.dtype)], axis=1)


def emit_coeffs(read_leaf, basis_ref, transfer_ref, ranks_ref, out_ref, leaves, rank_top):
    copies, mains, rhs, _ = out_ref.shape
    lane = lax.broadcasted_iota(jnp.int32, (rhs, rank_top), 1)
    coeffs = []
    for i in range(leaves):
        value = dot_t(read_leaf(i), basis_ref[i])
        coeffs.append(jnp.where(lane < ranks_ref[i], value, 0.0).astype(BF))
    for q in range(leaves // 2):
        value = dot(coeffs[2 * q], transfer_ref[2 * q]) + dot(coeffs[2 * q + 1], transfer_ref[2 * q + 1])
        coeffs.append(jnp.where(lane < ranks_ref[leaves + q], value, 0.0).astype(BF))
    wide = [widen(value.astype(F32)) for value in coeffs]
    for q in range(mains // 3):
        for k, tile in enumerate(packed(wide[3 * q : 3 * q + 3], wide[mains + q], rank_top)):
            tile = tile.astype(BF)
            for c in range(copies):
                out_ref[c, 3 * q + k] = tile


def fetch(pairs, sems):
    copies = [pltpu.make_async_copy(src, dst, sems.at[n]) for n, (src, dst) in enumerate(pairs)]
    for copy in copies:
        copy.start()
    return copies


def coeff_kernel(ranks_ref, v_hbm, basis_hbm, transfer_hbm, out_ref, v_ref, basis_ref, transfer_ref, sems):
    leaves, rank_top, _ = basis_ref.shape
    for copy in fetch([(v_hbm, v_ref), (basis_hbm, basis_ref), (transfer_hbm, transfer_ref)], sems):
        copy.wait()
    emit_coeffs(lambda i: v_ref[i], basis_ref, transfer_ref, ranks_ref, out_ref, leaves, rank_top)


def couple_kernel(source_ref, target_ref, coupling_ref, *refs, sets, unroll):
    in_refs, out_refs, (sources, total) = refs[:sets], refs[sets : 2 * sets], refs[2 * sets :]
    blocks, rank_top, _ = coupling_ref.shape
    chips, mains, rhs, _ = in_refs[0].shape
    quads = mains // 3
    clusters = mains + quads

    def split(d, _):
        for n, packed_ref in enumerate(in_refs):
            row = (n * chips + d) * clusters
            tiles = [packed_ref[d, c] for c in range(mains)]
            for c in range(mains):
                sources[row + c] = tiles[c]
            for q in range(quads):
                wide = [tile.astype(F32) for tile in tiles[3 * q : 3 * q + 3]]
                sources[row + mains + q] = fourth(wide, rank_top).astype(BF)
            for c in range(clusters):
                total[row + c] = jnp.zeros((rhs, LANES), F32)
        return 0

    lax.fori_loop(0, chips, split, 0)

    def some(s, _):
        for u in range(unroll):
            j = s * unroll + u
            term = dot(sources[source_ref[j], :, :rank_top], coupling_ref[j])
            at = target_ref[j]
            total[at, :, :rank_top] = total[at, :, :rank_top] + term
        return 0

    lax.fori_loop(0, blocks // unroll, some, 0)

    def pack(d, _):
        for n, packed_ref in enumerate(out_refs):
            row = (n * chips + d) * clusters
            for q in range(quads):
                mains_now = [total[row + 3 * q + k] for k in range(3)]
                for k, tile in enumerate(packed(mains_now, total[row + mains + q], rank_top)):
                    packed_ref[d, 3 * q + k] = tile.astype(BF)
        return 0

    lax.fori_loop(0, chips, pack, 0)


def near_kernel(v_ref, near_ref, out_ref):
    leaves = v_ref.shape[0]
    for i in range(leaves):
        total = dot(v_ref[i], near_ref[i, 1])
        if i > 0:
            total = total + dot(v_ref[i - 1], near_ref[i, 0])
        if i < leaves - 1:
            total = total + dot(v_ref[i + 1], near_ref[i, 2])
        out_ref[i] = total


def edge_kernel(before_ref, after_ref, first_ref, last_ref, out_ref):
    out_ref[0] = dot(before_ref[0], first_ref[0, 0])
    out_ref[1] = dot(after_ref[0], last_ref[0, 0])


def part_sum(parts_ref, t):
    tile = parts_ref[0, t].astype(F32)
    for p in range(1, parts_ref.shape[0]):
        tile = tile + parts_ref[p, t].astype(F32)
    return tile


def sum_kernel(parts_ref, out_ref):
    for t in range(out_ref.shape[0]):
        out_ref[t] = part_sum(parts_ref, t).astype(BF)


def copy_kernel(in_ref, out_ref):
    for t in range(in_ref.shape[0]):
        tile = in_ref[t]
        for c in range(out_ref.shape[0]):
            out_ref[c, t] = tile


def field_kernel(ranks_ref, near_ref, edge_ref, basis_ref, transfer_ref, parts_ref, *rest, away):
    term_refs, out_ref, coeff_ref = rest[:away], rest[away], rest[away + 1 :]
    leaves, rank_top, _ = basis_ref.shape
    _, mains, rhs, _ = parts_ref.shape
    tiles = []
    for t in range(mains):
        tile = part_sum(parts_ref, t)
        for term_ref in term_refs:
            tile = tile + term_ref[t].astype(F32)
        tiles.append(tile)
    sums = tiles + [fourth(tiles[3 * q : 3 * q + 3], rank_top) for q in range(mains // 3)]
    lane = lax.broadcasted_iota(jnp.int32, (rhs, rank_top), 1)
    fields = [
        jnp.where(lane < ranks_ref[c], total[:, :rank_top], 0.0).astype(BF) for c, total in enumerate(sums)
    ]
    for i in range(leaves):
        down = fields[i].astype(F32) + dot_t(fields[leaves + i // 2], transfer_ref[i])
        leaf_total = jnp.where(lane < ranks_ref[i], down, 0.0).astype(BF)
        result = near_ref[i] + dot(leaf_total, basis_ref[i])
        if i == 0:
            result = result + edge_ref[0]
        if i == leaves - 1:
            result = result + edge_ref[1]
        out_ref[i] = result.astype(BF)
    if coeff_ref:
        emit_coeffs(lambda i: out_ref[i], basis_ref, transfer_ref, ranks_ref, coeff_ref[0], leaves, rank_top)


def params(mebibytes):
    return pltpu.CompilerParams(vmem_limit_bytes=mebibytes << 20)


def local(charges, basis, transfer, near_field, coupling, ranks, block_source, block_target):
    leaves, rank_top, width = basis.shape
    rhs = charges.shape[1]
    clusters = ranks.shape[0]
    blocks = coupling.shape[0]
    devices = lax.axis_size("clu")
    mains = clusters * 3 // 4
    shape = jax.ShapeDtypeStruct

    cores, chips = 2, 8
    cube = cores * chips
    far = devices // cube
    half = chips * far
    cube_groups = [[f * cube + q * cores + k for q in range(chips)] for f in range(far) for k in range(cores)]

    def exchange(parts):
        return lax.all_to_all(
            parts, "clu", split_axis=0, concat_axis=0, tiled=True, axis_index_groups=cube_groups
        )

    def swap_far(part, shift):
        return lax.ppermute(part, "clu", [(d, (d + shift * cube) % devices) for d in range(devices)])

    def swap_cores(part):
        return lax.ppermute(part, "clu", [(d, d ^ 1) for d in range(devices)])

    me = lax.axis_index("clu")

    def rows(cluster, sign):
        device = cluster // clusters
        core = (device + me) % cores
        chip = (device // cores) % chips
        away = (sign * (device // cube - me // cube)) % far
        return ((core * far + away) * chips + chip) * clusters + cluster % clusters

    source_rows, target_rows = rows(block_source, -1), rows(block_target, 1)

    tile_shape = (mains, rhs, LANES)
    out_shape = shape((leaves, rhs, width), BF)
    part_shape = shape((chips,) + tile_shape, BF)
    first_coeffs = pl.pallas_call(
        coeff_kernel,
        out_shape=part_shape,
        in_specs=[SMEM, HBM, HBM, HBM],
        out_specs=VMEM,
        scratch_shapes=[
            pltpu.VMEM(charges.shape, BF),
            pltpu.VMEM(basis.shape, BF),
            pltpu.VMEM(transfer.shape, BF),
            pltpu.SemaphoreType.DMA((3,)),
        ],
    )(ranks, charges, basis, transfer)

    sets = cores * far
    couple = pl.pallas_call(
        functools.partial(couple_kernel, sets=sets, unroll=8),
        out_shape=[part_shape] * sets,
        in_specs=[SMEM, SMEM, VMEM] + [VMEM] * sets,
        out_specs=[VMEM] * sets,
        scratch_shapes=[
            pltpu.VMEM((devices * clusters, rhs, LANES), BF),
            pltpu.VMEM((devices * clusters, rhs, LANES), F32),
        ],
        compiler_params=params(32 if devices <= 32 else 60),
        cost_estimate=pl.CostEstimate(
            flops=2 * blocks * rhs * rank_top * rank_top, bytes_accessed=10 << 20, transcendentals=0
        ),
    )

    near = pl.pallas_call(
        near_kernel,
        out_shape=shape((leaves, rhs, width), F32),
        in_specs=[VMEM] * 2,
        out_specs=VMEM,
        compiler_params=params(16),
        cost_estimate=pl.CostEstimate(
            flops=2 * leaves * 3 * rhs * width * width, bytes_accessed=4 << 20, transcendentals=0
        ),
    )

    edge = pl.pallas_call(
        edge_kernel,
        out_shape=shape((2, rhs, width), F32),
        grid=(1,),
        in_specs=[
            VMEM,
            VMEM,
            pl.BlockSpec((1, 1, width, width), lambda i: (0, 0, 0, 0)),
            pl.BlockSpec((1, 1, width, width), lambda i: (leaves - 1, 2, 0, 0)),
        ],
        out_specs=VMEM,
        compiler_params=params(16),
    )

    add_parts = pl.pallas_call(
        sum_kernel, out_shape=shape(tile_shape, BF), in_specs=[VMEM], out_specs=VMEM, compiler_params=params(16)
    )
    copies = pl.pallas_call(
        copy_kernel, out_shape=part_shape, in_specs=[VMEM], out_specs=VMEM, compiler_params=params(16)
    )

    def finish(with_coeffs):
        return pl.pallas_call(
            functools.partial(field_kernel, away=far - 1),
            out_shape=[out_shape, part_shape] if with_coeffs else [out_shape],
            in_specs=[SMEM] + [VMEM] * (4 + far),
            out_specs=[VMEM, VMEM] if with_coeffs else [VMEM],
            compiler_params=params(16),
        )

    ends = devices - 1

    def apply_matrix(field_in, coeffs, with_coeffs):
        away = [swap_far(coeffs[0], s) for s in range(1, far)]
        before = lax.ppermute(field_in[leaves - 1 :], "clu", [(i, i + 1) for i in range(ends)])
        after = lax.ppermute(field_in[:1], "clu", [(i + 1, i) for i in range(ends)])
        own = [exchange(coeffs)]
        own += [exchange(copies(part)) for part in away]
        near_sum = near(field_in, near_field)
        edges = edge(before, after, near_field, near_field)
        own[-1], near_sum, edges = lax.optimization_barrier((own[-1], near_sum, edges))
        other = [swap_cores(part) for part in own]
        totals = couple(source_rows, target_rows, coupling, *own, *other)
        terms = []
        for s in list(range(1, far)) + [0]:
            chip_sum = totals[s].astype(F32) + swap_cores(totals[far + s]).astype(F32)
            parts = exchange(chip_sum.astype(BF))
            if s:
                terms.append(swap_far(add_parts(parts), s))
        return finish(with_coeffs)(ranks, near_sum, edges, basis, transfer, parts, *terms)

    first, second_coeffs = apply_matrix(charges, first_coeffs, True)
    (second,) = apply_matrix(first, second_coeffs, False)
    return (first, second)


def solution(mesh):
    in_specs = (
        P("clu", None, None),
        P("clu", None, None),
        P("clu", None, None),
        P("clu", None, None, None),
        P("clu", None, None),
        P("clu"),
        P("clu"),
        P("clu"),
    )
    out_specs = (P("clu", None, None), P("clu", None, None))
    return jax.shard_map(local, mesh=mesh, in_specs=in_specs, out_specs=out_specs, check_vma=False)
```

```python
import functools

import jax
import jax.numpy as jnp
from jax import lax
from jax.experimental import pallas as pl
from jax.experimental.pallas import tpu as pltpu
from jax.sharding import PartitionSpec as P

LANES = 128
BF = jnp.bfloat16
F32 = jnp.float32
VMEM = pl.BlockSpec(memory_space=pltpu.VMEM)
SMEM = pl.BlockSpec(memory_space=pltpu.SMEM)
HBM = pl.BlockSpec(memory_space=pltpu.HBM)


def dot(a, b):
    return lax.dot_general(a, b, (((1,), (0,)), ((), ())), preferred_element_type=F32)


def dot_t(a, b):
    return lax.dot_general(a, b, (((1,), (1,)), ((), ())), preferred_element_type=F32)


def lanes(rows):
    return lax.broadcasted_iota(jnp.int32, (rows, LANES), 1)


def fourth(tiles, rank_top):
    third = LANES - rank_top
    lane = lanes(tiles[0].shape[0])
    moved = [pltpu.roll(tile, third * (k + 1), 1) for k, tile in enumerate(tiles)]
    return jnp.where(lane < third, moved[0], jnp.where(lane < 2 * third, moved[1], moved[2]))


def packed(mains, pad, rank_top):
    lane = lanes(pad.shape[0])
    third = LANES - rank_top
    return [
        jnp.where(lane < rank_top, main, pltpu.roll(pad, rank_top - third * k, 1)) for k, main in enumerate(mains)
    ]


def widen(value):
    return jnp.concatenate([value, jnp.zeros((value.shape[0], LANES - value.shape[1]), value.dtype)], axis=1)


def emit_coeffs(read_leaf, basis_ref, transfer_ref, ranks_ref, out_ref, leaves, rank_top):
    mains, rhs, _ = out_ref.shape
    lane = lax.broadcasted_iota(jnp.int32, (rhs, rank_top), 1)
    coeffs = []
    for i in range(leaves):
        value = dot_t(read_leaf(i), basis_ref[i])
        coeffs.append(jnp.where(lane < ranks_ref[i], value, 0.0).astype(BF))
    for q in range(leaves // 2):
        value = dot(coeffs[2 * q], transfer_ref[2 * q]) + dot(coeffs[2 * q + 1], transfer_ref[2 * q + 1])
        coeffs.append(jnp.where(lane < ranks_ref[leaves + q], value, 0.0).astype(BF))
    wide = [widen(value.astype(F32)) for value in coeffs]
    for q in range(mains // 3):
        for k, tile in enumerate(packed(wide[3 * q : 3 * q + 3], wide[mains + q], rank_top)):
            out_ref[3 * q + k] = tile.astype(BF)


def fetch(pairs, sems):
    copies = [pltpu.make_async_copy(src, dst, sems.at[n]) for n, (src, dst) in enumerate(pairs)]
    for copy in copies:
        copy.start()
    return copies


def coeff_kernel(ranks_ref, v_hbm, basis_hbm, transfer_hbm, out_ref, v_ref, basis_ref, transfer_ref, sems):
    leaves, rank_top, _ = basis_ref.shape
    for copy in fetch([(v_hbm, v_ref), (basis_hbm, basis_ref), (transfer_hbm, transfer_ref)], sems):
        copy.wait()
    emit_coeffs(lambda i: v_ref[i], basis_ref, transfer_ref, ranks_ref, out_ref, leaves, rank_top)


def couple_kernel(source_ref, target_ref, coupling_ref, *refs, order, unroll):
    chips = sum(len(group) for group in order)
    in_refs, out_refs, (sources, total) = refs[: 2 * chips], refs[2 * chips : -2], refs[-2:]
    blocks, rank_top, _ = coupling_ref.shape
    far, mains, rhs, _ = in_refs[0].shape
    quads = mains // 3
    clusters = mains + quads

    def split(f, _):
        for n, packed_ref in enumerate(in_refs):
            row = (n * far + f) * clusters
            tiles = [packed_ref[f, c] for c in range(mains)]
            for c in range(mains):
                sources[row + c] = tiles[c]
            for q in range(quads):
                wide = [tile.astype(F32) for tile in tiles[3 * q : 3 * q + 3]]
                sources[row + mains + q] = fourth(wide, rank_top).astype(BF)
            for c in range(clusters):
                total[row + c] = jnp.zeros((rhs, LANES), F32)
        return 0

    lax.fori_loop(0, far, split, 0)

    def some(s, _):
        for u in range(unroll):
            j = s * unroll + u
            term = dot(sources[source_ref[j], :, :rank_top], coupling_ref[j])
            at = target_ref[j]
            total[at, :, :rank_top] = total[at, :, :rank_top] + term
        return 0

    lax.fori_loop(0, blocks // unroll, some, 0)

    def pack(f, _):
        for core in range(2):
            for g, group in enumerate(order):
                for place, chip in enumerate(group):
                    row = ((core * chips + chip) * far + f) * clusters
                    for q in range(quads):
                        mains_now = [total[row + 3 * q + k] for k in range(3)]
                        for k, tile in enumerate(packed(mains_now, total[row + mains + q], rank_top)):
                            out_refs[core * len(order) + g][place, f, 3 * q + k] = tile.astype(BF)
        return 0

    lax.fori_loop(0, far, pack, 0)


def near_kernel(v_ref, near_ref, out_ref):
    leaves = v_ref.shape[0]
    for i in range(leaves):
        total = dot(v_ref[i], near_ref[i, 1])
        if i > 0:
            total = total + dot(v_ref[i - 1], near_ref[i, 0])
        if i < leaves - 1:
            total = total + dot(v_ref[i + 1], near_ref[i, 2])
        out_ref[i] = total


def edge_kernel(before_ref, after_ref, first_ref, last_ref, out_ref):
    out_ref[0] = dot(before_ref[0], first_ref[0, 0])
    out_ref[1] = dot(after_ref[0], last_ref[0, 0])


def first_add_kernel(keep_ref, swap_ref, *out_refs):
    for n, out_ref in enumerate(out_refs):
        out_ref[...] = (keep_ref[n].astype(F32) + swap_ref[n].astype(F32)).astype(BF)


def second_add_kernel(keep_ref, swap_ref, y_ref, z_ref, own_out, y_out, z_out):
    own_out[...] = keep_ref[0].astype(F32) + swap_ref[0].astype(F32)
    for n, part_ref, out_ref in ((2, y_ref, y_out), (3, z_ref, z_out)):
        total = keep_ref[n].astype(F32) + swap_ref[n].astype(F32) + part_ref[...].astype(F32)
        out_ref[...] = total.astype(BF)


def third_add_kernel(keep_ref, swap_ref, x_ref, x_out):
    total = keep_ref[1].astype(F32) + swap_ref[1].astype(F32) + x_ref[...].astype(F32)
    x_out[...] = total.astype(BF)


def last_add_kernel(own_ref, x_ref, y_ref, z_ref, keep_out, *away_refs):
    for f in range(own_ref.shape[0]):
        total = own_ref[f] + x_ref[f].astype(F32) + y_ref[f].astype(F32) + z_ref[f].astype(F32)
        if f == 0:
            keep_out[...] = total
        else:
            away_refs[f - 1][...] = total.astype(BF)


def field_kernel(ranks_ref, near_ref, edge_ref, basis_ref, transfer_ref, keep_ref, *rest, away):
    term_refs, out_ref, coeff_ref = rest[:away], rest[away], rest[away + 1 :]
    leaves, rank_top, _ = basis_ref.shape
    mains, rhs, _ = keep_ref.shape
    tiles = []
    for t in range(mains):
        tile = keep_ref[t]
        for term_ref in term_refs:
            tile = tile + term_ref[t].astype(F32)
        tiles.append(tile)
    sums = tiles + [fourth(tiles[3 * q : 3 * q + 3], rank_top) for q in range(mains // 3)]
    lane = lax.broadcasted_iota(jnp.int32, (rhs, rank_top), 1)
    fields = [
        jnp.where(lane < ranks_ref[c], total[:, :rank_top], 0.0).astype(BF) for c, total in enumerate(sums)
    ]
    for i in range(leaves):
        down = fields[i].astype(F32) + dot_t(fields[leaves + i // 2], transfer_ref[i])
        leaf_total = jnp.where(lane < ranks_ref[i], down, 0.0).astype(BF)
        result = near_ref[i] + dot(leaf_total, basis_ref[i])
        if i == 0:
            result = result + edge_ref[0]
        if i == leaves - 1:
            result = result + edge_ref[1]
        out_ref[i] = result.astype(BF)
    if coeff_ref:
        emit_coeffs(lambda i: out_ref[i], basis_ref, transfer_ref, ranks_ref, coeff_ref[0], leaves, rank_top)


def params(mebibytes):
    return pltpu.CompilerParams(vmem_limit_bytes=mebibytes << 20)


def local(charges, basis, transfer, near_field, coupling, ranks, block_source, block_target):
    leaves, rank_top, width = basis.shape
    rhs = charges.shape[1]
    clusters = ranks.shape[0]
    blocks = coupling.shape[0]
    devices = lax.axis_size("clu")
    mains = clusters * 3 // 4
    shape = jax.ShapeDtypeStruct

    cores, chips = 2, 8
    cube = cores * chips
    far = devices // cube
    x, y, z = 1, 2, 4

    def swap_far(part, shift):
        return lax.ppermute(part, "clu", [(d, (d + shift * cube) % devices) for d in range(devices)])

    def swap(part, chip):
        return lax.ppermute(part, "clu", [(d, d ^ chip * cores) for d in range(devices)])

    def swap_cores(part):
        return lax.ppermute(part, "clu", [(d, d ^ 1) for d in range(devices)])

    me = lax.axis_index("clu")

    def rows(cluster, sign):
        device = cluster // clusters
        core = (device ^ me) % cores
        chip = ((device ^ me) // cores) % chips
        away = (sign * (device // cube - me // cube)) % far
        return ((core * chips + chip) * far + away) * clusters + cluster % clusters

    source_rows, target_rows = rows(block_source, -1), rows(block_target, 1)

    tile_shape = (mains, rhs, LANES)
    out_shape = shape((leaves, rhs, width), BF)
    tile_out = shape(tile_shape, BF)
    part_shape = shape((far,) + tile_shape, BF)
    first_coeffs = pl.pallas_call(
        coeff_kernel,
        out_shape=tile_out,
        in_specs=[SMEM, HBM, HBM, HBM],
        out_specs=VMEM,
        scratch_shapes=[
            pltpu.VMEM(charges.shape, BF),
            pltpu.VMEM(basis.shape, BF),
            pltpu.VMEM(transfer.shape, BF),
            pltpu.SemaphoreType.DMA((3,)),
        ],
    )(ranks, charges, basis, transfer)

    order = ((x | y | z, x | y, y | z, z | x), (0, x, y, z))
    couple = pl.pallas_call(
        functools.partial(couple_kernel, order=order, unroll=8),
        out_shape=[shape((4, far) + tile_shape, BF)] * 4,
        in_specs=[SMEM, SMEM, VMEM] + [VMEM] * (cores * chips),
        out_specs=[VMEM] * 4,
        scratch_shapes=[
            pltpu.VMEM((devices * clusters, rhs, LANES), BF),
            pltpu.VMEM((devices * clusters, rhs, LANES), F32),
        ],
        compiler_params=params(32 if devices <= 32 else 60),
        cost_estimate=pl.CostEstimate(
            flops=2 * blocks * rhs * rank_top * rank_top, bytes_accessed=10 << 20, transcendentals=0
        ),
    )

    near = pl.pallas_call(
        near_kernel,
        out_shape=shape((leaves, rhs, width), F32),
        in_specs=[VMEM] * 2,
        out_specs=VMEM,
        compiler_params=params(16),
        cost_estimate=pl.CostEstimate(
            flops=2 * leaves * 3 * rhs * width * width, bytes_accessed=4 << 20, transcendentals=0
        ),
    )

    edge = pl.pallas_call(
        edge_kernel,
        out_shape=shape((2, rhs, width), F32),
        grid=(1,),
        in_specs=[
            VMEM,
            VMEM,
            pl.BlockSpec((1, 1, width, width), lambda i: (0, 0, 0, 0)),
            pl.BlockSpec((1, 1, width, width), lambda i: (leaves - 1, 2, 0, 0)),
        ],
        out_specs=VMEM,
        compiler_params=params(16),
    )

    def adder(kernel, inputs, outputs):
        return pl.pallas_call(
            kernel,
            out_shape=outputs,
            in_specs=[VMEM] * inputs,
            out_specs=[VMEM] * len(outputs),
            compiler_params=params(16),
        )

    own_shape = shape((far,) + tile_shape, F32)
    first_add = adder(first_add_kernel, 2, [part_shape] * 4)
    second_add = adder(second_add_kernel, 4, [own_shape, part_shape, part_shape])
    third_add = adder(third_add_kernel, 3, [part_shape])
    last_add = adder(last_add_kernel, 4, [shape(tile_shape, F32)] + [tile_out] * (far - 1))

    def finish(with_coeffs):
        return pl.pallas_call(
            functools.partial(field_kernel, away=far - 1),
            out_shape=[out_shape, tile_out] if with_coeffs else [out_shape],
            in_specs=[SMEM] + [VMEM] * (4 + far),
            out_specs=[VMEM, VMEM] if with_coeffs else [VMEM],
            compiler_params=params(16),
        )

    ends = devices - 1

    def apply_matrix(field_in, coeffs, with_coeffs):
        got = {0: jnp.stack([coeffs] + [swap_far(coeffs, s) for s in range(1, far)])}
        got[x], got[y], got[z] = lax.optimization_barrier((swap(got[0], x), swap(got[0], y), swap(got[0], z)))
        got[x | y], got[y | z], got[z | x] = swap(got[x], y), swap(got[y], z), swap(got[z], x)
        got[x | y | z] = swap(got[x | y], z)
        before = lax.ppermute(field_in[leaves - 1 :], "clu", [(i, i + 1) for i in range(ends)])
        after = lax.ppermute(field_in[:1], "clu", [(i + 1, i) for i in range(ends)])
        near_sum = near(field_in, near_field)
        edges = edge(before, after, near_field, near_field)
        got[7], near_sum, edges = lax.optimization_barrier((got[7], near_sum, edges))
        own = [got[chip] for chip in range(chips)]
        other = [swap_cores(part) for part in own]
        keep_first, keep, send_first, send = couple(source_rows, target_rows, coupling, *own, *other)
        far_corner, xy, yz, zx = first_add(keep_first, swap_cores(send_first))
        swapped = swap_cores(send)
        yz, zx = swap(yz, z), swap(zx, x)
        xy = (xy.astype(F32) + swap(far_corner, z).astype(F32)).astype(BF)
        xy = swap(xy, y)
        mine, to_y, to_z = second_add(keep, swapped, yz, zx)
        (to_x,) = third_add(keep, swapped, xy)
        total, *away = last_add(mine, swap(to_x, x), swap(to_y, y), swap(to_z, z))
        terms = [swap_far(part, s + 1) for s, part in enumerate(away)]
        return finish(with_coeffs)(ranks, near_sum, edges, basis, transfer, total, *terms)

    first, second_coeffs = apply_matrix(charges, first_coeffs, True)
    (second,) = apply_matrix(first, second_coeffs, False)
    return (first, second)


def solution(mesh):
    in_specs = (
        P("clu", None, None),
        P("clu", None, None),
        P("clu", None, None),
        P("clu", None, None, None),
        P("clu", None, None),
        P("clu"),
        P("clu"),
        P("clu"),
    )
    out_specs = (P("clu", None, None), P("clu", None, None))
    return jax.shard_map(local, mesh=mesh, in_specs=in_specs, out_specs=out_specs, check_vma=False)
```

```python
import functools

import jax
import jax.numpy as jnp
from jax import lax
from jax.experimental import pallas as pl
from jax.experimental.pallas import tpu as pltpu
from jax.sharding import PartitionSpec as P

LANES = 128
BF = jnp.bfloat16
F32 = jnp.float32
VMEM = pl.BlockSpec(memory_space=pltpu.VMEM)
SMEM = pl.BlockSpec(memory_space=pltpu.SMEM)
HBM = pl.BlockSpec(memory_space=pltpu.HBM)


def dot(a, b):
    return lax.dot_general(a, b, (((1,), (0,)), ((), ())), preferred_element_type=F32)


def dot_t(a, b):
    return lax.dot_general(a, b, (((1,), (1,)), ((), ())), preferred_element_type=F32)


def lanes(rows):
    return lax.broadcasted_iota(jnp.int32, (rows, LANES), 1)


def fourth(tiles, rank_top):
    third = LANES - rank_top
    lane = lanes(tiles[0].shape[0])
    moved = [pltpu.roll(tile, third * (k + 1), 1) for k, tile in enumerate(tiles)]
    return jnp.where(lane < third, moved[0], jnp.where(lane < 2 * third, moved[1], moved[2]))


def packed(mains, pad, rank_top):
    lane = lanes(pad.shape[0])
    third = LANES - rank_top
    return [
        jnp.where(lane < rank_top, main, pltpu.roll(pad, rank_top - third * k, 1)) for k, main in enumerate(mains)
    ]


def widen(value):
    return jnp.concatenate([value, jnp.zeros((value.shape[0], LANES - value.shape[1]), value.dtype)], axis=1)


def emit_coeffs(read_leaf, basis_ref, transfer_ref, ranks_ref, out_ref, leaves, rank_top):
    mains, rhs, _ = out_ref.shape
    lane = lax.broadcasted_iota(jnp.int32, (rhs, rank_top), 1)
    coeffs = []
    for i in range(leaves):
        value = dot_t(read_leaf(i), basis_ref[i])
        coeffs.append(jnp.where(lane < ranks_ref[i], value, 0.0).astype(BF))
    for q in range(leaves // 2):
        value = dot(coeffs[2 * q], transfer_ref[2 * q]) + dot(coeffs[2 * q + 1], transfer_ref[2 * q + 1])
        coeffs.append(jnp.where(lane < ranks_ref[leaves + q], value, 0.0).astype(BF))
    wide = [widen(value.astype(F32)) for value in coeffs]
    for q in range(mains // 3):
        for k, tile in enumerate(packed(wide[3 * q : 3 * q + 3], wide[mains + q], rank_top)):
            out_ref[3 * q + k] = tile.astype(BF)


def fetch(pairs, sems):
    copies = [pltpu.make_async_copy(src, dst, sems.at[n]) for n, (src, dst) in enumerate(pairs)]
    for copy in copies:
        copy.start()
    return copies


def coeff_kernel(ranks_ref, v_hbm, basis_hbm, transfer_hbm, out_ref, v_ref, basis_ref, transfer_ref, sems):
    leaves, rank_top, _ = basis_ref.shape
    for copy in fetch([(v_hbm, v_ref), (basis_hbm, basis_ref), (transfer_hbm, transfer_ref)], sems):
        copy.wait()
    emit_coeffs(lambda i: v_ref[i], basis_ref, transfer_ref, ranks_ref, out_ref, leaves, rank_top)


def couple_kernel(source_ref, target_ref, coupling_ref, *refs, order, unroll):
    chips = sum(len(group) for group in order)
    in_refs, out_refs, (sources, total) = refs[: 2 * chips], refs[2 * chips : -2], refs[-2:]
    blocks, rank_top, _ = coupling_ref.shape
    far, mains, rhs, _ = in_refs[0].shape
    quads = mains // 3
    clusters = mains + quads

    def split(f, _):
        for n, packed_ref in enumerate(in_refs):
            row = (n * far + f) * clusters
            tiles = [packed_ref[f, c] for c in range(mains)]
            for c in range(mains):
                sources[row + c] = tiles[c]
            for q in range(quads):
                wide = [tile.astype(F32) for tile in tiles[3 * q : 3 * q + 3]]
                sources[row + mains + q] = fourth(wide, rank_top).astype(BF)
            for c in range(clusters):
                total[row + c] = jnp.zeros((rhs, LANES), F32)
        return 0

    lax.fori_loop(0, far, split, 0)

    def some(s, _):
        for u in range(unroll):
            j = s * unroll + u
            term = dot(sources[source_ref[j], :, :rank_top], coupling_ref[j])
            at = target_ref[j]
            total[at, :, :rank_top] = total[at, :, :rank_top] + term
        return 0

    lax.fori_loop(0, blocks // unroll, some, 0)

    def pack(f, _):
        for core in range(2):
            for g, group in enumerate(order):
                for place, chip in enumerate(group):
                    row = ((core * chips + chip) * far + f) * clusters
                    for q in range(quads):
                        mains_now = [total[row + 3 * q + k] for k in range(3)]
                        for k, tile in enumerate(packed(mains_now, total[row + mains + q], rank_top)):
                            out_refs[core * len(order) + g][place, f, 3 * q + k] = tile.astype(BF)
        return 0

    lax.fori_loop(0, far, pack, 0)


def near_kernel(v_ref, near_ref, out_ref):
    leaves = v_ref.shape[0]
    for i in range(leaves):
        total = dot(v_ref[i], near_ref[i, 1])
        if i > 0:
            total = total + dot(v_ref[i - 1], near_ref[i, 0])
        if i < leaves - 1:
            total = total + dot(v_ref[i + 1], near_ref[i, 2])
        out_ref[i] = total


def edge_kernel(core_ref, inner_ref, outer_ref, first_ref, last_ref, out_ref):
    inner, outer = inner_ref[0], outer_ref[0]
    even = core_ref[0] == 0
    out_ref[0] = dot(jnp.where(even, outer, inner), first_ref[0, 0])
    out_ref[1] = dot(jnp.where(even, inner, outer), last_ref[0, 0])


def first_add_kernel(keep_ref, swap_ref, *out_refs):
    for n, out_ref in enumerate(out_refs):
        out_ref[...] = (keep_ref[n].astype(F32) + swap_ref[n].astype(F32)).astype(BF)


def second_add_kernel(keep_ref, swap_ref, yz_ref, zx_ref, own_out, y_out, z_out):
    own_out[...] = keep_ref[0].astype(F32) + swap_ref[0].astype(F32)
    y_out[...] = (keep_ref[2].astype(F32) + swap_ref[2].astype(F32)).astype(BF)
    total = keep_ref[3].astype(F32) + swap_ref[3].astype(F32)
    z_out[...] = (total + yz_ref[...].astype(F32) + zx_ref[...].astype(F32)).astype(BF)


def third_add_kernel(keep_ref, swap_ref, x_ref, x_out):
    total = keep_ref[1].astype(F32) + swap_ref[1].astype(F32) + x_ref[...].astype(F32)
    x_out[...] = total.astype(BF)


def last_add_kernel(own_ref, x_ref, y_ref, z_ref, keep_out, *away_refs):
    for f in range(own_ref.shape[0]):
        total = own_ref[f] + x_ref[f].astype(F32) + y_ref[f].astype(F32) + z_ref[f].astype(F32)
        if f == 0:
            keep_out[...] = total
        else:
            away_refs[f - 1][...] = total.astype(BF)


def field_kernel(ranks_ref, near_ref, edge_ref, basis_ref, transfer_ref, keep_ref, *rest, away):
    term_refs, out_ref, coeff_ref = rest[:away], rest[away], rest[away + 1 :]
    leaves, rank_top, _ = basis_ref.shape
    mains, rhs, _ = keep_ref.shape
    tiles = []
    for t in range(mains):
        tile = keep_ref[t]
        for term_ref in term_refs:
            tile = tile + term_ref[t].astype(F32)
        tiles.append(tile)
    sums = tiles + [fourth(tiles[3 * q : 3 * q + 3], rank_top) for q in range(mains // 3)]
    lane = lax.broadcasted_iota(jnp.int32, (rhs, rank_top), 1)
    fields = [
        jnp.where(lane < ranks_ref[c], total[:, :rank_top], 0.0).astype(BF) for c, total in enumerate(sums)
    ]
    for i in range(leaves):
        down = fields[i].astype(F32) + dot_t(fields[leaves + i // 2], transfer_ref[i])
        leaf_total = jnp.where(lane < ranks_ref[i], down, 0.0).astype(BF)
        result = near_ref[i] + dot(leaf_total, basis_ref[i])
        if i == 0:
            result = result + edge_ref[0]
        if i == leaves - 1:
            result = result + edge_ref[1]
        out_ref[i] = result.astype(BF)
    if coeff_ref:
        emit_coeffs(lambda i: out_ref[i], basis_ref, transfer_ref, ranks_ref, coeff_ref[0], leaves, rank_top)


def params(mebibytes):
    return pltpu.CompilerParams(vmem_limit_bytes=mebibytes << 20)


def local(charges, basis, transfer, near_field, coupling, ranks, block_source, block_target):
    leaves, rank_top, width = basis.shape
    rhs = charges.shape[1]
    clusters = ranks.shape[0]
    blocks = coupling.shape[0]
    devices = lax.axis_size("clu")
    mains = clusters * 3 // 4
    shape = jax.ShapeDtypeStruct

    cores, chips = 2, 8
    cube = cores * chips
    far = devices // cube
    x, y, z = 1, 2, 4

    def swap_far(part, shift):
        return lax.ppermute(part, "clu", [(d, (d + shift * cube) % devices) for d in range(devices)])

    def swap(part, chip):
        return lax.ppermute(part, "clu", [(d, d ^ chip * cores) for d in range(devices)])

    def swap_cores(part):
        return lax.ppermute(part, "clu", [(d, d ^ 1) for d in range(devices)])

    me = lax.axis_index("clu")

    def rows(cluster, sign):
        device = cluster // clusters
        core = (device ^ me) % cores
        chip = ((device ^ me) // cores) % chips
        away = (sign * (device // cube - me // cube)) % far
        return ((core * chips + chip) * far + away) * clusters + cluster % clusters

    source_rows, target_rows = rows(block_source, -1), rows(block_target, 1)

    tile_shape = (mains, rhs, LANES)
    out_shape = shape((leaves, rhs, width), BF)
    tile_out = shape(tile_shape, BF)
    part_shape = shape((far,) + tile_shape, BF)
    first_coeffs = pl.pallas_call(
        coeff_kernel,
        out_shape=tile_out,
        in_specs=[SMEM, HBM, HBM, HBM],
        out_specs=VMEM,
        scratch_shapes=[
            pltpu.VMEM(charges.shape, BF),
            pltpu.VMEM(basis.shape, BF),
            pltpu.VMEM(transfer.shape, BF),
            pltpu.SemaphoreType.DMA((3,)),
        ],
    )(ranks, charges, basis, transfer)

    order = ((x | y | z, x | y, y | z, z | x), (0, x, y, z))
    couple = pl.pallas_call(
        functools.partial(couple_kernel, order=order, unroll=8),
        out_shape=[shape((4, far) + tile_shape, BF)] * 4,
        in_specs=[SMEM, SMEM, VMEM] + [VMEM] * (cores * chips),
        out_specs=[VMEM] * 4,
        scratch_shapes=[
            pltpu.VMEM((devices * clusters, rhs, LANES), BF),
            pltpu.VMEM((devices * clusters, rhs, LANES), F32),
        ],
        compiler_params=params(32 if devices <= 32 else 60),
        cost_estimate=pl.CostEstimate(
            flops=2 * blocks * rhs * rank_top * rank_top, bytes_accessed=10 << 20, transcendentals=0
        ),
    )

    near = pl.pallas_call(
        near_kernel,
        out_shape=shape((leaves, rhs, width), F32),
        in_specs=[VMEM] * 2,
        out_specs=VMEM,
        compiler_params=params(16),
        cost_estimate=pl.CostEstimate(
            flops=2 * leaves * 3 * rhs * width * width, bytes_accessed=4 << 20, transcendentals=0
        ),
    )

    edge = pl.pallas_call(
        edge_kernel,
        out_shape=shape((2, rhs, width), F32),
        grid=(1,),
        in_specs=[
            SMEM,
            VMEM,
            VMEM,
            pl.BlockSpec((1, 1, width, width), lambda i: (0, 0, 0, 0)),
            pl.BlockSpec((1, 1, width, width), lambda i: (leaves - 1, 2, 0, 0)),
        ],
        out_specs=VMEM,
        compiler_params=params(16),
    )

    def adder(kernel, inputs, outputs):
        return pl.pallas_call(
            kernel,
            out_shape=outputs,
            in_specs=[VMEM] * inputs,
            out_specs=[VMEM] * len(outputs),
            compiler_params=params(16),
        )

    own_shape = shape((far,) + tile_shape, F32)
    first_add = adder(first_add_kernel, 2, [part_shape] * 4)
    second_add = adder(second_add_kernel, 4, [own_shape, part_shape, part_shape])
    third_add = adder(third_add_kernel, 3, [part_shape])
    last_add = adder(last_add_kernel, 4, [shape(tile_shape, F32)] + [tile_out] * (far - 1))

    def finish(with_coeffs):
        return pl.pallas_call(
            functools.partial(field_kernel, away=far - 1),
            out_shape=[out_shape, tile_out] if with_coeffs else [out_shape],
            in_specs=[SMEM] + [VMEM] * (4 + far),
            out_specs=[VMEM, VMEM] if with_coeffs else [VMEM],
            compiler_params=params(16),
        )

    core = me % cores
    barrier = lax.optimization_barrier

    def halo(field_in):
        head, tail = field_in[:1], field_in[leaves - 1 :]
        inner = swap_cores(jnp.where(core == 0, tail, head))
        pairs = [(d, d + 1) for d in range(1, devices - 1, 2)]
        outer = lax.ppermute(
            jnp.where(core == 0, head, tail), "clu", pairs + [(b, a) for a, b in pairs]
        )
        return inner, outer

    def apply_matrix(field_in, coeffs, with_coeffs):
        away = [swap_far(coeffs, s) for s in range(1, far)]
        away, inner, outer = barrier((away, *halo(field_in)))
        got = {0: jnp.stack([coeffs] + away)}
        got[x], got[y], got[z] = barrier((swap(got[0], x), swap(got[0], y), swap(got[0], z)))
        near_sum = near(field_in, near_field)
        got[x | y], got[y | z], got[z | x], near_sum = barrier(
            (swap(got[x], y), swap(got[y], z), swap(got[z], x), near_sum)
        )
        edges = edge(core.reshape(1), inner, outer, near_field, near_field)
        other = {chip: swap_cores(got[chip]) for chip in (0, x, y, z)}
        got[x | y | z], edges, other = barrier((swap(got[x | y], z), edges, other))
        for chip in (x | y, y | z, z | x, x | y | z):
            other[chip] = swap_cores(got[chip])
        keep_first, keep, send_first, send = couple(
            source_rows,
            target_rows,
            coupling,
            *[got[chip] for chip in range(chips)],
            *[other[chip] for chip in range(chips)],
        )
        corner, xy, yz, zx = first_add(keep_first, swap_cores(send_first))
        swapped = swap_cores(send)
        corner, yz, zx = barrier((swap(corner, z), swap(yz, y), swap(zx, x)))
        xy = swap((xy.astype(F32) + corner.astype(F32)).astype(BF), y)
        mine, to_y, to_z = second_add(keep, swapped, yz, zx)
        to_y, to_z = swap(to_y, y), swap(to_z, z)
        (to_x,) = third_add(keep, swapped, xy)
        total, *away = last_add(mine, swap(to_x, x), to_y, to_z)
        terms = [swap_far(part, s + 1) for s, part in enumerate(away)]
        return finish(with_coeffs)(ranks, near_sum, edges, basis, transfer, total, *terms)

    first, second_coeffs = apply_matrix(charges, first_coeffs, True)
    (second,) = apply_matrix(first, second_coeffs, False)
    return (first, second)


def solution(mesh):
    in_specs = (
        P("clu", None, None),
        P("clu", None, None),
        P("clu", None, None),
        P("clu", None, None, None),
        P("clu", None, None),
        P("clu"),
        P("clu"),
        P("clu"),
    )
    out_specs = (P("clu", None, None), P("clu", None, None))
    return jax.shard_map(local, mesh=mesh, in_specs=in_specs, out_specs=out_specs, check_vma=False)
```

```python
import functools

import jax
import jax.numpy as jnp
from jax import lax
from jax.experimental import pallas as pl
from jax.experimental.pallas import tpu as pltpu
from jax.sharding import PartitionSpec as P

LANES = 128
BF = jnp.bfloat16
F32 = jnp.float32
VMEM = pl.BlockSpec(memory_space=pltpu.VMEM)
SMEM = pl.BlockSpec(memory_space=pltpu.SMEM)
HBM = pl.BlockSpec(memory_space=pltpu.HBM)


def dot(a, b):
    return lax.dot_general(a, b, (((1,), (0,)), ((), ())), preferred_element_type=F32)


def dot_t(a, b):
    return lax.dot_general(a, b, (((1,), (1,)), ((), ())), preferred_element_type=F32)


def lanes(rows):
    return lax.broadcasted_iota(jnp.int32, (rows, LANES), 1)


def fourth(tiles, rank_top):
    third = LANES - rank_top
    lane = lanes(tiles[0].shape[0])
    moved = [pltpu.roll(tile, third * (k + 1), 1) for k, tile in enumerate(tiles)]
    return jnp.where(lane < third, moved[0], jnp.where(lane < 2 * third, moved[1], moved[2]))


def packed(mains, pad, rank_top):
    lane = lanes(pad.shape[0])
    third = LANES - rank_top
    return [
        jnp.where(lane < rank_top, main, pltpu.roll(pad, rank_top - third * k, 1)) for k, main in enumerate(mains)
    ]


def widen(value):
    return jnp.concatenate([value, jnp.zeros((value.shape[0], LANES - value.shape[1]), value.dtype)], axis=1)


def emit_coeffs(read_leaf, basis_ref, transfer_ref, ranks_ref, out_ref, leaves, rank_top):
    mains, rhs, _ = out_ref.shape
    lane = lax.broadcasted_iota(jnp.int32, (rhs, rank_top), 1)
    coeffs = []
    for i in range(leaves):
        value = dot_t(read_leaf(i), basis_ref[i])
        coeffs.append(jnp.where(lane < ranks_ref[i], value, 0.0).astype(BF))
    for q in range(leaves // 2):
        value = dot(coeffs[2 * q], transfer_ref[2 * q]) + dot(coeffs[2 * q + 1], transfer_ref[2 * q + 1])
        coeffs.append(jnp.where(lane < ranks_ref[leaves + q], value, 0.0).astype(BF))
    wide = [widen(value.astype(F32)) for value in coeffs]
    for q in range(mains // 3):
        for k, tile in enumerate(packed(wide[3 * q : 3 * q + 3], wide[mains + q], rank_top)):
            out_ref[3 * q + k] = tile.astype(BF)


def fetch(pairs, sems):
    copies = [pltpu.make_async_copy(src, dst, sems.at[n]) for n, (src, dst) in enumerate(pairs)]
    for copy in copies:
        copy.start()
    return copies


def coeff_kernel(ranks_ref, v_hbm, basis_hbm, transfer_hbm, out_ref, v_ref, basis_ref, transfer_ref, sems):
    leaves, rank_top, _ = basis_ref.shape
    for copy in fetch([(v_hbm, v_ref), (basis_hbm, basis_ref), (transfer_hbm, transfer_ref)], sems):
        copy.wait()
    emit_coeffs(lambda i: v_ref[i], basis_ref, transfer_ref, ranks_ref, out_ref, leaves, rank_top)


def couple_kernel(source_ref, target_ref, coupling_ref, *refs, order, unroll):
    chips = sum(len(group) for group in order)
    in_refs, out_refs, (sources, total) = refs[: 2 * chips], refs[2 * chips : -2], refs[-2:]
    blocks, rank_top, _ = coupling_ref.shape
    far, mains, rhs, _ = in_refs[0].shape
    quads = mains // 3
    clusters = mains + quads

    def split(f, _):
        for n, packed_ref in enumerate(in_refs):
            row = (n * far + f) * clusters
            tiles = [packed_ref[f, c] for c in range(mains)]
            for c in range(mains):
                sources[row + c] = tiles[c]
            for q in range(quads):
                wide = [tile.astype(F32) for tile in tiles[3 * q : 3 * q + 3]]
                sources[row + mains + q] = fourth(wide, rank_top).astype(BF)
            for c in range(clusters):
                total[row + c] = jnp.zeros((rhs, LANES), F32)
        return 0

    lax.fori_loop(0, far, split, 0)

    def some(s, _):
        for u in range(unroll):
            j = s * unroll + u
            term = dot(sources[source_ref[j], :, :rank_top], coupling_ref[j])
            at = target_ref[j]
            total[at, :, :rank_top] = total[at, :, :rank_top] + term
        return 0

    lax.fori_loop(0, blocks // unroll, some, 0)

    def pack(f, _):
        for core in range(2):
            for g, group in enumerate(order):
                for place, chip in enumerate(group):
                    row = ((core * chips + chip) * far + f) * clusters
                    for q in range(quads):
                        mains_now = [total[row + 3 * q + k] for k in range(3)]
                        for k, tile in enumerate(packed(mains_now, total[row + mains + q], rank_top)):
                            out_refs[core * len(order) + g][place, f, 3 * q + k] = tile.astype(BF)
        return 0

    lax.fori_loop(0, far, pack, 0)


def near_kernel(v_ref, near_ref, out_ref):
    leaves = v_ref.shape[0]
    for i in range(leaves):
        total = dot(v_ref[i], near_ref[i, 1])
        if i > 0:
            total = total + dot(v_ref[i - 1], near_ref[i, 0])
        if i < leaves - 1:
            total = total + dot(v_ref[i + 1], near_ref[i, 2])
        out_ref[i] = total


def edge_kernel(core_ref, inner_ref, outer_ref, first_ref, last_ref, out_ref):
    inner, outer = inner_ref[0], outer_ref[0]
    even = core_ref[0] == 0
    out_ref[0] = dot(jnp.where(even, outer, inner), first_ref[0, 0])
    out_ref[1] = dot(jnp.where(even, inner, outer), last_ref[0, 0])


def first_add_kernel(keep_ref, swap_ref, *out_refs):
    for n, out_ref in enumerate(out_refs):
        out_ref[...] = (keep_ref[n].astype(F32) + swap_ref[n].astype(F32)).astype(BF)


def second_add_kernel(keep_ref, swap_ref, yz_ref, zx_ref, own_out, y_out, z_out):
    own_out[...] = keep_ref[0].astype(F32) + swap_ref[0].astype(F32)
    y_out[...] = (keep_ref[2].astype(F32) + swap_ref[2].astype(F32)).astype(BF)
    total = keep_ref[3].astype(F32) + swap_ref[3].astype(F32)
    z_out[...] = (total + yz_ref[...].astype(F32) + zx_ref[...].astype(F32)).astype(BF)


def third_add_kernel(keep_ref, swap_ref, x_ref, x_out):
    total = keep_ref[1].astype(F32) + swap_ref[1].astype(F32) + x_ref[...].astype(F32)
    x_out[...] = total.astype(BF)


def last_add_kernel(own_ref, x_ref, y_ref, z_ref, keep_out, *away_refs):
    for f in range(own_ref.shape[0]):
        total = own_ref[f] + x_ref[f].astype(F32) + y_ref[f].astype(F32) + z_ref[f].astype(F32)
        if f == 0:
            keep_out[...] = total
        else:
            away_refs[f - 1][...] = total.astype(BF)


def field_kernel(ranks_ref, near_ref, edge_ref, basis_ref, transfer_ref, keep_ref, *rest, away):
    term_refs, out_ref, coeff_ref = rest[:away], rest[away], rest[away + 1 :]
    leaves, rank_top, _ = basis_ref.shape
    mains, rhs, _ = keep_ref.shape
    tiles = []
    for t in range(mains):
        tile = keep_ref[t]
        for term_ref in term_refs:
            tile = tile + term_ref[t].astype(F32)
        tiles.append(tile)
    sums = tiles + [fourth(tiles[3 * q : 3 * q + 3], rank_top) for q in range(mains // 3)]
    lane = lax.broadcasted_iota(jnp.int32, (rhs, rank_top), 1)
    fields = [
        jnp.where(lane < ranks_ref[c], total[:, :rank_top], 0.0).astype(BF) for c, total in enumerate(sums)
    ]
    for i in range(leaves):
        down = fields[i].astype(F32) + dot_t(fields[leaves + i // 2], transfer_ref[i])
        leaf_total = jnp.where(lane < ranks_ref[i], down, 0.0).astype(BF)
        result = near_ref[i] + dot(leaf_total, basis_ref[i])
        if i == 0:
            result = result + edge_ref[0]
        if i == leaves - 1:
            result = result + edge_ref[1]
        out_ref[i] = result.astype(BF)
    if coeff_ref:
        emit_coeffs(lambda i: out_ref[i], basis_ref, transfer_ref, ranks_ref, coeff_ref[0], leaves, rank_top)


def params(mebibytes):
    return pltpu.CompilerParams(vmem_limit_bytes=mebibytes << 20)


def local(charges, basis, transfer, near_field, coupling, ranks, block_source, block_target):
    leaves, rank_top, width = basis.shape
    rhs = charges.shape[1]
    clusters = ranks.shape[0]
    blocks = coupling.shape[0]
    devices = lax.axis_size("clu")
    mains = clusters * 3 // 4
    shape = jax.ShapeDtypeStruct

    cores, chips = 2, 8
    cube = cores * chips
    far = devices // cube
    x, y, z = 1, 2, 4

    def swap_far(part, shift):
        return lax.ppermute(part, "clu", [(d, (d + shift * cube) % devices) for d in range(devices)])

    def swap(part, direction):
        turned = direction << 1 & 7 | direction >> 2
        return lax.ppermute(
            part, "clu", [(d, d ^ (turned if d % cores else direction) * cores) for d in range(devices)]
        )

    def swap_cores(part):
        return lax.ppermute(part, "clu", [(d, d ^ 1) for d in range(devices)])

    me = lax.axis_index("clu")

    def rows(cluster, sign):
        device = cluster // clusters
        core = (device ^ me) % cores
        chip = ((device ^ me) // cores) % chips
        chip = jnp.where(device % cores == 0, chip, chip >> 1 | (chip & 1) << 2)
        away = (sign * (device // cube - me // cube)) % far
        return ((core * chips + chip) * far + away) * clusters + cluster % clusters

    source_rows, target_rows = rows(block_source, -1), rows(block_target, 1)

    tile_shape = (mains, rhs, LANES)
    out_shape = shape((leaves, rhs, width), BF)
    tile_out = shape(tile_shape, BF)
    part_shape = shape((far,) + tile_shape, BF)
    first_coeffs = pl.pallas_call(
        coeff_kernel,
        out_shape=tile_out,
        in_specs=[SMEM, HBM, HBM, HBM],
        out_specs=VMEM,
        scratch_shapes=[
            pltpu.VMEM(charges.shape, BF),
            pltpu.VMEM(basis.shape, BF),
            pltpu.VMEM(transfer.shape, BF),
            pltpu.SemaphoreType.DMA((3,)),
        ],
    )(ranks, charges, basis, transfer)

    order = ((x | y | z, x | y, y | z, z | x), (0, x, y, z))
    couple = pl.pallas_call(
        functools.partial(couple_kernel, order=order, unroll=8),
        out_shape=[shape((4, far) + tile_shape, BF)] * 4,
        in_specs=[SMEM, SMEM, VMEM] + [VMEM] * (cores * chips),
        out_specs=[VMEM] * 4,
        scratch_shapes=[
            pltpu.VMEM((devices * clusters, rhs, LANES), BF),
            pltpu.VMEM((devices * clusters, rhs, LANES), F32),
        ],
        compiler_params=params(32 if devices <= 32 else 60),
        cost_estimate=pl.CostEstimate(
            flops=2 * blocks * rhs * rank_top * rank_top, bytes_accessed=10 << 20, transcendentals=0
        ),
    )

    near = pl.pallas_call(
        near_kernel,
        out_shape=shape((leaves, rhs, width), F32),
        in_specs=[VMEM] * 2,
        out_specs=VMEM,
        compiler_params=params(16),
        cost_estimate=pl.CostEstimate(
            flops=2 * leaves * 3 * rhs * width * width, bytes_accessed=4 << 20, transcendentals=0
        ),
    )

    edge = pl.pallas_call(
        edge_kernel,
        out_shape=shape((2, rhs, width), F32),
        grid=(1,),
        in_specs=[
            SMEM,
            VMEM,
            VMEM,
            pl.BlockSpec((1, 1, width, width), lambda i: (0, 0, 0, 0)),
            pl.BlockSpec((1, 1, width, width), lambda i: (leaves - 1, 2, 0, 0)),
        ],
        out_specs=VMEM,
        compiler_params=params(16),
    )

    def adder(kernel, inputs, outputs):
        return pl.pallas_call(
            kernel,
            out_shape=outputs,
            in_specs=[VMEM] * inputs,
            out_specs=[VMEM] * len(outputs),
            compiler_params=params(16),
        )

    own_shape = shape((far,) + tile_shape, F32)
    first_add = adder(first_add_kernel, 2, [part_shape] * 4)
    second_add = adder(second_add_kernel, 4, [own_shape, part_shape, part_shape])
    third_add = adder(third_add_kernel, 3, [part_shape])
    last_add = adder(last_add_kernel, 4, [shape(tile_shape, F32)] + [tile_out] * (far - 1))

    def finish(with_coeffs):
        return pl.pallas_call(
            functools.partial(field_kernel, away=far - 1),
            out_shape=[out_shape, tile_out] if with_coeffs else [out_shape],
            in_specs=[SMEM] + [VMEM] * (4 + far),
            out_specs=[VMEM, VMEM] if with_coeffs else [VMEM],
            compiler_params=params(16),
        )

    core = me % cores
    barrier = lax.optimization_barrier

    halo_pairs = [(d, d + cores) for d in range(1, devices - cores, cores)]
    halo_pairs += [(d, d - cores) for d in range(cores, devices, cores)]

    def halo(field_in):
        head, tail = field_in[:1], field_in[leaves - 1 :]
        inner = swap_cores(jnp.where(core == 0, tail, head))
        return inner, lax.ppermute(jnp.where(core == 0, head, tail), "clu", halo_pairs)

    def apply_matrix(field_in, coeffs, with_coeffs):
        away = [swap_far(coeffs, s) for s in range(1, far)]
        away, inner, outer = barrier((away, *halo(field_in)))
        got = {0: jnp.stack([coeffs] + away)}
        outer = swap_cores(outer)
        got[x], got[y], got[z], outer = barrier((swap(got[0], x), swap(got[0], y), swap(got[0], z), outer))
        near_sum = near(field_in, near_field)
        got[x | y], got[y | z], got[z | x], near_sum = barrier(
            (swap(got[x], y), swap(got[y], z), swap(got[z], x), near_sum)
        )
        edges = edge(core.reshape(1), inner, outer, near_field, near_field)
        other = {chip: swap_cores(got[chip]) for chip in (0, x, y, z)}
        got[x | y | z], edges, other = barrier((swap(got[x | y], z), edges, other))
        for chip in (x | y, y | z, z | x, x | y | z):
            other[chip] = swap_cores(got[chip])
        keep_first, keep, send_first, send = couple(
            source_rows,
            target_rows,
            coupling,
            *[got[chip] for chip in range(chips)],
            *[other[chip] for chip in range(chips)],
        )
        corner, xy, yz, zx = first_add(keep_first, swap_cores(send_first))
        swapped = swap_cores(send)
        corner, yz, zx = barrier((swap(corner, z), swap(yz, y), swap(zx, x)))
        xy = swap((xy.astype(F32) + corner.astype(F32)).astype(BF), y)
        mine, to_y, to_z = second_add(keep, swapped, yz, zx)
        to_y, to_z = swap(to_y, y), swap(to_z, z)
        (to_x,) = third_add(keep, swapped, xy)
        total, *away = last_add(mine, swap(to_x, x), to_y, to_z)
        terms = [swap_far(part, s + 1) for s, part in enumerate(away)]
        return finish(with_coeffs)(ranks, near_sum, edges, basis, transfer, total, *terms)

    first, second_coeffs = apply_matrix(charges, first_coeffs, True)
    (second,) = apply_matrix(first, second_coeffs, False)
    return (first, second)


def solution(mesh):
    in_specs = (
        P("clu", None, None),
        P("clu", None, None),
        P("clu", None, None),
        P("clu", None, None, None),
        P("clu", None, None),
        P("clu"),
        P("clu"),
        P("clu"),
    )
    out_specs = (P("clu", None, None), P("clu", None, None))
    return jax.shard_map(local, mesh=mesh, in_specs=in_specs, out_specs=out_specs, check_vma=False)
```

```python
import functools

import jax
import jax.numpy as jnp
from jax import lax
from jax.experimental import pallas as pl
from jax.experimental.pallas import tpu as pltpu
from jax.sharding import PartitionSpec as P

LANES = 128
BF = jnp.bfloat16
F32 = jnp.float32
VMEM = pl.BlockSpec(memory_space=pltpu.VMEM)
SMEM = pl.BlockSpec(memory_space=pltpu.SMEM)
HBM = pl.BlockSpec(memory_space=pltpu.HBM)


def dot(a, b):
    return lax.dot_general(a, b, (((1,), (0,)), ((), ())), preferred_element_type=F32)


def dot_t(a, b):
    return lax.dot_general(a, b, (((1,), (1,)), ((), ())), preferred_element_type=F32)


def lanes(rows):
    return lax.broadcasted_iota(jnp.int32, (rows, LANES), 1)


def fourth(tiles, rank_top):
    third = LANES - rank_top
    lane = lanes(tiles[0].shape[0])
    moved = [pltpu.roll(tile, third * (k + 1), 1) for k, tile in enumerate(tiles)]
    return jnp.where(lane < third, moved[0], jnp.where(lane < 2 * third, moved[1], moved[2]))


def packed(mains, pad, rank_top):
    lane = lanes(pad.shape[0])
    third = LANES - rank_top
    return [
        jnp.where(lane < rank_top, main, pltpu.roll(pad, rank_top - third * k, 1)) for k, main in enumerate(mains)
    ]


def widen(value):
    return jnp.concatenate([value, jnp.zeros((value.shape[0], LANES - value.shape[1]), value.dtype)], axis=1)


def emit_coeffs(read_leaf, basis_ref, transfer_ref, ranks_ref, out_ref, leaves, rank_top):
    mains, rhs, _ = out_ref.shape
    lane = lax.broadcasted_iota(jnp.int32, (rhs, rank_top), 1)
    coeffs = []
    for i in range(leaves):
        value = dot_t(read_leaf(i), basis_ref[i])
        coeffs.append(jnp.where(lane < ranks_ref[i], value, 0.0).astype(BF))
    for q in range(leaves // 2):
        value = dot(coeffs[2 * q], transfer_ref[2 * q]) + dot(coeffs[2 * q + 1], transfer_ref[2 * q + 1])
        coeffs.append(jnp.where(lane < ranks_ref[leaves + q], value, 0.0).astype(BF))
    wide = [widen(value.astype(F32)) for value in coeffs]
    for q in range(mains // 3):
        for k, tile in enumerate(packed(wide[3 * q : 3 * q + 3], wide[mains + q], rank_top)):
            out_ref[3 * q + k] = tile.astype(BF)


def fetch(pairs, sems):
    copies = [pltpu.make_async_copy(src, dst, sems.at[n]) for n, (src, dst) in enumerate(pairs)]
    for copy in copies:
        copy.start()
    return copies


def coeff_kernel(ranks_ref, v_hbm, basis_hbm, transfer_hbm, out_ref, v_ref, basis_ref, transfer_ref, sems):
    leaves, rank_top, _ = basis_ref.shape
    for copy in fetch([(v_hbm, v_ref), (basis_hbm, basis_ref), (transfer_hbm, transfer_ref)], sems):
        copy.wait()
    emit_coeffs(lambda i: v_ref[i], basis_ref, transfer_ref, ranks_ref, out_ref, leaves, rank_top)


def couple_kernel(source_ref, target_ref, coupling_ref, *refs, order, unroll):
    chips = sum(len(group) for group in order)
    in_refs, out_refs, (sources, total) = refs[: 2 * chips], refs[2 * chips : -2], refs[-2:]
    blocks, rank_top, _ = coupling_ref.shape
    far, mains, rhs, _ = in_refs[0].shape
    quads = mains // 3
    clusters = mains + quads

    def split(f, _):
        for n, packed_ref in enumerate(in_refs):
            row = (n * far + f) * clusters
            tiles = [packed_ref[f, c] for c in range(mains)]
            for c in range(mains):
                sources[row + c] = tiles[c]
            for q in range(quads):
                wide = [tile.astype(F32) for tile in tiles[3 * q : 3 * q + 3]]
                sources[row + mains + q] = fourth(wide, rank_top).astype(BF)
            for c in range(clusters):
                total[row + c] = jnp.zeros((rhs, LANES), F32)
        return 0

    lax.fori_loop(0, far, split, 0)

    def some(s, _):
        for u in range(unroll):
            j = s * unroll + u
            term = dot(sources[source_ref[j], :, :rank_top], coupling_ref[j])
            at = target_ref[j]
            total[at, :, :rank_top] = total[at, :, :rank_top] + term
        return 0

    lax.fori_loop(0, blocks // unroll, some, 0)

    def pack(f, _):
        for core in range(2):
            for g, group in enumerate(order):
                for place, chip in enumerate(group):
                    row = ((core * chips + chip) * far + f) * clusters
                    for q in range(quads):
                        mains_now = [total[row + 3 * q + k] for k in range(3)]
                        for k, tile in enumerate(packed(mains_now, total[row + mains + q], rank_top)):
                            out_refs[core * len(order) + g][place, f, 3 * q + k] = tile.astype(BF)
        return 0

    lax.fori_loop(0, far, pack, 0)


def near_kernel(v_ref, near_ref, out_ref):
    leaves = v_ref.shape[0]
    for i in range(leaves):
        total = dot(v_ref[i], near_ref[i, 1])
        if i > 0:
            total = total + dot(v_ref[i - 1], near_ref[i, 0])
        if i < leaves - 1:
            total = total + dot(v_ref[i + 1], near_ref[i, 2])
        out_ref[i] = total


def edge_kernel(core_ref, inner_ref, outer_ref, first_ref, last_ref, out_ref):
    inner, outer = inner_ref[0], outer_ref[0]
    even = core_ref[0] == 0
    out_ref[0] = dot(jnp.where(even, outer, inner), first_ref[0, 0])
    out_ref[1] = dot(jnp.where(even, inner, outer), last_ref[0, 0])


def first_add_kernel(keep_ref, swap_ref, *out_refs):
    for n, out_ref in enumerate(out_refs):
        out_ref[...] = (keep_ref[n].astype(F32) + swap_ref[n].astype(F32)).astype(BF)


def second_add_kernel(keep_ref, swap_ref, yz_ref, zx_ref, own_out, y_out, z_out):
    own_out[...] = keep_ref[0].astype(F32) + swap_ref[0].astype(F32)
    y_out[...] = (keep_ref[2].astype(F32) + swap_ref[2].astype(F32)).astype(BF)
    total = keep_ref[3].astype(F32) + swap_ref[3].astype(F32)
    z_out[...] = (total + yz_ref[...].astype(F32) + zx_ref[...].astype(F32)).astype(BF)


def third_add_kernel(keep_ref, swap_ref, x_ref, x_out):
    total = keep_ref[1].astype(F32) + swap_ref[1].astype(F32) + x_ref[...].astype(F32)
    x_out[...] = total.astype(BF)


def last_add_kernel(own_ref, x_ref, y_ref, z_ref, keep_out, *away_refs):
    for f in range(own_ref.shape[0]):
        total = own_ref[f] + x_ref[f].astype(F32) + y_ref[f].astype(F32) + z_ref[f].astype(F32)
        if f == 0:
            keep_out[...] = total
        else:
            away_refs[f - 1][...] = total.astype(BF)


def field_kernel(ranks_ref, near_ref, edge_ref, basis_ref, transfer_ref, keep_ref, *rest, away):
    term_refs, out_ref, coeff_ref = rest[:away], rest[away], rest[away + 1 :]
    leaves, rank_top, _ = basis_ref.shape
    mains, rhs, _ = keep_ref.shape
    tiles = []
    for t in range(mains):
        tile = keep_ref[t]
        for term_ref in term_refs:
            tile = tile + term_ref[t].astype(F32)
        tiles.append(tile)
    sums = tiles + [fourth(tiles[3 * q : 3 * q + 3], rank_top) for q in range(mains // 3)]
    lane = lax.broadcasted_iota(jnp.int32, (rhs, rank_top), 1)
    fields = [
        jnp.where(lane < ranks_ref[c], total[:, :rank_top], 0.0).astype(BF) for c, total in enumerate(sums)
    ]
    for i in range(leaves):
        down = fields[i].astype(F32) + dot_t(fields[leaves + i // 2], transfer_ref[i])
        leaf_total = jnp.where(lane < ranks_ref[i], down, 0.0).astype(BF)
        result = near_ref[i] + dot(leaf_total, basis_ref[i])
        if i == 0:
            result = result + edge_ref[0]
        if i == leaves - 1:
            result = result + edge_ref[1]
        out_ref[i] = result.astype(BF)
    if coeff_ref:
        emit_coeffs(lambda i: out_ref[i], basis_ref, transfer_ref, ranks_ref, coeff_ref[0], leaves, rank_top)


def params(mebibytes):
    return pltpu.CompilerParams(vmem_limit_bytes=mebibytes << 20)


def local(charges, basis, transfer, near_field, coupling, ranks, block_source, block_target):
    leaves, rank_top, width = basis.shape
    rhs = charges.shape[1]
    clusters = ranks.shape[0]
    blocks = coupling.shape[0]
    devices = lax.axis_size("clu")
    mains = clusters * 3 // 4
    shape = jax.ShapeDtypeStruct

    cores, chips = 2, 8
    cube = cores * chips
    far = devices // cube
    x, y, z = 1, 2, 4

    def swap_far(part, shift):
        return lax.ppermute(part, "clu", [(d, (d + shift * cube) % devices) for d in range(devices)])

    def swap(part, direction):
        turned = direction << 1 & 7 | direction >> 2
        return lax.ppermute(
            part, "clu", [(d, d ^ (turned if d % cores else direction) * cores) for d in range(devices)]
        )

    def swap_cores(part):
        return lax.ppermute(part, "clu", [(d, d ^ 1) for d in range(devices)])

    me = lax.axis_index("clu")

    def rows(cluster, sign):
        device = cluster // clusters
        core = (device ^ me) % cores
        chip = ((device ^ me) // cores) % chips
        chip = jnp.where(device % cores == 0, chip, chip >> 1 | (chip & 1) << 2)
        away = (sign * (device // cube - me // cube)) % far
        return ((core * chips + chip) * far + away) * clusters + cluster % clusters

    source_rows, target_rows = rows(block_source, -1), rows(block_target, 1)

    tile_shape = (mains, rhs, LANES)
    out_shape = shape((leaves, rhs, width), BF)
    tile_out = shape(tile_shape, BF)
    part_shape = shape((far,) + tile_shape, BF)
    first_coeffs = pl.pallas_call(
        coeff_kernel,
        out_shape=tile_out,
        in_specs=[SMEM, HBM, HBM, HBM],
        out_specs=VMEM,
        scratch_shapes=[
            pltpu.VMEM(charges.shape, BF),
            pltpu.VMEM(basis.shape, BF),
            pltpu.VMEM(transfer.shape, BF),
            pltpu.SemaphoreType.DMA((3,)),
        ],
    )(ranks, charges, basis, transfer)

    order = ((x | y | z, x | y, y | z, z | x), (0, x, y, z))
    couple = pl.pallas_call(
        functools.partial(couple_kernel, order=order, unroll=8),
        out_shape=[shape((4, far) + tile_shape, BF)] * 4,
        in_specs=[SMEM, SMEM, VMEM] + [VMEM] * (cores * chips),
        out_specs=[VMEM] * 4,
        scratch_shapes=[
            pltpu.VMEM((devices * clusters, rhs, LANES), BF),
            pltpu.VMEM((devices * clusters, rhs, LANES), F32),
        ],
        compiler_params=params(32 if devices <= 32 else 60),
        cost_estimate=pl.CostEstimate(
            flops=2 * blocks * rhs * rank_top * rank_top, bytes_accessed=10 << 20, transcendentals=0
        ),
    )

    near = pl.pallas_call(
        near_kernel,
        out_shape=shape((leaves, rhs, width), F32),
        in_specs=[VMEM] * 2,
        out_specs=VMEM,
        compiler_params=params(16),
        cost_estimate=pl.CostEstimate(
            flops=2 * leaves * 3 * rhs * width * width, bytes_accessed=4 << 20, transcendentals=0
        ),
    )

    edge = pl.pallas_call(
        edge_kernel,
        out_shape=shape((2, rhs, width), F32),
        grid=(1,),
        in_specs=[
            SMEM,
            VMEM,
            VMEM,
            pl.BlockSpec((1, 1, width, width), lambda i: (0, 0, 0, 0)),
            pl.BlockSpec((1, 1, width, width), lambda i: (leaves - 1, 2, 0, 0)),
        ],
        out_specs=VMEM,
        compiler_params=params(16),
    )

    def adder(kernel, inputs, outputs):
        return pl.pallas_call(
            kernel,
            out_shape=outputs,
            in_specs=[VMEM] * inputs,
            out_specs=[VMEM] * len(outputs),
            compiler_params=params(16),
        )

    own_shape = shape((far,) + tile_shape, F32)
    first_add = adder(first_add_kernel, 2, [part_shape] * 4)
    second_add = adder(second_add_kernel, 4, [own_shape, part_shape, part_shape])
    third_add = adder(third_add_kernel, 3, [part_shape])
    last_add = adder(last_add_kernel, 4, [shape(tile_shape, F32)] + [tile_out] * (far - 1))

    def finish(with_coeffs):
        return pl.pallas_call(
            functools.partial(field_kernel, away=far - 1),
            out_shape=[out_shape, tile_out] if with_coeffs else [out_shape],
            in_specs=[SMEM] + [VMEM] * (4 + far),
            out_specs=[VMEM, VMEM] if with_coeffs else [VMEM],
            compiler_params=params(16),
        )

    core = me % cores
    barrier = lax.optimization_barrier

    halo_pairs = [(d, d + cores) for d in range(1, devices - cores, cores)]
    halo_pairs += [(d, d - cores) for d in range(cores, devices, cores)]

    def apply_matrix(field_in, coeffs, coupling, with_coeffs):
        head, tail = field_in[:1], field_in[leaves - 1 :]
        away = [swap_far(coeffs, s) for s in range(1, far)]
        away, coupling = barrier((away, coupling))
        got = {0: jnp.stack([coeffs] + away)}
        got[x], got[y], got[z] = barrier((swap(got[0], x), swap(got[0], y), swap(got[0], z)))
        near_sum = near(field_in, near_field)
        got |= {x | y: swap(got[x], y), y | z: swap(got[y], z), z | x: swap(got[z], x)}
        got, near_sum = barrier((got, near_sum))
        other = {chip: swap_cores(got[chip]) for chip in got}
        got[x | y | z], outer = barrier((swap(got[x | y], z), jnp.where(core == 0, head, tail)))
        other[x | y | z] = swap_cores(got[x | y | z])
        outer = lax.ppermute(outer, "clu", halo_pairs)
        totals = couple(
            source_rows,
            target_rows,
            coupling,
            *[got[chip] for chip in range(chips)],
            *[other[chip] for chip in range(chips)],
        )
        (keep_first, keep, send_first, send), outer = barrier((totals, outer))
        corner, xy, yz, zx = first_add(keep_first, swap_cores(send_first))
        swapped = swap_cores(send)
        inner, outer = swap_cores(jnp.where(core == 0, tail, head)), swap_cores(outer)
        edges = edge(core.reshape(1), inner, outer, near_field, near_field)
        corner, yz, zx = barrier((swap(corner, z), swap(yz, y), swap(zx, x)))
        xy = swap((xy.astype(F32) + corner.astype(F32)).astype(BF), y)
        mine, to_y, to_z = second_add(keep, swapped, yz, zx)
        to_y, to_z = swap(to_y, y), swap(to_z, z)
        (to_x,) = third_add(keep, swapped, xy)
        total, *away = last_add(mine, swap(to_x, x), to_y, to_z)
        terms = [swap_far(part, s + 1) for s, part in enumerate(away)]
        return finish(with_coeffs)(ranks, near_sum, edges, basis, transfer, total, *terms)

    coupling, first_coeffs = barrier((coupling, first_coeffs))
    coupling = pl.pallas_call(
        lambda in_ref, out_ref: None,
        out_shape=shape(coupling.shape, BF),
        in_specs=[pl.BlockSpec(memory_space=pl.ANY)],
        out_specs=pl.BlockSpec(memory_space=pl.ANY),
        input_output_aliases={0: 0},
    )(coupling)
    first, second_coeffs = apply_matrix(charges, first_coeffs, coupling, True)
    (second,) = apply_matrix(first, second_coeffs, coupling, False)
    return (first, second)


def solution(mesh):
    in_specs = (
        P("clu", None, None),
        P("clu", None, None),
        P("clu", None, None),
        P("clu", None, None, None),
        P("clu", None, None),
        P("clu"),
        P("clu"),
        P("clu"),
    )
    out_specs = (P("clu", None, None), P("clu", None, None))
    return jax.shard_map(local, mesh=mesh, in_specs=in_specs, out_specs=out_specs, check_vma=False)
```

```python
import functools

import jax
import jax.numpy as jnp
from jax import lax
from jax.experimental import pallas as pl
from jax.experimental.pallas import tpu as pltpu
from jax.sharding import PartitionSpec as P

LANES = 128
BF = jnp.bfloat16
F32 = jnp.float32
VMEM = pl.BlockSpec(memory_space=pltpu.VMEM)
SMEM = pl.BlockSpec(memory_space=pltpu.SMEM)
HBM = pl.BlockSpec(memory_space=pltpu.HBM)


def dot(a, b):
    return lax.dot_general(a, b, (((1,), (0,)), ((), ())), preferred_element_type=F32)


def dot_t(a, b):
    return lax.dot_general(a, b, (((1,), (1,)), ((), ())), preferred_element_type=F32)


def lanes(rows):
    return lax.broadcasted_iota(jnp.int32, (rows, LANES), 1)


def fourth(tiles, rank_top):
    third = LANES - rank_top
    lane = lanes(tiles[0].shape[0])
    moved = [pltpu.roll(tile, third * (k + 1), 1) for k, tile in enumerate(tiles)]
    return jnp.where(lane < third, moved[0], jnp.where(lane < 2 * third, moved[1], moved[2]))


def packed(mains, pad, rank_top):
    lane = lanes(pad.shape[0])
    third = LANES - rank_top
    return [
        jnp.where(lane < rank_top, main, pltpu.roll(pad, rank_top - third * k, 1)) for k, main in enumerate(mains)
    ]


def widen(value):
    return jnp.concatenate([value, jnp.zeros((value.shape[0], LANES - value.shape[1]), value.dtype)], axis=1)


def emit_coeffs(read_leaf, basis_ref, transfer_ref, ranks_ref, out_ref, leaves, rank_top):
    mains, rhs, _ = out_ref.shape
    lane = lax.broadcasted_iota(jnp.int32, (rhs, rank_top), 1)
    coeffs = []
    for i in range(leaves):
        value = dot_t(read_leaf(i), basis_ref[i])
        coeffs.append(jnp.where(lane < ranks_ref[i], value, 0.0).astype(BF))
    for q in range(leaves // 2):
        value = dot(coeffs[2 * q], transfer_ref[2 * q]) + dot(coeffs[2 * q + 1], transfer_ref[2 * q + 1])
        coeffs.append(jnp.where(lane < ranks_ref[leaves + q], value, 0.0).astype(BF))
    wide = [widen(value.astype(F32)) for value in coeffs]
    for q in range(mains // 3):
        for k, tile in enumerate(packed(wide[3 * q : 3 * q + 3], wide[mains + q], rank_top)):
            out_ref[3 * q + k] = tile.astype(BF)


def fetch(pairs, sems):
    copies = [pltpu.make_async_copy(src, dst, sems.at[n]) for n, (src, dst) in enumerate(pairs)]
    for copy in copies:
        copy.start()
    return copies


def emit_edges(core_ref, v_ref, inner_ref, outer_ref):
    head, tail = v_ref[0], v_ref[v_ref.shape[0] - 1]
    even = core_ref[0] == 0
    inner_ref[0] = jnp.where(even, tail, head)
    outer_ref[0] = jnp.where(even, head, tail)


def coeff_kernel(
    ranks_ref, core_ref, v_hbm, basis_hbm, transfer_hbm, out_ref, inner_ref, outer_ref, v_ref, basis_ref, transfer_ref, sems
):
    leaves, rank_top, _ = basis_ref.shape
    for copy in fetch([(v_hbm, v_ref), (basis_hbm, basis_ref), (transfer_hbm, transfer_ref)], sems):
        copy.wait()
    emit_edges(core_ref, v_ref, inner_ref, outer_ref)
    emit_coeffs(lambda i: v_ref[i], basis_ref, transfer_ref, ranks_ref, out_ref, leaves, rank_top)


def couple_kernel(source_ref, target_ref, coupling_ref, *refs, order, unroll):
    chips = sum(len(group) for group in order)
    in_refs, out_refs, (sources, total) = refs[: 2 * chips], refs[2 * chips : -2], refs[-2:]
    blocks, rank_top, _ = coupling_ref.shape
    far, mains, rhs, _ = in_refs[0].shape
    quads = mains // 3
    clusters = mains + quads

    def split(f, _):
        for n, packed_ref in enumerate(in_refs):
            row = (n * far + f) * clusters
            tiles = [packed_ref[f, c] for c in range(mains)]
            for c in range(mains):
                sources[row + c] = tiles[c]
            for q in range(quads):
                wide = [tile.astype(F32) for tile in tiles[3 * q : 3 * q + 3]]
                sources[row + mains + q] = fourth(wide, rank_top).astype(BF)
            for c in range(clusters):
                total[row + c] = jnp.zeros((rhs, LANES), F32)
        return 0

    lax.fori_loop(0, far, split, 0)

    def some(s, _):
        for u in range(unroll):
            j = s * unroll + u
            term = dot(sources[source_ref[j], :, :rank_top], coupling_ref[j])
            at = target_ref[j]
            total[at, :, :rank_top] = total[at, :, :rank_top] + term
        return 0

    lax.fori_loop(0, blocks // unroll, some, 0)

    def pack(f, _):
        for core in range(2):
            for g, group in enumerate(order):
                for place, chip in enumerate(group):
                    row = ((core * chips + chip) * far + f) * clusters
                    for q in range(quads):
                        mains_now = [total[row + 3 * q + k] for k in range(3)]
                        for k, tile in enumerate(packed(mains_now, total[row + mains + q], rank_top)):
                            out_refs[core * len(order) + g][place, f, 3 * q + k] = tile.astype(BF)
        return 0

    lax.fori_loop(0, far, pack, 0)


def near_kernel(v_ref, near_ref, out_ref):
    leaves = v_ref.shape[0]
    for i in range(leaves):
        total = dot(v_ref[i], near_ref[i, 1])
        if i > 0:
            total = total + dot(v_ref[i - 1], near_ref[i, 0])
        if i < leaves - 1:
            total = total + dot(v_ref[i + 1], near_ref[i, 2])
        out_ref[i] = total


def edge_kernel(core_ref, inner_ref, outer_ref, first_ref, last_ref, out_ref):
    inner, outer = inner_ref[0], outer_ref[0]
    even = core_ref[0] == 0
    out_ref[0] = dot(jnp.where(even, outer, inner), first_ref[0, 0])
    out_ref[1] = dot(jnp.where(even, inner, outer), last_ref[0, 0])


def add_kernel(keep_ref, swap_ref, *out_refs):
    for n, out_ref in enumerate(out_refs):
        out_ref[...] = (keep_ref[n].astype(F32) + swap_ref[n].astype(F32)).astype(out_ref.dtype)


def last_add_kernel(own_ref, *refs, parts):
    part_refs, (keep_out, *away_refs) = refs[:parts], refs[parts:]
    for f in range(own_ref.shape[0]):
        total = own_ref[f]
        for part_ref in part_refs:
            total = total + part_ref[f].astype(F32)
        if f == 0:
            keep_out[...] = total
        else:
            away_refs[f - 1][...] = total.astype(BF)


def field_kernel(ranks_ref, core_ref, near_ref, edge_ref, basis_ref, transfer_ref, keep_ref, *rest, away):
    term_refs, out_ref, next_refs = rest[:away], rest[away], rest[away + 1 :]
    leaves, rank_top, _ = basis_ref.shape
    mains, rhs, _ = keep_ref.shape
    tiles = []
    for t in range(mains):
        tile = keep_ref[t]
        for term_ref in term_refs:
            tile = tile + term_ref[t].astype(F32)
        tiles.append(tile)
    sums = tiles + [fourth(tiles[3 * q : 3 * q + 3], rank_top) for q in range(mains // 3)]
    lane = lax.broadcasted_iota(jnp.int32, (rhs, rank_top), 1)
    fields = [
        jnp.where(lane < ranks_ref[c], total[:, :rank_top], 0.0).astype(BF) for c, total in enumerate(sums)
    ]
    for i in range(leaves):
        down = fields[i].astype(F32) + dot_t(fields[leaves + i // 2], transfer_ref[i])
        leaf_total = jnp.where(lane < ranks_ref[i], down, 0.0).astype(BF)
        result = near_ref[i] + dot(leaf_total, basis_ref[i])
        if i == 0:
            result = result + edge_ref[0]
        if i == leaves - 1:
            result = result + edge_ref[1]
        out_ref[i] = result.astype(BF)
    if next_refs:
        coeff_ref, inner_ref, outer_ref = next_refs
        emit_edges(core_ref, out_ref, inner_ref, outer_ref)
        emit_coeffs(lambda i: out_ref[i], basis_ref, transfer_ref, ranks_ref, coeff_ref, leaves, rank_top)


def params(mebibytes):
    return pltpu.CompilerParams(vmem_limit_bytes=mebibytes << 20)


def local(charges, basis, transfer, near_field, coupling, ranks, block_source, block_target):
    leaves, rank_top, width = basis.shape
    rhs = charges.shape[1]
    clusters = ranks.shape[0]
    blocks = coupling.shape[0]
    devices = lax.axis_size("clu")
    mains = clusters * 3 // 4
    shape = jax.ShapeDtypeStruct

    cores, chips = 2, 8
    cube = cores * chips
    far = devices // cube
    x, y, z = 1, 2, 4

    def swap_far(part, shift):
        return lax.ppermute(part, "clu", [(d, (d + shift * cube) % devices) for d in range(devices)])

    def swap(part, direction):
        turned = direction << 1 & 7 | direction >> 2
        return lax.ppermute(
            part, "clu", [(d, d ^ (turned if d % cores else direction) * cores) for d in range(devices)]
        )

    def swap_cores(part):
        return lax.ppermute(part, "clu", [(d, d ^ 1) for d in range(devices)])

    me = lax.axis_index("clu")
    core = me % cores
    barrier = lax.optimization_barrier

    def rows(cluster, sign):
        device = cluster // clusters
        core = (device ^ me) % cores
        chip = ((device ^ me) // cores) % chips
        chip = jnp.where(device % cores == 0, chip, chip >> 1 | (chip & 1) << 2)
        away = (sign * (device // cube - me // cube)) % far
        return ((core * chips + chip) * far + away) * clusters + cluster % clusters

    source_rows, target_rows = rows(block_source, -1), rows(block_target, 1)

    tile_shape = (mains, rhs, LANES)
    out_shape = shape((leaves, rhs, width), BF)
    tile_out = shape(tile_shape, BF)
    part_shape = shape((far,) + tile_shape, BF)
    edge_shape = shape((1, rhs, width), BF)
    core_index = core.reshape(1)
    first_coeffs, inner, outer = pl.pallas_call(
        coeff_kernel,
        out_shape=[tile_out, edge_shape, edge_shape],
        in_specs=[SMEM, SMEM, HBM, HBM, HBM],
        out_specs=[VMEM] * 3,
        scratch_shapes=[
            pltpu.VMEM(charges.shape, BF),
            pltpu.VMEM(basis.shape, BF),
            pltpu.VMEM(transfer.shape, BF),
            pltpu.SemaphoreType.DMA((3,)),
        ],
    )(ranks, core_index, charges, basis, transfer)

    order = ((x | y | z, x | y, y | z, z | x), (0, x, y, z))
    couple = pl.pallas_call(
        functools.partial(couple_kernel, order=order, unroll=8),
        out_shape=[shape((4, far) + tile_shape, BF)] * 4,
        in_specs=[SMEM, SMEM, VMEM] + [VMEM] * (cores * chips),
        out_specs=[VMEM] * 4,
        scratch_shapes=[
            pltpu.VMEM((devices * clusters, rhs, LANES), BF),
            pltpu.VMEM((devices * clusters, rhs, LANES), F32),
        ],
        compiler_params=params(32 if devices <= 32 else 60),
        cost_estimate=pl.CostEstimate(
            flops=2 * blocks * rhs * rank_top * rank_top, bytes_accessed=10 << 20, transcendentals=0
        ),
    )

    near = pl.pallas_call(
        near_kernel,
        out_shape=shape((leaves, rhs, width), F32),
        in_specs=[VMEM] * 2,
        out_specs=VMEM,
        compiler_params=params(16),
        cost_estimate=pl.CostEstimate(
            flops=2 * leaves * 3 * rhs * width * width, bytes_accessed=4 << 20, transcendentals=0
        ),
    )

    edge = pl.pallas_call(
        edge_kernel,
        out_shape=shape((2, rhs, width), F32),
        grid=(1,),
        in_specs=[
            SMEM,
            VMEM,
            VMEM,
            pl.BlockSpec((1, 1, width, width), lambda i: (0, 0, 0, 0)),
            pl.BlockSpec((1, 1, width, width), lambda i: (leaves - 1, 2, 0, 0)),
        ],
        out_specs=VMEM,
        compiler_params=params(16),
    )

    def adder(kernel, inputs, outputs):
        return pl.pallas_call(
            kernel,
            out_shape=outputs,
            in_specs=[VMEM] * inputs,
            out_specs=[VMEM] * len(outputs),
            compiler_params=params(16),
        )

    own_shape = shape((far,) + tile_shape, F32)
    far_add = adder(add_kernel, 2, [part_shape] * 4)
    near_add = adder(add_kernel, 2, [own_shape] + [part_shape] * 3)
    last_add = adder(
        functools.partial(last_add_kernel, parts=chips - 1),
        chips,
        [shape(tile_shape, F32)] + [tile_out] * (far - 1),
    )

    def finish(with_coeffs):
        return pl.pallas_call(
            functools.partial(field_kernel, away=far - 1),
            out_shape=[out_shape, tile_out, edge_shape, edge_shape] if with_coeffs else [out_shape],
            in_specs=[SMEM, SMEM] + [VMEM] * (4 + far),
            out_specs=[VMEM] * 4 if with_coeffs else [VMEM],
            compiler_params=params(16),
        )

    halo_pairs = [(d, d + cores) for d in range(1, devices - cores, cores)]
    halo_pairs += [(d, d - cores) for d in range(cores, devices, cores)]

    long, short = order[0], order[1][1:]

    def apply_matrix(field_in, coeffs, inner, outer, coupling, with_coeffs):
        away = [swap_far(coeffs, s) for s in range(1, far)]
        outer = lax.ppermute(outer, "clu", halo_pairs)
        away, outer, coupling = barrier((away, outer, coupling))
        column = jnp.stack([coeffs] + away)
        got = {chip: swap(column, chip) for chip in long + short}
        near_sum = near(field_in, near_field)
        got, near_sum = barrier((got, near_sum))
        got[0] = column
        other = {chip: swap_cores(got[chip]) for chip in got}
        keep_long, keep, send_long, send = couple(
            source_rows,
            target_rows,
            coupling,
            *[got[chip] for chip in range(chips)],
            *[other[chip] for chip in range(chips)],
        )
        parts = far_add(keep_long, swap_cores(send_long))
        own, *rest = near_add(keep, swap_cores(send))
        parts = [swap(part, chip) for part, chip in zip([*parts, *rest], long + short)]
        total, *away = last_add(own, *parts)
        terms = [swap_far(part, s + 1) for s, part in enumerate(away)]
        inner, outer = swap_cores(inner), swap_cores(outer)
        edges = edge(core_index, inner, outer, near_field, near_field)
        return finish(with_coeffs)(ranks, core_index, near_sum, edges, basis, transfer, total, *terms)

    coupling, first_coeffs = barrier((coupling, first_coeffs))
    coupling = pl.pallas_call(
        lambda in_ref, out_ref: None,
        out_shape=shape(coupling.shape, BF),
        in_specs=[pl.BlockSpec(memory_space=pl.ANY)],
        out_specs=pl.BlockSpec(memory_space=pl.ANY),
        input_output_aliases={0: 0},
    )(coupling)
    first, *second_args = apply_matrix(charges, first_coeffs, inner, outer, coupling, True)
    (second,) = apply_matrix(first, *second_args, coupling, False)
    return (first, second)


def solution(mesh):
    in_specs = (
        P("clu", None, None),
        P("clu", None, None),
        P("clu", None, None),
        P("clu", None, None, None),
        P("clu", None, None),
        P("clu"),
        P("clu"),
        P("clu"),
    )
    out_specs = (P("clu", None, None), P("clu", None, None))
    return jax.shard_map(local, mesh=mesh, in_specs=in_specs, out_specs=out_specs, check_vma=False)
```

```python
import functools

import jax
import jax.numpy as jnp
from jax import lax
from jax.experimental import pallas as pl
from jax.experimental.pallas import tpu as pltpu
from jax.sharding import PartitionSpec as P

LANES = 128
BF = jnp.bfloat16
F32 = jnp.float32
VMEM = pl.BlockSpec(memory_space=pltpu.VMEM)
SMEM = pl.BlockSpec(memory_space=pltpu.SMEM)
HBM = pl.BlockSpec(memory_space=pltpu.HBM)


def dot(a, b):
    return lax.dot_general(a, b, (((1,), (0,)), ((), ())), preferred_element_type=F32)


def dot_t(a, b):
    return lax.dot_general(a, b, (((1,), (1,)), ((), ())), preferred_element_type=F32)


def lanes(rows):
    return lax.broadcasted_iota(jnp.int32, (rows, LANES), 1)


def fourth(tiles, rank_top):
    third = LANES - rank_top
    lane = lanes(tiles[0].shape[0])
    moved = [pltpu.roll(tile, third * (k + 1), 1) for k, tile in enumerate(tiles)]
    return jnp.where(lane < third, moved[0], jnp.where(lane < 2 * third, moved[1], moved[2]))


def packed(mains, pad, rank_top):
    lane = lanes(pad.shape[0])
    third = LANES - rank_top
    return [
        jnp.where(lane < rank_top, main, pltpu.roll(pad, rank_top - third * k, 1)) for k, main in enumerate(mains)
    ]


def widen(value):
    return jnp.concatenate([value, jnp.zeros((value.shape[0], LANES - value.shape[1]), value.dtype)], axis=1)


def emit_coeffs(read_leaf, basis_ref, transfer_ref, ranks_ref, out_ref, leaves, rank_top):
    mains, rhs, _ = out_ref.shape
    lane = lax.broadcasted_iota(jnp.int32, (rhs, rank_top), 1)
    coeffs = []
    for i in range(leaves):
        value = dot_t(read_leaf(i), basis_ref[i])
        coeffs.append(jnp.where(lane < ranks_ref[i], value, 0.0).astype(BF))
    for q in range(leaves // 2):
        value = dot(coeffs[2 * q], transfer_ref[2 * q]) + dot(coeffs[2 * q + 1], transfer_ref[2 * q + 1])
        coeffs.append(jnp.where(lane < ranks_ref[leaves + q], value, 0.0).astype(BF))
    wide = [widen(value.astype(F32)) for value in coeffs]
    for q in range(mains // 3):
        for k, tile in enumerate(packed(wide[3 * q : 3 * q + 3], wide[mains + q], rank_top)):
            out_ref[3 * q + k] = tile.astype(BF)


def fetch(pairs, sems):
    copies = [pltpu.make_async_copy(src, dst, sems.at[n]) for n, (src, dst) in enumerate(pairs)]
    for copy in copies:
        copy.start()
    return copies


def emit_edges(core_ref, v_ref, inner_ref, outer_ref):
    head, tail = v_ref[0], v_ref[v_ref.shape[0] - 1]
    even = core_ref[0] == 0
    inner_ref[0] = jnp.where(even, tail, head)
    outer_ref[0] = jnp.where(even, head, tail)


def coeff_kernel(
    ranks_ref, core_ref, v_hbm, basis_hbm, transfer_hbm, out_ref, inner_ref, outer_ref, v_ref, basis_ref, transfer_ref, sems
):
    leaves, rank_top, _ = basis_ref.shape
    for copy in fetch([(v_hbm, v_ref), (basis_hbm, basis_ref), (transfer_hbm, transfer_ref)], sems):
        copy.wait()
    emit_edges(core_ref, v_ref, inner_ref, outer_ref)
    emit_coeffs(lambda i: v_ref[i], basis_ref, transfer_ref, ranks_ref, out_ref, leaves, rank_top)


def couple_kernel(source_ref, target_ref, coupling_ref, *refs, sets, unroll):
    in_refs, out_refs, (sources, total) = refs[:sets], refs[sets:-2], refs[-2:]
    blocks, rank_top, _ = coupling_ref.shape
    chips, far, mains, rhs, _ = in_refs[0].shape
    quads = mains // 3
    clusters = mains + quads

    def split(f, _):
        for n, packed_ref in enumerate(in_refs):
            for chip in range(chips):
                row = ((n * chips + chip) * far + f) * clusters
                tiles = [packed_ref[chip, f, c] for c in range(mains)]
                for c in range(mains):
                    sources[row + c] = tiles[c]
                for q in range(quads):
                    wide = [tile.astype(F32) for tile in tiles[3 * q : 3 * q + 3]]
                    sources[row + mains + q] = fourth(wide, rank_top).astype(BF)
                for c in range(clusters):
                    total[row + c] = jnp.zeros((rhs, LANES), F32)
        return 0

    lax.fori_loop(0, far, split, 0)

    def some(s, _):
        for u in range(unroll):
            j = s * unroll + u
            term = dot(sources[source_ref[j], :, :rank_top], coupling_ref[j])
            at = target_ref[j]
            total[at, :, :rank_top] = total[at, :, :rank_top] + term
        return 0

    lax.fori_loop(0, blocks // unroll, some, 0)

    def pack(f, _):
        for n, packed_ref in enumerate(out_refs):
            for chip in range(chips):
                row = ((n * chips + chip) * far + f) * clusters
                for q in range(quads):
                    mains_now = [total[row + 3 * q + k] for k in range(3)]
                    for k, tile in enumerate(packed(mains_now, total[row + mains + q], rank_top)):
                        packed_ref[chip, f, 3 * q + k] = tile.astype(BF)
        return 0

    lax.fori_loop(0, far, pack, 0)


def near_kernel(v_ref, near_ref, out_ref):
    leaves = v_ref.shape[0]
    for i in range(leaves):
        total = dot(v_ref[i], near_ref[i, 1])
        if i > 0:
            total = total + dot(v_ref[i - 1], near_ref[i, 0])
        if i < leaves - 1:
            total = total + dot(v_ref[i + 1], near_ref[i, 2])
        out_ref[i] = total


def edge_kernel(core_ref, inner_ref, outer_ref, first_ref, last_ref, out_ref):
    inner, outer = inner_ref[0], outer_ref[0]
    even = core_ref[0] == 0
    out_ref[0] = dot(jnp.where(even, outer, inner), first_ref[0, 0])
    out_ref[1] = dot(jnp.where(even, inner, outer), last_ref[0, 0])


def join_kernel(*refs):
    for n, part_ref in enumerate(refs[:-1]):
        refs[-1][n] = part_ref[...]


def halve_kernel(*refs, parts):
    part_refs, (keep_out, *send_refs) = refs[:parts], refs[parts:]
    pieces = 1 + len(send_refs)
    size = part_refs[0].shape[0] // pieces
    for n in range(pieces):
        total = None
        for part_ref in part_refs:
            part = part_ref[pl.ds(n * size, size)].astype(F32)
            total = part if total is None else total + part
        if n == 0:
            keep_out[...] = total
        else:
            send_refs[n - 1][...] = total.astype(BF)


def add_kernel(first_ref, second_ref, out_ref):
    out_ref[...] = (first_ref[...].astype(F32) + second_ref[...].astype(F32)).astype(BF)


def field_kernel(ranks_ref, core_ref, near_ref, edge_ref, basis_ref, transfer_ref, keep_ref, *rest, away):
    term_refs, out_ref, next_refs = rest[:away], rest[away], rest[away + 1 :]
    leaves, rank_top, _ = basis_ref.shape
    _, mains, rhs, _ = keep_ref.shape
    tiles = []
    for t in range(mains):
        tile = keep_ref[0, t]
        for term_ref in term_refs:
            tile = tile + term_ref[0, t].astype(F32)
        tiles.append(tile)
    sums = tiles + [fourth(tiles[3 * q : 3 * q + 3], rank_top) for q in range(mains // 3)]
    lane = lax.broadcasted_iota(jnp.int32, (rhs, rank_top), 1)
    fields = [
        jnp.where(lane < ranks_ref[c], total[:, :rank_top], 0.0).astype(BF) for c, total in enumerate(sums)
    ]
    for i in range(leaves):
        down = fields[i].astype(F32) + dot_t(fields[leaves + i // 2], transfer_ref[i])
        leaf_total = jnp.where(lane < ranks_ref[i], down, 0.0).astype(BF)
        result = near_ref[i] + dot(leaf_total, basis_ref[i])
        if i == 0:
            result = result + edge_ref[0]
        if i == leaves - 1:
            result = result + edge_ref[1]
        out_ref[i] = result.astype(BF)
    if next_refs:
        coeff_ref, inner_ref, outer_ref = next_refs
        emit_edges(core_ref, out_ref, inner_ref, outer_ref)
        emit_coeffs(lambda i: out_ref[i], basis_ref, transfer_ref, ranks_ref, coeff_ref, leaves, rank_top)


def params(mebibytes):
    return pltpu.CompilerParams(vmem_limit_bytes=mebibytes << 20)


def local(charges, basis, transfer, near_field, coupling, ranks, block_source, block_target):
    leaves, rank_top, width = basis.shape
    rhs = charges.shape[1]
    clusters = ranks.shape[0]
    blocks = coupling.shape[0]
    devices = lax.axis_size("clu")
    mains = clusters * 3 // 4
    shape = jax.ShapeDtypeStruct

    cores, chips = 2, 8
    cube = cores * chips
    far = devices // cube
    x, y, z = 1, 2, 4

    def swap_far(part, shift):
        return lax.ppermute(part, "clu", [(d, (d + shift * cube) % devices) for d in range(devices)])

    def swap(part, direction):
        turned = direction << 1 & 7 | direction >> 2
        return lax.ppermute(
            part, "clu", [(d, d ^ (turned if d % cores else direction) * cores) for d in range(devices)]
        )

    def swap_cores(part):
        return lax.ppermute(part, "clu", [(d, d ^ 1) for d in range(devices)])

    me = lax.axis_index("clu")
    core = me % cores
    barrier = lax.optimization_barrier

    def rows(cluster, sign):
        device = cluster // clusters
        core = (device ^ me) % cores
        chip = ((device ^ me) // cores) % chips
        chip = jnp.where(device % cores == 0, chip, chip >> 1 | (chip & 1) << 2)
        away = (sign * (device // cube - me // cube)) % far
        return ((core * chips + chip) * far + away) * clusters + cluster % clusters

    source_rows, target_rows = rows(block_source, -1), rows(block_target, 1)

    tile_shape = (mains, rhs, LANES)
    out_shape = shape((leaves, rhs, width), BF)
    tile_out = shape(tile_shape, BF)
    part_shape = shape((far,) + tile_shape, BF)
    edge_shape = shape((1, rhs, width), BF)
    core_index = core.reshape(1)
    first_coeffs, inner, outer = pl.pallas_call(
        coeff_kernel,
        out_shape=[tile_out, edge_shape, edge_shape],
        in_specs=[SMEM, SMEM, HBM, HBM, HBM],
        out_specs=[VMEM] * 3,
        scratch_shapes=[
            pltpu.VMEM(charges.shape, BF),
            pltpu.VMEM(basis.shape, BF),
            pltpu.VMEM(transfer.shape, BF),
            pltpu.SemaphoreType.DMA((3,)),
        ],
    )(ranks, core_index, charges, basis, transfer)

    sets = cores * 2
    half_shape = shape((chips // 2, far) + tile_shape, BF)
    couple = pl.pallas_call(
        functools.partial(couple_kernel, sets=sets, unroll=8),
        out_shape=[half_shape] * sets,
        in_specs=[SMEM, SMEM, VMEM] + [VMEM] * sets,
        out_specs=[VMEM] * sets,
        scratch_shapes=[
            pltpu.VMEM((devices * clusters, rhs, LANES), BF),
            pltpu.VMEM((devices * clusters, rhs, LANES), F32),
        ],
        compiler_params=params(32 if devices <= 32 else 60),
        cost_estimate=pl.CostEstimate(
            flops=2 * blocks * rhs * rank_top * rank_top, bytes_accessed=10 << 20, transcendentals=0
        ),
    )

    near = pl.pallas_call(
        near_kernel,
        out_shape=shape((leaves, rhs, width), F32),
        in_specs=[VMEM] * 2,
        out_specs=VMEM,
        compiler_params=params(16),
        cost_estimate=pl.CostEstimate(
            flops=2 * leaves * 3 * rhs * width * width, bytes_accessed=4 << 20, transcendentals=0
        ),
    )

    edge = pl.pallas_call(
        edge_kernel,
        out_shape=shape((2, rhs, width), F32),
        grid=(1,),
        in_specs=[
            SMEM,
            VMEM,
            VMEM,
            pl.BlockSpec((1, 1, width, width), lambda i: (0, 0, 0, 0)),
            pl.BlockSpec((1, 1, width, width), lambda i: (leaves - 1, 2, 0, 0)),
        ],
        out_specs=VMEM,
        compiler_params=params(16),
    )

    def call(kernel, outputs, *args):
        return pl.pallas_call(
            kernel,
            out_shape=outputs,
            in_specs=[VMEM] * len(args),
            out_specs=[VMEM] * len(outputs),
            compiler_params=params(16),
        )(*args)

    def join(*parts):
        return call(join_kernel, [shape((len(parts),) + parts[0].shape, BF)], *parts)[0]

    def halve(pieces, *parts):
        lead = parts[0].shape[0] // pieces
        sizes = (lead,) + parts[0].shape[1:]
        outputs = [shape(sizes, F32)] + [shape(sizes, BF)] * (pieces - 1)
        return call(functools.partial(halve_kernel, parts=len(parts)), outputs, *parts)

    def finish(with_coeffs):
        return pl.pallas_call(
            functools.partial(field_kernel, away=far - 1),
            out_shape=[out_shape, tile_out, edge_shape, edge_shape] if with_coeffs else [out_shape],
            in_specs=[SMEM, SMEM] + [VMEM] * (4 + far),
            out_specs=[VMEM] * 4 if with_coeffs else [VMEM],
            compiler_params=params(16),
        )

    halo_pairs = [(d, d + cores) for d in range(1, devices - cores, cores)]
    halo_pairs += [(d, d - cores) for d in range(cores, devices, cores)]

    def apply_matrix(field_in, coeffs, inner, outer, coupling, with_coeffs):
        early = coupling is not given
        away = [swap_far(coeffs, s) for s in range(1, far)]
        if not early:
            outer = lax.ppermute(outer, "clu", halo_pairs)
            near_sum = near(field_in, near_field)
            away, outer, near_sum = barrier((away, outer, near_sum))
            coupling = relaid
        column = join(coeffs, *away)
        square = join(column, swap(column, x))
        square = join(square, swap(square, y)).reshape(half_shape.shape)
        if early:
            square, outer = barrier((square, outer))
            outer = lax.ppermute(outer, "clu", halo_pairs)
            near_sum = near(field_in, near_field)
        beyond, other, coupling, near_sum = barrier((swap(square, z), swap_cores(square), coupling, near_sum))
        other_beyond, outer = barrier((swap_cores(beyond), outer))
        totals = couple(source_rows, target_rows, coupling, square, beyond, other, other_beyond)
        keep, keep_beyond, send, send_beyond = totals
        (sent,) = call(add_kernel, [half_shape], keep_beyond, swap_cores(send_beyond))
        sent, send = barrier((sent, send))
        inner, outer = swap_cores(inner), swap_cores(outer)
        edges = edge(core_index, inner, outer, near_field, near_field)
        sent, swapped, edges = barrier((swap(sent, z), swap_cores(send), edges))
        keep, sent = halve(2, *[part.reshape((2, 2 * far) + tile_shape) for part in (keep, swapped, sent)])
        keep, sent = halve(2, *[part.reshape((2, far) + tile_shape) for part in (keep, swap(sent, y))])
        total, *away = halve(far, *[part.reshape((far,) + tile_shape) for part in (keep, swap(sent, x))])
        terms = [swap_far(part, s + 1) for s, part in enumerate(away)]
        return finish(with_coeffs)(ranks, core_index, near_sum, edges, basis, transfer, total, *terms)

    given = coupling
    coupling, first_coeffs = barrier((coupling, first_coeffs))
    relaid = pl.pallas_call(
        lambda in_ref, out_ref: None,
        out_shape=shape(coupling.shape, BF),
        in_specs=[pl.BlockSpec(memory_space=pl.ANY)],
        out_specs=pl.BlockSpec(memory_space=pl.ANY),
        input_output_aliases={0: 0},
        compiler_params=params(1),
    )(coupling)
    first, *second_args = apply_matrix(charges, first_coeffs, inner, outer, given, True)
    (second,) = apply_matrix(first, *second_args, relaid, False)
    return (first, second)


def solution(mesh):
    in_specs = (
        P("clu", None, None),
        P("clu", None, None),
        P("clu", None, None),
        P("clu", None, None, None),
        P("clu", None, None),
        P("clu"),
        P("clu"),
        P("clu"),
    )
    out_specs = (P("clu", None, None), P("clu", None, None))
    return jax.shard_map(local, mesh=mesh, in_specs=in_specs, out_specs=out_specs, check_vma=False)
```

```python
import functools

import jax
import jax.numpy as jnp
from jax import lax
from jax.experimental import pallas as pl
from jax.experimental.pallas import tpu as pltpu
from jax.sharding import PartitionSpec as P

LANES = 128
BF = jnp.bfloat16
F32 = jnp.float32
VMEM = pl.BlockSpec(memory_space=pltpu.VMEM)
SMEM = pl.BlockSpec(memory_space=pltpu.SMEM)
HBM = pl.BlockSpec(memory_space=pltpu.HBM)


def dot(a, b):
    return lax.dot_general(a, b, (((1,), (0,)), ((), ())), preferred_element_type=F32)


def dot_t(a, b):
    return lax.dot_general(a, b, (((1,), (1,)), ((), ())), preferred_element_type=F32)


def lanes(rows):
    return lax.broadcasted_iota(jnp.int32, (rows, LANES), 1)


def fourth(tiles, rank_top):
    third = LANES - rank_top
    lane = lanes(tiles[0].shape[0])
    moved = [pltpu.roll(tile, third * (k + 1), 1) for k, tile in enumerate(tiles)]
    return jnp.where(lane < third, moved[0], jnp.where(lane < 2 * third, moved[1], moved[2]))


def packed(mains, pad, rank_top):
    lane = lanes(pad.shape[0])
    third = LANES - rank_top
    return [
        jnp.where(lane < rank_top, main, pltpu.roll(pad, rank_top - third * k, 1)) for k, main in enumerate(mains)
    ]


def widen(value):
    return jnp.concatenate([value, jnp.zeros((value.shape[0], LANES - value.shape[1]), value.dtype)], axis=1)


def emit_coeffs(read_leaf, basis_ref, transfer_ref, ranks_ref, out_ref, leaves, rank_top):
    mains, rhs, _ = out_ref.shape
    lane = lax.broadcasted_iota(jnp.int32, (rhs, rank_top), 1)
    coeffs = []
    for i in range(leaves):
        value = dot_t(read_leaf(i), basis_ref[i])
        coeffs.append(jnp.where(lane < ranks_ref[i], value, 0.0).astype(BF))
    for q in range(leaves // 2):
        value = dot(coeffs[2 * q], transfer_ref[2 * q]) + dot(coeffs[2 * q + 1], transfer_ref[2 * q + 1])
        coeffs.append(jnp.where(lane < ranks_ref[leaves + q], value, 0.0).astype(BF))
    wide = [widen(value.astype(F32)) for value in coeffs]
    for q in range(mains // 3):
        for k, tile in enumerate(packed(wide[3 * q : 3 * q + 3], wide[mains + q], rank_top)):
            out_ref[3 * q + k] = tile.astype(BF)


def fetch(pairs, sems):
    copies = [pltpu.make_async_copy(src, dst, sems.at[n]) for n, (src, dst) in enumerate(pairs)]
    for copy in copies:
        copy.start()
    return copies


def emit_edges(core_ref, v_ref, inner_ref, outer_ref):
    head, tail = v_ref[0], v_ref[v_ref.shape[0] - 1]
    even = core_ref[0] == 0
    inner_ref[0] = jnp.where(even, tail, head)
    outer_ref[0] = jnp.where(even, head, tail)


def coeff_kernel(
    ranks_ref, core_ref, v_hbm, basis_hbm, transfer_hbm, out_ref, inner_ref, outer_ref, v_ref, basis_ref, transfer_ref, sems
):
    leaves, rank_top, _ = basis_ref.shape
    for copy in fetch([(v_hbm, v_ref), (basis_hbm, basis_ref), (transfer_hbm, transfer_ref)], sems):
        copy.wait()
    emit_edges(core_ref, v_ref, inner_ref, outer_ref)
    emit_coeffs(lambda i: v_ref[i], basis_ref, transfer_ref, ranks_ref, out_ref, leaves, rank_top)


def couple_kernel(source_ref, target_ref, coupling_ref, *refs, order, unroll):
    chips = sum(len(group) for group in order)
    in_refs, out_refs, (sources, total) = refs[: 2 * chips], refs[2 * chips : -2], refs[-2:]
    blocks, rank_top, _ = coupling_ref.shape
    far, mains, rhs, _ = in_refs[0].shape
    quads = mains // 3
    clusters = mains + quads

    def split(f, _):
        for n, packed_ref in enumerate(in_refs):
            row = (n * far + f) * clusters
            tiles = [packed_ref[f, c] for c in range(mains)]
            for c in range(mains):
                sources[row + c] = tiles[c]
            for q in range(quads):
                wide = [tile.astype(F32) for tile in tiles[3 * q : 3 * q + 3]]
                sources[row + mains + q] = fourth(wide, rank_top).astype(BF)
            for c in range(clusters):
                total[row + c] = jnp.zeros((rhs, LANES), F32)
        return 0

    lax.fori_loop(0, far, split, 0)

    def some(s, _):
        for u in range(unroll):
            j = s * unroll + u
            term = dot(sources[source_ref[j], :, :rank_top], coupling_ref[j])
            at = target_ref[j]
            total[at, :, :rank_top] = total[at, :, :rank_top] + term
        return 0

    lax.fori_loop(0, blocks // unroll, some, 0)

    def pack(f, _):
        for core in range(2):
            for g, group in enumerate(order):
                for place, chip in enumerate(group):
                    row = ((core * chips + chip) * far + f) * clusters
                    for q in range(quads):
                        mains_now = [total[row + 3 * q + k] for k in range(3)]
                        for k, tile in enumerate(packed(mains_now, total[row + mains + q], rank_top)):
                            out_refs[core * len(order) + g][place, f, 3 * q + k] = tile.astype(BF)
        return 0

    lax.fori_loop(0, far, pack, 0)


def near_kernel(v_ref, near_ref, out_ref):
    leaves = v_ref.shape[0]
    for i in range(leaves):
        total = dot(v_ref[i], near_ref[i, 1])
        if i > 0:
            total = total + dot(v_ref[i - 1], near_ref[i, 0])
        if i < leaves - 1:
            total = total + dot(v_ref[i + 1], near_ref[i, 2])
        out_ref[i] = total


def edge_kernel(core_ref, inner_ref, outer_ref, first_ref, last_ref, out_ref):
    inner, outer = inner_ref[0], outer_ref[0]
    even = core_ref[0] == 0
    out_ref[0] = dot(jnp.where(even, outer, inner), first_ref[0, 0])
    out_ref[1] = dot(jnp.where(even, inner, outer), last_ref[0, 0])


def add_kernel(keep_ref, swap_ref, *out_refs):
    for n, out_ref in enumerate(out_refs):
        out_ref[...] = (keep_ref[n].astype(F32) + swap_ref[n].astype(F32)).astype(out_ref.dtype)


def middle_add_kernel(keep_ref, swap_ref, *refs, parts):
    part_refs, (own_out, *out_refs) = refs[:parts], refs[parts:]
    own_out[...] = keep_ref[0].astype(F32) + swap_ref[0].astype(F32)
    for n, (part_ref, out_ref) in enumerate(zip(part_refs, out_refs)):
        total = keep_ref[n + 1].astype(F32) + swap_ref[n + 1].astype(F32)
        out_ref[...] = (total + part_ref[...].astype(F32)).astype(BF)


def join_kernel(*refs):
    for n, part_ref in enumerate(refs[:-1]):
        refs[-1][n] = part_ref[...]


def last_add_kernel(own_ref, *refs, parts):
    part_refs, (keep_out, *away_refs) = refs[:parts], refs[parts:]
    for f in range(own_ref.shape[0]):
        total = own_ref[f]
        for part_ref in part_refs:
            total = total + part_ref[f].astype(F32)
        if f == 0:
            keep_out[...] = total
        else:
            away_refs[f - 1][...] = total.astype(BF)


def field_kernel(ranks_ref, core_ref, near_ref, edge_ref, basis_ref, transfer_ref, keep_ref, *rest, away):
    term_refs, out_ref, next_refs = rest[:away], rest[away], rest[away + 1 :]
    leaves, rank_top, _ = basis_ref.shape
    mains, rhs, _ = keep_ref.shape
    tiles = []
    for t in range(mains):
        tile = keep_ref[t]
        for term_ref in term_refs:
            tile = tile + term_ref[t].astype(F32)
        tiles.append(tile)
    sums = tiles + [fourth(tiles[3 * q : 3 * q + 3], rank_top) for q in range(mains // 3)]
    lane = lax.broadcasted_iota(jnp.int32, (rhs, rank_top), 1)
    fields = [
        jnp.where(lane < ranks_ref[c], total[:, :rank_top], 0.0).astype(BF) for c, total in enumerate(sums)
    ]
    for i in range(leaves):
        down = fields[i].astype(F32) + dot_t(fields[leaves + i // 2], transfer_ref[i])
        leaf_total = jnp.where(lane < ranks_ref[i], down, 0.0).astype(BF)
        result = near_ref[i] + dot(leaf_total, basis_ref[i])
        if i == 0:
            result = result + edge_ref[0]
        if i == leaves - 1:
            result = result + edge_ref[1]
        out_ref[i] = result.astype(BF)
    if next_refs:
        coeff_ref, inner_ref, outer_ref = next_refs
        emit_edges(core_ref, out_ref, inner_ref, outer_ref)
        emit_coeffs(lambda i: out_ref[i], basis_ref, transfer_ref, ranks_ref, coeff_ref, leaves, rank_top)


def params(mebibytes):
    return pltpu.CompilerParams(vmem_limit_bytes=mebibytes << 20)


def local(charges, basis, transfer, near_field, coupling, ranks, block_source, block_target):
    leaves, rank_top, width = basis.shape
    rhs = charges.shape[1]
    clusters = ranks.shape[0]
    blocks = coupling.shape[0]
    devices = lax.axis_size("clu")
    mains = clusters * 3 // 4
    shape = jax.ShapeDtypeStruct

    cores, chips = 2, 8
    cube = cores * chips
    far = devices // cube
    x, y, z = 1, 2, 4

    def swap_far(part, shift):
        return lax.ppermute(part, "clu", [(d, (d + shift * cube) % devices) for d in range(devices)])

    def swap(part, direction):
        turned = direction << 1 & 7 | direction >> 2
        return lax.ppermute(
            part, "clu", [(d, d ^ (turned if d % cores else direction) * cores) for d in range(devices)]
        )

    def swap_cores(part):
        return lax.ppermute(part, "clu", [(d, d ^ 1) for d in range(devices)])

    me = lax.axis_index("clu")
    core = me % cores
    barrier = lax.optimization_barrier

    def rows(cluster, sign):
        device = cluster // clusters
        core = (device ^ me) % cores
        chip = ((device ^ me) // cores) % chips
        chip = jnp.where(device % cores == 0, chip, chip >> 1 | (chip & 1) << 2)
        away = (sign * (device // cube - me // cube)) % far
        return ((core * chips + chip) * far + away) * clusters + cluster % clusters

    source_rows, target_rows = rows(block_source, -1), rows(block_target, 1)

    tile_shape = (mains, rhs, LANES)
    out_shape = shape((leaves, rhs, width), BF)
    tile_out = shape(tile_shape, BF)
    part_shape = shape((far,) + tile_shape, BF)
    edge_shape = shape((1, rhs, width), BF)
    core_index = core.reshape(1)
    first_coeffs, inner, outer = pl.pallas_call(
        coeff_kernel,
        out_shape=[tile_out, edge_shape, edge_shape],
        in_specs=[SMEM, SMEM, HBM, HBM, HBM],
        out_specs=[VMEM] * 3,
        scratch_shapes=[
            pltpu.VMEM(charges.shape, BF),
            pltpu.VMEM(basis.shape, BF),
            pltpu.VMEM(transfer.shape, BF),
            pltpu.SemaphoreType.DMA((3,)),
        ],
    )(ranks, core_index, charges, basis, transfer)

    order = ((x | y | z, x | y, y | z, z | x), (0, x, y, z))
    couple = pl.pallas_call(
        functools.partial(couple_kernel, order=order, unroll=8),
        out_shape=[shape((4, far) + tile_shape, BF)] * 4,
        in_specs=[SMEM, SMEM, VMEM] + [VMEM] * (cores * chips),
        out_specs=[VMEM] * 4,
        scratch_shapes=[
            pltpu.VMEM((devices * clusters, rhs, LANES), BF),
            pltpu.VMEM((devices * clusters, rhs, LANES), F32),
        ],
        compiler_params=params(32 if devices <= 32 else 60),
        cost_estimate=pl.CostEstimate(
            flops=2 * blocks * rhs * rank_top * rank_top, bytes_accessed=10 << 20, transcendentals=0
        ),
    )

    near = pl.pallas_call(
        near_kernel,
        out_shape=shape((leaves, rhs, width), F32),
        in_specs=[VMEM] * 2,
        out_specs=VMEM,
        compiler_params=params(16),
        cost_estimate=pl.CostEstimate(
            flops=2 * leaves * 3 * rhs * width * width, bytes_accessed=4 << 20, transcendentals=0
        ),
    )

    edge = pl.pallas_call(
        edge_kernel,
        out_shape=shape((2, rhs, width), F32),
        grid=(1,),
        in_specs=[
            SMEM,
            VMEM,
            VMEM,
            pl.BlockSpec((1, 1, width, width), lambda i: (0, 0, 0, 0)),
            pl.BlockSpec((1, 1, width, width), lambda i: (leaves - 1, 2, 0, 0)),
        ],
        out_specs=VMEM,
        compiler_params=params(16),
    )

    def adder(kernel, inputs, outputs):
        return pl.pallas_call(
            kernel,
            out_shape=outputs,
            in_specs=[VMEM] * inputs,
            out_specs=[VMEM] * len(outputs),
            compiler_params=params(16),
        )

    own_shape = shape((far,) + tile_shape, F32)
    join = adder(join_kernel, far, [part_shape])
    far_add = adder(add_kernel, 2, [part_shape] * 4)
    middle_add = adder(functools.partial(middle_add_kernel, parts=3), 5, [own_shape] + [part_shape] * 3)
    last_add = adder(
        functools.partial(last_add_kernel, parts=4), 5, [shape(tile_shape, F32)] + [tile_out] * (far - 1)
    )

    def finish(with_coeffs):
        return pl.pallas_call(
            functools.partial(field_kernel, away=far - 1),
            out_shape=[out_shape, tile_out, edge_shape, edge_shape] if with_coeffs else [out_shape],
            in_specs=[SMEM, SMEM] + [VMEM] * (4 + far),
            out_specs=[VMEM] * 4 if with_coeffs else [VMEM],
            compiler_params=params(16),
        )

    halo_pairs = [(d, d + cores) for d in range(1, devices - cores, cores)]
    halo_pairs += [(d, d - cores) for d in range(cores, devices, cores)]

    def apply_matrix(field_in, coeffs, inner, outer, coupling, with_coeffs):
        (column,) = join(coeffs, *[swap_far(coeffs, s) for s in range(1, far)])
        got = {0: column, x: swap(column, x), y: swap(column, y), z: swap(column, z)}
        got, coupling = barrier((got, coupling))
        corner = swap(column, x | y | z)
        other = {chip: swap_cores(part) for chip, part in got.items()}
        got |= {x | y: swap(got[x], y), y | z: swap(got[y], z), z | x: swap(got[z], x)}
        outer = lax.ppermute(outer, "clu", halo_pairs)
        near_sum = near(field_in, near_field)
        got, corner, outer, near_sum = barrier((got, corner, outer, near_sum))
        got[x | y | z] = corner
        other |= {chip: swap_cores(got[chip]) for chip in order[0]}
        keep_long, keep, send_long, send = couple(
            source_rows,
            target_rows,
            coupling,
            *[got[chip] for chip in range(chips)],
            *[other[chip] for chip in range(chips)],
        )
        corner, xy, yz, zx = far_add(keep_long, swap_cores(send_long))
        corner, xy, yz, zx, send = barrier((corner, xy, yz, zx, send))
        inner, outer = swap_cores(inner), swap_cores(outer)
        edges = edge(core_index, inner, outer, near_field, near_field)
        to_x, to_y, to_z, swapped, edges = barrier((swap(xy, y), swap(yz, z), swap(zx, x), swap_cores(send), edges))
        own, to_x, to_y, to_z = middle_add(keep, swapped, to_x, to_y, to_z)
        total, *away = last_add(own, swap(to_x, x), swap(to_y, y), swap(to_z, z), swap(corner, x | y | z))
        terms = [swap_far(part, s + 1) for s, part in enumerate(away)]
        return finish(with_coeffs)(ranks, core_index, near_sum, edges, basis, transfer, total, *terms)

    coupling, first_coeffs = barrier((coupling, first_coeffs))
    coupling = pl.pallas_call(
        lambda in_ref, out_ref: None,
        out_shape=shape(coupling.shape, BF),
        in_specs=[pl.BlockSpec(memory_space=pl.ANY)],
        out_specs=pl.BlockSpec(memory_space=pl.ANY),
        input_output_aliases={0: 0},
        compiler_params=params(1),
    )(coupling)
    first, *second_args = apply_matrix(charges, first_coeffs, inner, outer, coupling, True)
    (second,) = apply_matrix(first, *second_args, coupling, False)
    return (first, second)


def solution(mesh):
    in_specs = (
        P("clu", None, None),
        P("clu", None, None),
        P("clu", None, None),
        P("clu", None, None, None),
        P("clu", None, None),
        P("clu"),
        P("clu"),
        P("clu"),
    )
    out_specs = (P("clu", None, None), P("clu", None, None))
    return jax.shard_map(local, mesh=mesh, in_specs=in_specs, out_specs=out_specs, check_vma=False)
```

```python
import functools

import jax
import jax.numpy as jnp
from jax import lax
from jax.experimental import pallas as pl
from jax.experimental.pallas import tpu as pltpu
from jax.sharding import PartitionSpec as P

LANES = 128
BF = jnp.bfloat16
F32 = jnp.float32
VMEM = pl.BlockSpec(memory_space=pltpu.VMEM)
SMEM = pl.BlockSpec(memory_space=pltpu.SMEM)
HBM = pl.BlockSpec(memory_space=pltpu.HBM)


def dot(a, b):
    return lax.dot_general(a, b, (((1,), (0,)), ((), ())), preferred_element_type=F32)


def dot_t(a, b):
    return lax.dot_general(a, b, (((1,), (1,)), ((), ())), preferred_element_type=F32)


def lanes(rows):
    return lax.broadcasted_iota(jnp.int32, (rows, LANES), 1)


def fourth(tiles, rank_top):
    third = LANES - rank_top
    lane = lanes(tiles[0].shape[0])
    moved = [pltpu.roll(tile, third * (k + 1), 1) for k, tile in enumerate(tiles)]
    return jnp.where(lane < third, moved[0], jnp.where(lane < 2 * third, moved[1], moved[2]))


def packed(mains, pad, rank_top):
    lane = lanes(pad.shape[0])
    third = LANES - rank_top
    return [
        jnp.where(lane < rank_top, main, pltpu.roll(pad, rank_top - third * k, 1)) for k, main in enumerate(mains)
    ]


def widen(value):
    return jnp.concatenate([value, jnp.zeros((value.shape[0], LANES - value.shape[1]), value.dtype)], axis=1)


def emit_coeffs(read_leaf, basis_ref, transfer_ref, ranks_ref, out_ref, leaves, rank_top):
    mains, rhs, _ = out_ref.shape
    lane = lax.broadcasted_iota(jnp.int32, (rhs, rank_top), 1)
    coeffs = []
    for i in range(leaves):
        value = dot_t(read_leaf(i), basis_ref[i])
        coeffs.append(jnp.where(lane < ranks_ref[i], value, 0.0).astype(BF))
    for q in range(leaves // 2):
        value = dot(coeffs[2 * q], transfer_ref[2 * q]) + dot(coeffs[2 * q + 1], transfer_ref[2 * q + 1])
        coeffs.append(jnp.where(lane < ranks_ref[leaves + q], value, 0.0).astype(BF))
    wide = [widen(value.astype(F32)) for value in coeffs]
    for q in range(mains // 3):
        for k, tile in enumerate(packed(wide[3 * q : 3 * q + 3], wide[mains + q], rank_top)):
            out_ref[3 * q + k] = tile.astype(BF)


def fetch(pairs, sems):
    copies = [pltpu.make_async_copy(src, dst, sems.at[n]) for n, (src, dst) in enumerate(pairs)]
    for copy in copies:
        copy.start()
    return copies


def emit_edges(core_ref, v_ref, inner_ref, outer_ref):
    head, tail = v_ref[0], v_ref[v_ref.shape[0] - 1]
    even = core_ref[0] == 0
    inner_ref[0] = jnp.where(even, tail, head)
    outer_ref[0] = jnp.where(even, head, tail)


def coeff_kernel(
    ranks_ref, core_ref, v_hbm, basis_hbm, transfer_hbm, out_ref, inner_ref, outer_ref, v_ref, basis_ref, transfer_ref, sems
):
    leaves, rank_top, _ = basis_ref.shape
    for copy in fetch([(v_hbm, v_ref), (basis_hbm, basis_ref), (transfer_hbm, transfer_ref)], sems):
        copy.wait()
    emit_edges(core_ref, v_ref, inner_ref, outer_ref)
    emit_coeffs(lambda i: v_ref[i], basis_ref, transfer_ref, ranks_ref, out_ref, leaves, rank_top)


def couple_kernel(source_ref, target_ref, coupling_ref, *refs, order, unroll):
    chips = sum(len(group) for group in order)
    in_refs, out_refs, (sources, total) = refs[: 2 * chips], refs[2 * chips : -2], refs[-2:]
    blocks, rank_top, _ = coupling_ref.shape
    far, mains, rhs, _ = in_refs[0].shape
    quads = mains // 3
    clusters = mains + quads

    def split(f, _):
        for n, packed_ref in enumerate(in_refs):
            row = (n * far + f) * clusters
            tiles = [packed_ref[f, c] for c in range(mains)]
            for c in range(mains):
                sources[row + c] = tiles[c]
            for q in range(quads):
                wide = [tile.astype(F32) for tile in tiles[3 * q : 3 * q + 3]]
                sources[row + mains + q] = fourth(wide, rank_top).astype(BF)
            for c in range(clusters):
                total[row + c] = jnp.zeros((rhs, LANES), F32)
        return 0

    lax.fori_loop(0, far, split, 0)

    def some(s, _):
        for u in range(unroll):
            j = s * unroll + u
            term = dot(sources[source_ref[j], :, :rank_top], coupling_ref[j])
            at = target_ref[j]
            total[at, :, :rank_top] = total[at, :, :rank_top] + term
        return 0

    lax.fori_loop(0, blocks // unroll, some, 0)

    def pack(f, _):
        for core in range(2):
            for g, group in enumerate(order):
                for place, chip in enumerate(group):
                    row = ((core * chips + chip) * far + f) * clusters
                    for q in range(quads):
                        mains_now = [total[row + 3 * q + k] for k in range(3)]
                        for k, tile in enumerate(packed(mains_now, total[row + mains + q], rank_top)):
                            out_refs[core * len(order) + g][place, f, 3 * q + k] = tile.astype(BF)
        return 0

    lax.fori_loop(0, far, pack, 0)


def near_kernel(v_ref, near_ref, out_ref):
    leaves = v_ref.shape[0]
    for i in range(leaves):
        total = dot(v_ref[i], near_ref[i, 1])
        if i > 0:
            total = total + dot(v_ref[i - 1], near_ref[i, 0])
        if i < leaves - 1:
            total = total + dot(v_ref[i + 1], near_ref[i, 2])
        out_ref[i] = total


def edge_kernel(core_ref, inner_ref, outer_ref, first_ref, last_ref, out_ref):
    inner, outer = inner_ref[0], outer_ref[0]
    even = core_ref[0] == 0
    out_ref[0] = dot(jnp.where(even, outer, inner), first_ref[0, 0])
    out_ref[1] = dot(jnp.where(even, inner, outer), last_ref[0, 0])


def add_kernel(keep_ref, swap_ref, *out_refs):
    for n, out_ref in enumerate(out_refs):
        out_ref[...] = (keep_ref[n].astype(F32) + swap_ref[n].astype(F32)).astype(out_ref.dtype)


def middle_add_kernel(keep_ref, swap_ref, *refs, parts):
    part_refs, (own_out, *out_refs) = refs[:parts], refs[parts:]
    own_out[...] = keep_ref[0].astype(F32) + swap_ref[0].astype(F32)
    for n, (part_ref, out_ref) in enumerate(zip(part_refs, out_refs)):
        total = keep_ref[n + 1].astype(F32) + swap_ref[n + 1].astype(F32)
        out_ref[...] = (total + part_ref[...].astype(F32)).astype(BF)


def pick_kernel(flag_ref, first_ref, second_ref, out_ref):
    out_ref[...] = jnp.where(flag_ref[0] == 0, first_ref[...], second_ref[...])


def join_kernel(*refs):
    for n, part_ref in enumerate(refs[:-1]):
        refs[-1][n] = part_ref[...]


def last_add_kernel(own_ref, *refs, parts):
    part_refs, (keep_out, *away_refs) = refs[:parts], refs[parts:]
    for f in range(own_ref.shape[0]):
        total = own_ref[f]
        for part_ref in part_refs:
            total = total + part_ref[f].astype(F32)
        if f == 0:
            keep_out[...] = total
        else:
            away_refs[f - 1][...] = total.astype(BF)


def field_kernel(ranks_ref, core_ref, near_ref, edge_ref, basis_ref, transfer_ref, keep_ref, *rest, away):
    term_refs, out_ref, next_refs = rest[:away], rest[away], rest[away + 1 :]
    leaves, rank_top, _ = basis_ref.shape
    mains, rhs, _ = keep_ref.shape
    tiles = []
    for t in range(mains):
        tile = keep_ref[t]
        for term_ref in term_refs:
            tile = tile + term_ref[t].astype(F32)
        tiles.append(tile)
    sums = tiles + [fourth(tiles[3 * q : 3 * q + 3], rank_top) for q in range(mains // 3)]
    lane = lax.broadcasted_iota(jnp.int32, (rhs, rank_top), 1)
    fields = [
        jnp.where(lane < ranks_ref[c], total[:, :rank_top], 0.0).astype(BF) for c, total in enumerate(sums)
    ]
    for i in range(leaves):
        down = fields[i].astype(F32) + dot_t(fields[leaves + i // 2], transfer_ref[i])
        leaf_total = jnp.where(lane < ranks_ref[i], down, 0.0).astype(BF)
        result = near_ref[i] + dot(leaf_total, basis_ref[i])
        if i == 0:
            result = result + edge_ref[0]
        if i == leaves - 1:
            result = result + edge_ref[1]
        out_ref[i] = result.astype(BF)
    if next_refs:
        coeff_ref, inner_ref, outer_ref = next_refs
        emit_edges(core_ref, out_ref, inner_ref, outer_ref)
        emit_coeffs(lambda i: out_ref[i], basis_ref, transfer_ref, ranks_ref, coeff_ref, leaves, rank_top)


def params(mebibytes):
    return pltpu.CompilerParams(vmem_limit_bytes=mebibytes << 20)


def local(charges, basis, transfer, near_field, coupling, ranks, block_source, block_target):
    leaves, rank_top, width = basis.shape
    rhs = charges.shape[1]
    clusters = ranks.shape[0]
    blocks = coupling.shape[0]
    devices = lax.axis_size("clu")
    mains = clusters * 3 // 4
    shape = jax.ShapeDtypeStruct

    cores, chips = 2, 8
    cube = cores * chips
    far = devices // cube
    x, y, z = 1, 2, 4

    def swap_far(part, shift):
        return lax.ppermute(part, "clu", [(d, (d + shift * cube) % devices) for d in range(devices)])

    def swap(part, direction):
        turned = direction << 1 & 7 | direction >> 2
        return lax.ppermute(
            part, "clu", [(d, d ^ (turned if d % cores else direction) * cores) for d in range(devices)]
        )

    def swap_cores(part):
        return lax.ppermute(part, "clu", [(d, d ^ 1) for d in range(devices)])

    me = lax.axis_index("clu")
    core = me % cores
    barrier = lax.optimization_barrier

    def rows(cluster, sign):
        device = cluster // clusters
        core = (device ^ me) % cores
        chip = ((device ^ me) // cores) % chips
        chip = jnp.where(device % cores == 0, chip, chip >> 1 | (chip & 1) << 2)
        away = (sign * (device // cube - me // cube)) % far
        return ((core * chips + chip) * far + away) * clusters + cluster % clusters

    source_rows, target_rows = rows(block_source, -1), rows(block_target, 1)

    tile_shape = (mains, rhs, LANES)
    out_shape = shape((leaves, rhs, width), BF)
    tile_out = shape(tile_shape, BF)
    part_shape = shape((far,) + tile_shape, BF)
    edge_shape = shape((1, rhs, width), BF)
    core_index = core.reshape(1)
    first_coeffs, inner, outer = pl.pallas_call(
        coeff_kernel,
        out_shape=[tile_out, edge_shape, edge_shape],
        in_specs=[SMEM, SMEM, HBM, HBM, HBM],
        out_specs=[VMEM] * 3,
        scratch_shapes=[
            pltpu.VMEM(charges.shape, BF),
            pltpu.VMEM(basis.shape, BF),
            pltpu.VMEM(transfer.shape, BF),
            pltpu.SemaphoreType.DMA((3,)),
        ],
    )(ranks, core_index, charges, basis, transfer)

    order = ((x | y | z, x | y, y | z, z | x), (0, x, y, z))
    couple = pl.pallas_call(
        functools.partial(couple_kernel, order=order, unroll=32),
        out_shape=[shape((4, far) + tile_shape, BF)] * 4,
        in_specs=[SMEM, SMEM, VMEM] + [VMEM] * (cores * chips),
        out_specs=[VMEM] * 4,
        scratch_shapes=[
            pltpu.VMEM((devices * clusters, rhs, LANES), BF),
            pltpu.VMEM((devices * clusters, rhs, LANES), F32),
        ],
        compiler_params=params(32 if devices <= 32 else 60),
        cost_estimate=pl.CostEstimate(
            flops=2 * blocks * rhs * rank_top * rank_top, bytes_accessed=10 << 20, transcendentals=0
        ),
    )

    near = pl.pallas_call(
        near_kernel,
        out_shape=shape((leaves, rhs, width), F32),
        in_specs=[VMEM] * 2,
        out_specs=VMEM,
        compiler_params=params(16),
        cost_estimate=pl.CostEstimate(
            flops=2 * leaves * 3 * rhs * width * width, bytes_accessed=4 << 20, transcendentals=0
        ),
    )

    edge = pl.pallas_call(
        edge_kernel,
        out_shape=shape((2, rhs, width), F32),
        grid=(1,),
        in_specs=[
            SMEM,
            VMEM,
            VMEM,
            pl.BlockSpec((1, 1, width, width), lambda i: (0, 0, 0, 0)),
            pl.BlockSpec((1, 1, width, width), lambda i: (leaves - 1, 2, 0, 0)),
        ],
        out_specs=VMEM,
        compiler_params=params(16),
    )

    def adder(kernel, inputs, outputs):
        return pl.pallas_call(
            kernel,
            out_shape=outputs,
            in_specs=[VMEM] * inputs,
            out_specs=[VMEM] * len(outputs),
            compiler_params=params(16),
        )

    own_shape = shape((far,) + tile_shape, F32)
    join = adder(join_kernel, far, [part_shape])
    far_add = adder(add_kernel, 2, [part_shape] * 4)
    middle_add = adder(functools.partial(middle_add_kernel, parts=3), 5, [own_shape] + [part_shape] * 3)
    last_add = adder(
        functools.partial(last_add_kernel, parts=4), 5, [shape(tile_shape, F32)] + [tile_out] * (far - 1)
    )

    def finish(with_coeffs):
        return pl.pallas_call(
            functools.partial(field_kernel, away=far - 1),
            out_shape=[out_shape, tile_out, edge_shape, edge_shape] if with_coeffs else [out_shape],
            in_specs=[SMEM, SMEM] + [VMEM] * (4 + far),
            out_specs=[VMEM] * 4 if with_coeffs else [VMEM],
            compiler_params=params(16),
        )

    count = devices // cores
    halo_pairs = []
    for parity in range(2):
        chain = [(c, c + 1) for c in range(parity, count - 1, 2)]
        halo_pairs.append([(a * cores + k, b * cores + k) for p in chain for a, b in (p, p[::-1]) for k in range(cores)])
    halo_turn = ((me // cores + core) % 2).reshape(1)
    pick = pl.pallas_call(
        pick_kernel, out_shape=edge_shape, in_specs=[SMEM, VMEM, VMEM], out_specs=VMEM, compiler_params=params(1)
    )

    def swap_halo(edge_row):
        return [lax.ppermute(edge_row, "clu", pairs) for pairs in halo_pairs]

    def apply_matrix(field_in, coeffs, inner, outer, coupling, with_coeffs):
        away = [swap_far(coeffs, s) for s in range(1, far)]
        if with_coeffs:
            away, coupling = barrier((away, coupling))
        else:
            away, outer = barrier((away, swap_halo(outer)))
        (column,) = join(coeffs, *away)
        got = {0: column, x: swap(column, x), y: swap(column, y), z: swap(column, z)}
        if with_coeffs:
            got, outer = barrier((got, swap_halo(outer)))
        else:
            got = barrier(got)
        corner = swap(column, x | y | z)
        other = {chip: swap_cores(part) for chip, part in got.items()}
        got |= {x | y: swap(got[x], y), y | z: swap(got[y], z), z | x: swap(got[z], x)}
        near_sum = near(field_in, near_field)
        got, corner, near_sum = barrier((got, corner, near_sum))
        got[x | y | z] = corner
        other |= {chip: swap_cores(got[chip]) for chip in order[0]}
        keep_long, keep, send_long, send = couple(
            source_rows,
            target_rows,
            coupling,
            *[got[chip] for chip in range(chips)],
            *[other[chip] for chip in range(chips)],
        )
        corner, xy, yz, zx = far_add(keep_long, swap_cores(send_long))
        corner, xy, yz, zx, send = barrier((corner, xy, yz, zx, send))
        to_x, to_y, to_z, swapped = barrier((swap(xy, y), swap(yz, z), swap(zx, x), swap_cores(send)))
        own, to_x, to_y, to_z, inner, outer = barrier(
            (*middle_add(keep, swapped, to_x, to_y, to_z), inner, pick(halo_turn, *outer))
        )
        edges = edge(core_index, swap_cores(inner), swap_cores(outer), near_field, near_field)
        own, to_x, to_y, to_z, corner, edges = barrier(
            (own, swap(to_x, x), swap(to_y, y), swap(to_z, z), swap(corner, x | y | z), edges)
        )
        total, *away = last_add(own, to_x, to_y, to_z, corner)
        terms = [swap_far(part, s + 1) for s, part in enumerate(away)]
        return finish(with_coeffs)(ranks, core_index, near_sum, edges, basis, transfer, total, *terms)

    coupling, first_coeffs = barrier((coupling, first_coeffs))
    coupling = pl.pallas_call(
        lambda in_ref, out_ref: None,
        out_shape=shape(coupling.shape, BF),
        in_specs=[pl.BlockSpec(memory_space=pl.ANY)],
        out_specs=pl.BlockSpec(memory_space=pl.ANY),
        input_output_aliases={0: 0},
        compiler_params=params(1),
    )(coupling)
    first, *second_args = apply_matrix(charges, first_coeffs, inner, outer, coupling, True)
    (second,) = apply_matrix(first, *second_args, coupling, False)
    return (first, second)


def solution(mesh):
    in_specs = (
        P("clu", None, None),
        P("clu", None, None),
        P("clu", None, None),
        P("clu", None, None, None),
        P("clu", None, None),
        P("clu"),
        P("clu"),
        P("clu"),
    )
    out_specs = (P("clu", None, None), P("clu", None, None))
    return jax.shard_map(local, mesh=mesh, in_specs=in_specs, out_specs=out_specs, check_vma=False)
```

```python
import functools

import jax
import jax.numpy as jnp
from jax import lax
from jax.experimental import pallas as pl
from jax.experimental.pallas import tpu as pltpu
from jax.sharding import PartitionSpec as P

LANES = 128
BF = jnp.bfloat16
F32 = jnp.float32
VMEM = pl.BlockSpec(memory_space=pltpu.VMEM)
SMEM = pl.BlockSpec(memory_space=pltpu.SMEM)
HBM = pl.BlockSpec(memory_space=pltpu.HBM)


def dot(a, b):
    return lax.dot_general(a, b, (((1,), (0,)), ((), ())), preferred_element_type=F32)


def dot_t(a, b):
    return lax.dot_general(a, b, (((1,), (1,)), ((), ())), preferred_element_type=F32)


def lanes(rows):
    return lax.broadcasted_iota(jnp.int32, (rows, LANES), 1)


def fourth(tiles, rank_top):
    third = LANES - rank_top
    lane = lanes(tiles[0].shape[0])
    moved = [pltpu.roll(tile, third * (k + 1), 1) for k, tile in enumerate(tiles)]
    return jnp.where(lane < third, moved[0], jnp.where(lane < 2 * third, moved[1], moved[2]))


def packed(mains, pad, rank_top):
    lane = lanes(pad.shape[0])
    third = LANES - rank_top
    return [
        jnp.where(lane < rank_top, main, pltpu.roll(pad, rank_top - third * k, 1)) for k, main in enumerate(mains)
    ]


def widen(value):
    return jnp.concatenate([value, jnp.zeros((value.shape[0], LANES - value.shape[1]), value.dtype)], axis=1)


def emit_coeffs(read_leaf, basis_ref, transfer_ref, ranks_ref, out_ref, leaves, rank_top):
    mains, rhs, _ = out_ref.shape
    lane = lax.broadcasted_iota(jnp.int32, (rhs, rank_top), 1)
    coeffs = []
    for i in range(leaves):
        value = dot_t(read_leaf(i), basis_ref[i])
        coeffs.append(jnp.where(lane < ranks_ref[i], value, 0.0).astype(BF))
    for q in range(leaves // 2):
        value = dot(coeffs[2 * q], transfer_ref[2 * q]) + dot(coeffs[2 * q + 1], transfer_ref[2 * q + 1])
        coeffs.append(jnp.where(lane < ranks_ref[leaves + q], value, 0.0).astype(BF))
    wide = [widen(value.astype(F32)) for value in coeffs]
    for q in range(mains // 3):
        for k, tile in enumerate(packed(wide[3 * q : 3 * q + 3], wide[mains + q], rank_top)):
            out_ref[3 * q + k] = tile.astype(BF)


def fetch(pairs, sems):
    copies = [pltpu.make_async_copy(src, dst, sems.at[n]) for n, (src, dst) in enumerate(pairs)]
    for copy in copies:
        copy.start()
    return copies


def emit_edges(core_ref, v_ref, inner_ref, outer_ref):
    head, tail = v_ref[0], v_ref[v_ref.shape[0] - 1]
    even = core_ref[0] == 0
    inner_ref[0] = jnp.where(even, tail, head)
    outer_ref[0] = jnp.where(even, head, tail)


def coeff_kernel(
    ranks_ref, core_ref, v_hbm, basis_hbm, transfer_hbm, out_ref, inner_ref, outer_ref, v_ref, basis_ref, transfer_ref, sems
):
    leaves, rank_top, _ = basis_ref.shape
    for copy in fetch([(v_hbm, v_ref), (basis_hbm, basis_ref), (transfer_hbm, transfer_ref)], sems):
        copy.wait()
    emit_edges(core_ref, v_ref, inner_ref, outer_ref)
    emit_coeffs(lambda i: v_ref[i], basis_ref, transfer_ref, ranks_ref, out_ref, leaves, rank_top)


def couple_kernel(source_ref, target_ref, coupling_ref, *refs, order, unroll):
    chips = sum(len(group) for group in order)
    in_refs, out_refs, (sources, total) = refs[: 2 * chips], refs[2 * chips : -2], refs[-2:]
    blocks, rank_top, _ = coupling_ref.shape
    far, mains, rhs, _ = in_refs[0].shape
    quads = mains // 3
    clusters = mains + quads

    def split(f, _):
        for n, packed_ref in enumerate(in_refs):
            row = (n * far + f) * clusters
            tiles = [packed_ref[f, c] for c in range(mains)]
            for c in range(mains):
                sources[row + c] = tiles[c]
            for q in range(quads):
                wide = [tile.astype(F32) for tile in tiles[3 * q : 3 * q + 3]]
                sources[row + mains + q] = fourth(wide, rank_top).astype(BF)
            for c in range(clusters):
                total[row + c] = jnp.zeros((rhs, LANES), F32)
        return 0

    lax.fori_loop(0, far, split, 0)

    def some(s, _):
        for u in range(unroll):
            j = s * unroll + u
            term = dot(sources[source_ref[j], :, :rank_top], coupling_ref[j])
            at = target_ref[j]
            total[at, :, :rank_top] = total[at, :, :rank_top] + term
        return 0

    lax.fori_loop(0, blocks // unroll, some, 0)

    def pack(f, _):
        for core in range(2):
            for g, group in enumerate(order):
                for place, chip in enumerate(group):
                    row = ((core * chips + chip) * far + f) * clusters
                    for q in range(quads):
                        mains_now = [total[row + 3 * q + k] for k in range(3)]
                        for k, tile in enumerate(packed(mains_now, total[row + mains + q], rank_top)):
                            out_refs[core * len(order) + g][place, f, 3 * q + k] = tile.astype(BF)
        return 0

    lax.fori_loop(0, far, pack, 0)


def near_kernel(v_ref, near_ref, _, out_ref):
    leaves = v_ref.shape[0]
    for i in range(leaves):
        total = dot(v_ref[i], near_ref[i, 1])
        if i > 0:
            total = total + dot(v_ref[i - 1], near_ref[i, 0])
        if i < leaves - 1:
            total = total + dot(v_ref[i + 1], near_ref[i, 2])
        out_ref[i] = total


def edge_kernel(core_ref, inner_ref, outer_ref, first_ref, last_ref, out_ref):
    inner, outer = inner_ref[0], outer_ref[0]
    even = core_ref[0] == 0
    out_ref[0] = dot(jnp.where(even, outer, inner), first_ref[0, 0])
    out_ref[1] = dot(jnp.where(even, inner, outer), last_ref[0, 0])


def add_kernel(keep_ref, swap_ref, *out_refs):
    for n, out_ref in enumerate(out_refs):
        out_ref[...] = (keep_ref[n].astype(F32) + swap_ref[n].astype(F32)).astype(out_ref.dtype)


def middle_add_kernel(keep_ref, swap_ref, *refs, parts):
    part_refs, (own_out, *out_refs) = refs[:parts], refs[parts:]
    own_out[...] = keep_ref[0].astype(F32) + swap_ref[0].astype(F32)
    for n, (part_ref, out_ref) in enumerate(zip(part_refs, out_refs)):
        total = keep_ref[n + 1].astype(F32) + swap_ref[n + 1].astype(F32)
        out_ref[...] = (total + part_ref[...].astype(F32)).astype(BF)


def pick_kernel(flag_ref, first_ref, second_ref, out_ref):
    out_ref[...] = jnp.where(flag_ref[0] == 0, first_ref[...], second_ref[...])


def join_kernel(*refs):
    for n, part_ref in enumerate(refs[:-1]):
        refs[-1][n] = part_ref[...]


def last_add_kernel(own_ref, *refs, parts):
    part_refs, (keep_out, *away_refs) = refs[:parts], refs[parts:]
    for f in range(own_ref.shape[0]):
        total = own_ref[f]
        for part_ref in part_refs:
            total = total + part_ref[f].astype(F32)
        if f == 0:
            keep_out[...] = total
        else:
            away_refs[f - 1][...] = total.astype(BF)


def field_kernel(ranks_ref, core_ref, near_ref, edge_ref, basis_ref, transfer_ref, keep_ref, *rest, away):
    term_refs, out_ref, next_refs = rest[:away], rest[away], rest[away + 1 :]
    leaves, rank_top, _ = basis_ref.shape
    mains, rhs, _ = keep_ref.shape
    tiles = []
    for t in range(mains):
        tile = keep_ref[t]
        for term_ref in term_refs:
            tile = tile + term_ref[t].astype(F32)
        tiles.append(tile)
    sums = tiles + [fourth(tiles[3 * q : 3 * q + 3], rank_top) for q in range(mains // 3)]
    lane = lax.broadcasted_iota(jnp.int32, (rhs, rank_top), 1)
    fields = [
        jnp.where(lane < ranks_ref[c], total[:, :rank_top], 0.0).astype(BF) for c, total in enumerate(sums)
    ]
    for i in range(leaves):
        down = fields[i].astype(F32) + dot_t(fields[leaves + i // 2], transfer_ref[i])
        leaf_total = jnp.where(lane < ranks_ref[i], down, 0.0).astype(BF)
        result = near_ref[i] + dot(leaf_total, basis_ref[i])
        if i == 0:
            result = result + edge_ref[0]
        if i == leaves - 1:
            result = result + edge_ref[1]
        out_ref[i] = result.astype(BF)
    if next_refs:
        coeff_ref, inner_ref, outer_ref = next_refs
        emit_edges(core_ref, out_ref, inner_ref, outer_ref)
        emit_coeffs(lambda i: out_ref[i], basis_ref, transfer_ref, ranks_ref, coeff_ref, leaves, rank_top)


def params(mebibytes):
    return pltpu.CompilerParams(vmem_limit_bytes=mebibytes << 20)


def local(charges, basis, transfer, near_field, coupling, ranks, block_source, block_target):
    leaves, rank_top, width = basis.shape
    rhs = charges.shape[1]
    clusters = ranks.shape[0]
    blocks = coupling.shape[0]
    devices = lax.axis_size("clu")
    mains = clusters * 3 // 4
    shape = jax.ShapeDtypeStruct

    cores, chips = 2, 8
    cube = cores * chips
    far = devices // cube
    x, y, z = 1, 2, 4

    def swap_far(part, shift):
        return lax.ppermute(part, "clu", [(d, (d + shift * cube) % devices) for d in range(devices)])

    def swap(part, direction):
        turned = direction << 1 & 7 | direction >> 2
        return lax.ppermute(
            part, "clu", [(d, d ^ (turned if d % cores else direction) * cores) for d in range(devices)]
        )

    def swap_cores(part):
        return lax.ppermute(part, "clu", [(d, d ^ 1) for d in range(devices)])

    me = lax.axis_index("clu")
    core = me % cores
    barrier = lax.optimization_barrier

    def rows(cluster, sign):
        device = cluster // clusters
        core = (device ^ me) % cores
        chip = ((device ^ me) // cores) % chips
        chip = jnp.where(device % cores == 0, chip, chip >> 1 | (chip & 1) << 2)
        away = (sign * (device // cube - me // cube)) % far
        return ((core * chips + chip) * far + away) * clusters + cluster % clusters

    source_rows, target_rows = rows(block_source, -1), rows(block_target, 1)

    tile_shape = (mains, rhs, LANES)
    out_shape = shape((leaves, rhs, width), BF)
    tile_out = shape(tile_shape, BF)
    part_shape = shape((far,) + tile_shape, BF)
    edge_shape = shape((1, rhs, width), BF)
    core_index = core.reshape(1)
    first_coeffs, inner, outer = pl.pallas_call(
        coeff_kernel,
        out_shape=[tile_out, edge_shape, edge_shape],
        in_specs=[SMEM, SMEM, HBM, HBM, HBM],
        out_specs=[VMEM] * 3,
        scratch_shapes=[
            pltpu.VMEM(charges.shape, BF),
            pltpu.VMEM(basis.shape, BF),
            pltpu.VMEM(transfer.shape, BF),
            pltpu.SemaphoreType.DMA((3,)),
        ],
    )(ranks, core_index, charges, basis, transfer)

    order = ((x | y | z, x | y, y | z, z | x), (0, x, y, z))
    couple = pl.pallas_call(
        functools.partial(couple_kernel, order=order, unroll=64),
        out_shape=[shape((4, far) + tile_shape, BF)] * 4,
        in_specs=[SMEM, SMEM, VMEM] + [VMEM] * (cores * chips),
        out_specs=[VMEM] * 4,
        scratch_shapes=[
            pltpu.VMEM((devices * clusters, rhs, LANES), BF),
            pltpu.VMEM((devices * clusters, rhs, LANES), F32),
        ],
        compiler_params=params(24 if devices <= 32 else 60),
        cost_estimate=pl.CostEstimate(
            flops=2 * blocks * rhs * rank_top * rank_top, bytes_accessed=10 << 20, transcendentals=0
        ),
    )

    near = pl.pallas_call(
        near_kernel,
        out_shape=shape((leaves, rhs, width), F32),
        in_specs=[VMEM, VMEM, pl.BlockSpec(memory_space=pl.ANY)],
        out_specs=VMEM,
        compiler_params=params(16),
        cost_estimate=pl.CostEstimate(
            flops=2 * leaves * 3 * rhs * width * width, bytes_accessed=4 << 20, transcendentals=0
        ),
    )

    edge = pl.pallas_call(
        edge_kernel,
        out_shape=shape((2, rhs, width), F32),
        grid=(1,),
        in_specs=[
            SMEM,
            VMEM,
            VMEM,
            pl.BlockSpec((1, 1, width, width), lambda i: (0, 0, 0, 0)),
            pl.BlockSpec((1, 1, width, width), lambda i: (leaves - 1, 2, 0, 0)),
        ],
        out_specs=VMEM,
        compiler_params=params(16),
    )

    def adder(kernel, inputs, outputs):
        return pl.pallas_call(
            kernel,
            out_shape=outputs,
            in_specs=[VMEM] * inputs,
            out_specs=[VMEM] * len(outputs),
            compiler_params=params(16),
        )

    own_shape = shape((far,) + tile_shape, F32)
    join = adder(join_kernel, far, [part_shape])
    far_add = adder(add_kernel, 2, [part_shape] * 4)
    middle_add = adder(functools.partial(middle_add_kernel, parts=3), 5, [own_shape] + [part_shape] * 3)
    last_add = adder(
        functools.partial(last_add_kernel, parts=4), 5, [shape(tile_shape, F32)] + [tile_out] * (far - 1)
    )

    def finish(with_coeffs):
        return pl.pallas_call(
            functools.partial(field_kernel, away=far - 1),
            out_shape=[out_shape, tile_out, edge_shape, edge_shape] if with_coeffs else [out_shape],
            in_specs=[SMEM, SMEM] + [VMEM] * (4 + far),
            out_specs=[VMEM] * 4 if with_coeffs else [VMEM],
            compiler_params=params(16),
        )

    count = devices // cores
    halo_pairs = []
    for parity in range(2):
        chain = [(c, c + 1) for c in range(parity, count - 1, 2)]
        halo_pairs.append([(a * cores + k, b * cores + k) for p in chain for a, b in (p, p[::-1]) for k in range(cores)])
    halo_turn = ((me // cores + core) % 2).reshape(1)
    pick = pl.pallas_call(
        pick_kernel, out_shape=edge_shape, in_specs=[SMEM, VMEM, VMEM], out_specs=VMEM, compiler_params=params(1)
    )

    def swap_halo(edge_row):
        return [lax.ppermute(edge_row, "clu", pairs) for pairs in halo_pairs]

    def apply_matrix(field_in, coeffs, inner, outer, coupling, with_coeffs):
        (column,) = join(coeffs, *[swap_far(coeffs, s) for s in range(1, far)])
        got = {0: column, x: swap(column, x), y: swap(column, y), z: swap(column, z)}
        near_sum = near(field_in, near_field, coupling)
        got, near_sum = barrier((got, near_sum))
        corner = swap(column, x | y | z)
        other = {chip: swap_cores(part) for chip, part in got.items()}
        got |= {x | y: swap(got[x], y), y | z: swap(got[y], z), z | x: swap(got[z], x)}
        got, corner = barrier((got, corner))
        got[x | y | z] = corner
        other |= {chip: swap_cores(got[chip]) for chip in order[0]}
        totals = couple(
            source_rows,
            target_rows,
            coupling,
            *[got[chip] for chip in range(chips)],
            *[other[chip] for chip in range(chips)],
        )
        (keep_long, keep, send_long, send), outer = barrier((totals, outer))
        corner, xy, yz, zx = far_add(keep_long, swap_cores(send_long))
        corner, xy, yz, zx, send, outer = barrier((corner, xy, yz, zx, send, swap_halo(outer)))
        to_x, to_y, to_z, swapped = barrier((swap(xy, y), swap(yz, z), swap(zx, x), swap_cores(send)))
        own, to_x, to_y, to_z, inner, outer = barrier(
            (*middle_add(keep, swapped, to_x, to_y, to_z), inner, pick(halo_turn, *outer))
        )
        edges = edge(core_index, swap_cores(inner), swap_cores(outer), near_field, near_field)
        own, to_x, to_y, to_z, corner, edges = barrier(
            (own, swap(to_x, x), swap(to_y, y), swap(to_z, z), swap(corner, x | y | z), edges)
        )
        total, *away = last_add(own, to_x, to_y, to_z, corner)
        terms = [swap_far(part, s + 1) for s, part in enumerate(away)]
        return finish(with_coeffs)(ranks, core_index, near_sum, edges, basis, transfer, total, *terms)

    first, *second_args = apply_matrix(charges, first_coeffs, inner, outer, coupling, True)
    (second,) = apply_matrix(first, *second_args, coupling, False)
    return (first, second)


def solution(mesh):
    in_specs = (
        P("clu", None, None),
        P("clu", None, None),
        P("clu", None, None),
        P("clu", None, None, None),
        P("clu", None, None),
        P("clu"),
        P("clu"),
        P("clu"),
    )
    out_specs = (P("clu", None, None), P("clu", None, None))
    return jax.shard_map(local, mesh=mesh, in_specs=in_specs, out_specs=out_specs, check_vma=False)
```

```python
import functools

import jax
import jax.numpy as jnp
import numpy as np
from jax import lax
from jax.experimental import pallas as pl
from jax.experimental.pallas import tpu as pltpu
from jax.sharding import PartitionSpec as P

LANES = 128
CORES, CHIPS = 2, 8
BF = jnp.bfloat16
F32 = jnp.float32
VMEM = pl.BlockSpec(memory_space=pltpu.VMEM)
SMEM = pl.BlockSpec(memory_space=pltpu.SMEM)
HBM = pl.BlockSpec(memory_space=pltpu.HBM)


def dot(a, b):
    return lax.dot_general(a, b, (((1,), (0,)), ((), ())), preferred_element_type=F32)


def dot_t(a, b):
    return lax.dot_general(a, b, (((1,), (1,)), ((), ())), preferred_element_type=F32)


def lanes(rows):
    return lax.broadcasted_iota(jnp.int32, (rows, LANES), 1)


def fourth(tiles, rank_top):
    third = LANES - rank_top
    lane = lanes(tiles[0].shape[0])
    moved = [pltpu.roll(tile, third * (k + 1), 1) for k, tile in enumerate(tiles)]
    return jnp.where(lane < third, moved[0], jnp.where(lane < 2 * third, moved[1], moved[2]))


def packed(mains, pad, rank_top):
    lane = lanes(pad.shape[0])
    third = LANES - rank_top
    return [
        jnp.where(lane < rank_top, main, pltpu.roll(pad, rank_top - third * k, 1)) for k, main in enumerate(mains)
    ]


def widen(value):
    return jnp.concatenate([value, jnp.zeros((value.shape[0], LANES - value.shape[1]), value.dtype)], axis=1)


def emit_coeffs(read_leaf, basis_ref, transfer_ref, ranks_ref, out_ref, leaves, rank_top):
    mains, rhs, _ = out_ref.shape
    lane = lax.broadcasted_iota(jnp.int32, (rhs, rank_top), 1)
    coeffs = []
    for i in range(leaves):
        value = dot_t(read_leaf(i), basis_ref[i])
        coeffs.append(jnp.where(lane < ranks_ref[i], value, 0.0).astype(BF))
    for q in range(leaves // 2):
        value = dot(coeffs[2 * q], transfer_ref[2 * q]) + dot(coeffs[2 * q + 1], transfer_ref[2 * q + 1])
        coeffs.append(jnp.where(lane < ranks_ref[leaves + q], value, 0.0).astype(BF))
    wide = [widen(value.astype(F32)) for value in coeffs]
    for q in range(mains // 3):
        for k, tile in enumerate(packed(wide[3 * q : 3 * q + 3], wide[mains + q], rank_top)):
            out_ref[3 * q + k] = tile.astype(BF)


def fetch(pairs, sems):
    copies = [pltpu.make_async_copy(src, dst, sems.at[n]) for n, (src, dst) in enumerate(pairs)]
    for copy in copies:
        copy.start()
    return copies


def emit_edges(v_ref, inner_ref, outer_ref):
    head, tail = v_ref[0], v_ref[v_ref.shape[0] - 1]
    even = lax.axis_index("clu") % CORES == 0
    inner_ref[0] = jnp.where(even, tail, head)
    outer_ref[0] = jnp.where(even, head, tail)


def coeff_kernel(
    ranks_ref, v_hbm, basis_hbm, transfer_hbm, out_ref, inner_ref, outer_ref, v_ref, basis_ref, transfer_ref, sems
):
    leaves, rank_top, _ = basis_ref.shape
    for copy in fetch([(v_hbm, v_ref), (basis_hbm, basis_ref), (transfer_hbm, transfer_ref)], sems):
        copy.wait()
    emit_edges(v_ref, inner_ref, outer_ref)
    emit_coeffs(lambda i: v_ref[i], basis_ref, transfer_ref, ranks_ref, out_ref, leaves, rank_top)


def couple_kernel(source_ref, target_ref, coupling_ref, *refs, order, unroll):
    chips = sum(len(group) for group in order)
    in_refs, out_refs, (sources, total) = refs[: 2 * chips], refs[2 * chips : -2], refs[-2:]
    blocks, rank_top, _ = coupling_ref.shape
    far, mains, rhs, _ = in_refs[0].shape
    quads = mains // 3
    clusters = mains + quads

    def split(f, _):
        for n, packed_ref in enumerate(in_refs):
            row = (n * far + f) * clusters
            tiles = [packed_ref[f, c] for c in range(mains)]
            for c in range(mains):
                sources[row + c] = tiles[c]
            for q in range(quads):
                wide = [tile.astype(F32) for tile in tiles[3 * q : 3 * q + 3]]
                sources[row + mains + q] = fourth(wide, rank_top).astype(BF)
            for c in range(clusters):
                total[row + c] = jnp.zeros((rhs, LANES), F32)
        return 0

    lax.fori_loop(0, far, split, 0)

    def some(s, _):
        for u in range(unroll):
            j = s * unroll + u
            term = dot(sources[source_ref[j], :, :rank_top], coupling_ref[j])
            at = target_ref[j]
            total[at, :, :rank_top] = total[at, :, :rank_top] + term
        return 0

    lax.fori_loop(0, blocks // unroll, some, 0)

    def pack(f, _):
        for core in range(2):
            for g, group in enumerate(order):
                for place, chip in enumerate(group):
                    row = ((core * chips + chip) * far + f) * clusters
                    for q in range(quads):
                        mains_now = [total[row + 3 * q + k] for k in range(3)]
                        for k, tile in enumerate(packed(mains_now, total[row + mains + q], rank_top)):
                            out_refs[core * len(order) + g][place, f, 3 * q + k] = tile.astype(BF)
        return 0

    lax.fori_loop(0, far, pack, 0)


def near_kernel(v_ref, near_ref, out_ref):
    leaves = v_ref.shape[0]
    for i in range(leaves):
        total = dot(v_ref[i], near_ref[i, 1])
        if i > 0:
            total = total + dot(v_ref[i - 1], near_ref[i, 0])
        if i < leaves - 1:
            total = total + dot(v_ref[i + 1], near_ref[i, 2])
        out_ref[i] = total


def edge_kernel(inner_ref, outer_ref, first_ref, last_ref, out_ref):
    inner, outer = inner_ref[0], outer_ref[0]
    even = lax.axis_index("clu") % CORES == 0
    out_ref[0] = dot(jnp.where(even, outer, inner), first_ref[0, 0])
    out_ref[1] = dot(jnp.where(even, inner, outer), last_ref[0, 0])


def add_kernel(keep_ref, swap_ref, *out_refs):
    for n, out_ref in enumerate(out_refs):
        out_ref[...] = (keep_ref[n].astype(F32) + swap_ref[n].astype(F32)).astype(out_ref.dtype)


def middle_add_kernel(keep_ref, swap_ref, *refs, parts):
    part_refs, (own_out, *out_refs) = refs[:parts], refs[parts:]
    own_out[...] = keep_ref[0].astype(F32) + swap_ref[0].astype(F32)
    for n, (part_ref, out_ref) in enumerate(zip(part_refs, out_refs)):
        total = keep_ref[n + 1].astype(F32) + swap_ref[n + 1].astype(F32)
        out_ref[...] = (total + part_ref[...].astype(F32)).astype(BF)


def pick_kernel(even_ref, odd_ref, out_ref):
    me, devices = lax.axis_index("clu"), lax.axis_size("clu")
    row = jnp.where((me // CORES + me % CORES) % 2 == 0, even_ref[...], odd_ref[...])
    inside = (me != CORES - 1) & (me != devices - CORES)
    out_ref[...] = jnp.where(inside, row, jnp.zeros_like(row))


def rows_kernel(source_ref, target_ref, source_out, target_out, *, clusters, far, magic, shift):
    me = lax.axis_index("clu")
    for sign, in_ref, out_ref in ((-1, source_ref, source_out), (1, target_ref, target_out)):
        cluster = in_ref[...]
        device = cluster * magic >> shift
        chip = ((device ^ me) >> 1) & (CHIPS - 1)
        chip = jnp.where((device & 1) == 0, chip, chip >> 1 | (chip & 1) << 2)
        away = (sign * ((device >> 4) - (me >> 4))) & (far - 1)
        core = (device ^ me) & 1
        out_ref[...] = ((core * CHIPS + chip) * far + away) * clusters + cluster - device * clusters


def join_kernel(*refs):
    for n, part_ref in enumerate(refs[:-1]):
        refs[-1][n] = part_ref[...]


def last_add_kernel(own_ref, *refs, parts):
    part_refs, (keep_out, *away_refs) = refs[:parts], refs[parts:]
    for f in range(own_ref.shape[0]):
        total = own_ref[f]
        for part_ref in part_refs:
            total = total + part_ref[f].astype(F32)
        if f == 0:
            keep_out[...] = total
        else:
            away_refs[f - 1][...] = total.astype(BF)


def field_kernel(ranks_ref, near_ref, edge_ref, basis_ref, transfer_ref, keep_ref, *rest, away):
    term_refs, out_ref, next_refs = rest[:away], rest[away], rest[away + 1 :]
    leaves, rank_top, _ = basis_ref.shape
    mains, rhs, _ = keep_ref.shape
    tiles = []
    for t in range(mains):
        tile = keep_ref[t]
        for term_ref in term_refs:
            tile = tile + term_ref[t].astype(F32)
        tiles.append(tile)
    sums = tiles + [fourth(tiles[3 * q : 3 * q + 3], rank_top) for q in range(mains // 3)]
    lane = lax.broadcasted_iota(jnp.int32, (rhs, rank_top), 1)
    fields = [
        jnp.where(lane < ranks_ref[c], total[:, :rank_top], 0.0).astype(BF) for c, total in enumerate(sums)
    ]
    for i in range(leaves):
        down = fields[i].astype(F32) + dot_t(fields[leaves + i // 2], transfer_ref[i])
        leaf_total = jnp.where(lane < ranks_ref[i], down, 0.0).astype(BF)
        result = near_ref[i] + dot(leaf_total, basis_ref[i])
        if i == 0:
            result = result + edge_ref[0]
        if i == leaves - 1:
            result = result + edge_ref[1]
        out_ref[i] = result.astype(BF)
    if next_refs:
        coeff_ref, inner_ref, outer_ref = next_refs
        emit_edges(out_ref, inner_ref, outer_ref)
        emit_coeffs(lambda i: out_ref[i], basis_ref, transfer_ref, ranks_ref, coeff_ref, leaves, rank_top)


def params(mebibytes):
    return pltpu.CompilerParams(vmem_limit_bytes=mebibytes << 20)


def local(charges, basis, transfer, near_field, coupling, ranks, block_source, block_target):
    leaves, rank_top, width = basis.shape
    rhs = charges.shape[1]
    clusters = ranks.shape[0]
    blocks = coupling.shape[0]
    devices = lax.axis_size("clu")
    mains = clusters * 3 // 4
    shape = jax.ShapeDtypeStruct

    cores, chips = CORES, CHIPS
    cube = cores * chips
    far = devices // cube
    x, y, z = 1, 2, 4

    def swap_far(part, shift):
        return lax.ppermute(part, "clu", [(d, (d + shift * cube) % devices) for d in range(devices)])

    def swap(part, direction):
        turned = direction << 1 & 7 | direction >> 2
        return lax.ppermute(
            part, "clu", [(d, d ^ (turned if d % cores else direction) * cores) for d in range(devices)]
        )

    def swap_cores(part):
        return lax.ppermute(part, "clu", [(d, d ^ 1) for d in range(devices)])

    barrier = lax.optimization_barrier

    shift = 19
    magic = -(-(1 << shift) // clusters)
    numbers = np.arange(devices * clusters)
    assert (numbers * magic >> shift == numbers // clusters).all() and far & far - 1 == 0
    list_shape = jax.ShapeDtypeStruct((1, blocks), jnp.int32)
    source_rows, target_rows = pl.pallas_call(
        functools.partial(rows_kernel, clusters=clusters, far=far, magic=magic, shift=shift),
        out_shape=[list_shape] * 2,
        in_specs=[VMEM] * 2,
        out_specs=[VMEM] * 2,
        compiler_params=params(1),
    )(block_source.reshape(1, blocks), block_target.reshape(1, blocks))
    source_rows, target_rows = source_rows.reshape(blocks), target_rows.reshape(blocks)

    tile_shape = (mains, rhs, LANES)
    out_shape = shape((leaves, rhs, width), BF)
    tile_out = shape(tile_shape, BF)
    part_shape = shape((far,) + tile_shape, BF)
    edge_shape = shape((1, rhs, width), BF)
    first_coeffs, inner, outer = pl.pallas_call(
        coeff_kernel,
        out_shape=[tile_out, edge_shape, edge_shape],
        in_specs=[SMEM, HBM, HBM, HBM],
        out_specs=[VMEM] * 3,
        scratch_shapes=[
            pltpu.VMEM(charges.shape, BF),
            pltpu.VMEM(basis.shape, BF),
            pltpu.VMEM(transfer.shape, BF),
            pltpu.SemaphoreType.DMA((3,)),
        ],
    )(ranks, charges, basis, transfer)

    order = ((x | y | z, x | y, y | z, z | x), (0, x, y, z))
    couple = pl.pallas_call(
        functools.partial(couple_kernel, order=order, unroll=64),
        out_shape=[shape((4, far) + tile_shape, BF)] * 4,
        in_specs=[SMEM, SMEM, VMEM] + [VMEM] * (cores * chips),
        out_specs=[VMEM] * 4,
        scratch_shapes=[
            pltpu.VMEM((devices * clusters, rhs, LANES), BF),
            pltpu.VMEM((devices * clusters, rhs, LANES), F32),
        ],
        compiler_params=params(24 if devices <= 32 else 60),
        cost_estimate=pl.CostEstimate(
            flops=2 * blocks * rhs * rank_top * rank_top, bytes_accessed=10 << 20, transcendentals=0
        ),
    )

    near = pl.pallas_call(
        near_kernel,
        out_shape=shape((leaves, rhs, width), F32),
        in_specs=[VMEM, VMEM],
        out_specs=VMEM,
        compiler_params=params(16),
        cost_estimate=pl.CostEstimate(
            flops=2 * leaves * 3 * rhs * width * width, bytes_accessed=4 << 20, transcendentals=0
        ),
    )

    edge = pl.pallas_call(
        edge_kernel,
        out_shape=shape((2, rhs, width), F32),
        grid=(1,),
        in_specs=[
            VMEM,
            VMEM,
            pl.BlockSpec((1, 1, width, width), lambda i: (0, 0, 0, 0)),
            pl.BlockSpec((1, 1, width, width), lambda i: (leaves - 1, 2, 0, 0)),
        ],
        out_specs=VMEM,
        compiler_params=params(16),
    )

    def adder(kernel, inputs, outputs):
        return pl.pallas_call(
            kernel,
            out_shape=outputs,
            in_specs=[VMEM] * inputs,
            out_specs=[VMEM] * len(outputs),
            compiler_params=params(16),
        )

    own_shape = shape((far,) + tile_shape, F32)
    join = adder(join_kernel, far, [part_shape])
    first_join = pl.pallas_call(
        lambda _, *refs: join_kernel(*refs),
        out_shape=[part_shape],
        in_specs=[pl.BlockSpec(memory_space=pl.ANY)] + [VMEM] * far,
        out_specs=[VMEM],
    )
    far_add = adder(add_kernel, 2, [part_shape] * 4)
    middle_add = adder(functools.partial(middle_add_kernel, parts=3), 5, [own_shape] + [part_shape] * 3)
    last_add = adder(
        functools.partial(last_add_kernel, parts=4), 5, [shape(tile_shape, F32)] + [tile_out] * (far - 1)
    )

    def finish(with_coeffs):
        return pl.pallas_call(
            functools.partial(field_kernel, away=far - 1),
            out_shape=[out_shape, tile_out, edge_shape, edge_shape] if with_coeffs else [out_shape],
            in_specs=[SMEM] + [VMEM] * (4 + far),
            out_specs=[VMEM] * 4 if with_coeffs else [VMEM],
            compiler_params=params(16),
        )

    count = devices // cores
    halo_pairs = []
    for parity in range(2):
        chain = [(c, c + 1) for c in range(parity, count - 1, 2)]
        ends = [(c, c) for c in (0, count - 1) if parity]
        links = [link for pair in chain for link in (pair, pair[::-1])] + ends
        halo_pairs.append([(a * cores + k, b * cores + k) for a, b in links for k in range(cores)])
    pick = pl.pallas_call(
        pick_kernel, out_shape=edge_shape, in_specs=[VMEM, VMEM], out_specs=VMEM, compiler_params=params(1)
    )

    def swap_halo(edge_row):
        return [lax.ppermute(edge_row, "clu", pairs) for pairs in halo_pairs]

    def apply_matrix(field_in, coeffs, inner, outer, coupling, with_coeffs):
        away = [swap_far(coeffs, s) for s in range(1, far)]
        (column,) = first_join(coupling, coeffs, *away) if with_coeffs else join(coeffs, *away)
        got = {0: column, x: swap(column, x), y: swap(column, y), z: swap(column, z)}
        near_sum = near(field_in, near_field)
        got, near_sum = barrier((got, near_sum))
        corner = swap(column, x | y | z)
        other = {chip: swap_cores(part) for chip, part in got.items()}
        got |= {x | y: swap(got[x], y), y | z: swap(got[y], z), z | x: swap(got[z], x)}
        got, corner = barrier((got, corner))
        got[x | y | z] = corner
        other |= {chip: swap_cores(got[chip]) for chip in order[0]}
        totals = couple(
            source_rows,
            target_rows,
            coupling,
            *[got[chip] for chip in range(chips)],
            *[other[chip] for chip in range(chips)],
        )
        (keep_long, keep, send_long, send), outer = barrier((totals, outer))
        corner, xy, yz, zx = far_add(keep_long, swap_cores(send_long))
        corner, xy, yz, zx, send, outer = barrier((corner, xy, yz, zx, send, swap_halo(outer)))
        to_x, to_y, to_z, swapped = barrier((swap(xy, y), swap(yz, z), swap(zx, x), swap_cores(send)))
        own, to_x, to_y, to_z, inner, outer = barrier(
            (*middle_add(keep, swapped, to_x, to_y, to_z), inner, pick(*outer))
        )
        edges = edge(swap_cores(inner), swap_cores(outer), near_field, near_field)
        own, to_x, to_y, to_z, corner, edges = barrier(
            (own, swap(to_x, x), swap(to_y, y), swap(to_z, z), swap(corner, x | y | z), edges)
        )
        total, *away = last_add(own, to_x, to_y, to_z, corner)
        terms = [swap_far(part, s + 1) for s, part in enumerate(away)]
        return finish(with_coeffs)(ranks, near_sum, edges, basis, transfer, total, *terms)

    first, *second_args = apply_matrix(charges, first_coeffs, inner, outer, coupling, True)
    (second,) = apply_matrix(first, *second_args, coupling, False)
    return (first, second)


def solution(mesh):
    in_specs = (
        P("clu", None, None),
        P("clu", None, None),
        P("clu", None, None),
        P("clu", None, None, None),
        P("clu", None, None),
        P("clu"),
        P("clu"),
        P("clu"),
    )
    out_specs = (P("clu", None, None), P("clu", None, None))
    return jax.shard_map(local, mesh=mesh, in_specs=in_specs, out_specs=out_specs, check_vma=False)
```

```python
import functools

import jax
import jax.numpy as jnp
import numpy as np
from jax import lax
from jax.experimental import pallas as pl
from jax.experimental.pallas import tpu as pltpu
from jax.sharding import PartitionSpec as P

LANES = 128
CORES, CHIPS = 2, 8
BF = jnp.bfloat16
F32 = jnp.float32
VMEM = pl.BlockSpec(memory_space=pltpu.VMEM)
SMEM = pl.BlockSpec(memory_space=pltpu.SMEM)
HBM = pl.BlockSpec(memory_space=pltpu.HBM)


def dot(a, b):
    return lax.dot_general(a, b, (((1,), (0,)), ((), ())), preferred_element_type=F32)


def dot_t(a, b):
    return lax.dot_general(a, b, (((1,), (1,)), ((), ())), preferred_element_type=F32)


def lanes(rows):
    return lax.broadcasted_iota(jnp.int32, (rows, LANES), 1)


def fourth(tiles, rank_top):
    third = LANES - rank_top
    lane = lanes(tiles[0].shape[0])
    moved = [pltpu.roll(tile, third * (k + 1), 1) for k, tile in enumerate(tiles)]
    return jnp.where(lane < third, moved[0], jnp.where(lane < 2 * third, moved[1], moved[2]))


def packed(mains, pad, rank_top):
    lane = lanes(pad.shape[0])
    third = LANES - rank_top
    return [
        jnp.where(lane < rank_top, main, pltpu.roll(pad, rank_top - third * k, 1)) for k, main in enumerate(mains)
    ]


def widen(value):
    return jnp.concatenate([value, jnp.zeros((value.shape[0], LANES - value.shape[1]), value.dtype)], axis=1)


def emit_coeffs(values, basis_ref, transfer_ref, ranks_ref, out_ref, ready=None):
    mains, rhs, _ = out_ref.shape
    leaves, rank_top, _ = basis_ref.shape
    lane = lax.broadcasted_iota(jnp.int32, (rhs, rank_top), 1)
    coeffs = []
    for i in range(leaves):
        value = dot_t(values[i], basis_ref[i])
        coeffs.append(jnp.where(lane < ranks_ref[i], value, 0.0).astype(BF))
    if ready is not None:
        ready()
    for q in range(leaves // 2):
        value = dot(coeffs[2 * q], transfer_ref[2 * q]) + dot(coeffs[2 * q + 1], transfer_ref[2 * q + 1])
        coeffs.append(jnp.where(lane < ranks_ref[leaves + q], value, 0.0).astype(BF))
    wide = [widen(value.astype(F32)) for value in coeffs]
    for q in range(mains // 3):
        for k, tile in enumerate(packed(wide[3 * q : 3 * q + 3], wide[mains + q], rank_top)):
            out_ref[3 * q + k] = tile.astype(BF)


def fetch(pairs, sems):
    copies = [pltpu.make_async_copy(src, dst, sems.at[n]) for n, (src, dst) in enumerate(pairs)]
    for copy in copies:
        copy.start()
    return copies


def emit_edges(v_ref, inner_ref, outer_ref):
    head, tail = v_ref[0], v_ref[v_ref.shape[0] - 1]
    even = lax.axis_index("clu") % CORES == 0
    inner_ref[0] = jnp.where(even, tail, head)
    outer_ref[0] = jnp.where(even, head, tail)


def coeff_kernel(
    ranks_ref, v_hbm, basis_hbm, transfer_hbm, out_ref, inner_ref, outer_ref, v_ref, basis_ref, transfer_ref, sems
):
    leaves = basis_ref.shape[0]
    copies = fetch([(v_hbm, v_ref), (basis_hbm, basis_ref), (transfer_hbm, transfer_ref)], sems)
    copies[0].wait()
    emit_edges(v_ref, inner_ref, outer_ref)
    copies[1].wait()
    values = [v_ref[i] for i in range(leaves)]
    emit_coeffs(values, basis_ref, transfer_ref, ranks_ref, out_ref, copies[2].wait)


def couple_kernel(source_ref, target_ref, coupling_ref, *refs, order, unroll):
    chips = sum(len(group) for group in order)
    in_refs, out_refs, (sources, total) = refs[: 2 * chips], refs[2 * chips : -2], refs[-2:]
    blocks, rank_top, _ = coupling_ref.shape
    far, mains, rhs, _ = in_refs[0].shape
    quads = mains // 3
    clusters = mains + quads

    def split(f, _):
        for n, packed_ref in enumerate(in_refs):
            row = (n * far + f) * clusters
            tiles = [packed_ref[f, c] for c in range(mains)]
            for c in range(mains):
                sources[row + c] = tiles[c]
            for q in range(quads):
                wide = [tile.astype(F32) for tile in tiles[3 * q : 3 * q + 3]]
                sources[row + mains + q] = fourth(wide, rank_top).astype(BF)
            for c in range(clusters):
                total[row + c] = jnp.zeros((rhs, LANES), F32)
        return 0

    lax.fori_loop(0, far, split, 0)

    def some(s, _):
        for u in range(unroll):
            j = s * unroll + u
            term = dot(sources[source_ref[j], :, :rank_top], coupling_ref[j])
            at = target_ref[j]
            total[at, :, :rank_top] = total[at, :, :rank_top] + term
        return 0

    lax.fori_loop(0, blocks // unroll, some, 0)

    def pack(f, _):
        for core in range(2):
            for g, group in enumerate(order):
                for place, chip in enumerate(group):
                    row = ((core * chips + chip) * far + f) * clusters
                    for q in range(quads):
                        mains_now = [total[row + 3 * q + k] for k in range(3)]
                        for k, tile in enumerate(packed(mains_now, total[row + mains + q], rank_top)):
                            out_refs[core * len(order) + g][place, f, 3 * q + k] = tile.astype(BF)
        return 0

    lax.fori_loop(0, far, pack, 0)


def near_kernel(v_ref, near_ref, out_ref):
    leaves = v_ref.shape[0]
    for i in range(leaves):
        total = dot(v_ref[i], near_ref[i, 1])
        if i > 0:
            total = total + dot(v_ref[i - 1], near_ref[i, 0])
        if i < leaves - 1:
            total = total + dot(v_ref[i + 1], near_ref[i, 2])
        out_ref[i] = total


def edge_kernel(inner_ref, outer_ref, first_ref, last_ref, out_ref):
    inner, outer = inner_ref[0], outer_ref[0]
    even = lax.axis_index("clu") % CORES == 0
    out_ref[0] = dot(jnp.where(even, outer, inner), first_ref[0, 0])
    out_ref[1] = dot(jnp.where(even, inner, outer), last_ref[0, 0])


def add_kernel(keep_ref, swap_ref, *out_refs):
    for n, out_ref in enumerate(out_refs):
        out_ref[...] = (keep_ref[n].astype(F32) + swap_ref[n].astype(F32)).astype(out_ref.dtype)


def middle_add_kernel(keep_ref, swap_ref, *refs, parts):
    part_refs, (own_out, *out_refs) = refs[:parts], refs[parts:]
    own_out[...] = keep_ref[0].astype(F32) + swap_ref[0].astype(F32)
    for n, out_ref in enumerate(out_refs):
        total = keep_ref[n + 1].astype(F32) + swap_ref[n + 1].astype(F32)
        for part_ref in part_refs[n :: len(out_refs)]:
            total = total + part_ref[...].astype(F32)
        out_ref[...] = total.astype(BF)


def rows_kernel(source_ref, target_ref, source_out, target_out, *, clusters, far, magic, shift):
    me = lax.axis_index("clu")
    for sign, in_ref, out_ref in ((-1, source_ref, source_out), (1, target_ref, target_out)):
        cluster = in_ref[...]
        device = cluster * magic >> shift
        chip = ((device ^ me) >> 1) & (CHIPS - 1)
        chip = jnp.where((device & 1) == 0, chip, chip >> 1 | (chip & 1) << 2)
        away = (sign * ((device >> 4) - (me >> 4))) & (far - 1)
        core = (device ^ me) & 1
        out_ref[...] = ((core * CHIPS + chip) * far + away) * clusters + cluster - device * clusters


def join_kernel(*refs):
    for n, part_ref in enumerate(refs[:-1]):
        refs[-1][n] = part_ref[...]


def last_add_kernel(own_ref, *refs, parts):
    part_refs, (keep_out, *away_refs) = refs[:parts], refs[parts:]
    for f in range(own_ref.shape[0]):
        total = own_ref[f]
        for part_ref in part_refs:
            total = total + part_ref[f].astype(F32)
        if f == 0:
            keep_out[...] = total
        else:
            away_refs[f - 1][...] = total.astype(BF)


def field_kernel(ranks_ref, near_ref, edge_ref, basis_ref, transfer_ref, keep_ref, *rest, away):
    term_refs, out_ref, next_refs = rest[:away], rest[away], rest[away + 1 :]
    leaves, rank_top, _ = basis_ref.shape
    mains, rhs, _ = keep_ref.shape
    tiles = []
    for t in range(mains):
        tile = keep_ref[t]
        for term_ref in term_refs:
            tile = tile + term_ref[t].astype(F32)
        tiles.append(tile)
    sums = tiles + [fourth(tiles[3 * q : 3 * q + 3], rank_top) for q in range(mains // 3)]
    lane = lax.broadcasted_iota(jnp.int32, (rhs, rank_top), 1)
    fields = [
        jnp.where(lane < ranks_ref[c], total[:, :rank_top], 0.0).astype(BF) for c, total in enumerate(sums)
    ]
    downs = [fields[i].astype(F32) + dot_t(fields[leaves + i // 2], transfer_ref[i]) for i in range(leaves)]
    leaf_totals = [jnp.where(lane < ranks_ref[i], down, 0.0).astype(BF) for i, down in enumerate(downs)]
    results = [near_ref[i] + dot(leaf_total, basis_ref[i]) for i, leaf_total in enumerate(leaf_totals)]
    results[0] = results[0] + edge_ref[0]
    results[-1] = results[-1] + edge_ref[1]
    results = [result.astype(BF) for result in results]
    for i, result in enumerate(results):
        out_ref[i] = result
    if next_refs:
        coeff_ref, inner_ref, outer_ref = next_refs
        emit_edges(out_ref, inner_ref, outer_ref)
        emit_coeffs(results, basis_ref, transfer_ref, ranks_ref, coeff_ref)


def params(mebibytes):
    return pltpu.CompilerParams(vmem_limit_bytes=mebibytes << 20)


def local(charges, basis, transfer, near_field, coupling, ranks, block_source, block_target):
    leaves, rank_top, width = basis.shape
    rhs = charges.shape[1]
    clusters = ranks.shape[0]
    blocks = coupling.shape[0]
    devices = lax.axis_size("clu")
    mains = clusters * 3 // 4
    shape = jax.ShapeDtypeStruct

    cores, chips = CORES, CHIPS
    cube = cores * chips
    far = devices // cube
    x, y, z = 1, 2, 4

    def swap_far(part, shift):
        return lax.ppermute(part, "clu", [(d, (d + shift * cube) % devices) for d in range(devices)])

    def swap(part, direction):
        turned = direction << 1 & 7 | direction >> 2
        return lax.ppermute(
            part, "clu", [(d, d ^ (turned if d % cores else direction) * cores) for d in range(devices)]
        )

    def swap_cores(part):
        return lax.ppermute(part, "clu", [(d, d ^ 1) for d in range(devices)])

    barrier = lax.optimization_barrier

    shift = 19
    magic = -(-(1 << shift) // clusters)
    numbers = np.arange(devices * clusters)
    assert (numbers * magic >> shift == numbers // clusters).all() and far & far - 1 == 0
    list_shape = jax.ShapeDtypeStruct((1, blocks), jnp.int32)
    source_rows, target_rows = pl.pallas_call(
        functools.partial(rows_kernel, clusters=clusters, far=far, magic=magic, shift=shift),
        out_shape=[list_shape] * 2,
        in_specs=[VMEM] * 2,
        out_specs=[VMEM] * 2,
        compiler_params=params(1),
    )(block_source.reshape(1, blocks), block_target.reshape(1, blocks))
    source_rows, target_rows = source_rows.reshape(blocks), target_rows.reshape(blocks)

    tile_shape = (mains, rhs, LANES)
    out_shape = shape((leaves, rhs, width), BF)
    tile_out = shape(tile_shape, BF)
    part_shape = shape((far,) + tile_shape, BF)
    edge_shape = shape((1, rhs, width), BF)
    first_coeffs, inner, outer = pl.pallas_call(
        coeff_kernel,
        out_shape=[tile_out, edge_shape, edge_shape],
        in_specs=[SMEM, HBM, HBM, HBM],
        out_specs=[VMEM] * 3,
        scratch_shapes=[
            pltpu.VMEM(charges.shape, BF),
            pltpu.VMEM(basis.shape, BF),
            pltpu.VMEM(transfer.shape, BF),
            pltpu.SemaphoreType.DMA((3,)),
        ],
    )(ranks, charges, basis, transfer)

    order = ((x | y | z, x | y, y | z, z | x), (0, x, y, z))
    couple = pl.pallas_call(
        functools.partial(couple_kernel, order=order, unroll=64),
        out_shape=[shape((4, far) + tile_shape, BF)] * 4,
        in_specs=[SMEM, SMEM, VMEM] + [VMEM] * (cores * chips),
        out_specs=[VMEM] * 4,
        scratch_shapes=[
            pltpu.VMEM((devices * clusters, rhs, LANES), BF),
            pltpu.VMEM((devices * clusters, rhs, LANES), F32),
        ],
        compiler_params=params(24 if devices <= 32 else 60),
        cost_estimate=pl.CostEstimate(
            flops=2 * blocks * rhs * rank_top * rank_top, bytes_accessed=10 << 20, transcendentals=0
        ),
    )

    near = pl.pallas_call(
        near_kernel,
        out_shape=shape((leaves, rhs, width), F32),
        in_specs=[VMEM, VMEM],
        out_specs=VMEM,
        compiler_params=params(16),
        cost_estimate=pl.CostEstimate(
            flops=2 * leaves * 3 * rhs * width * width, bytes_accessed=4 << 20, transcendentals=0
        ),
    )

    edge = pl.pallas_call(
        edge_kernel,
        out_shape=shape((2, rhs, width), F32),
        grid=(1,),
        in_specs=[
            VMEM,
            VMEM,
            pl.BlockSpec((1, 1, width, width), lambda i: (0, 0, 0, 0)),
            pl.BlockSpec((1, 1, width, width), lambda i: (leaves - 1, 2, 0, 0)),
        ],
        out_specs=VMEM,
        compiler_params=params(16),
    )

    def adder(kernel, inputs, outputs):
        return pl.pallas_call(
            kernel,
            out_shape=outputs,
            in_specs=[VMEM] * inputs,
            out_specs=[VMEM] * len(outputs),
            compiler_params=params(16),
        )

    own_shape = shape((far,) + tile_shape, F32)
    join = adder(join_kernel, far, [part_shape])
    first_join = pl.pallas_call(
        lambda _, *refs: join_kernel(*refs),
        out_shape=[part_shape],
        in_specs=[pl.BlockSpec(memory_space=pl.ANY)] + [VMEM] * far,
        out_specs=[VMEM],
    )
    far_add = adder(add_kernel, 2, [part_shape] * 4)
    middle_add = adder(functools.partial(middle_add_kernel, parts=4), 6, [own_shape] + [part_shape] * 3)
    last_add = adder(
        functools.partial(last_add_kernel, parts=3), 4, [shape(tile_shape, F32)] + [tile_out] * (far - 1)
    )

    def finish(with_coeffs):
        return pl.pallas_call(
            functools.partial(field_kernel, away=far - 1),
            out_shape=[out_shape, tile_out, edge_shape, edge_shape] if with_coeffs else [out_shape],
            in_specs=[SMEM] + [VMEM] * (4 + far),
            out_specs=[VMEM] * 4 if with_coeffs else [VMEM],
            compiler_params=params(16),
        )

    halo_pairs = [(d, d + cores) for d in range(1, devices - cores, cores)]
    halo_pairs += [(d, d - cores) for d in range(cores, devices, cores)]

    def apply_matrix(field_in, coeffs, inner, outer, coupling, with_coeffs):
        away = [swap_far(coeffs, s) for s in range(1, far)]
        (column,) = first_join(coupling, coeffs, *away) if with_coeffs else join(coeffs, *away)
        got = {0: column, x: swap(column, x), y: swap(column, y), z: swap(column, z)}
        near_sum, outer = barrier((near(field_in, near_field), outer))
        got, near_sum, outer = barrier((got, near_sum, lax.ppermute(outer, "clu", halo_pairs)))
        other = {chip: swap_cores(part) for chip, part in got.items()}
        corner = swap(got[x], y | z)
        got |= {x | y: swap(got[x], y), y | z: swap(got[y], z), z | x: swap(got[z], x)}
        got, corner = barrier((got, corner))
        got[x | y | z] = corner
        other |= {chip: swap_cores(got[chip]) for chip in order[0]}
        totals = couple(
            source_rows,
            target_rows,
            coupling,
            *[got[chip] for chip in range(chips)],
            *[other[chip] for chip in range(chips)],
        )
        keep_long, keep, send_long, send = totals
        corner, xy, yz, zx = far_add(keep_long, swap_cores(send_long))
        corner, xy, yz, zx, send = barrier((corner, xy, yz, zx, send))
        to_x, to_y, to_z, corner, swapped = barrier(
            (swap(xy, y), swap(yz, z), swap(zx, x), swap(corner, y | z), swap_cores(send))
        )
        own, to_x, to_y, to_z, inner, outer = barrier(
            (*middle_add(keep, swapped, to_x, to_y, to_z, corner), inner, outer)
        )
        edges = edge(swap_cores(inner), swap_cores(outer), near_field, near_field)
        own, to_x, to_y, to_z, edges = barrier((own, swap(to_x, x), swap(to_y, y), swap(to_z, z), edges))
        total, *away = last_add(own, to_x, to_y, to_z)
        terms = [swap_far(part, s + 1) for s, part in enumerate(away)]
        return finish(with_coeffs)(ranks, near_sum, edges, basis, transfer, total, *terms)

    first, *second_args = apply_matrix(charges, first_coeffs, inner, outer, coupling, True)
    (second,) = apply_matrix(first, *second_args, coupling, False)
    return (first, second)


def solution(mesh):
    in_specs = (
        P("clu", None, None),
        P("clu", None, None),
        P("clu", None, None),
        P("clu", None, None, None),
        P("clu", None, None),
        P("clu"),
        P("clu"),
        P("clu"),
    )
    out_specs = (P("clu", None, None), P("clu", None, None))
    return jax.shard_map(local, mesh=mesh, in_specs=in_specs, out_specs=out_specs, check_vma=False)
```

```python
import functools

import jax
import jax.numpy as jnp
import numpy as np
from jax import lax
from jax.experimental import pallas as pl
from jax.experimental.pallas import tpu as pltpu
from jax.sharding import PartitionSpec as P

LANES = 128
CORES, CHIPS = 2, 8
BF = jnp.bfloat16
F32 = jnp.float32
VMEM = pl.BlockSpec(memory_space=pltpu.VMEM)
SMEM = pl.BlockSpec(memory_space=pltpu.SMEM)
HBM = pl.BlockSpec(memory_space=pltpu.HBM)


def dot(a, b):
    return lax.dot_general(a, b, (((1,), (0,)), ((), ())), preferred_element_type=F32)


def dot_t(a, b):
    return lax.dot_general(a, b, (((1,), (1,)), ((), ())), preferred_element_type=F32)


def lanes(rows):
    return lax.broadcasted_iota(jnp.int32, (rows, LANES), 1)


def fourth(tiles, rank_top):
    third = LANES - rank_top
    lane = lanes(tiles[0].shape[0])
    moved = [pltpu.roll(tile, third * (k + 1), 1) for k, tile in enumerate(tiles)]
    return jnp.where(lane < third, moved[0], jnp.where(lane < 2 * third, moved[1], moved[2]))


def packed(mains, pad, rank_top):
    lane = lanes(pad.shape[0])
    third = LANES - rank_top
    return [
        jnp.where(lane < rank_top, main, pltpu.roll(pad, rank_top - third * k, 1)) for k, main in enumerate(mains)
    ]


def widen(value):
    return jnp.concatenate([value, jnp.zeros((value.shape[0], LANES - value.shape[1]), value.dtype)], axis=1)


def emit_coeffs(values, basis_ref, transfer_ref, ranks_ref, out_ref, ready=None):
    mains, rhs, _ = out_ref.shape
    leaves, rank_top, _ = basis_ref.shape
    lane = lax.broadcasted_iota(jnp.int32, (rhs, rank_top), 1)
    coeffs = []
    for i in range(leaves):
        value = dot_t(values[i], basis_ref[i])
        coeffs.append(jnp.where(lane < ranks_ref[i], value, 0.0).astype(BF))
    if ready is not None:
        ready()
    for q in range(leaves // 2):
        value = dot(coeffs[2 * q], transfer_ref[2 * q]) + dot(coeffs[2 * q + 1], transfer_ref[2 * q + 1])
        coeffs.append(jnp.where(lane < ranks_ref[leaves + q], value, 0.0).astype(BF))
    wide = [widen(value.astype(F32)) for value in coeffs]
    for q in range(mains // 3):
        for k, tile in enumerate(packed(wide[3 * q : 3 * q + 3], wide[mains + q], rank_top)):
            out_ref[3 * q + k] = tile.astype(BF)


def fetch(pairs, sems):
    copies = [pltpu.make_async_copy(src, dst, sems.at[n]) for n, (src, dst) in enumerate(pairs)]
    for copy in copies:
        copy.start()
    return copies


def emit_edges(v_ref, inner_ref, outer_ref):
    head, tail = v_ref[0], v_ref[v_ref.shape[0] - 1]
    even = lax.axis_index("clu") % CORES == 0
    inner_ref[0] = jnp.where(even, tail, head)
    outer_ref[0] = jnp.where(even, head, tail)


def coeff_kernel(
    ranks_ref, v_hbm, basis_hbm, transfer_hbm, out_ref, inner_ref, outer_ref, v_ref, basis_ref, transfer_ref, sems
):
    leaves = basis_ref.shape[0]
    copies = fetch([(v_hbm, v_ref), (basis_hbm, basis_ref), (transfer_hbm, transfer_ref)], sems)
    copies[0].wait()
    emit_edges(v_ref, inner_ref, outer_ref)
    copies[1].wait()
    values = [v_ref[i] for i in range(leaves)]
    emit_coeffs(values, basis_ref, transfer_ref, ranks_ref, out_ref, copies[2].wait)


def couple_kernel(source_ref, target_ref, coupling_ref, *refs, order, unroll):
    chips = sum(len(group) for group in order)
    blocks, rank_top, _ = coupling_ref.shape
    near_size, far, mains, rhs, _ = refs[0].shape
    per_core = 1 + chips - near_size
    in_refs, out_refs, (sources, total) = [], refs[2 * per_core : -2], refs[-2:]
    for core in range(2):
        joined, *single = refs[core * per_core : (core + 1) * per_core]
        pieces = {chip: joined.at[place] for place, chip in enumerate(order[1])} | dict(zip(order[0], single))
        in_refs += [pieces[chip] for chip in range(chips)]
    quads = mains // 3
    clusters = mains + quads

    def split(f, _):
        for n, packed_ref in enumerate(in_refs):
            row = (n * far + f) * clusters
            tiles = [packed_ref[f, c] for c in range(mains)]
            for c in range(mains):
                sources[row + c] = tiles[c]
            for q in range(quads):
                wide = [tile.astype(F32) for tile in tiles[3 * q : 3 * q + 3]]
                sources[row + mains + q] = fourth(wide, rank_top).astype(BF)
            for c in range(clusters):
                total[row + c] = jnp.zeros((rhs, LANES), F32)
        return 0

    lax.fori_loop(0, far, split, 0)

    def some(s, _):
        for u in range(unroll):
            j = s * unroll + u
            term = dot(sources[source_ref[j], :, :rank_top], coupling_ref[j])
            at = target_ref[j]
            total[at, :, :rank_top] = total[at, :, :rank_top] + term
        return 0

    lax.fori_loop(0, blocks // unroll, some, 0)

    def pack(f, _):
        for core in range(2):
            for g, group in enumerate(order):
                for place, chip in enumerate(group):
                    row = ((core * chips + chip) * far + f) * clusters
                    for q in range(quads):
                        mains_now = [total[row + 3 * q + k] for k in range(3)]
                        for k, tile in enumerate(packed(mains_now, total[row + mains + q], rank_top)):
                            out_refs[core * len(order) + g][place, f, 3 * q + k] = tile.astype(BF)
        return 0

    lax.fori_loop(0, far, pack, 0)


def order_kernel(_, __, out_ref):
    out_ref[...] = jnp.zeros_like(out_ref)


def near_kernel(v_ref, near_ref, out_ref):
    leaves = v_ref.shape[0]
    for i in range(leaves):
        total = dot(v_ref[i], near_ref[i, 1])
        if i > 0:
            total = total + dot(v_ref[i - 1], near_ref[i, 0])
        if i < leaves - 1:
            total = total + dot(v_ref[i + 1], near_ref[i, 2])
        out_ref[i] = total


def edge_kernel(inner_ref, outer_ref, first_ref, last_ref, out_ref):
    inner, outer = inner_ref[0], outer_ref[0]
    even = lax.axis_index("clu") % CORES == 0
    out_ref[0] = dot(jnp.where(even, outer, inner), first_ref[0, 0])
    out_ref[1] = dot(jnp.where(even, inner, outer), last_ref[0, 0])


def add_kernel(keep_ref, swap_ref, *out_refs):
    for n, out_ref in enumerate(out_refs):
        out_ref[...] = (keep_ref[n].astype(F32) + swap_ref[n].astype(F32)).astype(out_ref.dtype)


def middle_add_kernel(keep_ref, swap_ref, *refs, parts):
    part_refs, (own_out, *out_refs) = refs[:parts], refs[parts:]
    own_out[...] = keep_ref[0].astype(F32) + swap_ref[0].astype(F32)
    for n, out_ref in enumerate(out_refs):
        total = keep_ref[n + 1].astype(F32) + swap_ref[n + 1].astype(F32)
        for part_ref in part_refs[n :: len(out_refs)]:
            total = total + part_ref[...].astype(F32)
        out_ref[...] = total.astype(BF)


def rows_kernel(source_ref, target_ref, source_out, target_out, *, clusters, far, magic, shift):
    me = lax.axis_index("clu")
    for sign, in_ref, out_ref in ((-1, source_ref, source_out), (1, target_ref, target_out)):
        cluster = in_ref[...]
        device = cluster * magic >> shift
        chip = ((device ^ me) >> 1) & (CHIPS - 1)
        chip = jnp.where((device & 1) == 0, chip, chip >> 1 | (chip & 1) << 2)
        away = (sign * ((device >> 4) - (me >> 4))) & (far - 1)
        core = (device ^ me) & 1
        out_ref[...] = ((core * CHIPS + chip) * far + away) * clusters + cluster - device * clusters


def join_kernel(*refs):
    for n, part_ref in enumerate(refs[:-1]):
        refs[-1][n] = part_ref[...]


def last_add_kernel(own_ref, *refs, parts):
    part_refs, (keep_out, *away_refs) = refs[:parts], refs[parts:]
    for f in range(own_ref.shape[0]):
        total = own_ref[f]
        for part_ref in part_refs:
            total = total + part_ref[f].astype(F32)
        if f == 0:
            keep_out[...] = total
        else:
            away_refs[f - 1][...] = total.astype(BF)


def field_kernel(ranks_ref, near_ref, edge_ref, basis_ref, transfer_ref, keep_ref, *rest, away):
    term_refs, out_ref, next_refs = rest[:away], rest[away], rest[away + 1 :]
    leaves, rank_top, _ = basis_ref.shape
    mains, rhs, _ = keep_ref.shape
    tiles = []
    for t in range(mains):
        tile = keep_ref[t]
        for term_ref in term_refs:
            tile = tile + term_ref[t].astype(F32)
        tiles.append(tile)
    sums = tiles + [fourth(tiles[3 * q : 3 * q + 3], rank_top) for q in range(mains // 3)]
    lane = lax.broadcasted_iota(jnp.int32, (rhs, rank_top), 1)
    fields = [
        jnp.where(lane < ranks_ref[c], total[:, :rank_top], 0.0).astype(BF) for c, total in enumerate(sums)
    ]
    downs = [fields[i].astype(F32) + dot_t(fields[leaves + i // 2], transfer_ref[i]) for i in range(leaves)]
    leaf_totals = [jnp.where(lane < ranks_ref[i], down, 0.0).astype(BF) for i, down in enumerate(downs)]
    results = [near_ref[i] + dot(leaf_total, basis_ref[i]) for i, leaf_total in enumerate(leaf_totals)]
    results[0] = results[0] + edge_ref[0]
    results[-1] = results[-1] + edge_ref[1]
    results = [result.astype(BF) for result in results]
    for i, result in enumerate(results):
        out_ref[i] = result
    if next_refs:
        coeff_ref, inner_ref, outer_ref = next_refs
        emit_edges(out_ref, inner_ref, outer_ref)
        emit_coeffs(results, basis_ref, transfer_ref, ranks_ref, coeff_ref)


def params(mebibytes):
    return pltpu.CompilerParams(vmem_limit_bytes=mebibytes << 20)


def local(charges, basis, transfer, near_field, coupling, ranks, block_source, block_target):
    leaves, rank_top, width = basis.shape
    rhs = charges.shape[1]
    clusters = ranks.shape[0]
    blocks = coupling.shape[0]
    devices = lax.axis_size("clu")
    mains = clusters * 3 // 4
    shape = jax.ShapeDtypeStruct

    cores, chips = CORES, CHIPS
    cube = cores * chips
    far = devices // cube
    x, y, z = 1, 2, 4

    def swap_far(part, shift):
        return lax.ppermute(part, "clu", [(d, (d + shift * cube) % devices) for d in range(devices)])

    def swap(part, direction):
        turned = direction << 1 & 7 | direction >> 2
        return lax.ppermute(
            part, "clu", [(d, d ^ (turned if d % cores else direction) * cores) for d in range(devices)]
        )

    def swap_cores(part):
        return lax.ppermute(part, "clu", [(d, d ^ 1) for d in range(devices)])

    barrier = lax.optimization_barrier

    shift = 19
    magic = -(-(1 << shift) // clusters)
    numbers = np.arange(devices * clusters)
    assert (numbers * magic >> shift == numbers // clusters).all() and far & far - 1 == 0
    list_shape = jax.ShapeDtypeStruct((1, blocks), jnp.int32)
    source_rows, target_rows = pl.pallas_call(
        functools.partial(rows_kernel, clusters=clusters, far=far, magic=magic, shift=shift),
        out_shape=[list_shape] * 2,
        in_specs=[VMEM] * 2,
        out_specs=[VMEM] * 2,
        compiler_params=params(1),
    )(block_source.reshape(1, blocks), block_target.reshape(1, blocks))
    source_rows, target_rows = source_rows.reshape(blocks), target_rows.reshape(blocks)

    tile_shape = (mains, rhs, LANES)
    out_shape = shape((leaves, rhs, width), BF)
    tile_out = shape(tile_shape, BF)
    part_shape = shape((far,) + tile_shape, BF)
    edge_shape = shape((1, rhs, width), BF)
    first_coeffs, inner, outer = pl.pallas_call(
        coeff_kernel,
        out_shape=[tile_out, edge_shape, edge_shape],
        in_specs=[SMEM, HBM, HBM, HBM],
        out_specs=[VMEM] * 3,
        scratch_shapes=[
            pltpu.VMEM(charges.shape, BF),
            pltpu.VMEM(basis.shape, BF),
            pltpu.VMEM(transfer.shape, BF),
            pltpu.SemaphoreType.DMA((3,)),
        ],
    )(ranks, charges, basis, transfer)

    order = ((x | y | z, x | y, y | z, z | x), (0, x, y, z))
    couple = pl.pallas_call(
        functools.partial(couple_kernel, order=order, unroll=64),
        out_shape=[shape((4, far) + tile_shape, BF)] * 4,
        in_specs=[SMEM, SMEM, VMEM] + [VMEM] * (cores * (1 + len(order[0]))),
        out_specs=[VMEM] * 4,
        scratch_shapes=[
            pltpu.VMEM((devices * clusters, rhs, LANES), BF),
            pltpu.VMEM((devices * clusters, rhs, LANES), F32),
        ],
        compiler_params=params(24 if devices <= 32 else 60),
        cost_estimate=pl.CostEstimate(
            flops=2 * blocks * rhs * rank_top * rank_top, bytes_accessed=10 << 20, transcendentals=0
        ),
    )

    near = pl.pallas_call(
        near_kernel,
        out_shape=shape((leaves, rhs, width), F32),
        in_specs=[VMEM, VMEM],
        out_specs=VMEM,
        compiler_params=params(16),
        cost_estimate=pl.CostEstimate(
            flops=2 * leaves * 3 * rhs * width * width, bytes_accessed=4 << 20, transcendentals=0
        ),
    )

    edge = pl.pallas_call(
        edge_kernel,
        out_shape=shape((2, rhs, width), F32),
        grid=(1,),
        in_specs=[
            VMEM,
            VMEM,
            pl.BlockSpec((1, 1, width, width), lambda i: (0, 0, 0, 0)),
            pl.BlockSpec((1, 1, width, width), lambda i: (leaves - 1, 2, 0, 0)),
        ],
        out_specs=VMEM,
        compiler_params=params(16),
    )

    def adder(kernel, inputs, outputs):
        return pl.pallas_call(
            kernel,
            out_shape=outputs,
            in_specs=[VMEM] * inputs,
            out_specs=[VMEM] * len(outputs),
            compiler_params=params(16),
        )

    own_shape = shape((far,) + tile_shape, F32)
    join = adder(join_kernel, far, [part_shape])
    join_near = adder(join_kernel, 4, [shape((4,) + part_shape.shape, BF)])
    relaid = pl.pallas_call(
        order_kernel,
        out_shape=shape((8, LANES), F32),
        in_specs=[pl.BlockSpec(memory_space=pl.ANY)] * 2,
        out_specs=VMEM,
    )
    first_join = pl.pallas_call(
        lambda _, *refs: join_kernel(*refs),
        out_shape=[part_shape],
        in_specs=[pl.BlockSpec(memory_space=pl.ANY)] + [VMEM] * far,
        out_specs=[VMEM],
        compiler_params=params(16),
    )
    far_add = adder(add_kernel, 2, [part_shape] * 4)
    middle_add = adder(functools.partial(middle_add_kernel, parts=4), 6, [own_shape] + [part_shape] * 3)
    last_add = adder(
        functools.partial(last_add_kernel, parts=3), 4, [shape(tile_shape, F32)] + [tile_out] * (far - 1)
    )

    def finish(with_coeffs):
        return pl.pallas_call(
            functools.partial(field_kernel, away=far - 1),
            out_shape=[out_shape, tile_out, edge_shape, edge_shape] if with_coeffs else [out_shape],
            in_specs=[SMEM] + [VMEM] * (4 + far),
            out_specs=[VMEM] * 4 if with_coeffs else [VMEM],
            compiler_params=params(16),
        )

    halo_pairs = [(d, d + cores) for d in range(1, devices - cores, cores)]
    halo_pairs += [(d, d - cores) for d in range(cores, devices, cores)]

    def apply_matrix(field_in, coeffs, inner, outer, coupling, with_coeffs):
        away = [swap_far(coeffs, s) for s in range(1, far)]
        (column,) = first_join(relaid(coupling, coeffs), coeffs, *away) if with_coeffs else join(coeffs, *away)
        got = {0: column, x: swap(column, x), y: swap(column, y), z: swap(column, z)}
        near_sum = near(field_in, near_field)
        got, near_sum = barrier((got, near_sum))
        corner = swap(got[x], y | z)
        (near_pieces,) = join_near(*[got[chip] for chip in order[1]])
        got |= {x | y: swap(got[x], y), y | z: swap(got[y], z), z | x: swap(got[z], x)}
        got[x | y | z] = corner
        far_pieces, other_near = barrier(([got[chip] for chip in order[0]], swap_cores(near_pieces)))
        other_far = [swap_cores(part) for part in far_pieces]
        totals = couple(source_rows, target_rows, coupling, near_pieces, *far_pieces, other_near, *other_far)
        keep_long, keep, send_long, send = totals
        corner, xy, yz, zx = far_add(keep_long, swap_cores(send_long))
        corner, xy, yz, zx, send = barrier((corner, xy, yz, zx, send))
        to_x, to_y, to_z, corner, swapped = barrier(
            (swap(xy, y), swap(yz, z), swap(zx, x), swap(corner, y | z), swap_cores(send))
        )
        own, to_x, to_y, to_z, inner, outer = barrier(
            (*middle_add(keep, swapped, to_x, to_y, to_z, corner), inner, outer)
        )
        own, to_x, to_y, to_z, inner, outer = barrier(
            (own, swap(to_x, x), swap(to_y, y), swap(to_z, z), inner, lax.ppermute(outer, "clu", halo_pairs))
        )
        total, *away = last_add(own, to_x, to_y, to_z)
        edges = edge(swap_cores(inner), swap_cores(outer), near_field, near_field)
        terms, edges = barrier(([swap_far(part, s + 1) for s, part in enumerate(away)], edges))
        return finish(with_coeffs)(ranks, near_sum, edges, basis, transfer, total, *terms)

    first, *second_args = apply_matrix(charges, first_coeffs, inner, outer, coupling, True)
    (second,) = apply_matrix(first, *second_args, coupling, False)
    return (first, second)


def solution(mesh):
    in_specs = (
        P("clu", None, None),
        P("clu", None, None),
        P("clu", None, None),
        P("clu", None, None, None),
        P("clu", None, None),
        P("clu"),
        P("clu"),
        P("clu"),
    )
    out_specs = (P("clu", None, None), P("clu", None, None))
    return jax.shard_map(local, mesh=mesh, in_specs=in_specs, out_specs=out_specs, check_vma=False)
```

```python
import functools

import jax
import jax.numpy as jnp
import numpy as np
from jax import lax
from jax.experimental import pallas as pl
from jax.experimental.pallas import tpu as pltpu
from jax.sharding import PartitionSpec as P

LANES = 128
CORES, CHIPS = 2, 8
BF = jnp.bfloat16
F32 = jnp.float32
VMEM = pl.BlockSpec(memory_space=pltpu.VMEM)
SMEM = pl.BlockSpec(memory_space=pltpu.SMEM)
HBM = pl.BlockSpec(memory_space=pltpu.HBM)


def dot(a, b):
    return lax.dot_general(a, b, (((1,), (0,)), ((), ())), preferred_element_type=F32)


def dot_t(a, b):
    return lax.dot_general(a, b, (((1,), (1,)), ((), ())), preferred_element_type=F32)


def lanes(rows):
    return lax.broadcasted_iota(jnp.int32, (rows, LANES), 1)


def fourth(tiles, rank_top):
    third = LANES - rank_top
    lane = lanes(tiles[0].shape[0])
    moved = [pltpu.roll(tile, third * (k + 1), 1) for k, tile in enumerate(tiles)]
    return jnp.where(lane < third, moved[0], jnp.where(lane < 2 * third, moved[1], moved[2]))


def packed(mains, pad, rank_top):
    lane = lanes(pad.shape[0])
    third = LANES - rank_top
    return [
        jnp.where(lane < rank_top, main, pltpu.roll(pad, rank_top - third * k, 1)) for k, main in enumerate(mains)
    ]


def widen(value):
    return jnp.concatenate([value, jnp.zeros((value.shape[0], LANES - value.shape[1]), value.dtype)], axis=1)


def emit_coeffs(values, basis_ref, transfer_ref, ranks_ref, out_ref, ready=None):
    mains, rhs, _ = out_ref.shape
    leaves, rank_top, _ = basis_ref.shape
    lane = lax.broadcasted_iota(jnp.int32, (rhs, rank_top), 1)
    coeffs = []
    for i in range(leaves):
        value = dot_t(values[i], basis_ref[i])
        coeffs.append(jnp.where(lane < ranks_ref[i], value, 0.0).astype(BF))
    if ready is not None:
        ready()
    for q in range(leaves // 2):
        value = dot(coeffs[2 * q], transfer_ref[2 * q]) + dot(coeffs[2 * q + 1], transfer_ref[2 * q + 1])
        coeffs.append(jnp.where(lane < ranks_ref[leaves + q], value, 0.0).astype(BF))
    wide = [widen(value.astype(F32)) for value in coeffs]
    for q in range(mains // 3):
        for k, tile in enumerate(packed(wide[3 * q : 3 * q + 3], wide[mains + q], rank_top)):
            out_ref[3 * q + k] = tile.astype(BF)


def fetch(pairs, sems):
    copies = [pltpu.make_async_copy(src, dst, sems.at[n]) for n, (src, dst) in enumerate(pairs)]
    for copy in copies:
        copy.start()
    return copies


def emit_edges(v_ref, inner_ref, outer_ref):
    head, tail = v_ref[0], v_ref[v_ref.shape[0] - 1]
    even = lax.axis_index("clu") % CORES == 0
    inner_ref[0] = jnp.where(even, tail, head)
    outer_ref[0] = jnp.where(even, head, tail)


def coeff_kernel(
    ranks_ref, v_hbm, basis_hbm, transfer_hbm, out_ref, inner_ref, outer_ref, v_ref, basis_ref, transfer_ref, sems
):
    leaves = basis_ref.shape[0]
    copies = fetch([(v_hbm, v_ref), (basis_hbm, basis_ref), (transfer_hbm, transfer_ref)], sems)
    copies[0].wait()
    emit_edges(v_ref, inner_ref, outer_ref)
    copies[1].wait()
    values = [v_ref[i] for i in range(leaves)]
    emit_coeffs(values, basis_ref, transfer_ref, ranks_ref, out_ref, copies[2].wait)


def couple_kernel(source_ref, target_ref, coupling_ref, *refs, order, unroll):
    chips = sum(len(group) for group in order)
    blocks, rank_top, _ = coupling_ref.shape
    near_size, far, mains, rhs, _ = refs[0].shape
    per_core = 1 + chips - near_size
    in_refs, out_refs, (sources, total) = [], refs[2 * per_core : -2], refs[-2:]
    for core in range(2):
        joined, *single = refs[core * per_core : (core + 1) * per_core]
        pieces = {chip: joined.at[place] for place, chip in enumerate(order[1])} | dict(zip(order[0], single))
        in_refs += [pieces[chip] for chip in range(chips)]
    quads = mains // 3
    clusters = mains + quads

    def split(f, _):
        for n, packed_ref in enumerate(in_refs):
            row = (n * far + f) * clusters
            tiles = [packed_ref[f, c] for c in range(mains)]
            for c in range(mains):
                sources[row + c] = tiles[c]
            for q in range(quads):
                wide = [tile.astype(F32) for tile in tiles[3 * q : 3 * q + 3]]
                sources[row + mains + q] = fourth(wide, rank_top).astype(BF)
            for c in range(clusters):
                total[row + c] = jnp.zeros((rhs, LANES), F32)
        return 0

    lax.fori_loop(0, far, split, 0)

    def some(s, _):
        for u in range(unroll):
            j = s * unroll + u
            term = dot(sources[source_ref[j], :, :rank_top], coupling_ref[j])
            at = target_ref[j]
            total[at, :, :rank_top] = total[at, :, :rank_top] + term
        return 0

    lax.fori_loop(0, blocks // unroll, some, 0)

    def pack(f, _):
        for core in range(2):
            for g, group in enumerate(order):
                for place, chip in enumerate(group):
                    row = ((core * chips + chip) * far + f) * clusters
                    for q in range(quads):
                        mains_now = [total[row + 3 * q + k] for k in range(3)]
                        for k, tile in enumerate(packed(mains_now, total[row + mains + q], rank_top)):
                            out_refs[core * len(order) + g][place, f, 3 * q + k] = tile.astype(BF)
        return 0

    lax.fori_loop(0, far, pack, 0)


def order_kernel(_, __, out_ref):
    out_ref[...] = jnp.zeros_like(out_ref)


def near_kernel(v_ref, near_ref, out_ref):
    leaves = v_ref.shape[0]
    for i in range(leaves):
        total = dot(v_ref[i], near_ref[i, 1])
        if i > 0:
            total = total + dot(v_ref[i - 1], near_ref[i, 0])
        if i < leaves - 1:
            total = total + dot(v_ref[i + 1], near_ref[i, 2])
        out_ref[i] = total


def edge_kernel(inner_ref, outer_ref, first_ref, last_ref, out_ref):
    inner, outer = inner_ref[0], outer_ref[0]
    even = lax.axis_index("clu") % CORES == 0
    out_ref[0] = dot(jnp.where(even, outer, inner), first_ref[0, 0])
    out_ref[1] = dot(jnp.where(even, inner, outer), last_ref[0, 0])


def add_kernel(keep_ref, swap_ref, *out_refs):
    for n, out_ref in enumerate(out_refs):
        out_ref[...] = (keep_ref[n].astype(F32) + swap_ref[n].astype(F32)).astype(out_ref.dtype)


def middle_add_kernel(keep_ref, swap_ref, *refs, parts):
    part_refs, (own_out, *out_refs) = refs[:parts], refs[parts:]
    own_out[...] = keep_ref[0].astype(F32) + swap_ref[0].astype(F32)
    for n, out_ref in enumerate(out_refs):
        total = keep_ref[n + 1].astype(F32) + swap_ref[n + 1].astype(F32)
        out_ref[...] = (total + part_refs[n][...].astype(F32)).astype(BF)


def rows_kernel(source_ref, target_ref, source_out, target_out, *, clusters, far, magic, shift):
    me = lax.axis_index("clu")
    for sign, in_ref, out_ref in ((-1, source_ref, source_out), (1, target_ref, target_out)):
        cluster = in_ref[...]
        device = cluster * magic >> shift
        chip = ((device ^ me) >> 1) & (CHIPS - 1)
        chip = jnp.where((device & 1) == 0, chip, chip >> 1 | (chip & 1) << 2)
        away = (sign * ((device >> 4) - (me >> 4))) & (far - 1)
        core = (device ^ me) & 1
        out_ref[...] = ((core * CHIPS + chip) * far + away) * clusters + cluster - device * clusters


def join_kernel(*refs):
    for n, part_ref in enumerate(refs[:-1]):
        refs[-1][n] = part_ref[...]


def last_add_kernel(own_ref, *refs, parts):
    part_refs, (keep_out, *away_refs) = refs[:parts], refs[parts:]
    for f in range(own_ref.shape[0]):
        total = own_ref[f]
        for part_ref in part_refs:
            total = total + part_ref[f].astype(F32)
        if f == 0:
            keep_out[...] = total
        else:
            away_refs[f - 1][...] = total.astype(BF)


def field_kernel(ranks_ref, near_ref, edge_ref, basis_ref, transfer_ref, keep_ref, *rest, away):
    term_refs, out_ref, next_refs = rest[:away], rest[away], rest[away + 1 :]
    leaves, rank_top, _ = basis_ref.shape
    mains, rhs, _ = keep_ref.shape
    tiles = []
    for t in range(mains):
        tile = keep_ref[t]
        for term_ref in term_refs:
            tile = tile + term_ref[t].astype(F32)
        tiles.append(tile)
    sums = tiles + [fourth(tiles[3 * q : 3 * q + 3], rank_top) for q in range(mains // 3)]
    lane = lax.broadcasted_iota(jnp.int32, (rhs, rank_top), 1)
    fields = [
        jnp.where(lane < ranks_ref[c], total[:, :rank_top], 0.0).astype(BF) for c, total in enumerate(sums)
    ]
    downs = [fields[i].astype(F32) + dot_t(fields[leaves + i // 2], transfer_ref[i]) for i in range(leaves)]
    leaf_totals = [jnp.where(lane < ranks_ref[i], down, 0.0).astype(BF) for i, down in enumerate(downs)]
    results = [near_ref[i] + dot(leaf_total, basis_ref[i]) for i, leaf_total in enumerate(leaf_totals)]
    results[0] = results[0] + edge_ref[0]
    results[-1] = results[-1] + edge_ref[1]
    results = [result.astype(BF) for result in results]
    for i, result in enumerate(results):
        out_ref[i] = result
    if next_refs:
        coeff_ref, inner_ref, outer_ref = next_refs
        emit_edges(out_ref, inner_ref, outer_ref)
        emit_coeffs(results, basis_ref, transfer_ref, ranks_ref, coeff_ref)


def params(mebibytes):
    return pltpu.CompilerParams(vmem_limit_bytes=mebibytes << 20)


def local(charges, basis, transfer, near_field, coupling, ranks, block_source, block_target):
    leaves, rank_top, width = basis.shape
    rhs = charges.shape[1]
    clusters = ranks.shape[0]
    blocks = coupling.shape[0]
    devices = lax.axis_size("clu")
    mains = clusters * 3 // 4
    shape = jax.ShapeDtypeStruct

    cores, chips = CORES, CHIPS
    cube = cores * chips
    far = devices // cube
    x, y, z = 1, 2, 4

    def swap_far(part, shift):
        return lax.ppermute(part, "clu", [(d, (d + shift * cube) % devices) for d in range(devices)])

    def swap(part, direction):
        turned = direction << 1 & 7 | direction >> 2
        return lax.ppermute(
            part, "clu", [(d, d ^ (turned if d % cores else direction) * cores) for d in range(devices)]
        )

    def swap_cores(part):
        return lax.ppermute(part, "clu", [(d, d ^ 1) for d in range(devices)])

    barrier = lax.optimization_barrier

    shift = 19
    magic = -(-(1 << shift) // clusters)
    numbers = np.arange(devices * clusters)
    assert (numbers * magic >> shift == numbers // clusters).all() and far & far - 1 == 0
    list_shape = jax.ShapeDtypeStruct((1, blocks), jnp.int32)
    source_rows, target_rows = pl.pallas_call(
        functools.partial(rows_kernel, clusters=clusters, far=far, magic=magic, shift=shift),
        out_shape=[list_shape] * 2,
        in_specs=[VMEM] * 2,
        out_specs=[VMEM] * 2,
        compiler_params=params(1),
    )(block_source.reshape(1, blocks), block_target.reshape(1, blocks))
    source_rows, target_rows = source_rows.reshape(blocks), target_rows.reshape(blocks)

    tile_shape = (mains, rhs, LANES)
    out_shape = shape((leaves, rhs, width), BF)
    tile_out = shape(tile_shape, BF)
    part_shape = shape((far,) + tile_shape, BF)
    edge_shape = shape((1, rhs, width), BF)
    first_coeffs, inner, outer = pl.pallas_call(
        coeff_kernel,
        out_shape=[tile_out, edge_shape, edge_shape],
        in_specs=[SMEM, HBM, HBM, HBM],
        out_specs=[VMEM] * 3,
        scratch_shapes=[
            pltpu.VMEM(charges.shape, BF),
            pltpu.VMEM(basis.shape, BF),
            pltpu.VMEM(transfer.shape, BF),
            pltpu.SemaphoreType.DMA((3,)),
        ],
    )(ranks, charges, basis, transfer)

    order = ((x | y | z, x | y, y | z, z | x), (0, x, y, z))
    couple = pl.pallas_call(
        functools.partial(couple_kernel, order=order, unroll=64),
        out_shape=[shape((4, far) + tile_shape, BF)] * 4,
        in_specs=[SMEM, SMEM, VMEM] + [VMEM] * (cores * (1 + len(order[0]))),
        out_specs=[VMEM] * 4,
        scratch_shapes=[
            pltpu.VMEM((devices * clusters, rhs, LANES), BF),
            pltpu.VMEM((devices * clusters, rhs, LANES), F32),
        ],
        compiler_params=params(24 if devices <= 32 else 60),
        cost_estimate=pl.CostEstimate(
            flops=2 * blocks * rhs * rank_top * rank_top, bytes_accessed=10 << 20, transcendentals=0
        ),
    )

    near = pl.pallas_call(
        near_kernel,
        out_shape=shape((leaves, rhs, width), F32),
        in_specs=[VMEM, VMEM],
        out_specs=VMEM,
        compiler_params=params(16),
        cost_estimate=pl.CostEstimate(
            flops=2 * leaves * 3 * rhs * width * width, bytes_accessed=4 << 20, transcendentals=0
        ),
    )

    edge = pl.pallas_call(
        edge_kernel,
        out_shape=shape((2, rhs, width), F32),
        grid=(1,),
        in_specs=[
            VMEM,
            VMEM,
            pl.BlockSpec((1, 1, width, width), lambda i: (0, 0, 0, 0)),
            pl.BlockSpec((1, 1, width, width), lambda i: (leaves - 1, 2, 0, 0)),
        ],
        out_specs=VMEM,
        compiler_params=params(16),
    )

    def adder(kernel, inputs, outputs):
        return pl.pallas_call(
            kernel,
            out_shape=outputs,
            in_specs=[VMEM] * inputs,
            out_specs=[VMEM] * len(outputs),
            compiler_params=params(16),
        )

    own_shape = shape((far,) + tile_shape, F32)
    join = adder(join_kernel, far, [part_shape])
    join_near = adder(join_kernel, 4, [shape((4,) + part_shape.shape, BF)])
    relaid = pl.pallas_call(
        order_kernel,
        out_shape=shape((8, LANES), F32),
        in_specs=[pl.BlockSpec(memory_space=pl.ANY)] * 2,
        out_specs=VMEM,
    )
    first_join = pl.pallas_call(
        lambda _, *refs: join_kernel(*refs),
        out_shape=[part_shape],
        in_specs=[pl.BlockSpec(memory_space=pl.ANY)] + [VMEM] * far,
        out_specs=[VMEM],
        compiler_params=params(16),
    )
    far_add = adder(add_kernel, 2, [part_shape] * 4)
    middle_add = adder(functools.partial(middle_add_kernel, parts=3), 5, [own_shape] + [part_shape] * 3)
    last_add = adder(
        functools.partial(last_add_kernel, parts=4), 5, [shape(tile_shape, F32)] + [tile_out] * (far - 1)
    )

    def finish(with_coeffs):
        return pl.pallas_call(
            functools.partial(field_kernel, away=far - 1),
            out_shape=[out_shape, tile_out, edge_shape, edge_shape] if with_coeffs else [out_shape],
            in_specs=[SMEM] + [VMEM] * (4 + far),
            out_specs=[VMEM] * 4 if with_coeffs else [VMEM],
            compiler_params=params(16),
        )

    halo_pairs = [(d, d + cores) for d in range(1, devices - cores, cores)]
    halo_pairs += [(d, d - cores) for d in range(cores, devices, cores)]

    def apply_matrix(field_in, coeffs, inner, outer, coupling, with_coeffs):
        away = [swap_far(coeffs, s) for s in range(1, far)]
        (column,) = first_join(relaid(coupling, coeffs), coeffs, *away) if with_coeffs else join(coeffs, *away)
        got = {0: column, x: swap(column, x), y: swap(column, y), z: swap(column, z)}
        near_sum = near(field_in, near_field)
        got, near_sum = barrier((got, near_sum))
        corner = swap(got[x], y | z)
        (near_pieces,) = join_near(*[got[chip] for chip in order[1]])
        got |= {x | y: swap(got[x], y), y | z: swap(got[y], z), z | x: swap(got[z], x)}
        got[x | y | z] = corner
        far_pieces, other_near = barrier(([got[chip] for chip in order[0]], swap_cores(near_pieces)))
        other_far = [swap_cores(part) for part in far_pieces]
        totals = couple(source_rows, target_rows, coupling, near_pieces, *far_pieces, other_near, *other_far)
        keep_long, keep, send_long, send = totals
        corner, xy, yz, zx = far_add(keep_long, swap_cores(send_long))
        corner, xy, yz, zx, send = barrier((corner, xy, yz, zx, send))
        to_x, to_y, to_z, swapped = barrier((swap(xy, y), swap(yz, z), swap(zx, x), swap_cores(send)))
        own, to_x, to_y, to_z, inner, outer = barrier(
            (*middle_add(keep, swapped, to_x, to_y, to_z), inner, outer)
        )
        parts = [swap(to_x, x), swap(to_y, y), swap(to_z, z), swap(corner, x | y | z)]
        own, parts, inner, outer = barrier((own, parts, inner, lax.ppermute(outer, "clu", halo_pairs)))
        total, *away = last_add(own, *parts)
        edges = edge(swap_cores(inner), swap_cores(outer), near_field, near_field)
        terms, edges = barrier(([swap_far(part, s + 1) for s, part in enumerate(away)], edges))
        return finish(with_coeffs)(ranks, near_sum, edges, basis, transfer, total, *terms)

    first, *second_args = apply_matrix(charges, first_coeffs, inner, outer, coupling, True)
    (second,) = apply_matrix(first, *second_args, coupling, False)
    return (first, second)


def solution(mesh):
    in_specs = (
        P("clu", None, None),
        P("clu", None, None),
        P("clu", None, None),
        P("clu", None, None, None),
        P("clu", None, None),
        P("clu"),
        P("clu"),
        P("clu"),
    )
    out_specs = (P("clu", None, None), P("clu", None, None))
    return jax.shard_map(local, mesh=mesh, in_specs=in_specs, out_specs=out_specs, check_vma=False)
```

```python
import functools

import jax
import jax.numpy as jnp
import numpy as np
from jax import lax
from jax.experimental import pallas as pl
from jax.experimental.pallas import tpu as pltpu
from jax.sharding import PartitionSpec as P

LANES = 128
CORES, CHIPS = 2, 8
BF = jnp.bfloat16
F32 = jnp.float32
VMEM = pl.BlockSpec(memory_space=pltpu.VMEM)
SMEM = pl.BlockSpec(memory_space=pltpu.SMEM)
HBM = pl.BlockSpec(memory_space=pltpu.HBM)


def dot(a, b):
    return lax.dot_general(a, b, (((1,), (0,)), ((), ())), preferred_element_type=F32)


def dot_t(a, b):
    return lax.dot_general(a, b, (((1,), (1,)), ((), ())), preferred_element_type=F32)


def lanes(rows):
    return lax.broadcasted_iota(jnp.int32, (rows, LANES), 1)


def fourth(tiles, rank_top):
    third = LANES - rank_top
    lane = lanes(tiles[0].shape[0])
    moved = [pltpu.roll(tile, third * (k + 1), 1) for k, tile in enumerate(tiles)]
    return jnp.where(lane < third, moved[0], jnp.where(lane < 2 * third, moved[1], moved[2]))


def packed(mains, pad, rank_top):
    lane = lanes(pad.shape[0])
    third = LANES - rank_top
    return [
        jnp.where(lane < rank_top, main, pltpu.roll(pad, rank_top - third * k, 1)) for k, main in enumerate(mains)
    ]


def widen(value):
    return jnp.concatenate([value, jnp.zeros((value.shape[0], LANES - value.shape[1]), value.dtype)], axis=1)


def emit_coeffs(values, basis_ref, transfer_ref, ranks_ref, out_ref, ready=None):
    mains, rhs, _ = out_ref.shape
    leaves, rank_top, _ = basis_ref.shape
    lane = lax.broadcasted_iota(jnp.int32, (rhs, rank_top), 1)
    coeffs = []
    for i in range(leaves):
        value = dot_t(values[i], basis_ref[i])
        coeffs.append(jnp.where(lane < ranks_ref[i], value, 0.0).astype(BF))
    if ready is not None:
        ready()
    for q in range(leaves // 2):
        value = dot(coeffs[2 * q], transfer_ref[2 * q]) + dot(coeffs[2 * q + 1], transfer_ref[2 * q + 1])
        coeffs.append(jnp.where(lane < ranks_ref[leaves + q], value, 0.0).astype(BF))
    wide = [widen(value.astype(F32)) for value in coeffs]
    for q in range(mains // 3):
        for k, tile in enumerate(packed(wide[3 * q : 3 * q + 3], wide[mains + q], rank_top)):
            out_ref[3 * q + k] = tile.astype(BF)


def fetch(pairs, sems):
    copies = [pltpu.make_async_copy(src, dst, sems.at[n]) for n, (src, dst) in enumerate(pairs)]
    for copy in copies:
        copy.start()
    return copies


def emit_edges(v_ref, inner_ref, outer_ref):
    head, tail = v_ref[0], v_ref[v_ref.shape[0] - 1]
    even = lax.axis_index("clu") % CORES == 0
    inner_ref[0] = jnp.where(even, tail, head)
    outer_ref[0] = jnp.where(even, head, tail)


def coeff_kernel(
    ranks_ref, v_hbm, basis_hbm, transfer_hbm, out_ref, inner_ref, outer_ref, v_ref, basis_ref, transfer_ref, sems
):
    leaves = basis_ref.shape[0]
    copies = fetch([(v_hbm, v_ref), (basis_hbm, basis_ref), (transfer_hbm, transfer_ref)], sems)
    copies[0].wait()
    emit_edges(v_ref, inner_ref, outer_ref)
    copies[1].wait()
    values = [v_ref[i] for i in range(leaves)]
    emit_coeffs(values, basis_ref, transfer_ref, ranks_ref, out_ref, copies[2].wait)


def couple_kernel(source_ref, target_ref, coupling_ref, *refs, order, unroll):
    chips = sum(len(group) for group in order)
    in_refs, out_refs, (sources, total) = refs[: 2 * chips], refs[2 * chips : -2], refs[-2:]
    blocks, rank_top, _ = coupling_ref.shape
    far, mains, rhs, _ = in_refs[0].shape
    quads = mains // 3
    clusters = mains + quads

    def split(f, _):
        for n, packed_ref in enumerate(in_refs):
            row = (n * far + f) * clusters
            tiles = [packed_ref[f, c] for c in range(mains)]
            for c in range(mains):
                sources[row + c] = tiles[c]
            for q in range(quads):
                wide = [tile.astype(F32) for tile in tiles[3 * q : 3 * q + 3]]
                sources[row + mains + q] = fourth(wide, rank_top).astype(BF)
            for c in range(clusters):
                total[row + c] = jnp.zeros((rhs, LANES), F32)
        return 0

    lax.fori_loop(0, far, split, 0)

    def some(s, _):
        for u in range(unroll):
            j = s * unroll + u
            term = dot(sources[source_ref[j], :, :rank_top], coupling_ref[j])
            at = target_ref[j]
            total[at, :, :rank_top] = total[at, :, :rank_top] + term
        return 0

    lax.fori_loop(0, blocks // unroll, some, 0)

    def pack(f, _):
        for core in range(2):
            for g, group in enumerate(order):
                for place, chip in enumerate(group):
                    row = ((core * chips + chip) * far + f) * clusters
                    for q in range(quads):
                        mains_now = [total[row + 3 * q + k] for k in range(3)]
                        for k, tile in enumerate(packed(mains_now, total[row + mains + q], rank_top)):
                            out_refs[core * len(order) + g][place, f, 3 * q + k] = tile.astype(BF)
        return 0

    lax.fori_loop(0, far, pack, 0)


def order_kernel(_, __, out_ref):
    out_ref[...] = jnp.zeros_like(out_ref)


def near_kernel(v_ref, near_ref, out_ref):
    leaves = v_ref.shape[0]
    for i in range(leaves):
        total = dot(v_ref[i], near_ref[i, 1])
        if i > 0:
            total = total + dot(v_ref[i - 1], near_ref[i, 0])
        if i < leaves - 1:
            total = total + dot(v_ref[i + 1], near_ref[i, 2])
        out_ref[i] = total


def edge_kernel(inner_ref, outer_ref, first_ref, last_ref, out_ref):
    inner, outer = inner_ref[0], outer_ref[0]
    even = lax.axis_index("clu") % CORES == 0
    out_ref[0] = dot(jnp.where(even, outer, inner), first_ref[0, 0])
    out_ref[1] = dot(jnp.where(even, inner, outer), last_ref[0, 0])


def add_kernel(keep_ref, swap_ref, *out_refs):
    for n, out_ref in enumerate(out_refs):
        out_ref[...] = (keep_ref[n].astype(F32) + swap_ref[n].astype(F32)).astype(out_ref.dtype)


def middle_add_kernel(keep_ref, swap_ref, *refs, parts):
    part_refs, (own_out, *out_refs) = refs[:parts], refs[parts:]
    own_out[...] = keep_ref[0].astype(F32) + swap_ref[0].astype(F32)
    for n, out_ref in enumerate(out_refs):
        total = keep_ref[n + 1].astype(F32) + swap_ref[n + 1].astype(F32)
        out_ref[...] = (total + part_refs[n][...].astype(F32)).astype(BF)


def rows_kernel(source_ref, target_ref, source_out, target_out, *, clusters, far, magic, shift):
    me = lax.axis_index("clu")
    for sign, in_ref, out_ref in ((-1, source_ref, source_out), (1, target_ref, target_out)):
        cluster = in_ref[...]
        device = cluster * magic >> shift
        chip = ((device ^ me) >> 1) & (CHIPS - 1)
        chip = jnp.where((device & 1) == 0, chip, chip >> 1 | (chip & 1) << 2)
        away = (sign * ((device >> 4) - (me >> 4))) & (far - 1)
        core = (device ^ me) & 1
        out_ref[...] = ((core * CHIPS + chip) * far + away) * clusters + cluster - device * clusters


def join_kernel(*refs):
    for n, part_ref in enumerate(refs[:-1]):
        refs[-1][n] = part_ref[...]


def last_add_kernel(own_ref, *refs, parts):
    part_refs, (keep_out, *away_refs) = refs[:parts], refs[parts:]
    for f in range(own_ref.shape[0]):
        total = own_ref[f]
        for part_ref in part_refs:
            total = total + part_ref[f].astype(F32)
        if f == 0:
            keep_out[...] = total
        else:
            away_refs[f - 1][...] = total.astype(BF)


def field_kernel(ranks_ref, near_ref, edge_ref, basis_ref, transfer_ref, keep_ref, *rest, away):
    term_refs, out_ref, next_refs = rest[:away], rest[away], rest[away + 1 :]
    leaves, rank_top, _ = basis_ref.shape
    mains, rhs, _ = keep_ref.shape
    tiles = []
    for t in range(mains):
        tile = keep_ref[t]
        for term_ref in term_refs:
            tile = tile + term_ref[t].astype(F32)
        tiles.append(tile)
    sums = tiles + [fourth(tiles[3 * q : 3 * q + 3], rank_top) for q in range(mains // 3)]
    lane = lax.broadcasted_iota(jnp.int32, (rhs, rank_top), 1)
    fields = [
        jnp.where(lane < ranks_ref[c], total[:, :rank_top], 0.0).astype(BF) for c, total in enumerate(sums)
    ]
    downs = [fields[i].astype(F32) + dot_t(fields[leaves + i // 2], transfer_ref[i]) for i in range(leaves)]
    leaf_totals = [jnp.where(lane < ranks_ref[i], down, 0.0).astype(BF) for i, down in enumerate(downs)]
    results = [near_ref[i] + dot(leaf_total, basis_ref[i]) for i, leaf_total in enumerate(leaf_totals)]
    results[0] = results[0] + edge_ref[0]
    results[-1] = results[-1] + edge_ref[1]
    results = [result.astype(BF) for result in results]
    for i, result in enumerate(results):
        out_ref[i] = result
    if next_refs:
        coeff_ref, inner_ref, outer_ref = next_refs
        emit_edges(out_ref, inner_ref, outer_ref)
        emit_coeffs(results, basis_ref, transfer_ref, ranks_ref, coeff_ref)


def params(mebibytes):
    return pltpu.CompilerParams(vmem_limit_bytes=mebibytes << 20)


def local(charges, basis, transfer, near_field, coupling, ranks, block_source, block_target):
    leaves, rank_top, width = basis.shape
    rhs = charges.shape[1]
    clusters = ranks.shape[0]
    blocks = coupling.shape[0]
    devices = lax.axis_size("clu")
    mains = clusters * 3 // 4
    shape = jax.ShapeDtypeStruct

    cores, chips = CORES, CHIPS
    cube = cores * chips
    far = devices // cube
    x, y, z = 1, 2, 4

    def swap_far(part, shift):
        return lax.ppermute(part, "clu", [(d, (d + shift * cube) % devices) for d in range(devices)])

    def swap(part, direction):
        turned = direction << 1 & 7 | direction >> 2
        return lax.ppermute(
            part, "clu", [(d, d ^ (turned if d % cores else direction) * cores) for d in range(devices)]
        )

    def swap_cores(part):
        return lax.ppermute(part, "clu", [(d, d ^ 1) for d in range(devices)])

    barrier = lax.optimization_barrier

    shift = 19
    magic = -(-(1 << shift) // clusters)
    numbers = np.arange(devices * clusters)
    assert (numbers * magic >> shift == numbers // clusters).all() and far & far - 1 == 0
    list_shape = jax.ShapeDtypeStruct((1, blocks), jnp.int32)
    source_rows, target_rows = pl.pallas_call(
        functools.partial(rows_kernel, clusters=clusters, far=far, magic=magic, shift=shift),
        out_shape=[list_shape] * 2,
        in_specs=[VMEM] * 2,
        out_specs=[VMEM] * 2,
        compiler_params=params(1),
    )(block_source.reshape(1, blocks), block_target.reshape(1, blocks))
    source_rows, target_rows = source_rows.reshape(blocks), target_rows.reshape(blocks)

    tile_shape = (mains, rhs, LANES)
    out_shape = shape((leaves, rhs, width), BF)
    tile_out = shape(tile_shape, BF)
    part_shape = shape((far,) + tile_shape, BF)
    edge_shape = shape((1, rhs, width), BF)
    first_coeffs, inner, outer = pl.pallas_call(
        coeff_kernel,
        out_shape=[tile_out, edge_shape, edge_shape],
        in_specs=[SMEM, HBM, HBM, HBM],
        out_specs=[VMEM] * 3,
        scratch_shapes=[
            pltpu.VMEM(charges.shape, BF),
            pltpu.VMEM(basis.shape, BF),
            pltpu.VMEM(transfer.shape, BF),
            pltpu.SemaphoreType.DMA((3,)),
        ],
    )(ranks, charges, basis, transfer)

    order = ((x | y | z, x | y, y | z, z | x), (0, x, y, z))
    couple = pl.pallas_call(
        functools.partial(couple_kernel, order=order, unroll=64),
        out_shape=[shape((4, far) + tile_shape, BF)] * 4,
        in_specs=[SMEM, SMEM, VMEM] + [VMEM] * (cores * chips),
        out_specs=[VMEM] * 4,
        scratch_shapes=[
            pltpu.VMEM((devices * clusters, rhs, LANES), BF),
            pltpu.VMEM((devices * clusters, rhs, LANES), F32),
        ],
        compiler_params=params(24 if devices <= 32 else 60),
        cost_estimate=pl.CostEstimate(
            flops=2 * blocks * rhs * rank_top * rank_top, bytes_accessed=10 << 20, transcendentals=0
        ),
    )

    near = pl.pallas_call(
        near_kernel,
        out_shape=shape((leaves, rhs, width), F32),
        in_specs=[VMEM, VMEM],
        out_specs=VMEM,
        compiler_params=params(16),
        cost_estimate=pl.CostEstimate(
            flops=2 * leaves * 3 * rhs * width * width, bytes_accessed=4 << 20, transcendentals=0
        ),
    )

    edge = pl.pallas_call(
        edge_kernel,
        out_shape=shape((2, rhs, width), F32),
        grid=(1,),
        in_specs=[
            VMEM,
            VMEM,
            pl.BlockSpec((1, 1, width, width), lambda i: (0, 0, 0, 0)),
            pl.BlockSpec((1, 1, width, width), lambda i: (leaves - 1, 2, 0, 0)),
        ],
        out_specs=VMEM,
        compiler_params=params(16),
    )

    def adder(kernel, inputs, outputs):
        return pl.pallas_call(
            kernel,
            out_shape=outputs,
            in_specs=[VMEM] * inputs,
            out_specs=[VMEM] * len(outputs),
            compiler_params=params(16),
        )

    own_shape = shape((far,) + tile_shape, F32)
    join = adder(join_kernel, far, [part_shape])
    relaid = pl.pallas_call(
        order_kernel,
        out_shape=shape((8, LANES), F32),
        in_specs=[pl.BlockSpec(memory_space=pl.ANY)] * 2,
        out_specs=VMEM,
    )
    first_join = pl.pallas_call(
        lambda _, *refs: join_kernel(*refs),
        out_shape=[part_shape],
        in_specs=[pl.BlockSpec(memory_space=pl.ANY)] + [VMEM] * far,
        out_specs=[VMEM],
        compiler_params=params(16),
    )
    far_add = adder(add_kernel, 2, [part_shape] * 4)
    middle_add = adder(functools.partial(middle_add_kernel, parts=3), 5, [own_shape] + [part_shape] * 3)
    last_add = adder(
        functools.partial(last_add_kernel, parts=4), 5, [shape(tile_shape, F32)] + [tile_out] * (far - 1)
    )

    def finish(with_coeffs):
        return pl.pallas_call(
            functools.partial(field_kernel, away=far - 1),
            out_shape=[out_shape, tile_out, edge_shape, edge_shape] if with_coeffs else [out_shape],
            in_specs=[SMEM] + [VMEM] * (4 + far),
            out_specs=[VMEM] * 4 if with_coeffs else [VMEM],
            compiler_params=params(16),
        )

    halo_pairs = [(d, d + cores) for d in range(1, devices - cores, cores)]
    halo_pairs += [(d, d - cores) for d in range(cores, devices, cores)]

    def apply_matrix(field_in, coeffs, inner, outer, coupling, with_coeffs):
        away = [swap_far(coeffs, s) for s in range(1, far)]
        (column,) = first_join(relaid(coupling, coeffs), coeffs, *away) if with_coeffs else join(coeffs, *away)
        got = {0: column, x: swap(column, x), y: swap(column, y), z: swap(column, z)}
        near_sum = near(field_in, near_field)
        got, near_sum = barrier((got, near_sum))
        corner = swap(column, x | y | z)
        other = {chip: swap_cores(part) for chip, part in got.items()}
        got |= {x | y: swap(got[x], y), y | z: swap(got[y], z), z | x: swap(got[z], x)}
        got, corner, outer = barrier((got, corner, lax.ppermute(outer, "clu", halo_pairs)))
        got[x | y | z] = corner
        other |= {chip: swap_cores(got[chip]) for chip in order[0]}
        totals = couple(
            source_rows,
            target_rows,
            coupling,
            *[got[chip] for chip in range(chips)],
            *[other[chip] for chip in range(chips)],
        )
        keep_long, keep, send_long, send = totals
        corner, xy, yz, zx = far_add(keep_long, swap_cores(send_long))
        corner, xy, yz, zx, send = barrier((corner, xy, yz, zx, send))
        to_x, to_y, to_z, swapped = barrier((swap(xy, y), swap(yz, z), swap(zx, x), swap_cores(send)))
        own, to_x, to_y, to_z, inner, outer = barrier(
            (*middle_add(keep, swapped, to_x, to_y, to_z), inner, outer)
        )
        edges = edge(swap_cores(inner), swap_cores(outer), near_field, near_field)
        parts = [swap(to_x, x), swap(to_y, y), swap(to_z, z), swap(corner, x | y | z)]
        own, parts, edges = barrier((own, parts, edges))
        total, *away = last_add(own, *parts)
        terms = [swap_far(part, s + 1) for s, part in enumerate(away)]
        return finish(with_coeffs)(ranks, near_sum, edges, basis, transfer, total, *terms)

    first, *second_args = apply_matrix(charges, first_coeffs, inner, outer, coupling, True)
    (second,) = apply_matrix(first, *second_args, coupling, False)
    return (first, second)


def solution(mesh):
    in_specs = (
        P("clu", None, None),
        P("clu", None, None),
        P("clu", None, None),
        P("clu", None, None, None),
        P("clu", None, None),
        P("clu"),
        P("clu"),
        P("clu"),
    )
    out_specs = (P("clu", None, None), P("clu", None, None))
    return jax.shard_map(local, mesh=mesh, in_specs=in_specs, out_specs=out_specs, check_vma=False)
```

```python
import functools

import jax
import jax.numpy as jnp
import numpy as np
from jax import lax
from jax.experimental import pallas as pl
from jax.experimental.pallas import tpu as pltpu
from jax.sharding import PartitionSpec as P

LANES = 128
CORES, CHIPS = 2, 8
BF = jnp.bfloat16
F32 = jnp.float32
VMEM = pl.BlockSpec(memory_space=pltpu.VMEM)
SMEM = pl.BlockSpec(memory_space=pltpu.SMEM)
HBM = pl.BlockSpec(memory_space=pltpu.HBM)


def dot(a, b):
    return lax.dot_general(a, b, (((1,), (0,)), ((), ())), preferred_element_type=F32)


def dot_t(a, b):
    return lax.dot_general(a, b, (((1,), (1,)), ((), ())), preferred_element_type=F32)


def lanes(rows):
    return lax.broadcasted_iota(jnp.int32, (rows, LANES), 1)


def fourth(tiles, rank_top):
    third = LANES - rank_top
    lane = lanes(tiles[0].shape[0])
    moved = [pltpu.roll(tile, third * (k + 1), 1) for k, tile in enumerate(tiles)]
    return jnp.where(lane < third, moved[0], jnp.where(lane < 2 * third, moved[1], moved[2]))


def packed(mains, pad, rank_top):
    lane = lanes(pad.shape[0])
    third = LANES - rank_top
    return [
        jnp.where(lane < rank_top, main, pltpu.roll(pad, rank_top - third * k, 1)) for k, main in enumerate(mains)
    ]


def widen(value):
    return jnp.concatenate([value, jnp.zeros((value.shape[0], LANES - value.shape[1]), value.dtype)], axis=1)


def emit_coeffs(values, basis_ref, transfer_ref, ranks_ref, out_ref, ready=None):
    mains, rhs, _ = out_ref.shape
    leaves, rank_top, _ = basis_ref.shape
    lane = lax.broadcasted_iota(jnp.int32, (rhs, rank_top), 1)
    coeffs = []
    for i in range(leaves):
        value = dot_t(values[i], basis_ref[i])
        coeffs.append(jnp.where(lane < ranks_ref[i], value, 0.0).astype(BF))
    if ready is not None:
        ready()
    for q in range(leaves // 2):
        value = dot(coeffs[2 * q], transfer_ref[2 * q]) + dot(coeffs[2 * q + 1], transfer_ref[2 * q + 1])
        coeffs.append(jnp.where(lane < ranks_ref[leaves + q], value, 0.0).astype(BF))
    wide = [widen(value.astype(F32)) for value in coeffs]
    for q in range(mains // 3):
        for k, tile in enumerate(packed(wide[3 * q : 3 * q + 3], wide[mains + q], rank_top)):
            out_ref[3 * q + k] = tile.astype(BF)


def fetch(pairs, sems):
    copies = [pltpu.make_async_copy(src, dst, sems.at[n]) for n, (src, dst) in enumerate(pairs)]
    for copy in copies:
        copy.start()
    return copies


def emit_edges(v_ref, inner_ref, outer_ref):
    head, tail = v_ref[0], v_ref[v_ref.shape[0] - 1]
    even = lax.axis_index("clu") % CORES == 0
    inner_ref[0] = jnp.where(even, tail, head)
    outer_ref[0] = jnp.where(even, head, tail)


def coeff_kernel(
    ranks_ref, v_hbm, basis_hbm, transfer_hbm, out_ref, inner_ref, outer_ref, v_ref, basis_ref, transfer_ref, sems
):
    leaves = basis_ref.shape[0]
    copies = fetch([(v_hbm, v_ref), (basis_hbm, basis_ref), (transfer_hbm, transfer_ref)], sems)
    copies[0].wait()
    emit_edges(v_ref, inner_ref, outer_ref)
    copies[1].wait()
    values = [v_ref[i] for i in range(leaves)]
    emit_coeffs(values, basis_ref, transfer_ref, ranks_ref, out_ref, copies[2].wait)


def couple_kernel(source_ref, target_ref, coupling_ref, *refs, order, unroll):
    chips = sum(len(group) for group in order)
    in_refs, out_refs, (sources, total) = refs[: 2 * chips], refs[2 * chips : -2], refs[-2:]
    blocks, rank_top, _ = coupling_ref.shape
    far, mains, rhs, _ = in_refs[0].shape
    quads = mains // 3
    clusters = mains + quads

    def split(f, _):
        for n, packed_ref in enumerate(in_refs):
            row = (n * far + f) * clusters
            tiles = [packed_ref[f, c] for c in range(mains)]
            for c in range(mains):
                sources[row + c] = tiles[c]
            for q in range(quads):
                wide = [tile.astype(F32) for tile in tiles[3 * q : 3 * q + 3]]
                sources[row + mains + q] = fourth(wide, rank_top).astype(BF)
            for c in range(clusters):
                total[row + c] = jnp.zeros((rhs, LANES), F32)
        return 0

    lax.fori_loop(0, far, split, 0)

    def some(s, _):
        for u in range(unroll):
            j = s * unroll + u
            term = dot(sources[source_ref[j], :, :rank_top], coupling_ref[j])
            at = target_ref[j]
            total[at, :, :rank_top] = total[at, :, :rank_top] + term
        return 0

    lax.fori_loop(0, blocks // unroll, some, 0)

    def pack(f, _):
        for core in range(2):
            for g, group in enumerate(order):
                for place, chip in enumerate(group):
                    row = ((core * chips + chip) * far + f) * clusters
                    for q in range(quads):
                        mains_now = [total[row + 3 * q + k] for k in range(3)]
                        for k, tile in enumerate(packed(mains_now, total[row + mains + q], rank_top)):
                            out_refs[core * len(order) + g][place, f, 3 * q + k] = tile.astype(BF)
        return 0

    lax.fori_loop(0, far, pack, 0)


def order_kernel(_, __, out_ref):
    out_ref[...] = jnp.zeros_like(out_ref)


def near_kernel(v_ref, near_ref, out_ref):
    leaves = v_ref.shape[0]
    for i in range(leaves):
        total = dot(v_ref[i], near_ref[i, 1])
        if i > 0:
            total = total + dot(v_ref[i - 1], near_ref[i, 0])
        if i < leaves - 1:
            total = total + dot(v_ref[i + 1], near_ref[i, 2])
        out_ref[i] = total


def edge_kernel(inner_ref, outer_ref, first_ref, last_ref, out_ref):
    inner, outer = inner_ref[0], outer_ref[0]
    even = lax.axis_index("clu") % CORES == 0
    out_ref[0] = dot(jnp.where(even, outer, inner), first_ref[0, 0])
    out_ref[1] = dot(jnp.where(even, inner, outer), last_ref[0, 0])


def add_kernel(keep_ref, swap_ref, *out_refs):
    for n, out_ref in enumerate(out_refs):
        out_ref[...] = (keep_ref[n].astype(F32) + swap_ref[n].astype(F32)).astype(out_ref.dtype)


def middle_add_kernel(keep_ref, swap_ref, *refs, parts):
    part_refs, (own_out, *out_refs) = refs[:parts], refs[parts:]
    own_out[...] = keep_ref[0].astype(F32) + swap_ref[0].astype(F32)
    for n, out_ref in enumerate(out_refs):
        total = keep_ref[n + 1].astype(F32) + swap_ref[n + 1].astype(F32)
        for part_ref in part_refs[n :: len(out_refs)]:
            total = total + part_ref[...].astype(F32)
        out_ref[...] = total.astype(BF)


def rows_kernel(source_ref, target_ref, source_out, target_out, *, clusters, far, magic, shift):
    me = lax.axis_index("clu")
    for sign, in_ref, out_ref in ((-1, source_ref, source_out), (1, target_ref, target_out)):
        cluster = in_ref[...]
        device = cluster * magic >> shift
        chip = ((device ^ me) >> 1) & (CHIPS - 1)
        chip = jnp.where((device & 1) == 0, chip, chip >> 1 | (chip & 1) << 2)
        away = (sign * ((device >> 4) - (me >> 4))) & (far - 1)
        core = (device ^ me) & 1
        out_ref[...] = ((core * CHIPS + chip) * far + away) * clusters + cluster - device * clusters


def join_kernel(*refs):
    for n, part_ref in enumerate(refs[:-1]):
        refs[-1][n] = part_ref[...]


def last_add_kernel(own_ref, *refs, parts):
    part_refs, (keep_out, *away_refs) = refs[:parts], refs[parts:]
    for f in range(own_ref.shape[0]):
        total = own_ref[f]
        for part_ref in part_refs:
            total = total + part_ref[f].astype(F32)
        if f == 0:
            keep_out[...] = total
        else:
            away_refs[f - 1][...] = total.astype(BF)


def field_kernel(ranks_ref, near_ref, edge_ref, basis_ref, transfer_ref, keep_ref, *rest, away):
    term_refs, out_ref, next_refs = rest[:away], rest[away], rest[away + 1 :]
    leaves, rank_top, _ = basis_ref.shape
    mains, rhs, _ = keep_ref.shape
    tiles = []
    for t in range(mains):
        tile = keep_ref[t]
        for term_ref in term_refs:
            tile = tile + term_ref[t].astype(F32)
        tiles.append(tile)
    sums = tiles + [fourth(tiles[3 * q : 3 * q + 3], rank_top) for q in range(mains // 3)]
    lane = lax.broadcasted_iota(jnp.int32, (rhs, rank_top), 1)
    fields = [
        jnp.where(lane < ranks_ref[c], total[:, :rank_top], 0.0).astype(BF) for c, total in enumerate(sums)
    ]
    downs = [fields[i].astype(F32) + dot_t(fields[leaves + i // 2], transfer_ref[i]) for i in range(leaves)]
    leaf_totals = [jnp.where(lane < ranks_ref[i], down, 0.0).astype(BF) for i, down in enumerate(downs)]
    results = [near_ref[i] + dot(leaf_total, basis_ref[i]) for i, leaf_total in enumerate(leaf_totals)]
    results[0] = results[0] + edge_ref[0]
    results[-1] = results[-1] + edge_ref[1]
    results = [result.astype(BF) for result in results]
    for i, result in enumerate(results):
        out_ref[i] = result
    if next_refs:
        coeff_ref, inner_ref, outer_ref = next_refs
        emit_edges(out_ref, inner_ref, outer_ref)
        emit_coeffs(results, basis_ref, transfer_ref, ranks_ref, coeff_ref)


def params(mebibytes):
    return pltpu.CompilerParams(vmem_limit_bytes=mebibytes << 20)


def local(charges, basis, transfer, near_field, coupling, ranks, block_source, block_target):
    leaves, rank_top, width = basis.shape
    rhs = charges.shape[1]
    clusters = ranks.shape[0]
    blocks = coupling.shape[0]
    devices = lax.axis_size("clu")
    mains = clusters * 3 // 4
    shape = jax.ShapeDtypeStruct

    cores, chips = CORES, CHIPS
    cube = cores * chips
    far = devices // cube
    x, y, z = 1, 2, 4

    def swap_far(part, shift):
        return lax.ppermute(part, "clu", [(d, (d + shift * cube) % devices) for d in range(devices)])

    def swap(part, direction):
        turned = direction << 1 & 7 | direction >> 2
        return lax.ppermute(
            part, "clu", [(d, d ^ (turned if d % cores else direction) * cores) for d in range(devices)]
        )

    def swap_cores(part):
        return lax.ppermute(part, "clu", [(d, d ^ 1) for d in range(devices)])

    barrier = lax.optimization_barrier

    shift = 19
    magic = -(-(1 << shift) // clusters)
    numbers = np.arange(devices * clusters)
    assert (numbers * magic >> shift == numbers // clusters).all() and far & far - 1 == 0
    list_shape = jax.ShapeDtypeStruct((1, blocks), jnp.int32)
    source_rows, target_rows = pl.pallas_call(
        functools.partial(rows_kernel, clusters=clusters, far=far, magic=magic, shift=shift),
        out_shape=[list_shape] * 2,
        in_specs=[VMEM] * 2,
        out_specs=[VMEM] * 2,
        compiler_params=params(1),
    )(block_source.reshape(1, blocks), block_target.reshape(1, blocks))
    source_rows, target_rows = source_rows.reshape(blocks), target_rows.reshape(blocks)

    tile_shape = (mains, rhs, LANES)
    out_shape = shape((leaves, rhs, width), BF)
    tile_out = shape(tile_shape, BF)
    part_shape = shape((far,) + tile_shape, BF)
    edge_shape = shape((1, rhs, width), BF)
    first_coeffs, inner, outer = pl.pallas_call(
        coeff_kernel,
        out_shape=[tile_out, edge_shape, edge_shape],
        in_specs=[SMEM, HBM, HBM, HBM],
        out_specs=[VMEM] * 3,
        scratch_shapes=[
            pltpu.VMEM(charges.shape, BF),
            pltpu.VMEM(basis.shape, BF),
            pltpu.VMEM(transfer.shape, BF),
            pltpu.SemaphoreType.DMA((3,)),
        ],
    )(ranks, charges, basis, transfer)

    order = ((x | y | z, x | y, y | z, z | x), (0, x, y, z))
    couple = pl.pallas_call(
        functools.partial(couple_kernel, order=order, unroll=64),
        out_shape=[shape((4, far) + tile_shape, BF)] * 4,
        in_specs=[SMEM, SMEM, VMEM] + [VMEM] * (cores * chips),
        out_specs=[VMEM] * 4,
        scratch_shapes=[
            pltpu.VMEM((devices * clusters, rhs, LANES), BF),
            pltpu.VMEM((devices * clusters, rhs, LANES), F32),
        ],
        compiler_params=params(24 if devices <= 32 else 60),
        cost_estimate=pl.CostEstimate(
            flops=2 * blocks * rhs * rank_top * rank_top, bytes_accessed=10 << 20, transcendentals=0
        ),
    )

    near = pl.pallas_call(
        near_kernel,
        out_shape=shape((leaves, rhs, width), F32),
        in_specs=[VMEM, VMEM],
        out_specs=VMEM,
        compiler_params=params(16),
        cost_estimate=pl.CostEstimate(
            flops=2 * leaves * 3 * rhs * width * width, bytes_accessed=4 << 20, transcendentals=0
        ),
    )

    edge = pl.pallas_call(
        edge_kernel,
        out_shape=shape((2, rhs, width), F32),
        grid=(1,),
        in_specs=[
            VMEM,
            VMEM,
            pl.BlockSpec((1, 1, width, width), lambda i: (0, 0, 0, 0)),
            pl.BlockSpec((1, 1, width, width), lambda i: (leaves - 1, 2, 0, 0)),
        ],
        out_specs=VMEM,
        compiler_params=params(16),
    )

    def adder(kernel, inputs, outputs):
        return pl.pallas_call(
            kernel,
            out_shape=outputs,
            in_specs=[VMEM] * inputs,
            out_specs=[VMEM] * len(outputs),
            compiler_params=params(16),
        )

    own_shape = shape((far,) + tile_shape, F32)
    join = adder(join_kernel, far, [part_shape])
    relaid = pl.pallas_call(
        order_kernel,
        out_shape=shape((8, LANES), F32),
        in_specs=[pl.BlockSpec(memory_space=pl.ANY)] * 2,
        out_specs=VMEM,
    )
    first_join = pl.pallas_call(
        lambda _, *refs: join_kernel(*refs),
        out_shape=[part_shape],
        in_specs=[pl.BlockSpec(memory_space=pl.ANY)] + [VMEM] * far,
        out_specs=[VMEM],
        compiler_params=params(16),
    )
    far_add = adder(add_kernel, 2, [part_shape] * 4)
    middle_add = adder(functools.partial(middle_add_kernel, parts=4), 6, [own_shape] + [part_shape] * 3)
    last_add = adder(
        functools.partial(last_add_kernel, parts=3), 4, [shape(tile_shape, F32)] + [tile_out] * (far - 1)
    )

    def finish(with_coeffs):
        return pl.pallas_call(
            functools.partial(field_kernel, away=far - 1),
            out_shape=[out_shape, tile_out, edge_shape, edge_shape] if with_coeffs else [out_shape],
            in_specs=[SMEM] + [VMEM] * (4 + far),
            out_specs=[VMEM] * 4 if with_coeffs else [VMEM],
            compiler_params=params(16),
        )

    halo_pairs = [(d, d + cores) for d in range(1, devices - cores, cores)]
    halo_pairs += [(d, d - cores) for d in range(cores, devices, cores)]

    def apply_matrix(field_in, coeffs, inner, outer, coupling, with_coeffs):
        away = [swap_far(coeffs, s) for s in range(1, far)]
        (column,) = first_join(relaid(coupling, coeffs), coeffs, *away) if with_coeffs else join(coeffs, *away)
        got = {0: column, x: swap(column, x), y: swap(column, y), z: swap(column, z)}
        near_sum = near(field_in, near_field)
        got, near_sum = barrier((got, near_sum))
        corner = swap(column, x | y | z)
        other = {chip: swap_cores(part) for chip, part in got.items()}
        got |= {x | y: swap(got[x], y), y | z: swap(got[y], z), z | x: swap(got[z], x)}
        got, corner, outer = barrier((got, corner, lax.ppermute(outer, "clu", halo_pairs)))
        got[x | y | z] = corner
        other |= {chip: swap_cores(got[chip]) for chip in order[0]}
        totals = couple(
            source_rows,
            target_rows,
            coupling,
            *[got[chip] for chip in range(chips)],
            *[other[chip] for chip in range(chips)],
        )
        keep_long, keep, send_long, send = totals
        corner, xy, yz, zx = far_add(keep_long, swap_cores(send_long))
        corner, xy, yz, zx, send = barrier((corner, xy, yz, zx, send))
        to_x, to_y, to_z, corner, swapped = barrier(
            (swap(xy, y), swap(yz, z), swap(zx, x), swap(corner, y | z), swap_cores(send))
        )
        own, to_x, to_y, to_z, inner, outer = barrier(
            (*middle_add(keep, swapped, to_x, to_y, to_z, corner), inner, outer)
        )
        edges = edge(swap_cores(inner), swap_cores(outer), near_field, near_field)
        own, to_x, to_y, to_z, edges = barrier((own, swap(to_x, x), swap(to_y, y), swap(to_z, z), edges))
        total, *away = last_add(own, to_x, to_y, to_z)
        terms = [swap_far(part, s + 1) for s, part in enumerate(away)]
        return finish(with_coeffs)(ranks, near_sum, edges, basis, transfer, total, *terms)

    first, *second_args = apply_matrix(charges, first_coeffs, inner, outer, coupling, True)
    (second,) = apply_matrix(first, *second_args, coupling, False)
    return (first, second)


def solution(mesh):
    in_specs = (
        P("clu", None, None),
        P("clu", None, None),
        P("clu", None, None),
        P("clu", None, None, None),
        P("clu", None, None),
        P("clu"),
        P("clu"),
        P("clu"),
    )
    out_specs = (P("clu", None, None), P("clu", None, None))
    return jax.shard_map(local, mesh=mesh, in_specs=in_specs, out_specs=out_specs, check_vma=False)
```

```python
import functools

import jax
import jax.numpy as jnp
import numpy as np
from jax import lax
from jax.experimental import pallas as pl
from jax.experimental.pallas import tpu as pltpu
from jax.sharding import PartitionSpec as P

LANES = 128
CORES, CHIPS = 2, 8
BF = jnp.bfloat16
F32 = jnp.float32
VMEM = pl.BlockSpec(memory_space=pltpu.VMEM)
SMEM = pl.BlockSpec(memory_space=pltpu.SMEM)
HBM = pl.BlockSpec(memory_space=pltpu.HBM)


def dot(a, b):
    return lax.dot_general(a, b, (((1,), (0,)), ((), ())), preferred_element_type=F32)


def dot_t(a, b):
    return lax.dot_general(a, b, (((1,), (1,)), ((), ())), preferred_element_type=F32)


def lanes(rows):
    return lax.broadcasted_iota(jnp.int32, (rows, LANES), 1)


def fourth(tiles, rank_top):
    third = LANES - rank_top
    lane = lanes(tiles[0].shape[0])
    moved = [pltpu.roll(tile, third * (k + 1), 1) for k, tile in enumerate(tiles)]
    return jnp.where(lane < third, moved[0], jnp.where(lane < 2 * third, moved[1], moved[2]))


def packed(mains, pad, rank_top):
    lane = lanes(pad.shape[0])
    third = LANES - rank_top
    return [
        jnp.where(lane < rank_top, main, pltpu.roll(pad, rank_top - third * k, 1)) for k, main in enumerate(mains)
    ]


def widen(value):
    return jnp.concatenate([value, jnp.zeros((value.shape[0], LANES - value.shape[1]), value.dtype)], axis=1)


def emit_coeffs(values, basis_ref, transfer_ref, ranks_ref, out_ref, ready=None):
    mains, rhs, _ = out_ref.shape
    leaves, rank_top, _ = basis_ref.shape
    lane = lax.broadcasted_iota(jnp.int32, (rhs, rank_top), 1)
    coeffs = []
    for i in range(leaves):
        value = dot_t(values[i], basis_ref[i])
        coeffs.append(jnp.where(lane < ranks_ref[i], value, 0.0).astype(BF))
    if ready is not None:
        ready()
    for q in range(leaves // 2):
        value = dot(coeffs[2 * q], transfer_ref[2 * q]) + dot(coeffs[2 * q + 1], transfer_ref[2 * q + 1])
        coeffs.append(jnp.where(lane < ranks_ref[leaves + q], value, 0.0).astype(BF))
    wide = [widen(value.astype(F32)) for value in coeffs]
    for q in range(mains // 3):
        for k, tile in enumerate(packed(wide[3 * q : 3 * q + 3], wide[mains + q], rank_top)):
            out_ref[3 * q + k] = tile.astype(BF)


def fetch(pairs, sems):
    copies = [pltpu.make_async_copy(src, dst, sems.at[n]) for n, (src, dst) in enumerate(pairs)]
    for copy in copies:
        copy.start()
    return copies


def emit_edges(v_ref, inner_ref, outer_ref):
    head, tail = v_ref[0], v_ref[v_ref.shape[0] - 1]
    even = lax.axis_index("clu") % CORES == 0
    inner_ref[0] = jnp.where(even, tail, head)
    outer_ref[0] = jnp.where(even, head, tail)


def coeff_kernel(
    ranks_ref, v_hbm, basis_hbm, transfer_hbm, out_ref, inner_ref, outer_ref, v_ref, basis_ref, transfer_ref, sems
):
    leaves = basis_ref.shape[0]
    copies = fetch([(v_hbm, v_ref), (basis_hbm, basis_ref), (transfer_hbm, transfer_ref)], sems)
    copies[0].wait()
    emit_edges(v_ref, inner_ref, outer_ref)
    copies[1].wait()
    values = [v_ref[i] for i in range(leaves)]
    emit_coeffs(values, basis_ref, transfer_ref, ranks_ref, out_ref, copies[2].wait)


def couple_kernel(source_ref, target_ref, coupling_ref, *refs, order, unroll):
    chips = sum(len(group) for group in order)
    in_refs, out_refs, (sources, total) = refs[: 2 * chips], refs[2 * chips : -2], refs[-2:]
    blocks, rank_top, _ = coupling_ref.shape
    far, mains, rhs, _ = in_refs[0].shape
    quads = mains // 3
    clusters = mains + quads

    def split(f, _):
        for n, packed_ref in enumerate(in_refs):
            row = (n * far + f) * clusters
            tiles = [packed_ref[f, c] for c in range(mains)]
            for c in range(mains):
                sources[row + c] = tiles[c]
            for q in range(quads):
                wide = [tile.astype(F32) for tile in tiles[3 * q : 3 * q + 3]]
                sources[row + mains + q] = fourth(wide, rank_top).astype(BF)
            for c in range(clusters):
                total[row + c] = jnp.zeros((rhs, LANES), F32)
        return 0

    lax.fori_loop(0, far, split, 0)

    def some(s, _):
        for u in range(unroll):
            j = s * unroll + u
            term = dot(sources[source_ref[j], :, :rank_top], coupling_ref[j])
            at = target_ref[j]
            total[at, :, :rank_top] = total[at, :, :rank_top] + term
        return 0

    lax.fori_loop(0, blocks // unroll, some, 0)

    def pack(f, _):
        for core in range(2):
            for g, group in enumerate(order):
                for place, chip in enumerate(group):
                    row = ((core * chips + chip) * far + f) * clusters
                    for q in range(quads):
                        mains_now = [total[row + 3 * q + k] for k in range(3)]
                        for k, tile in enumerate(packed(mains_now, total[row + mains + q], rank_top)):
                            out_refs[core * len(order) + g][place, f, 3 * q + k] = tile.astype(BF)
        return 0

    lax.fori_loop(0, far, pack, 0)


def order_kernel(_, __, out_ref):
    out_ref[...] = jnp.zeros_like(out_ref)


def near_kernel(v_ref, near_ref, out_ref):
    leaves = v_ref.shape[0]
    for i in range(leaves):
        total = dot(v_ref[i], near_ref[i, 1])
        if i > 0:
            total = total + dot(v_ref[i - 1], near_ref[i, 0])
        if i < leaves - 1:
            total = total + dot(v_ref[i + 1], near_ref[i, 2])
        out_ref[i] = total


def edge_kernel(inner_ref, outer_ref, first_ref, last_ref, out_ref):
    inner, outer = inner_ref[0], outer_ref[0]
    even = lax.axis_index("clu") % CORES == 0
    out_ref[0] = dot(jnp.where(even, outer, inner), first_ref[0, 0])
    out_ref[1] = dot(jnp.where(even, inner, outer), last_ref[0, 0])


def add_kernel(keep_ref, swap_ref, *out_refs):
    for n, out_ref in enumerate(out_refs):
        out_ref[...] = (keep_ref[n].astype(F32) + swap_ref[n].astype(F32)).astype(out_ref.dtype)


def middle_add_kernel(keep_ref, swap_ref, *refs, parts):
    part_refs, (own_out, *out_refs) = refs[:parts], refs[parts:]
    own_out[...] = keep_ref[0].astype(F32) + swap_ref[0].astype(F32)
    for n, out_ref in enumerate(out_refs):
        total = keep_ref[n + 1].astype(F32) + swap_ref[n + 1].astype(F32)
        for part_ref in part_refs[n :: len(out_refs)]:
            total = total + part_ref[...].astype(F32)
        out_ref[...] = total.astype(BF)


def rows_kernel(source_ref, target_ref, source_out, target_out, *, clusters, far, magic, shift):
    me = lax.axis_index("clu")
    for sign, in_ref, out_ref in ((-1, source_ref, source_out), (1, target_ref, target_out)):
        cluster = in_ref[...]
        device = cluster * magic >> shift
        chip = ((device ^ me) >> 1) & (CHIPS - 1)
        chip = jnp.where((device & 1) == 0, chip, chip >> 1 | (chip & 1) << 2)
        away = (sign * ((device >> 4) - (me >> 4))) & (far - 1)
        core = (device ^ me) & 1
        out_ref[...] = ((core * CHIPS + chip) * far + away) * clusters + cluster - device * clusters


def join_kernel(*refs):
    for n, part_ref in enumerate(refs[:-1]):
        refs[-1][n] = part_ref[...]


def last_add_kernel(own_ref, *refs, parts):
    part_refs, (keep_out, *away_refs) = refs[:parts], refs[parts:]
    for f in range(own_ref.shape[0]):
        total = own_ref[f]
        for part_ref in part_refs:
            total = total + part_ref[f].astype(F32)
        if f == 0:
            keep_out[...] = total
        else:
            away_refs[f - 1][...] = total.astype(BF)


def field_kernel(ranks_ref, near_ref, edge_ref, basis_ref, transfer_ref, keep_ref, *rest, away):
    term_refs, out_ref, next_refs = rest[:away], rest[away], rest[away + 1 :]
    leaves, rank_top, _ = basis_ref.shape
    mains, rhs, _ = keep_ref.shape
    tiles = []
    for t in range(mains):
        tile = keep_ref[t]
        for term_ref in term_refs:
            tile = tile + term_ref[t].astype(F32)
        tiles.append(tile)
    sums = tiles + [fourth(tiles[3 * q : 3 * q + 3], rank_top) for q in range(mains // 3)]
    lane = lax.broadcasted_iota(jnp.int32, (rhs, rank_top), 1)
    fields = [
        jnp.where(lane < ranks_ref[c], total[:, :rank_top], 0.0).astype(BF) for c, total in enumerate(sums)
    ]
    downs = [fields[i].astype(F32) + dot_t(fields[leaves + i // 2], transfer_ref[i]) for i in range(leaves)]
    leaf_totals = [jnp.where(lane < ranks_ref[i], down, 0.0).astype(BF) for i, down in enumerate(downs)]
    results = [near_ref[i] + dot(leaf_total, basis_ref[i]) for i, leaf_total in enumerate(leaf_totals)]
    results[0] = results[0] + edge_ref[0]
    results[-1] = results[-1] + edge_ref[1]
    results = [result.astype(BF) for result in results]
    for i, result in enumerate(results):
        out_ref[i] = result
    if next_refs:
        coeff_ref, inner_ref, outer_ref = next_refs
        emit_edges(out_ref, inner_ref, outer_ref)
        emit_coeffs(results, basis_ref, transfer_ref, ranks_ref, coeff_ref)


def params(mebibytes):
    return pltpu.CompilerParams(vmem_limit_bytes=mebibytes << 20)


def local(charges, basis, transfer, near_field, coupling, ranks, block_source, block_target):
    leaves, rank_top, width = basis.shape
    rhs = charges.shape[1]
    clusters = ranks.shape[0]
    blocks = coupling.shape[0]
    devices = lax.axis_size("clu")
    mains = clusters * 3 // 4
    shape = jax.ShapeDtypeStruct

    cores, chips = CORES, CHIPS
    cube = cores * chips
    far = devices // cube
    x, y, z = 1, 2, 4

    def swap_far(part, shift):
        return lax.ppermute(part, "clu", [(d, (d + shift * cube) % devices) for d in range(devices)])

    def swap(part, direction):
        turned = direction << 1 & 7 | direction >> 2
        return lax.ppermute(
            part, "clu", [(d, d ^ (turned if d % cores else direction) * cores) for d in range(devices)]
        )

    def swap_cores(part):
        return lax.ppermute(part, "clu", [(d, d ^ 1) for d in range(devices)])

    barrier = lax.optimization_barrier

    shift = 19
    magic = -(-(1 << shift) // clusters)
    numbers = np.arange(devices * clusters)
    assert (numbers * magic >> shift == numbers // clusters).all() and far & far - 1 == 0
    list_shape = jax.ShapeDtypeStruct((1, blocks), jnp.int32)
    source_rows, target_rows = pl.pallas_call(
        functools.partial(rows_kernel, clusters=clusters, far=far, magic=magic, shift=shift),
        out_shape=[list_shape] * 2,
        in_specs=[VMEM] * 2,
        out_specs=[VMEM] * 2,
        compiler_params=params(1),
    )(block_source.reshape(1, blocks), block_target.reshape(1, blocks))
    source_rows, target_rows = source_rows.reshape(blocks), target_rows.reshape(blocks)

    tile_shape = (mains, rhs, LANES)
    out_shape = shape((leaves, rhs, width), BF)
    tile_out = shape(tile_shape, BF)
    part_shape = shape((far,) + tile_shape, BF)
    edge_shape = shape((1, rhs, width), BF)
    first_coeffs, inner, outer = pl.pallas_call(
        coeff_kernel,
        out_shape=[tile_out, edge_shape, edge_shape],
        in_specs=[SMEM, HBM, HBM, HBM],
        out_specs=[VMEM] * 3,
        scratch_shapes=[
            pltpu.VMEM(charges.shape, BF),
            pltpu.VMEM(basis.shape, BF),
            pltpu.VMEM(transfer.shape, BF),
            pltpu.SemaphoreType.DMA((3,)),
        ],
    )(ranks, charges, basis, transfer)

    order = ((x | y | z, x | y, y | z, z | x), (0, x, y, z))
    couple = pl.pallas_call(
        functools.partial(couple_kernel, order=order, unroll=64),
        out_shape=[shape((4, far) + tile_shape, BF)] * 4,
        in_specs=[SMEM, SMEM, VMEM] + [VMEM] * (cores * chips),
        out_specs=[VMEM] * 4,
        scratch_shapes=[
            pltpu.VMEM((devices * clusters, rhs, LANES), BF),
            pltpu.VMEM((devices * clusters, rhs, LANES), F32),
        ],
        compiler_params=params(24 if devices <= 32 else 60),
        cost_estimate=pl.CostEstimate(
            flops=2 * blocks * rhs * rank_top * rank_top, bytes_accessed=10 << 20, transcendentals=0
        ),
    )

    near = pl.pallas_call(
        near_kernel,
        out_shape=shape((leaves, rhs, width), F32),
        in_specs=[VMEM, VMEM],
        out_specs=VMEM,
        compiler_params=params(16),
        cost_estimate=pl.CostEstimate(
            flops=2 * leaves * 3 * rhs * width * width, bytes_accessed=4 << 20, transcendentals=0
        ),
    )

    edge = pl.pallas_call(
        edge_kernel,
        out_shape=shape((2, rhs, width), F32),
        grid=(1,),
        in_specs=[
            VMEM,
            VMEM,
            pl.BlockSpec((1, 1, width, width), lambda i: (0, 0, 0, 0)),
            pl.BlockSpec((1, 1, width, width), lambda i: (leaves - 1, 2, 0, 0)),
        ],
        out_specs=VMEM,
        compiler_params=params(16),
    )

    def adder(kernel, inputs, outputs):
        return pl.pallas_call(
            kernel,
            out_shape=outputs,
            in_specs=[VMEM] * inputs,
            out_specs=[VMEM] * len(outputs),
            compiler_params=params(16),
        )

    own_shape = shape((far,) + tile_shape, F32)
    join = adder(join_kernel, far, [part_shape])
    relaid = pl.pallas_call(
        order_kernel,
        out_shape=shape((8, LANES), F32),
        in_specs=[pl.BlockSpec(memory_space=pl.ANY)] * 2,
        out_specs=VMEM,
    )
    first_join = pl.pallas_call(
        lambda _, *refs: join_kernel(*refs),
        out_shape=[part_shape],
        in_specs=[pl.BlockSpec(memory_space=pl.ANY)] + [VMEM] * far,
        out_specs=[VMEM],
        compiler_params=params(16),
    )
    far_add = adder(add_kernel, 2, [part_shape] * 4)
    middle_add = adder(functools.partial(middle_add_kernel, parts=4), 6, [own_shape] + [part_shape] * 3)
    last_add = adder(
        functools.partial(last_add_kernel, parts=3), 4, [shape(tile_shape, F32)] + [tile_out] * (far - 1)
    )

    def finish(with_coeffs):
        return pl.pallas_call(
            functools.partial(field_kernel, away=far - 1),
            out_shape=[out_shape, tile_out, edge_shape, edge_shape] if with_coeffs else [out_shape],
            in_specs=[SMEM] + [VMEM] * (4 + far),
            out_specs=[VMEM] * 4 if with_coeffs else [VMEM],
            compiler_params=params(16),
        )

    halo_pairs = [(d, d + cores) for d in range(1, devices - cores, cores)]
    halo_pairs += [(d, d - cores) for d in range(cores, devices, cores)]

    def apply_matrix(field_in, coeffs, inner, outer, coupling, with_coeffs):
        away = [swap_far(coeffs, s) for s in range(1, far)]
        if with_coeffs:
            outer, away = barrier((lax.ppermute(outer, "clu", halo_pairs), away))
            (column,) = first_join(relaid(coupling, coeffs), coeffs, *away)
        else:
            (column,) = join(coeffs, *away)
        got = {0: column, x: swap(column, x), y: swap(column, y), z: swap(column, z)}
        near_sum = near(field_in, near_field)
        got, near_sum = barrier((got, near_sum))
        corner = swap(column, x | y | z)
        other = {chip: swap_cores(part) for chip, part in got.items()}
        got |= {x | y: swap(got[x], y), y | z: swap(got[y], z), z | x: swap(got[z], x)}
        if not with_coeffs:
            outer = lax.ppermute(outer, "clu", halo_pairs)
        got, corner, outer = barrier((got, corner, outer))
        got[x | y | z] = corner
        other |= {chip: swap_cores(got[chip]) for chip in order[0]}
        totals = couple(
            source_rows,
            target_rows,
            coupling,
            *[got[chip] for chip in range(chips)],
            *[other[chip] for chip in range(chips)],
        )
        keep_long, keep, send_long, send = totals
        corner, xy, yz, zx = far_add(keep_long, swap_cores(send_long))
        corner, xy, yz, zx, send = barrier((corner, xy, yz, zx, send))
        to_x, to_y, to_z, corner, swapped = barrier(
            (swap(xy, y), swap(yz, z), swap(zx, x), swap(corner, y | z), swap_cores(send))
        )
        own, to_x, to_y, to_z, inner, outer = barrier(
            (*middle_add(keep, swapped, to_x, to_y, to_z, corner), inner, outer)
        )
        edges = edge(swap_cores(inner), swap_cores(outer), near_field, near_field)
        own, to_x, to_y, to_z, edges = barrier((own, swap(to_x, x), swap(to_y, y), swap(to_z, z), edges))
        total, *away = last_add(own, to_x, to_y, to_z)
        terms = [swap_far(part, s + 1) for s, part in enumerate(away)]
        return finish(with_coeffs)(ranks, near_sum, edges, basis, transfer, total, *terms)

    first, *second_args = apply_matrix(charges, first_coeffs, inner, outer, coupling, True)
    (second,) = apply_matrix(first, *second_args, coupling, False)
    return (first, second)


def solution(mesh):
    in_specs = (
        P("clu", None, None),
        P("clu", None, None),
        P("clu", None, None),
        P("clu", None, None, None),
        P("clu", None, None),
        P("clu"),
        P("clu"),
        P("clu"),
    )
    out_specs = (P("clu", None, None), P("clu", None, None))
    return jax.shard_map(local, mesh=mesh, in_specs=in_specs, out_specs=out_specs, check_vma=False)
```

```python
import functools

import jax
import jax.numpy as jnp
import numpy as np
from jax import lax
from jax.experimental import pallas as pl
from jax.experimental.pallas import tpu as pltpu
from jax.sharding import PartitionSpec as P

LANES = 128
CORES, CHIPS = 2, 8
BF = jnp.bfloat16
F32 = jnp.float32
VMEM = pl.BlockSpec(memory_space=pltpu.VMEM)
SMEM = pl.BlockSpec(memory_space=pltpu.SMEM)
HBM = pl.BlockSpec(memory_space=pltpu.HBM)


def dot(a, b):
    return lax.dot_general(a, b, (((1,), (0,)), ((), ())), preferred_element_type=F32)


def dot_t(a, b):
    return lax.dot_general(a, b, (((1,), (1,)), ((), ())), preferred_element_type=F32)


def lanes(rows):
    return lax.broadcasted_iota(jnp.int32, (rows, LANES), 1)


def fourth(tiles, rank_top):
    third = LANES - rank_top
    lane = lanes(tiles[0].shape[0])
    moved = [pltpu.roll(tile, third * (k + 1), 1) for k, tile in enumerate(tiles)]
    return jnp.where(lane < third, moved[0], jnp.where(lane < 2 * third, moved[1], moved[2]))


def packed(mains, pad, rank_top):
    lane = lanes(pad.shape[0])
    third = LANES - rank_top
    return [
        jnp.where(lane < rank_top, main, pltpu.roll(pad, rank_top - third * k, 1)) for k, main in enumerate(mains)
    ]


def widen(value):
    return jnp.concatenate([value, jnp.zeros((value.shape[0], LANES - value.shape[1]), value.dtype)], axis=1)


def emit_coeffs(values, basis_ref, transfer_ref, ranks_ref, out_ref, ready=None):
    mains, rhs, _ = out_ref.shape
    leaves, rank_top, _ = basis_ref.shape
    lane = lax.broadcasted_iota(jnp.int32, (rhs, rank_top), 1)
    coeffs = []
    for i in range(leaves):
        value = dot_t(values[i], basis_ref[i])
        coeffs.append(jnp.where(lane < ranks_ref[i], value, 0.0).astype(BF))
    if ready is not None:
        ready()
    for q in range(leaves // 2):
        value = dot(coeffs[2 * q], transfer_ref[2 * q]) + dot(coeffs[2 * q + 1], transfer_ref[2 * q + 1])
        coeffs.append(jnp.where(lane < ranks_ref[leaves + q], value, 0.0).astype(BF))
    wide = [widen(value.astype(F32)) for value in coeffs]
    for q in range(mains // 3):
        for k, tile in enumerate(packed(wide[3 * q : 3 * q + 3], wide[mains + q], rank_top)):
            out_ref[3 * q + k] = tile.astype(BF)


def fetch(pairs, sems):
    copies = [pltpu.make_async_copy(src, dst, sems.at[n]) for n, (src, dst) in enumerate(pairs)]
    for copy in copies:
        copy.start()
    return copies


def emit_edges(v_ref, inner_ref, outer_ref):
    head, tail = v_ref[0], v_ref[v_ref.shape[0] - 1]
    even = lax.axis_index("clu") % CORES == 0
    inner_ref[0] = jnp.where(even, tail, head)
    outer_ref[0] = jnp.where(even, head, tail)


def coeff_kernel(
    ranks_ref, v_hbm, basis_hbm, transfer_hbm, out_ref, inner_ref, outer_ref, v_ref, basis_ref, transfer_ref, sems
):
    leaves = basis_ref.shape[0]
    copies = fetch([(v_hbm, v_ref), (basis_hbm, basis_ref), (transfer_hbm, transfer_ref)], sems)
    copies[0].wait()
    emit_edges(v_ref, inner_ref, outer_ref)
    copies[1].wait()
    values = [v_ref[i] for i in range(leaves)]
    emit_coeffs(values, basis_ref, transfer_ref, ranks_ref, out_ref, copies[2].wait)


def couple_kernel(source_ref, target_ref, coupling_ref, *refs, order, joined, unroll):
    chips = sum(len(group) for group in order)
    in_refs, out_refs, (sources, total) = refs[: -2 - 2 * len(order)], refs[-2 - 2 * len(order) : -2], refs[-2:]
    blocks, rank_top, _ = coupling_ref.shape
    far, mains, rhs, _ = in_refs[-1].shape
    if joined:
        cores, in_refs = (in_refs[: len(in_refs) // 2], in_refs[len(in_refs) // 2 :]), []
        for near_pieces, *far_pieces in cores:
            pieces = {chip: near_pieces.at[place] for place, chip in enumerate(order[1])}
            pieces |= dict(zip(order[0], far_pieces))
            in_refs += [pieces[chip] for chip in range(chips)]
    quads = mains // 3
    clusters = mains + quads

    def split(f, _):
        for n, packed_ref in enumerate(in_refs):
            row = (n * far + f) * clusters
            tiles = [packed_ref[f, c] for c in range(mains)]
            for c in range(mains):
                sources[row + c] = tiles[c]
            for q in range(quads):
                wide = [tile.astype(F32) for tile in tiles[3 * q : 3 * q + 3]]
                sources[row + mains + q] = fourth(wide, rank_top).astype(BF)
            for c in range(clusters):
                total[row + c] = jnp.zeros((rhs, LANES), F32)
        return 0

    lax.fori_loop(0, far, split, 0)

    def some(s, _):
        for u in range(unroll):
            j = s * unroll + u
            term = dot(sources[source_ref[j], :, :rank_top], coupling_ref[j])
            at = target_ref[j]
            total[at, :, :rank_top] = total[at, :, :rank_top] + term
        return 0

    lax.fori_loop(0, blocks // unroll, some, 0)

    def pack(f, _):
        for core in range(2):
            for g, group in enumerate(order):
                for place, chip in enumerate(group):
                    row = ((core * chips + chip) * far + f) * clusters
                    for q in range(quads):
                        mains_now = [total[row + 3 * q + k] for k in range(3)]
                        for k, tile in enumerate(packed(mains_now, total[row + mains + q], rank_top)):
                            out_refs[core * len(order) + g][place, f, 3 * q + k] = tile.astype(BF)
        return 0

    lax.fori_loop(0, far, pack, 0)


def order_kernel(_, __, out_ref):
    out_ref[...] = jnp.zeros_like(out_ref)


def near_kernel(v_ref, near_ref, out_ref):
    leaves = v_ref.shape[0]
    for i in range(leaves):
        total = dot(v_ref[i], near_ref[i, 1])
        if i > 0:
            total = total + dot(v_ref[i - 1], near_ref[i, 0])
        if i < leaves - 1:
            total = total + dot(v_ref[i + 1], near_ref[i, 2])
        out_ref[i] = total


def edge_kernel(inner_ref, outer_ref, first_ref, last_ref, out_ref):
    inner, outer = inner_ref[0], outer_ref[0]
    even = lax.axis_index("clu") % CORES == 0
    out_ref[0] = dot(jnp.where(even, outer, inner), first_ref[0, 0])
    out_ref[1] = dot(jnp.where(even, inner, outer), last_ref[0, 0])


def add_kernel(keep_ref, swap_ref, *out_refs):
    for n, out_ref in enumerate(out_refs):
        out_ref[...] = (keep_ref[n].astype(F32) + swap_ref[n].astype(F32)).astype(out_ref.dtype)


def middle_add_kernel(keep_ref, swap_ref, *refs, parts):
    part_refs, (own_out, *out_refs) = refs[:parts], refs[parts:]
    own_out[...] = keep_ref[0].astype(F32) + swap_ref[0].astype(F32)
    for n, out_ref in enumerate(out_refs):
        total = keep_ref[n + 1].astype(F32) + swap_ref[n + 1].astype(F32)
        for part_ref in part_refs[n :: len(out_refs)]:
            total = total + part_ref[...].astype(F32)
        out_ref[...] = total.astype(BF)


def rows_kernel(source_ref, target_ref, source_out, target_out, *, clusters, far, magic, shift):
    me = lax.axis_index("clu")
    for sign, in_ref, out_ref in ((-1, source_ref, source_out), (1, target_ref, target_out)):
        cluster = in_ref[...]
        device = cluster * magic >> shift
        chip = ((device ^ me) >> 1) & (CHIPS - 1)
        chip = jnp.where((device & 1) == 0, chip, chip >> 1 | (chip & 1) << 2)
        away = (sign * ((device >> 4) - (me >> 4))) & (far - 1)
        core = (device ^ me) & 1
        out_ref[...] = ((core * CHIPS + chip) * far + away) * clusters + cluster - device * clusters


def join_kernel(*refs):
    for n, part_ref in enumerate(refs[:-1]):
        refs[-1][n] = part_ref[...]


def last_add_kernel(own_ref, *refs, parts):
    part_refs, (keep_out, *away_refs) = refs[:parts], refs[parts:]
    for f in range(own_ref.shape[0]):
        total = own_ref[f]
        for part_ref in part_refs:
            total = total + part_ref[f].astype(F32)
        if f == 0:
            keep_out[...] = total
        else:
            away_refs[f - 1][...] = total.astype(BF)


def field_kernel(ranks_ref, near_ref, edge_ref, basis_ref, transfer_ref, keep_ref, *rest, away):
    term_refs, out_ref, next_refs = rest[:away], rest[away], rest[away + 1 :]
    leaves, rank_top, _ = basis_ref.shape
    mains, rhs, _ = keep_ref.shape
    tiles = []
    for t in range(mains):
        tile = keep_ref[t]
        for term_ref in term_refs:
            tile = tile + term_ref[t].astype(F32)
        tiles.append(tile)
    sums = tiles + [fourth(tiles[3 * q : 3 * q + 3], rank_top) for q in range(mains // 3)]
    lane = lax.broadcasted_iota(jnp.int32, (rhs, rank_top), 1)
    fields = [
        jnp.where(lane < ranks_ref[c], total[:, :rank_top], 0.0).astype(BF) for c, total in enumerate(sums)
    ]
    downs = [fields[i].astype(F32) + dot_t(fields[leaves + i // 2], transfer_ref[i]) for i in range(leaves)]
    leaf_totals = [jnp.where(lane < ranks_ref[i], down, 0.0).astype(BF) for i, down in enumerate(downs)]
    results = [near_ref[i] + dot(leaf_total, basis_ref[i]) for i, leaf_total in enumerate(leaf_totals)]
    results[0] = results[0] + edge_ref[0]
    results[-1] = results[-1] + edge_ref[1]
    results = [result.astype(BF) for result in results]
    for i, result in enumerate(results):
        out_ref[i] = result
    if next_refs:
        coeff_ref, inner_ref, outer_ref, values_ref = next_refs
        for i, result in enumerate(results):
            values_ref[i] = result
        emit_edges(out_ref, inner_ref, outer_ref)
        emit_coeffs(results, basis_ref, transfer_ref, ranks_ref, coeff_ref)


def params(mebibytes):
    return pltpu.CompilerParams(vmem_limit_bytes=mebibytes << 20)


def local(charges, basis, transfer, near_field, coupling, ranks, block_source, block_target):
    leaves, rank_top, width = basis.shape
    rhs = charges.shape[1]
    clusters = ranks.shape[0]
    blocks = coupling.shape[0]
    devices = lax.axis_size("clu")
    mains = clusters * 3 // 4
    shape = jax.ShapeDtypeStruct

    cores, chips = CORES, CHIPS
    cube = cores * chips
    far = devices // cube
    x, y, z = 1, 2, 4

    def swap_far(part, shift):
        return lax.ppermute(part, "clu", [(d, (d + shift * cube) % devices) for d in range(devices)])

    def swap(part, direction):
        turned = direction << 1 & 7 | direction >> 2
        return lax.ppermute(
            part, "clu", [(d, d ^ (turned if d % cores else direction) * cores) for d in range(devices)]
        )

    def swap_cores(part):
        return lax.ppermute(part, "clu", [(d, d ^ 1) for d in range(devices)])

    barrier = lax.optimization_barrier

    shift = 19
    magic = -(-(1 << shift) // clusters)
    numbers = np.arange(devices * clusters)
    assert (numbers * magic >> shift == numbers // clusters).all() and far & far - 1 == 0
    list_shape = jax.ShapeDtypeStruct((1, blocks), jnp.int32)
    source_rows, target_rows = pl.pallas_call(
        functools.partial(rows_kernel, clusters=clusters, far=far, magic=magic, shift=shift),
        out_shape=[list_shape] * 2,
        in_specs=[VMEM] * 2,
        out_specs=[VMEM] * 2,
        compiler_params=params(1),
    )(block_source.reshape(1, blocks), block_target.reshape(1, blocks))
    source_rows, target_rows = source_rows.reshape(blocks), target_rows.reshape(blocks)

    tile_shape = (mains, rhs, LANES)
    out_shape = shape((leaves, rhs, width), BF)
    tile_out = shape(tile_shape, BF)
    part_shape = shape((far,) + tile_shape, BF)
    edge_shape = shape((1, rhs, width), BF)
    first_coeffs, inner, outer = pl.pallas_call(
        coeff_kernel,
        out_shape=[tile_out, edge_shape, edge_shape],
        in_specs=[SMEM, HBM, HBM, HBM],
        out_specs=[VMEM] * 3,
        scratch_shapes=[
            pltpu.VMEM(charges.shape, BF),
            pltpu.VMEM(basis.shape, BF),
            pltpu.VMEM(transfer.shape, BF),
            pltpu.SemaphoreType.DMA((3,)),
        ],
    )(ranks, charges, basis, transfer)

    order = ((x | y | z, x | y, y | z, z | x), (0, x, y, z))
    def couple(joined, *args):
        return pl.pallas_call(
            functools.partial(couple_kernel, order=order, joined=joined, unroll=64),
            out_shape=[shape((4, far) + tile_shape, BF)] * 4,
            in_specs=[SMEM, SMEM] + [VMEM] * (len(args) - 2),
            out_specs=[VMEM] * 4,
            scratch_shapes=[
                pltpu.VMEM((devices * clusters, rhs, LANES), BF),
                pltpu.VMEM((devices * clusters, rhs, LANES), F32),
            ],
            compiler_params=params(24 if devices <= 32 else 60),
            cost_estimate=pl.CostEstimate(
                flops=2 * blocks * rhs * rank_top * rank_top, bytes_accessed=10 << 20, transcendentals=0
            ),
        )(*args)

    near = pl.pallas_call(
        near_kernel,
        out_shape=shape((leaves, rhs, width), F32),
        in_specs=[VMEM, VMEM],
        out_specs=VMEM,
        compiler_params=params(16),
        cost_estimate=pl.CostEstimate(
            flops=2 * leaves * 3 * rhs * width * width, bytes_accessed=4 << 20, transcendentals=0
        ),
    )

    edge = pl.pallas_call(
        edge_kernel,
        out_shape=shape((2, rhs, width), F32),
        grid=(1,),
        in_specs=[
            VMEM,
            VMEM,
            pl.BlockSpec((1, 1, width, width), lambda i: (0, 0, 0, 0)),
            pl.BlockSpec((1, 1, width, width), lambda i: (leaves - 1, 2, 0, 0)),
        ],
        out_specs=VMEM,
        compiler_params=params(16),
    )

    def adder(kernel, inputs, outputs):
        return pl.pallas_call(
            kernel,
            out_shape=outputs,
            in_specs=[VMEM] * inputs,
            out_specs=[VMEM] * len(outputs),
            compiler_params=params(16),
        )

    own_shape = shape((far,) + tile_shape, F32)
    join = adder(join_kernel, far, [part_shape])
    relaid = pl.pallas_call(
        order_kernel,
        out_shape=shape((8, LANES), F32),
        in_specs=[pl.BlockSpec(memory_space=pl.ANY)] * 2,
        out_specs=VMEM,
    )
    first_join = pl.pallas_call(
        lambda _, *refs: join_kernel(*refs),
        out_shape=[part_shape],
        in_specs=[pl.BlockSpec(memory_space=pl.ANY)] + [VMEM] * far,
        out_specs=[VMEM],
        compiler_params=params(16),
    )
    far_add = adder(add_kernel, 2, [part_shape] * 4)
    join_near = adder(join_kernel, 4, [shape((4,) + part_shape.shape, BF)])

    def middle_add(*args):
        kernel = functools.partial(middle_add_kernel, parts=len(args) - 2)
        return adder(kernel, len(args), [own_shape] + [part_shape] * 3)(*args)

    def last_add(*args):
        kernel = functools.partial(last_add_kernel, parts=len(args) - 1)
        return adder(kernel, len(args), [shape(tile_shape, F32)] + [tile_out] * (far - 1))(*args)

    def finish(with_coeffs):
        return pl.pallas_call(
            functools.partial(field_kernel, away=far - 1),
            out_shape=[out_shape, tile_out, edge_shape, edge_shape, out_shape] if with_coeffs else [out_shape],
            in_specs=[SMEM] + [VMEM] * (4 + far),
            out_specs=[VMEM] * 5 if with_coeffs else [VMEM],
            compiler_params=params(16),
        )

    halo_pairs = [(d, d + cores) for d in range(1, devices - cores, cores)]
    halo_pairs += [(d, d - cores) for d in range(cores, devices, cores)]

    def apply_matrix(field_in, coeffs, inner, outer, coupling, with_coeffs):
        away = [swap_far(coeffs, s) for s in range(1, far)]
        (column,) = first_join(relaid(coupling, coeffs), coeffs, *away) if with_coeffs else join(coeffs, *away)
        got = {0: column, x: swap(column, x), y: swap(column, y), z: swap(column, z)}
        near_sum = near(field_in, near_field)
        got, near_sum = barrier((got, near_sum))
        second_round = {x | y: swap(got[x], y), y | z: swap(got[y], z), z | x: swap(got[z], x)}
        if with_coeffs:
            second_round[x | y | z] = swap(got[x], y | z)
            (near_pieces,) = join_near(*[got[chip] for chip in order[1]])
            far_pieces, other_near = barrier(([second_round[chip] for chip in order[0]], swap_cores(near_pieces)))
            other_far = [swap_cores(part) for part in far_pieces]
            args = (near_pieces, *far_pieces, other_near, *other_far)
        else:
            corner = swap(column, x | y | z)
            other = {chip: swap_cores(part) for chip, part in got.items()}
            got |= second_round
            got, corner, outer = barrier((got, corner, lax.ppermute(outer, "clu", halo_pairs)))
            got[x | y | z] = corner
            other |= {chip: swap_cores(got[chip]) for chip in order[0]}
            args = [got[chip] for chip in range(chips)] + [other[chip] for chip in range(chips)]
        keep_long, keep, send_long, send = couple(with_coeffs, source_rows, target_rows, coupling, *args)

        corner, xy, yz, zx = far_add(keep_long, swap_cores(send_long))
        corner, xy, yz, zx, send = barrier((corner, xy, yz, zx, send))
        arrived = [swap(xy, y), swap(yz, z), swap(zx, x)]
        if not with_coeffs:
            arrived.append(swap(corner, y | z))
        arrived, swapped = barrier((arrived, swap_cores(send)))
        (own, *sums), inner, outer = barrier((middle_add(keep, swapped, *arrived), inner, outer))
        if with_coeffs:
            parts = [swap(part, way) for part, way in zip(sums + [corner], (x, y, z, x | y | z))]
            own, parts, inner, outer = barrier((own, parts, inner, lax.ppermute(outer, "clu", halo_pairs)))
            total, *away = last_add(own, *parts)
            edges = edge(swap_cores(inner), swap_cores(outer), near_field, near_field)
            terms, edges = barrier(([swap_far(part, s + 1) for s, part in enumerate(away)], edges))
        else:
            edges = edge(swap_cores(inner), swap_cores(outer), near_field, near_field)
            parts = [swap(part, way) for part, way in zip(sums, (x, y, z))]
            own, parts, edges = barrier((own, parts, edges))
            total, *away = last_add(own, *parts)
            terms = [swap_far(part, s + 1) for s, part in enumerate(away)]
        return finish(with_coeffs)(ranks, near_sum, edges, basis, transfer, total, *terms)

    first, *second_args, values = apply_matrix(charges, first_coeffs, inner, outer, coupling, True)
    (second,) = apply_matrix(values, *second_args, coupling, False)
    return (first, second)


def solution(mesh):
    in_specs = (
        P("clu", None, None),
        P("clu", None, None),
        P("clu", None, None),
        P("clu", None, None, None),
        P("clu", None, None),
        P("clu"),
        P("clu"),
        P("clu"),
    )
    out_specs = (P("clu", None, None), P("clu", None, None))
    return jax.shard_map(local, mesh=mesh, in_specs=in_specs, out_specs=out_specs, check_vma=False)
```

```python
import functools

import jax
import jax.numpy as jnp
import numpy as np
from jax import lax
from jax.experimental import pallas as pl
from jax.experimental.pallas import tpu as pltpu
from jax.sharding import PartitionSpec as P

LANES = 128
CORES, CHIPS = 2, 8
BF = jnp.bfloat16
F32 = jnp.float32
VMEM = pl.BlockSpec(memory_space=pltpu.VMEM)
SMEM = pl.BlockSpec(memory_space=pltpu.SMEM)
HBM = pl.BlockSpec(memory_space=pltpu.HBM)


def dot(a, b):
    return lax.dot_general(a, b, (((1,), (0,)), ((), ())), preferred_element_type=F32)


def dot_t(a, b):
    return lax.dot_general(a, b, (((1,), (1,)), ((), ())), preferred_element_type=F32)


def lanes(rows):
    return lax.broadcasted_iota(jnp.int32, (rows, LANES), 1)


def fourth(tiles, rank_top):
    third = LANES - rank_top
    lane = lanes(tiles[0].shape[0])
    moved = [pltpu.roll(tile, third * (k + 1), 1) for k, tile in enumerate(tiles)]
    return jnp.where(lane < third, moved[0], jnp.where(lane < 2 * third, moved[1], moved[2]))


def packed(mains, pad, rank_top):
    lane = lanes(pad.shape[0])
    third = LANES - rank_top
    return [
        jnp.where(lane < rank_top, main, pltpu.roll(pad, rank_top - third * k, 1)) for k, main in enumerate(mains)
    ]


def widen(value):
    return jnp.concatenate([value, jnp.zeros((value.shape[0], LANES - value.shape[1]), value.dtype)], axis=1)


def emit_coeffs(values, basis_ref, transfer_ref, ranks_ref, out_ref, ready=None):
    mains, rhs, _ = out_ref.shape
    leaves, rank_top, _ = basis_ref.shape
    lane = lax.broadcasted_iota(jnp.int32, (rhs, rank_top), 1)
    coeffs = []
    for i in range(leaves):
        value = dot_t(values[i], basis_ref[i])
        coeffs.append(jnp.where(lane < ranks_ref[i], value, 0.0).astype(BF))
    if ready is not None:
        ready()
    for q in range(leaves // 2):
        value = dot(coeffs[2 * q], transfer_ref[2 * q]) + dot(coeffs[2 * q + 1], transfer_ref[2 * q + 1])
        coeffs.append(jnp.where(lane < ranks_ref[leaves + q], value, 0.0).astype(BF))
    wide = [widen(value.astype(F32)) for value in coeffs]
    for q in range(mains // 3):
        for k, tile in enumerate(packed(wide[3 * q : 3 * q + 3], wide[mains + q], rank_top)):
            out_ref[3 * q + k] = tile.astype(BF)


def fetch(pairs, sems):
    copies = [pltpu.make_async_copy(src, dst, sems.at[n]) for n, (src, dst) in enumerate(pairs)]
    for copy in copies:
        copy.start()
    return copies


def emit_edges(v_ref, inner_ref, outer_ref):
    head, tail = v_ref[0], v_ref[v_ref.shape[0] - 1]
    even = lax.axis_index("clu") % CORES == 0
    inner_ref[0] = jnp.where(even, tail, head)
    outer_ref[0] = jnp.where(even, head, tail)


def coeff_kernel(
    ranks_ref, v_hbm, basis_hbm, transfer_hbm, out_ref, inner_ref, outer_ref, v_ref, basis_ref, transfer_ref, sems
):
    leaves = basis_ref.shape[0]
    copies = fetch([(v_hbm, v_ref), (basis_hbm, basis_ref), (transfer_hbm, transfer_ref)], sems)
    copies[0].wait()
    emit_edges(v_ref, inner_ref, outer_ref)
    copies[1].wait()
    values = [v_ref[i] for i in range(leaves)]
    emit_coeffs(values, basis_ref, transfer_ref, ranks_ref, out_ref, copies[2].wait)


def couple_kernel(source_ref, target_ref, coupling_ref, *refs, order, joined, unroll):
    chips = sum(len(group) for group in order)
    in_refs, out_refs, (sources, total) = refs[: -2 - 2 * len(order)], refs[-2 - 2 * len(order) : -2], refs[-2:]
    blocks, rank_top, _ = coupling_ref.shape
    far, mains, rhs, _ = in_refs[-1].shape
    if joined:
        cores, in_refs = (in_refs[: len(in_refs) // 2], in_refs[len(in_refs) // 2 :]), []
        for near_pieces, *far_pieces in cores:
            pieces = {chip: near_pieces.at[place] for place, chip in enumerate(order[1])}
            pieces |= dict(zip(order[0], far_pieces))
            in_refs += [pieces[chip] for chip in range(chips)]
    quads = mains // 3
    clusters = mains + quads

    def split(f, _):
        for n, packed_ref in enumerate(in_refs):
            row = (n * far + f) * clusters
            tiles = [packed_ref[f, c] for c in range(mains)]
            for c in range(mains):
                sources[row + c] = tiles[c]
            for q in range(quads):
                wide = [tile.astype(F32) for tile in tiles[3 * q : 3 * q + 3]]
                sources[row + mains + q] = fourth(wide, rank_top).astype(BF)
            for c in range(clusters):
                total[row + c] = jnp.zeros((rhs, LANES), F32)
        return 0

    lax.fori_loop(0, far, split, 0)

    def some(s, _):
        for u in range(unroll):
            j = s * unroll + u
            term = dot(sources[source_ref[j], :, :rank_top], coupling_ref[j])
            at = target_ref[j]
            total[at, :, :rank_top] = total[at, :, :rank_top] + term
        return 0

    lax.fori_loop(0, blocks // unroll, some, 0)

    def pack(f, _):
        for core in range(2):
            for g, group in enumerate(order):
                for place, chip in enumerate(group):
                    row = ((core * chips + chip) * far + f) * clusters
                    for q in range(quads):
                        mains_now = [total[row + 3 * q + k] for k in range(3)]
                        for k, tile in enumerate(packed(mains_now, total[row + mains + q], rank_top)):
                            out_refs[core * len(order) + g][place, f, 3 * q + k] = tile.astype(BF)
        return 0

    lax.fori_loop(0, far, pack, 0)


def order_kernel(_, __, out_ref):
    out_ref[...] = jnp.zeros_like(out_ref)


def near_kernel(v_ref, near_ref, out_ref):
    leaves = v_ref.shape[0]
    for i in range(leaves):
        total = dot(v_ref[i], near_ref[i, 1])
        if i > 0:
            total = total + dot(v_ref[i - 1], near_ref[i, 0])
        if i < leaves - 1:
            total = total + dot(v_ref[i + 1], near_ref[i, 2])
        out_ref[i] = total


def edge_kernel(inner_ref, outer_ref, first_ref, last_ref, out_ref):
    inner, outer = inner_ref[0], outer_ref[0]
    even = lax.axis_index("clu") % CORES == 0
    out_ref[0] = dot(jnp.where(even, outer, inner), first_ref[0, 0])
    out_ref[1] = dot(jnp.where(even, inner, outer), last_ref[0, 0])


def add_kernel(keep_ref, swap_ref, *out_refs):
    for n, out_ref in enumerate(out_refs):
        out_ref[...] = (keep_ref[n].astype(F32) + swap_ref[n].astype(F32)).astype(out_ref.dtype)


def middle_add_kernel(keep_ref, swap_ref, *refs, parts):
    part_refs, (own_out, *out_refs) = refs[:parts], refs[parts:]
    own_out[...] = keep_ref[0].astype(F32) + swap_ref[0].astype(F32)
    for n, out_ref in enumerate(out_refs):
        total = keep_ref[n + 1].astype(F32) + swap_ref[n + 1].astype(F32)
        for part_ref in part_refs[n :: len(out_refs)]:
            total = total + part_ref[...].astype(F32)
        out_ref[...] = total.astype(BF)


def rows_kernel(source_ref, target_ref, source_out, target_out, *, clusters, far, magic, shift):
    me = lax.axis_index("clu")
    for sign, in_ref, out_ref in ((-1, source_ref, source_out), (1, target_ref, target_out)):
        cluster = in_ref[...]
        device = cluster * magic >> shift
        chip = ((device ^ me) >> 1) & (CHIPS - 1)
        chip = jnp.where((device & 1) == 0, chip, chip >> 1 | (chip & 1) << 2)
        away = (sign * ((device >> 4) - (me >> 4))) & (far - 1)
        core = (device ^ me) & 1
        out_ref[...] = ((core * CHIPS + chip) * far + away) * clusters + cluster - device * clusters


def join_kernel(*refs):
    for n, part_ref in enumerate(refs[:-1]):
        refs[-1][n] = part_ref[...]


def last_add_kernel(own_ref, *refs, parts):
    part_refs, (keep_out, *away_refs) = refs[:parts], refs[parts:]
    for f in range(own_ref.shape[0]):
        total = own_ref[f]
        for part_ref in part_refs:
            total = total + part_ref[f].astype(F32)
        if f == 0:
            keep_out[...] = total
        else:
            away_refs[f - 1][...] = total.astype(BF)


def field_kernel(ranks_ref, near_ref, edge_ref, basis_ref, transfer_ref, keep_ref, *rest, away):
    term_refs, out_ref, next_refs = rest[:away], rest[away], rest[away + 1 :]
    leaves, rank_top, _ = basis_ref.shape
    mains, rhs, _ = keep_ref.shape
    tiles = []
    for t in range(mains):
        tile = keep_ref[t]
        for term_ref in term_refs:
            tile = tile + term_ref[t].astype(F32)
        tiles.append(tile)
    sums = tiles + [fourth(tiles[3 * q : 3 * q + 3], rank_top) for q in range(mains // 3)]
    lane = lax.broadcasted_iota(jnp.int32, (rhs, rank_top), 1)
    fields = [
        jnp.where(lane < ranks_ref[c], total[:, :rank_top], 0.0).astype(BF) for c, total in enumerate(sums)
    ]
    downs = [fields[i].astype(F32) + dot_t(fields[leaves + i // 2], transfer_ref[i]) for i in range(leaves)]
    leaf_totals = [jnp.where(lane < ranks_ref[i], down, 0.0).astype(BF) for i, down in enumerate(downs)]
    results = [near_ref[i] + dot(leaf_total, basis_ref[i]) for i, leaf_total in enumerate(leaf_totals)]
    results[0] = results[0] + edge_ref[0]
    results[-1] = results[-1] + edge_ref[1]
    results = [result.astype(BF) for result in results]
    for i, result in enumerate(results):
        out_ref[i] = result
    if next_refs:
        coeff_ref, inner_ref, outer_ref, values_ref = next_refs
        for i, result in enumerate(results):
            values_ref[i] = result
        emit_edges(out_ref, inner_ref, outer_ref)
        emit_coeffs(results, basis_ref, transfer_ref, ranks_ref, coeff_ref)


def params(mebibytes):
    return pltpu.CompilerParams(vmem_limit_bytes=mebibytes << 20)


def local(charges, basis, transfer, near_field, coupling, ranks, block_source, block_target):
    leaves, rank_top, width = basis.shape
    rhs = charges.shape[1]
    clusters = ranks.shape[0]
    blocks = coupling.shape[0]
    devices = lax.axis_size("clu")
    mains = clusters * 3 // 4
    shape = jax.ShapeDtypeStruct

    cores, chips = CORES, CHIPS
    cube = cores * chips
    far = devices // cube
    x, y, z = 1, 2, 4

    def swap_far(part, shift):
        return lax.ppermute(part, "clu", [(d, (d + shift * cube) % devices) for d in range(devices)])

    def swap(part, direction):
        turned = direction << 1 & 7 | direction >> 2
        return lax.ppermute(
            part, "clu", [(d, d ^ (turned if d % cores else direction) * cores) for d in range(devices)]
        )

    def swap_cores(part):
        return lax.ppermute(part, "clu", [(d, d ^ 1) for d in range(devices)])

    barrier = lax.optimization_barrier

    shift = 19
    magic = -(-(1 << shift) // clusters)
    numbers = np.arange(devices * clusters)
    assert (numbers * magic >> shift == numbers // clusters).all() and far & far - 1 == 0
    list_shape = jax.ShapeDtypeStruct((1, blocks), jnp.int32)
    source_rows, target_rows = pl.pallas_call(
        functools.partial(rows_kernel, clusters=clusters, far=far, magic=magic, shift=shift),
        out_shape=[list_shape] * 2,
        in_specs=[VMEM] * 2,
        out_specs=[VMEM] * 2,
        compiler_params=params(1),
    )(block_source.reshape(1, blocks), block_target.reshape(1, blocks))
    source_rows, target_rows = source_rows.reshape(blocks), target_rows.reshape(blocks)

    tile_shape = (mains, rhs, LANES)
    out_shape = shape((leaves, rhs, width), BF)
    tile_out = shape(tile_shape, BF)
    part_shape = shape((far,) + tile_shape, BF)
    edge_shape = shape((1, rhs, width), BF)
    first_coeffs, inner, outer = pl.pallas_call(
        coeff_kernel,
        out_shape=[tile_out, edge_shape, edge_shape],
        in_specs=[SMEM, HBM, HBM, HBM],
        out_specs=[VMEM] * 3,
        scratch_shapes=[
            pltpu.VMEM(charges.shape, BF),
            pltpu.VMEM(basis.shape, BF),
            pltpu.VMEM(transfer.shape, BF),
            pltpu.SemaphoreType.DMA((3,)),
        ],
    )(ranks, charges, basis, transfer)

    order = ((x | y | z, x | y, y | z, z | x), (0, x, y, z))
    def couple(joined, *args):
        return pl.pallas_call(
            functools.partial(couple_kernel, order=order, joined=joined, unroll=blocks),
            out_shape=[shape((4, far) + tile_shape, BF)] * 4,
            in_specs=[SMEM, SMEM] + [VMEM] * (len(args) - 2),
            out_specs=[VMEM] * 4,
            scratch_shapes=[
                pltpu.VMEM((devices * clusters, rhs, LANES), BF),
                pltpu.VMEM((devices * clusters, rhs, LANES), F32),
            ],
            compiler_params=params(24 if devices <= 32 else 60),
            cost_estimate=pl.CostEstimate(
                flops=2 * blocks * rhs * rank_top * rank_top, bytes_accessed=10 << 20, transcendentals=0
            ),
        )(*args)

    near = pl.pallas_call(
        near_kernel,
        out_shape=shape((leaves, rhs, width), F32),
        in_specs=[VMEM, VMEM],
        out_specs=VMEM,
        compiler_params=params(16),
        cost_estimate=pl.CostEstimate(
            flops=2 * leaves * 3 * rhs * width * width, bytes_accessed=4 << 20, transcendentals=0
        ),
    )

    edge = pl.pallas_call(
        edge_kernel,
        out_shape=shape((2, rhs, width), F32),
        grid=(1,),
        in_specs=[
            VMEM,
            VMEM,
            pl.BlockSpec((1, 1, width, width), lambda i: (0, 0, 0, 0)),
            pl.BlockSpec((1, 1, width, width), lambda i: (leaves - 1, 2, 0, 0)),
        ],
        out_specs=VMEM,
        compiler_params=params(16),
    )

    def adder(kernel, inputs, outputs):
        return pl.pallas_call(
            kernel,
            out_shape=outputs,
            in_specs=[VMEM] * inputs,
            out_specs=[VMEM] * len(outputs),
            compiler_params=params(16),
        )

    own_shape = shape((far,) + tile_shape, F32)
    join = adder(join_kernel, far, [part_shape])
    relaid = pl.pallas_call(
        order_kernel,
        out_shape=shape((8, LANES), F32),
        in_specs=[pl.BlockSpec(memory_space=pl.ANY)] * 2,
        out_specs=VMEM,
    )
    first_join = pl.pallas_call(
        lambda _, *refs: join_kernel(*refs),
        out_shape=[part_shape],
        in_specs=[pl.BlockSpec(memory_space=pl.ANY)] + [VMEM] * far,
        out_specs=[VMEM],
        compiler_params=params(16),
    )
    far_add = adder(add_kernel, 2, [part_shape] * 4)
    join_near = adder(join_kernel, 4, [shape((4,) + part_shape.shape, BF)])

    def middle_add(*args):
        kernel = functools.partial(middle_add_kernel, parts=len(args) - 2)
        return adder(kernel, len(args), [own_shape] + [part_shape] * 3)(*args)

    def last_add(*args):
        kernel = functools.partial(last_add_kernel, parts=len(args) - 1)
        return adder(kernel, len(args), [shape(tile_shape, F32)] + [tile_out] * (far - 1))(*args)

    def finish(with_coeffs):
        return pl.pallas_call(
            functools.partial(field_kernel, away=far - 1),
            out_shape=[out_shape, tile_out, edge_shape, edge_shape, out_shape] if with_coeffs else [out_shape],
            in_specs=[SMEM] + [VMEM] * (4 + far),
            out_specs=[VMEM] * 5 if with_coeffs else [VMEM],
            compiler_params=params(16),
        )

    halo_pairs = [(d, d + cores) for d in range(1, devices - cores, cores)]
    halo_pairs += [(d, d - cores) for d in range(cores, devices, cores)]

    def apply_matrix(field_in, coeffs, inner, outer, coupling, with_coeffs):
        away = [swap_far(coeffs, s) for s in range(1, far)]
        (column,) = first_join(relaid(coupling, coeffs), coeffs, *away) if with_coeffs else join(coeffs, *away)
        got = {0: column, x: swap(column, x), y: swap(column, y), z: swap(column, z)}
        near_sum = near(field_in, near_field)
        got, near_sum = barrier((got, near_sum))
        second_round = {x | y: swap(got[x], y), y | z: swap(got[y], z), z | x: swap(got[z], x)}
        if with_coeffs:
            second_round[x | y | z] = swap(got[x], y | z)
            (near_pieces,) = join_near(*[got[chip] for chip in order[1]])
            far_pieces, other_near = barrier(([second_round[chip] for chip in order[0]], swap_cores(near_pieces)))
            other_far = [swap_cores(part) for part in far_pieces]
            args = (near_pieces, *far_pieces, other_near, *other_far)
        else:
            corner = swap(column, x | y | z)
            other = {chip: swap_cores(part) for chip, part in got.items()}
            got |= second_round
            got, corner, outer = barrier((got, corner, lax.ppermute(outer, "clu", halo_pairs)))
            got[x | y | z] = corner
            other |= {chip: swap_cores(got[chip]) for chip in order[0]}
            args = [got[chip] for chip in range(chips)] + [other[chip] for chip in range(chips)]
        keep_long, keep, send_long, send = couple(with_coeffs, source_rows, target_rows, coupling, *args)

        corner, xy, yz, zx = far_add(keep_long, swap_cores(send_long))
        corner, xy, yz, zx, send = barrier((corner, xy, yz, zx, send))
        arrived = [swap(xy, y), swap(yz, z), swap(zx, x)]
        if not with_coeffs:
            arrived.append(swap(corner, y | z))
        arrived, swapped = barrier((arrived, swap_cores(send)))
        (own, *sums), inner, outer = barrier((middle_add(keep, swapped, *arrived), inner, outer))
        ways = (x, y, z)
        if with_coeffs:
            sums, ways = sums + [corner], ways + (x | y | z,)
            outer = lax.ppermute(outer, "clu", halo_pairs)
        parts = [swap(part, way) for part, way in zip(sums, ways)]
        own, parts, inner, outer = barrier((own, parts, inner, outer))
        total, *away = last_add(own, *parts)
        edges = edge(swap_cores(inner), swap_cores(outer), near_field, near_field)
        terms, edges = barrier(([swap_far(part, s + 1) for s, part in enumerate(away)], edges))
        return finish(with_coeffs)(ranks, near_sum, edges, basis, transfer, total, *terms)

    first, *second_args, values = apply_matrix(charges, first_coeffs, inner, outer, coupling, True)
    (second,) = apply_matrix(values, *second_args, coupling, False)
    return (first, second)


def solution(mesh):
    in_specs = (
        P("clu", None, None),
        P("clu", None, None),
        P("clu", None, None),
        P("clu", None, None, None),
        P("clu", None, None),
        P("clu"),
        P("clu"),
        P("clu"),
    )
    out_specs = (P("clu", None, None), P("clu", None, None))
    return jax.shard_map(local, mesh=mesh, in_specs=in_specs, out_specs=out_specs, check_vma=False)
```

```python
import functools

import jax
import jax.numpy as jnp
import numpy as np
from jax import lax
from jax.experimental import pallas as pl
from jax.experimental.pallas import tpu as pltpu
from jax.sharding import PartitionSpec as P

LANES = 128
CORES, CHIPS = 2, 8
BF = jnp.bfloat16
F32 = jnp.float32
VMEM = pl.BlockSpec(memory_space=pltpu.VMEM)
SMEM = pl.BlockSpec(memory_space=pltpu.SMEM)
HBM = pl.BlockSpec(memory_space=pltpu.HBM)


def dot(a, b):
    return lax.dot_general(a, b, (((1,), (0,)), ((), ())), preferred_element_type=F32)


def dot_t(a, b):
    return lax.dot_general(a, b, (((1,), (1,)), ((), ())), preferred_element_type=F32)


def lanes(rows):
    return lax.broadcasted_iota(jnp.int32, (rows, LANES), 1)


def fourth(tiles, rank_top):
    third = LANES - rank_top
    lane = lanes(tiles[0].shape[0])
    moved = [pltpu.roll(tile, third * (k + 1), 1) for k, tile in enumerate(tiles)]
    return jnp.where(lane < third, moved[0], jnp.where(lane < 2 * third, moved[1], moved[2]))


def packed(mains, pad, rank_top):
    lane = lanes(pad.shape[0])
    third = LANES - rank_top
    return [
        jnp.where(lane < rank_top, main, pltpu.roll(pad, rank_top - third * k, 1)) for k, main in enumerate(mains)
    ]


def widen(value):
    return jnp.concatenate([value, jnp.zeros((value.shape[0], LANES - value.shape[1]), value.dtype)], axis=1)


def emit_coeffs(values, basis_ref, transfer_ref, ranks_ref, out_ref, ready=None):
    mains, rhs, _ = out_ref.shape
    leaves, rank_top, _ = basis_ref.shape
    lane = lax.broadcasted_iota(jnp.int32, (rhs, rank_top), 1)
    coeffs = []
    for i in range(leaves):
        value = dot_t(values[i], basis_ref[i])
        coeffs.append(jnp.where(lane < ranks_ref[i], value, 0.0).astype(BF))
    if ready is not None:
        ready()
    for q in range(leaves // 2):
        value = dot(coeffs[2 * q], transfer_ref[2 * q]) + dot(coeffs[2 * q + 1], transfer_ref[2 * q + 1])
        coeffs.append(jnp.where(lane < ranks_ref[leaves + q], value, 0.0).astype(BF))
    wide = [widen(value.astype(F32)) for value in coeffs]
    for q in range(mains // 3):
        for k, tile in enumerate(packed(wide[3 * q : 3 * q + 3], wide[mains + q], rank_top)):
            out_ref[3 * q + k] = tile.astype(BF)


def fetch(pairs, sems):
    copies = [pltpu.make_async_copy(src, dst, sems.at[n]) for n, (src, dst) in enumerate(pairs)]
    for copy in copies:
        copy.start()
    return copies


def emit_edges(v_ref, inner_ref, outer_ref):
    head, tail = v_ref[0], v_ref[v_ref.shape[0] - 1]
    even = lax.axis_index("clu") % CORES == 0
    inner_ref[0] = jnp.where(even, tail, head)
    outer_ref[0] = jnp.where(even, head, tail)


def coeff_kernel(
    ranks_ref, v_hbm, basis_hbm, transfer_hbm, out_ref, inner_ref, outer_ref, v_ref, basis_ref, transfer_ref, sems
):
    leaves = basis_ref.shape[0]
    copies = fetch([(v_hbm, v_ref), (basis_hbm, basis_ref), (transfer_hbm, transfer_ref)], sems)
    copies[0].wait()
    emit_edges(v_ref, inner_ref, outer_ref)
    copies[1].wait()
    values = [v_ref[i] for i in range(leaves)]
    emit_coeffs(values, basis_ref, transfer_ref, ranks_ref, out_ref, copies[2].wait)


def couple_kernel(source_ref, target_ref, coupling_ref, *refs, order, distant, joined, unroll):
    chips = sum(len(group) for group in order)
    in_refs, out_refs, (sources, total) = refs[: -2 - 2 * len(order)], refs[-2 - 2 * len(order) : -2], refs[-2:]
    blocks, rank_top, _ = coupling_ref.shape
    far, mains, rhs, _ = in_refs[-1].shape
    if joined:
        cores, in_refs = (in_refs[: len(in_refs) // 2], in_refs[len(in_refs) // 2 :]), []
        for near_pieces, *far_pieces in cores:
            pieces = {chip: near_pieces.at[place] for place, chip in enumerate(order[-1])}
            pieces |= dict(zip(distant, far_pieces))
            in_refs += [pieces[chip] for chip in range(chips)]
    quads = mains // 3
    clusters = mains + quads

    def split(f, _):
        for n, packed_ref in enumerate(in_refs):
            row = (n * far + f) * clusters
            tiles = [packed_ref[f, c] for c in range(mains)]
            for c in range(mains):
                sources[row + c] = tiles[c]
            for q in range(quads):
                wide = [tile.astype(F32) for tile in tiles[3 * q : 3 * q + 3]]
                sources[row + mains + q] = fourth(wide, rank_top).astype(BF)
            for c in range(clusters):
                total[row + c] = jnp.zeros((rhs, LANES), F32)
        return 0

    lax.fori_loop(0, far, split, 0)

    def some(s, _):
        for u in range(unroll):
            j = s * unroll + u
            term = dot(sources[source_ref[j], :, :rank_top], coupling_ref[j])
            at = target_ref[j]
            total[at, :, :rank_top] = total[at, :, :rank_top] + term
        return 0

    lax.fori_loop(0, blocks // unroll, some, 0)

    def pack(f, _):
        for core in range(2):
            for g, group in enumerate(order):
                for place, chip in enumerate(group):
                    row = ((core * chips + chip) * far + f) * clusters
                    for q in range(quads):
                        mains_now = [total[row + 3 * q + k] for k in range(3)]
                        for k, tile in enumerate(packed(mains_now, total[row + mains + q], rank_top)):
                            out_refs[core * len(order) + g][place, f, 3 * q + k] = tile.astype(BF)
        return 0

    lax.fori_loop(0, far, pack, 0)


def order_kernel(_, __, out_ref):
    out_ref[...] = jnp.zeros_like(out_ref)


def near_kernel(v_ref, near_ref, out_ref):
    leaves = v_ref.shape[0]
    for i in range(leaves):
        total = dot(v_ref[i], near_ref[i, 1])
        if i > 0:
            total = total + dot(v_ref[i - 1], near_ref[i, 0])
        if i < leaves - 1:
            total = total + dot(v_ref[i + 1], near_ref[i, 2])
        out_ref[i] = total


def edge_kernel(inner_ref, outer_ref, first_ref, last_ref, out_ref):
    inner, outer = inner_ref[0], outer_ref[0]
    even = lax.axis_index("clu") % CORES == 0
    out_ref[0] = dot(jnp.where(even, outer, inner), first_ref[0, 0])
    out_ref[1] = dot(jnp.where(even, inner, outer), last_ref[0, 0])


def add_kernel(keep_ref, swap_ref, *out_refs):
    for n, out_ref in enumerate(out_refs):
        out_ref[...] = (keep_ref[n].astype(F32) + swap_ref[n].astype(F32)).astype(out_ref.dtype)


def middle_add_kernel(keep_ref, swap_ref, *refs, parts):
    part_refs, (own_out, *out_refs) = refs[:parts], refs[parts:]
    own_out[...] = keep_ref[0].astype(F32) + swap_ref[0].astype(F32)
    for n, out_ref in enumerate(out_refs):
        total = keep_ref[n + 1].astype(F32) + swap_ref[n + 1].astype(F32)
        for part_ref in part_refs[n :: len(out_refs)]:
            total = total + part_ref[...].astype(F32)
        out_ref[...] = total.astype(BF)


def rows_kernel(source_ref, target_ref, source_out, target_out, *, clusters, far, magic, shift):
    me = lax.axis_index("clu")
    for sign, in_ref, out_ref in ((-1, source_ref, source_out), (1, target_ref, target_out)):
        cluster = in_ref[...]
        device = cluster * magic >> shift
        chip = ((device ^ me) >> 1) & (CHIPS - 1)
        chip = jnp.where((device & 1) == 0, chip, chip >> 1 | (chip & 1) << 2)
        away = (sign * ((device >> 4) - (me >> 4))) & (far - 1)
        core = (device ^ me) & 1
        out_ref[...] = ((core * CHIPS + chip) * far + away) * clusters + cluster - device * clusters


def join_kernel(*refs):
    for n, part_ref in enumerate(refs[:-1]):
        refs[-1][n] = part_ref[...]


def last_add_kernel(own_ref, *refs, parts):
    part_refs, (keep_out, *away_refs) = refs[:parts], refs[parts:]
    for f in range(own_ref.shape[0]):
        total = own_ref[f]
        for part_ref in part_refs:
            total = total + part_ref[f].astype(F32)
        if f == 0:
            keep_out[...] = total
        else:
            away_refs[f - 1][...] = total.astype(BF)


def field_kernel(ranks_ref, near_ref, edge_ref, basis_ref, transfer_ref, keep_ref, *rest, away):
    term_refs, out_ref, next_refs = rest[:away], rest[away], rest[away + 1 :]
    leaves, rank_top, _ = basis_ref.shape
    mains, rhs, _ = keep_ref.shape
    tiles = []
    for t in range(mains):
        tile = keep_ref[t]
        for term_ref in term_refs:
            tile = tile + term_ref[t].astype(F32)
        tiles.append(tile)
    sums = tiles + [fourth(tiles[3 * q : 3 * q + 3], rank_top) for q in range(mains // 3)]
    lane = lax.broadcasted_iota(jnp.int32, (rhs, rank_top), 1)
    fields = [
        jnp.where(lane < ranks_ref[c], total[:, :rank_top], 0.0).astype(BF) for c, total in enumerate(sums)
    ]
    downs = [fields[i].astype(F32) + dot_t(fields[leaves + i // 2], transfer_ref[i]) for i in range(leaves)]
    leaf_totals = [jnp.where(lane < ranks_ref[i], down, 0.0).astype(BF) for i, down in enumerate(downs)]
    results = [near_ref[i] + dot(leaf_total, basis_ref[i]) for i, leaf_total in enumerate(leaf_totals)]
    results[0] = results[0] + edge_ref[0]
    results[-1] = results[-1] + edge_ref[1]
    results = [result.astype(BF) for result in results]
    for i, result in enumerate(results):
        out_ref[i] = result
    if next_refs:
        coeff_ref, inner_ref, outer_ref, values_ref = next_refs
        for i, result in enumerate(results):
            values_ref[i] = result
        emit_edges(out_ref, inner_ref, outer_ref)
        emit_coeffs(results, basis_ref, transfer_ref, ranks_ref, coeff_ref)


def params(mebibytes):
    return pltpu.CompilerParams(vmem_limit_bytes=mebibytes << 20)


def local(charges, basis, transfer, near_field, coupling, ranks, block_source, block_target):
    leaves, rank_top, width = basis.shape
    rhs = charges.shape[1]
    clusters = ranks.shape[0]
    blocks = coupling.shape[0]
    devices = lax.axis_size("clu")
    mains = clusters * 3 // 4
    shape = jax.ShapeDtypeStruct

    cores, chips = CORES, CHIPS
    cube = cores * chips
    far = devices // cube
    x, y, z = 1, 2, 4

    def swap_far(part, shift):
        return lax.ppermute(part, "clu", [(d, (d + shift * cube) % devices) for d in range(devices)])

    def swap(part, direction):
        turned = direction << 1 & 7 | direction >> 2
        return lax.ppermute(
            part, "clu", [(d, d ^ (turned if d % cores else direction) * cores) for d in range(devices)]
        )

    def swap_cores(part):
        return lax.ppermute(part, "clu", [(d, d ^ 1) for d in range(devices)])

    barrier = lax.optimization_barrier

    shift = 19
    magic = -(-(1 << shift) // clusters)
    numbers = np.arange(devices * clusters)
    assert (numbers * magic >> shift == numbers // clusters).all() and far & far - 1 == 0
    list_shape = jax.ShapeDtypeStruct((1, blocks), jnp.int32)
    source_rows, target_rows = pl.pallas_call(
        functools.partial(rows_kernel, clusters=clusters, far=far, magic=magic, shift=shift),
        out_shape=[list_shape] * 2,
        in_specs=[VMEM] * 2,
        out_specs=[VMEM] * 2,
        compiler_params=params(1),
    )(block_source.reshape(1, blocks), block_target.reshape(1, blocks))
    source_rows, target_rows = source_rows.reshape(blocks), target_rows.reshape(blocks)

    tile_shape = (mains, rhs, LANES)
    out_shape = shape((leaves, rhs, width), BF)
    tile_out = shape(tile_shape, BF)
    part_shape = shape((far,) + tile_shape, BF)
    edge_shape = shape((1, rhs, width), BF)
    first_coeffs, inner, outer = pl.pallas_call(
        coeff_kernel,
        out_shape=[tile_out, edge_shape, edge_shape],
        in_specs=[SMEM, HBM, HBM, HBM],
        out_specs=[VMEM] * 3,
        scratch_shapes=[
            pltpu.VMEM(charges.shape, BF),
            pltpu.VMEM(basis.shape, BF),
            pltpu.VMEM(transfer.shape, BF),
            pltpu.SemaphoreType.DMA((3,)),
        ],
    )(ranks, charges, basis, transfer)

    distant = (x | y, y | z, z | x, x | y | z)
    order = (distant[:2], distant[2:], (0, x, y, z))
    def couple(joined, *args):
        return pl.pallas_call(
            functools.partial(couple_kernel, order=order, distant=distant, joined=joined, unroll=blocks),
            out_shape=[shape((len(group), far) + tile_shape, BF) for group in order] * cores,
            in_specs=[SMEM, SMEM] + [VMEM] * (len(args) - 2),
            out_specs=[VMEM] * (cores * len(order)),
            scratch_shapes=[
                pltpu.VMEM((devices * clusters, rhs, LANES), BF),
                pltpu.VMEM((devices * clusters, rhs, LANES), F32),
            ],
            compiler_params=params(24 if devices <= 32 else 60),
            cost_estimate=pl.CostEstimate(
                flops=2 * blocks * rhs * rank_top * rank_top, bytes_accessed=10 << 20, transcendentals=0
            ),
        )(*args)

    near = pl.pallas_call(
        near_kernel,
        out_shape=shape((leaves, rhs, width), F32),
        in_specs=[VMEM, VMEM],
        out_specs=VMEM,
        compiler_params=params(16),
        cost_estimate=pl.CostEstimate(
            flops=2 * leaves * 3 * rhs * width * width, bytes_accessed=4 << 20, transcendentals=0
        ),
    )

    edge = pl.pallas_call(
        edge_kernel,
        out_shape=shape((2, rhs, width), F32),
        grid=(1,),
        in_specs=[
            VMEM,
            VMEM,
            pl.BlockSpec((1, 1, width, width), lambda i: (0, 0, 0, 0)),
            pl.BlockSpec((1, 1, width, width), lambda i: (leaves - 1, 2, 0, 0)),
        ],
        out_specs=VMEM,
        compiler_params=params(16),
    )

    def adder(kernel, inputs, outputs):
        return pl.pallas_call(
            kernel,
            out_shape=outputs,
            in_specs=[VMEM] * inputs,
            out_specs=[VMEM] * len(outputs),
            compiler_params=params(16),
        )

    own_shape = shape((far,) + tile_shape, F32)
    join = adder(join_kernel, far, [part_shape])
    relaid = pl.pallas_call(
        order_kernel,
        out_shape=shape((8, LANES), F32),
        in_specs=[pl.BlockSpec(memory_space=pl.ANY)] * 2,
        out_specs=VMEM,
    )
    first_join = pl.pallas_call(
        lambda _, *refs: join_kernel(*refs),
        out_shape=[part_shape],
        in_specs=[pl.BlockSpec(memory_space=pl.ANY)] + [VMEM] * far,
        out_specs=[VMEM],
        compiler_params=params(16),
    )
    far_add = adder(add_kernel, 2, [part_shape] * 2)
    join_near = adder(join_kernel, 4, [shape((4,) + part_shape.shape, BF)])

    def middle_add(*args):
        kernel = functools.partial(middle_add_kernel, parts=len(args) - 2)
        return adder(kernel, len(args), [own_shape] + [part_shape] * 3)(*args)

    def last_add(*args):
        kernel = functools.partial(last_add_kernel, parts=len(args) - 1)
        return adder(kernel, len(args), [shape(tile_shape, F32)] + [tile_out] * (far - 1))(*args)

    def finish(with_coeffs):
        return pl.pallas_call(
            functools.partial(field_kernel, away=far - 1),
            out_shape=[out_shape, tile_out, edge_shape, edge_shape, out_shape] if with_coeffs else [out_shape],
            in_specs=[SMEM] + [VMEM] * (4 + far),
            out_specs=[VMEM] * 5 if with_coeffs else [VMEM],
            compiler_params=params(16),
        )

    halo_pairs = [(d, d + cores) for d in range(1, devices - cores, cores)]
    halo_pairs += [(d, d - cores) for d in range(cores, devices, cores)]

    def apply_matrix(field_in, coeffs, inner, outer, coupling, with_coeffs):
        away = [swap_far(coeffs, s) for s in range(1, far)]
        (column,) = first_join(relaid(coupling, coeffs), coeffs, *away) if with_coeffs else join(coeffs, *away)
        got = {0: column, x: swap(column, x), y: swap(column, y), z: swap(column, z)}
        near_sum = near(field_in, near_field)
        got, near_sum = barrier((got, near_sum))
        second_round = {x | y: swap(got[x], y), y | z: swap(got[y], z), z | x: swap(got[z], x)}
        if with_coeffs:
            second_round[x | y | z] = swap(got[x], y | z)
            (near_pieces,) = join_near(*[got[chip] for chip in order[-1]])
            far_pieces, other_near = barrier(([second_round[chip] for chip in distant], swap_cores(near_pieces)))
            other_far = [swap_cores(part) for part in far_pieces]
            args = (near_pieces, *far_pieces, other_near, *other_far)
        else:
            corner = swap(column, x | y | z)
            other = {chip: swap_cores(part) for chip, part in got.items()}
            got |= second_round
            got, corner, outer = barrier((got, corner, lax.ppermute(outer, "clu", halo_pairs)))
            got[x | y | z] = corner
            other |= {chip: swap_cores(got[chip]) for chip in distant}
            args = [got[chip] for chip in range(chips)] + [other[chip] for chip in range(chips)]
        totals = couple(with_coeffs, source_rows, target_rows, coupling, *args)
        *keep_far, keep, send_first, send_second, send = totals

        xy, yz = far_add(keep_far[0], swap_cores(send_first))
        zx, corner = far_add(keep_far[1], swap_cores(send_second))
        xy, yz, send = barrier((xy, yz, send))
        arrived = [swap(xy, y), swap(yz, z), swap(zx, x)]
        if not with_coeffs:
            arrived.append(swap(corner, y | z))
        arrived, swapped = barrier((arrived, swap_cores(send)))
        (own, *sums), inner, outer = barrier((middle_add(keep, swapped, *arrived), inner, outer))
        ways = (x, y, z)
        if with_coeffs:
            sums, ways = sums + [corner], ways + (x | y | z,)
            outer = lax.ppermute(outer, "clu", halo_pairs)
        parts = [swap(part, way) for part, way in zip(sums, ways)]
        own, parts, inner, outer = barrier((own, parts, inner, outer))
        total, *away = last_add(own, *parts)
        edges = edge(swap_cores(inner), swap_cores(outer), near_field, near_field)
        terms, edges = barrier(([swap_far(part, s + 1) for s, part in enumerate(away)], edges))
        return finish(with_coeffs)(ranks, near_sum, edges, basis, transfer, total, *terms)

    first, *second_args, values = apply_matrix(charges, first_coeffs, inner, outer, coupling, True)
    (second,) = apply_matrix(values, *second_args, coupling, False)
    return (first, second)


def solution(mesh):
    in_specs = (
        P("clu", None, None),
        P("clu", None, None),
        P("clu", None, None),
        P("clu", None, None, None),
        P("clu", None, None),
        P("clu"),
        P("clu"),
        P("clu"),
    )
    out_specs = (P("clu", None, None), P("clu", None, None))
    return jax.shard_map(local, mesh=mesh, in_specs=in_specs, out_specs=out_specs, check_vma=False)
```

```python
import functools

import jax
import jax.numpy as jnp
import numpy as np
from jax import lax
from jax.experimental import pallas as pl
from jax.experimental.pallas import tpu as pltpu
from jax.sharding import PartitionSpec as P

LANES = 128
CORES, CHIPS = 2, 8
BF = jnp.bfloat16
F32 = jnp.float32
VMEM = pl.BlockSpec(memory_space=pltpu.VMEM)
SMEM = pl.BlockSpec(memory_space=pltpu.SMEM)
HBM = pl.BlockSpec(memory_space=pltpu.HBM)


def dot(a, b):
    return lax.dot_general(a, b, (((1,), (0,)), ((), ())), preferred_element_type=F32)


def dot_t(a, b):
    return lax.dot_general(a, b, (((1,), (1,)), ((), ())), preferred_element_type=F32)


def lanes(rows):
    return lax.broadcasted_iota(jnp.int32, (rows, LANES), 1)


def fourth(tiles, rank_top):
    third = LANES - rank_top
    lane = lanes(tiles[0].shape[0])
    moved = [pltpu.roll(tile, third * (k + 1), 1) for k, tile in enumerate(tiles)]
    return jnp.where(lane < third, moved[0], jnp.where(lane < 2 * third, moved[1], moved[2]))


def packed(mains, pad, rank_top):
    lane = lanes(pad.shape[0])
    third = LANES - rank_top
    return [
        jnp.where(lane < rank_top, main, pltpu.roll(pad, rank_top - third * k, 1)) for k, main in enumerate(mains)
    ]


def widen(value):
    return jnp.concatenate([value, jnp.zeros((value.shape[0], LANES - value.shape[1]), value.dtype)], axis=1)


def emit_coeffs(values, basis_ref, transfer_ref, ranks_ref, out_ref, ready=None):
    mains, rhs, _ = out_ref.shape
    leaves, rank_top, _ = basis_ref.shape
    lane = lax.broadcasted_iota(jnp.int32, (rhs, rank_top), 1)
    coeffs = []
    for i in range(leaves):
        value = dot_t(values[i], basis_ref[i])
        coeffs.append(jnp.where(lane < ranks_ref[i], value, 0.0).astype(BF))
    if ready is not None:
        ready()
    for q in range(leaves // 2):
        value = dot(coeffs[2 * q], transfer_ref[2 * q]) + dot(coeffs[2 * q + 1], transfer_ref[2 * q + 1])
        coeffs.append(jnp.where(lane < ranks_ref[leaves + q], value, 0.0).astype(BF))
    wide = [widen(value.astype(F32)) for value in coeffs]
    for q in range(mains // 3):
        for k, tile in enumerate(packed(wide[3 * q : 3 * q + 3], wide[mains + q], rank_top)):
            out_ref[3 * q + k] = tile.astype(BF)


def fetch(pairs, sems):
    copies = [pltpu.make_async_copy(src, dst, sems.at[n]) for n, (src, dst) in enumerate(pairs)]
    for copy in copies:
        copy.start()
    return copies


def emit_edges(v_ref, inner_ref, outer_ref):
    head, tail = v_ref[0], v_ref[v_ref.shape[0] - 1]
    even = lax.axis_index("clu") % CORES == 0
    inner_ref[0] = jnp.where(even, tail, head)
    outer_ref[0] = jnp.where(even, head, tail)


def coeff_kernel(
    ranks_ref, v_hbm, basis_hbm, transfer_hbm, out_ref, inner_ref, outer_ref, v_ref, basis_ref, transfer_ref, sems
):
    leaves = basis_ref.shape[0]
    copies = fetch([(v_hbm, v_ref), (basis_hbm, basis_ref), (transfer_hbm, transfer_ref)], sems)
    copies[0].wait()
    emit_edges(v_ref, inner_ref, outer_ref)
    copies[1].wait()
    values = [v_ref[i] for i in range(leaves)]
    emit_coeffs(values, basis_ref, transfer_ref, ranks_ref, out_ref, copies[2].wait)


def couple_kernel(source_ref, target_ref, coupling_ref, *refs, order, joined, unroll):
    chips = sum(len(group) for group in order)
    in_refs, out_refs, (sources, total) = refs[: -2 - 2 * len(order)], refs[-2 - 2 * len(order) : -2], refs[-2:]
    blocks, rank_top, _ = coupling_ref.shape
    far, mains, rhs, _ = in_refs[-1].shape
    if joined:
        cores, in_refs = (in_refs[: len(in_refs) // 2], in_refs[len(in_refs) // 2 :]), []
        for near_pieces, *far_pieces in cores:
            pieces = {chip: near_pieces.at[place] for place, chip in enumerate(order[1])}
            pieces |= dict(zip(order[0], far_pieces))
            in_refs += [pieces[chip] for chip in range(chips)]
    quads = mains // 3
    clusters = mains + quads

    def split(f, _):
        for n, packed_ref in enumerate(in_refs):
            row = (n * far + f) * clusters
            tiles = [packed_ref[f, c] for c in range(mains)]
            for c in range(mains):
                sources[row + c] = tiles[c]
            for q in range(quads):
                wide = [tile.astype(F32) for tile in tiles[3 * q : 3 * q + 3]]
                sources[row + mains + q] = fourth(wide, rank_top).astype(BF)
            for c in range(clusters):
                total[row + c] = jnp.zeros((rhs, LANES), F32)
        return 0

    lax.fori_loop(0, far, split, 0)

    def some(s, _):
        for u in range(unroll):
            j = s * unroll + u
            term = dot(sources[source_ref[j], :, :rank_top], coupling_ref[j])
            at = target_ref[j]
            total[at, :, :rank_top] = total[at, :, :rank_top] + term
        return 0

    lax.fori_loop(0, blocks // unroll, some, 0)

    def pack(f, _):
        for core in range(2):
            for g, group in enumerate(order):
                for place, chip in enumerate(group):
                    row = ((core * chips + chip) * far + f) * clusters
                    for q in range(quads):
                        mains_now = [total[row + 3 * q + k] for k in range(3)]
                        for k, tile in enumerate(packed(mains_now, total[row + mains + q], rank_top)):
                            out_refs[core * len(order) + g][place, f, 3 * q + k] = tile.astype(BF)
        return 0

    lax.fori_loop(0, far, pack, 0)


def order_kernel(_, __, out_ref):
    out_ref[...] = jnp.zeros_like(out_ref)


def near_kernel(v_ref, near_ref, out_ref):
    leaves = v_ref.shape[0]
    for i in range(leaves):
        total = dot(v_ref[i], near_ref[i, 1])
        if i > 0:
            total = total + dot(v_ref[i - 1], near_ref[i, 0])
        if i < leaves - 1:
            total = total + dot(v_ref[i + 1], near_ref[i, 2])
        out_ref[i] = total


def edge_kernel(inner_ref, outer_ref, first_ref, last_ref, out_ref):
    inner, outer = inner_ref[0], outer_ref[0]
    even = lax.axis_index("clu") % CORES == 0
    out_ref[0] = dot(jnp.where(even, outer, inner), first_ref[0, 0])
    out_ref[1] = dot(jnp.where(even, inner, outer), last_ref[0, 0])


def add_kernel(keep_ref, swap_ref, *out_refs):
    for n, out_ref in enumerate(out_refs):
        out_ref[...] = (keep_ref[n].astype(F32) + swap_ref[n].astype(F32)).astype(out_ref.dtype)


def middle_add_kernel(keep_ref, swap_ref, *refs, parts):
    part_refs, (own_out, *out_refs) = refs[:parts], refs[parts:]
    own_out[...] = keep_ref[0].astype(F32) + swap_ref[0].astype(F32)
    for n, out_ref in enumerate(out_refs):
        total = keep_ref[n + 1].astype(F32) + swap_ref[n + 1].astype(F32)
        for part_ref in part_refs[n :: len(out_refs)]:
            total = total + part_ref[...].astype(F32)
        out_ref[...] = total.astype(BF)


def rows_kernel(source_ref, target_ref, source_out, target_out, *, clusters, far, magic, shift):
    me = lax.axis_index("clu")
    for sign, in_ref, out_ref in ((-1, source_ref, source_out), (1, target_ref, target_out)):
        cluster = in_ref[...]
        device = cluster * magic >> shift
        chip = ((device ^ me) >> 1) & (CHIPS - 1)
        chip = jnp.where((device & 1) == 0, chip, chip >> 1 | (chip & 1) << 2)
        away = (sign * ((device >> 4) - (me >> 4))) & (far - 1)
        core = (device ^ me) & 1
        out_ref[...] = ((core * CHIPS + chip) * far + away) * clusters + cluster - device * clusters


def join_kernel(*refs):
    for n, part_ref in enumerate(refs[:-1]):
        refs[-1][n] = part_ref[...]


def last_add_kernel(own_ref, *refs, parts):
    part_refs, (keep_out, *away_refs) = refs[:parts], refs[parts:]
    for f in range(own_ref.shape[0]):
        total = own_ref[f]
        for part_ref in part_refs:
            total = total + part_ref[f].astype(F32)
        if f == 0:
            keep_out[...] = total
        else:
            away_refs[f - 1][...] = total.astype(BF)


def field_kernel(ranks_ref, near_ref, edge_ref, basis_ref, transfer_ref, keep_ref, *rest, away):
    term_refs, out_ref, next_refs = rest[:away], rest[away], rest[away + 1 :]
    leaves, rank_top, _ = basis_ref.shape
    mains, rhs, _ = keep_ref.shape
    tiles = []
    for t in range(mains):
        tile = keep_ref[t]
        for term_ref in term_refs:
            tile = tile + term_ref[t].astype(F32)
        tiles.append(tile)
    sums = tiles + [fourth(tiles[3 * q : 3 * q + 3], rank_top) for q in range(mains // 3)]
    lane = lax.broadcasted_iota(jnp.int32, (rhs, rank_top), 1)
    fields = [
        jnp.where(lane < ranks_ref[c], total[:, :rank_top], 0.0).astype(BF) for c, total in enumerate(sums)
    ]
    downs = [fields[i].astype(F32) + dot_t(fields[leaves + i // 2], transfer_ref[i]) for i in range(leaves)]
    leaf_totals = [jnp.where(lane < ranks_ref[i], down, 0.0).astype(BF) for i, down in enumerate(downs)]
    results = [near_ref[i] + dot(leaf_total, basis_ref[i]) for i, leaf_total in enumerate(leaf_totals)]
    results[0] = results[0] + edge_ref[0]
    results[-1] = results[-1] + edge_ref[1]
    results = [result.astype(BF) for result in results]
    for i, result in enumerate(results):
        out_ref[i] = result
    if next_refs:
        coeff_ref, inner_ref, outer_ref, values_ref = next_refs
        for i, result in enumerate(results):
            values_ref[i] = result
        emit_edges(out_ref, inner_ref, outer_ref)
        emit_coeffs(results, basis_ref, transfer_ref, ranks_ref, coeff_ref)


def params(mebibytes):
    return pltpu.CompilerParams(vmem_limit_bytes=mebibytes << 20)


def local(charges, basis, transfer, near_field, coupling, ranks, block_source, block_target):
    leaves, rank_top, width = basis.shape
    rhs = charges.shape[1]
    clusters = ranks.shape[0]
    blocks = coupling.shape[0]
    devices = lax.axis_size("clu")
    mains = clusters * 3 // 4
    shape = jax.ShapeDtypeStruct

    cores, chips = CORES, CHIPS
    cube = cores * chips
    far = devices // cube
    x, y, z = 1, 2, 4

    def swap_far(part, shift):
        return lax.ppermute(part, "clu", [(d, (d + shift * cube) % devices) for d in range(devices)])

    def swap(part, direction):
        turned = direction << 1 & 7 | direction >> 2
        return lax.ppermute(
            part, "clu", [(d, d ^ (turned if d % cores else direction) * cores) for d in range(devices)]
        )

    def swap_cores(part):
        return lax.ppermute(part, "clu", [(d, d ^ 1) for d in range(devices)])

    barrier = lax.optimization_barrier

    shift = 19
    magic = -(-(1 << shift) // clusters)
    numbers = np.arange(devices * clusters)
    assert (numbers * magic >> shift == numbers // clusters).all() and far & far - 1 == 0
    list_shape = jax.ShapeDtypeStruct((1, blocks), jnp.int32)
    source_rows, target_rows = pl.pallas_call(
        functools.partial(rows_kernel, clusters=clusters, far=far, magic=magic, shift=shift),
        out_shape=[list_shape] * 2,
        in_specs=[VMEM] * 2,
        out_specs=[VMEM] * 2,
        compiler_params=params(1),
    )(block_source.reshape(1, blocks), block_target.reshape(1, blocks))
    source_rows, target_rows = source_rows.reshape(blocks), target_rows.reshape(blocks)

    tile_shape = (mains, rhs, LANES)
    out_shape = shape((leaves, rhs, width), BF)
    tile_out = shape(tile_shape, BF)
    part_shape = shape((far,) + tile_shape, BF)
    edge_shape = shape((1, rhs, width), BF)
    first_coeffs, inner, outer = pl.pallas_call(
        coeff_kernel,
        out_shape=[tile_out, edge_shape, edge_shape],
        in_specs=[SMEM, HBM, HBM, HBM],
        out_specs=[VMEM] * 3,
        scratch_shapes=[
            pltpu.VMEM(charges.shape, BF),
            pltpu.VMEM(basis.shape, BF),
            pltpu.VMEM(transfer.shape, BF),
            pltpu.SemaphoreType.DMA((3,)),
        ],
    )(ranks, charges, basis, transfer)

    order = ((x | y | z, x | y, y | z, z | x), (0, x, y, z))
    def couple(joined, *args):
        return pl.pallas_call(
            functools.partial(couple_kernel, order=order, joined=joined, unroll=blocks),
            out_shape=[shape((4, far) + tile_shape, BF)] * 4,
            in_specs=[SMEM, SMEM] + [VMEM] * (len(args) - 2),
            out_specs=[VMEM] * 4,
            scratch_shapes=[
                pltpu.VMEM((devices * clusters, rhs, LANES), BF),
                pltpu.VMEM((devices * clusters, rhs, LANES), F32),
            ],
            compiler_params=params(24 if devices <= 32 else 60),
            cost_estimate=pl.CostEstimate(
                flops=2 * blocks * rhs * rank_top * rank_top, bytes_accessed=10 << 20, transcendentals=0
            ),
        )(*args)

    near = pl.pallas_call(
        near_kernel,
        out_shape=shape((leaves, rhs, width), F32),
        in_specs=[VMEM, VMEM],
        out_specs=VMEM,
        compiler_params=params(16),
        cost_estimate=pl.CostEstimate(
            flops=2 * leaves * 3 * rhs * width * width, bytes_accessed=4 << 20, transcendentals=0
        ),
    )

    edge = pl.pallas_call(
        edge_kernel,
        out_shape=shape((2, rhs, width), F32),
        grid=(1,),
        in_specs=[
            VMEM,
            VMEM,
            pl.BlockSpec((1, 1, width, width), lambda i: (0, 0, 0, 0)),
            pl.BlockSpec((1, 1, width, width), lambda i: (leaves - 1, 2, 0, 0)),
        ],
        out_specs=VMEM,
        compiler_params=params(16),
    )

    def adder(kernel, inputs, outputs):
        return pl.pallas_call(
            kernel,
            out_shape=outputs,
            in_specs=[VMEM] * inputs,
            out_specs=[VMEM] * len(outputs),
            compiler_params=params(16),
        )

    own_shape = shape((far,) + tile_shape, F32)
    join = adder(join_kernel, far, [part_shape])
    relaid = pl.pallas_call(
        order_kernel,
        out_shape=shape((8, LANES), F32),
        in_specs=[pl.BlockSpec(memory_space=pl.ANY)] * 2,
        out_specs=VMEM,
    )
    first_join = pl.pallas_call(
        lambda _, *refs: join_kernel(*refs),
        out_shape=[part_shape],
        in_specs=[pl.BlockSpec(memory_space=pl.ANY)] + [VMEM] * far,
        out_specs=[VMEM],
        compiler_params=params(16),
    )
    far_add = adder(add_kernel, 2, [part_shape] * 4)
    join_near = adder(join_kernel, 4, [shape((4,) + part_shape.shape, BF)])

    def middle_add(*args):
        kernel = functools.partial(middle_add_kernel, parts=len(args) - 2)
        return adder(kernel, len(args), [own_shape] + [part_shape] * 3)(*args)

    def last_add(*args):
        kernel = functools.partial(last_add_kernel, parts=len(args) - 1)
        return adder(kernel, len(args), [shape(tile_shape, F32)] + [tile_out] * (far - 1))(*args)

    def finish(with_coeffs):
        return pl.pallas_call(
            functools.partial(field_kernel, away=far - 1),
            out_shape=[out_shape, tile_out, edge_shape, edge_shape, out_shape] if with_coeffs else [out_shape],
            in_specs=[SMEM] + [VMEM] * (4 + far),
            out_specs=[VMEM] * 5 if with_coeffs else [VMEM],
            compiler_params=params(16),
        )

    halo_pairs = [(d, d + cores) for d in range(1, devices - cores, cores)]
    halo_pairs += [(d, d - cores) for d in range(cores, devices, cores)]

    def apply_matrix(field_in, coeffs, inner, outer, coupling, with_coeffs):
        away = [swap_far(coeffs, s) for s in range(1, far)]
        if not with_coeffs:
            away, outer = barrier((away, lax.ppermute(outer, "clu", halo_pairs)))
        (column,) = first_join(relaid(coupling, coeffs), coeffs, *away) if with_coeffs else join(coeffs, *away)
        got = {0: column, x: swap(column, x), y: swap(column, y), z: swap(column, z)}
        near_sum = near(field_in, near_field)
        got, near_sum = barrier((got, near_sum))
        second_round = {x | y: swap(got[x], y), y | z: swap(got[y], z), z | x: swap(got[z], x)}
        if with_coeffs:
            second_round[x | y | z] = swap(got[x], y | z)
            (near_pieces,) = join_near(*[got[chip] for chip in order[1]])
            far_pieces, other_near = barrier(([second_round[chip] for chip in order[0]], swap_cores(near_pieces)))
            other_far = [swap_cores(part) for part in far_pieces]
            args = (near_pieces, *far_pieces, other_near, *other_far)
        else:
            corner = swap(column, x | y | z)
            other = {chip: swap_cores(part) for chip, part in got.items()}
            got |= second_round
            got, corner = barrier((got, corner))
            got[x | y | z] = corner
            other |= {chip: swap_cores(got[chip]) for chip in order[0]}
            args = [got[chip] for chip in range(chips)] + [other[chip] for chip in range(chips)]
        keep_long, keep, send_long, send = couple(with_coeffs, source_rows, target_rows, coupling, *args)

        corner, xy, yz, zx = far_add(keep_long, swap_cores(send_long))
        corner, xy, yz, zx, send = barrier((corner, xy, yz, zx, send))
        arrived = [swap(xy, y), swap(yz, z), swap(zx, x)]
        if not with_coeffs:
            arrived.append(swap(corner, y | z))
        arrived, swapped = barrier((arrived, swap_cores(send)))
        (own, *sums), inner, outer = barrier((middle_add(keep, swapped, *arrived), inner, outer))
        ways = (x, y, z)
        if with_coeffs:
            sums, ways = sums + [corner], ways + (x | y | z,)
            outer = lax.ppermute(outer, "clu", halo_pairs)
        parts = [swap(part, way) for part, way in zip(sums, ways)]
        own, parts, inner, outer = barrier((own, parts, inner, outer))
        total, *away = last_add(own, *parts)
        edges = edge(swap_cores(inner), swap_cores(outer), near_field, near_field)
        terms, edges = barrier(([swap_far(part, s + 1) for s, part in enumerate(away)], edges))
        return finish(with_coeffs)(ranks, near_sum, edges, basis, transfer, total, *terms)

    first, *second_args, values = apply_matrix(charges, first_coeffs, inner, outer, coupling, True)
    (second,) = apply_matrix(values, *second_args, coupling, False)
    return (first, second)


def solution(mesh):
    in_specs = (
        P("clu", None, None),
        P("clu", None, None),
        P("clu", None, None),
        P("clu", None, None, None),
        P("clu", None, None),
        P("clu"),
        P("clu"),
        P("clu"),
    )
    out_specs = (P("clu", None, None), P("clu", None, None))
    return jax.shard_map(local, mesh=mesh, in_specs=in_specs, out_specs=out_specs, check_vma=False)
```

```python
import functools

import jax
import jax.numpy as jnp
import numpy as np
from jax import lax
from jax.experimental import pallas as pl
from jax.experimental.pallas import tpu as pltpu
from jax.sharding import PartitionSpec as P

LANES = 128
CORES, CHIPS = 2, 8
BF = jnp.bfloat16
F32 = jnp.float32
VMEM = pl.BlockSpec(memory_space=pltpu.VMEM)
SMEM = pl.BlockSpec(memory_space=pltpu.SMEM)
HBM = pl.BlockSpec(memory_space=pltpu.HBM)


def dot(a, b):
    return lax.dot_general(a, b, (((1,), (0,)), ((), ())), preferred_element_type=F32)


def dot_t(a, b):
    return lax.dot_general(a, b, (((1,), (1,)), ((), ())), preferred_element_type=F32)


def lanes(rows):
    return lax.broadcasted_iota(jnp.int32, (rows, LANES), 1)


def fourth(tiles, rank_top):
    third = LANES - rank_top
    lane = lanes(tiles[0].shape[0])
    moved = [pltpu.roll(tile, third * (k + 1), 1) for k, tile in enumerate(tiles)]
    return jnp.where(lane < third, moved[0], jnp.where(lane < 2 * third, moved[1], moved[2]))


def packed(mains, pad, rank_top):
    lane = lanes(pad.shape[0])
    third = LANES - rank_top
    return [
        jnp.where(lane < rank_top, main, pltpu.roll(pad, rank_top - third * k, 1)) for k, main in enumerate(mains)
    ]


def widen(value):
    return jnp.concatenate([value, jnp.zeros((value.shape[0], LANES - value.shape[1]), value.dtype)], axis=1)


def emit_coeffs(values, basis_ref, transfer_ref, ranks_ref, out_ref, ready=None):
    mains, rhs, _ = out_ref.shape
    leaves, rank_top, _ = basis_ref.shape
    lane = lax.broadcasted_iota(jnp.int32, (rhs, rank_top), 1)
    coeffs = []
    for i in range(leaves):
        value = dot_t(values[i], basis_ref[i])
        coeffs.append(jnp.where(lane < ranks_ref[i], value, 0.0).astype(BF))
    if ready is not None:
        ready()
    for q in range(leaves // 2):
        value = dot(coeffs[2 * q], transfer_ref[2 * q]) + dot(coeffs[2 * q + 1], transfer_ref[2 * q + 1])
        coeffs.append(jnp.where(lane < ranks_ref[leaves + q], value, 0.0).astype(BF))
    wide = [widen(value.astype(F32)) for value in coeffs]
    for q in range(mains // 3):
        for k, tile in enumerate(packed(wide[3 * q : 3 * q + 3], wide[mains + q], rank_top)):
            out_ref[3 * q + k] = tile.astype(BF)


def fetch(pairs, sems):
    copies = [pltpu.make_async_copy(src, dst, sems.at[n]) for n, (src, dst) in enumerate(pairs)]
    for copy in copies:
        copy.start()
    return copies


def emit_edges(v_ref, inner_ref, outer_ref):
    head, tail = v_ref[0], v_ref[v_ref.shape[0] - 1]
    even = lax.axis_index("clu") % CORES == 0
    inner_ref[0] = jnp.where(even, tail, head)
    outer_ref[0] = jnp.where(even, head, tail)


def coeff_kernel(
    ranks_ref, v_hbm, basis_hbm, transfer_hbm, out_ref, inner_ref, outer_ref, v_ref, basis_ref, transfer_ref, sems
):
    leaves = basis_ref.shape[0]
    copies = fetch([(v_hbm, v_ref), (basis_hbm, basis_ref), (transfer_hbm, transfer_ref)], sems)
    copies[0].wait()
    emit_edges(v_ref, inner_ref, outer_ref)
    copies[1].wait()
    values = [v_ref[i] for i in range(leaves)]
    emit_coeffs(values, basis_ref, transfer_ref, ranks_ref, out_ref, copies[2].wait)


def couple_kernel(source_ref, target_ref, coupling_ref, *refs, order, joined, unroll):
    chips = sum(len(group) for group in order)
    in_refs, out_refs, (sources, total) = refs[: -2 - 2 * len(order)], refs[-2 - 2 * len(order) : -2], refs[-2:]
    blocks, rank_top, _ = coupling_ref.shape
    far, mains, rhs, _ = in_refs[-1].shape
    if joined:
        cores, in_refs = (in_refs[: len(in_refs) // 2], in_refs[len(in_refs) // 2 :]), []
        for near_pieces, *far_pieces in cores:
            pieces = {chip: near_pieces.at[place] for place, chip in enumerate(order[1])}
            pieces |= dict(zip(order[0], far_pieces))
            in_refs += [pieces[chip] for chip in range(chips)]
    quads = mains // 3
    clusters = mains + quads

    def split(f, _):
        for n, packed_ref in enumerate(in_refs):
            row = (n * far + f) * clusters
            tiles = [packed_ref[f, c] for c in range(mains)]
            for c in range(mains):
                sources[row + c] = tiles[c]
            for q in range(quads):
                wide = [tile.astype(F32) for tile in tiles[3 * q : 3 * q + 3]]
                sources[row + mains + q] = fourth(wide, rank_top).astype(BF)
            for c in range(clusters):
                total[row + c] = jnp.zeros((rhs, LANES), F32)
        return 0

    lax.fori_loop(0, far, split, 0, unroll=far <= 2)

    def some(s, _):
        for u in range(unroll):
            j = s * unroll + u
            term = dot(sources[source_ref[j], :, :rank_top], coupling_ref[j])
            at = target_ref[j]
            total[at, :, :rank_top] = total[at, :, :rank_top] + term
        return 0

    lax.fori_loop(0, blocks // unroll, some, 0)

    def pack(f, _):
        for core in range(2):
            for g, group in enumerate(order):
                for place, chip in enumerate(group):
                    row = ((core * chips + chip) * far + f) * clusters
                    for q in range(quads):
                        mains_now = [total[row + 3 * q + k] for k in range(3)]
                        for k, tile in enumerate(packed(mains_now, total[row + mains + q], rank_top)):
                            out_refs[core * len(order) + g][place, f, 3 * q + k] = tile.astype(BF)
        return 0

    lax.fori_loop(0, far, pack, 0, unroll=far <= 2)


def order_kernel(_, __, out_ref):
    out_ref[...] = jnp.zeros_like(out_ref)


def near_kernel(v_ref, near_ref, out_ref):
    leaves = v_ref.shape[0]
    for i in range(leaves):
        total = dot(v_ref[i], near_ref[i, 1])
        if i > 0:
            total = total + dot(v_ref[i - 1], near_ref[i, 0])
        if i < leaves - 1:
            total = total + dot(v_ref[i + 1], near_ref[i, 2])
        out_ref[i] = total


def edge_kernel(inner_ref, outer_ref, first_ref, last_ref, out_ref):
    inner, outer = inner_ref[0], outer_ref[0]
    even = lax.axis_index("clu") % CORES == 0
    out_ref[0] = dot(jnp.where(even, outer, inner), first_ref[0, 0])
    out_ref[1] = dot(jnp.where(even, inner, outer), last_ref[0, 0])


def add_kernel(keep_ref, swap_ref, *out_refs):
    for n, out_ref in enumerate(out_refs):
        out_ref[...] = (keep_ref[n].astype(F32) + swap_ref[n].astype(F32)).astype(out_ref.dtype)


def middle_add_kernel(keep_ref, swap_ref, *refs, parts):
    part_refs, (own_out, *out_refs) = refs[:parts], refs[parts:]
    own_out[...] = keep_ref[0].astype(F32) + swap_ref[0].astype(F32)
    for n, out_ref in enumerate(out_refs):
        total = keep_ref[n + 1].astype(F32) + swap_ref[n + 1].astype(F32)
        for part_ref in part_refs[n :: len(out_refs)]:
            total = total + part_ref[...].astype(F32)
        out_ref[...] = total.astype(BF)


def rows_kernel(source_ref, target_ref, source_out, target_out, *, clusters, far, magic, shift):
    me = lax.axis_index("clu")
    for sign, in_ref, out_ref in ((-1, source_ref, source_out), (1, target_ref, target_out)):
        cluster = in_ref[...]
        device = cluster * magic >> shift
        chip = ((device ^ me) >> 1) & (CHIPS - 1)
        chip = jnp.where((device & 1) == 0, chip, chip >> 1 | (chip & 1) << 2)
        away = (sign * ((device >> 4) - (me >> 4))) & (far - 1)
        core = (device ^ me) & 1
        out_ref[...] = ((core * CHIPS + chip) * far + away) * clusters + cluster - device * clusters


def join_kernel(*refs):
    for n, part_ref in enumerate(refs[:-1]):
        refs[-1][n] = part_ref[...]


def last_add_kernel(own_ref, *refs, parts):
    part_refs, (keep_out, *away_refs) = refs[:parts], refs[parts:]
    for f in range(own_ref.shape[0]):
        total = own_ref[f]
        for part_ref in part_refs:
            total = total + part_ref[f].astype(F32)
        if f == 0:
            keep_out[...] = total
        else:
            away_refs[f - 1][...] = total.astype(BF)


def field_kernel(ranks_ref, near_ref, edge_ref, basis_ref, transfer_ref, keep_ref, *rest, away):
    term_refs, out_ref, next_refs = rest[:away], rest[away], rest[away + 1 :]
    leaves, rank_top, _ = basis_ref.shape
    mains, rhs, _ = keep_ref.shape
    tiles = []
    for t in range(mains):
        tile = keep_ref[t]
        for term_ref in term_refs:
            tile = tile + term_ref[t].astype(F32)
        tiles.append(tile)
    sums = tiles + [fourth(tiles[3 * q : 3 * q + 3], rank_top) for q in range(mains // 3)]
    lane = lax.broadcasted_iota(jnp.int32, (rhs, rank_top), 1)
    fields = [
        jnp.where(lane < ranks_ref[c], total[:, :rank_top], 0.0).astype(BF) for c, total in enumerate(sums)
    ]
    downs = [fields[i].astype(F32) + dot_t(fields[leaves + i // 2], transfer_ref[i]) for i in range(leaves)]
    leaf_totals = [jnp.where(lane < ranks_ref[i], down, 0.0).astype(BF) for i, down in enumerate(downs)]
    results = [near_ref[i] + dot(leaf_total, basis_ref[i]) for i, leaf_total in enumerate(leaf_totals)]
    results[0] = results[0] + edge_ref[0]
    results[-1] = results[-1] + edge_ref[1]
    results = [result.astype(BF) for result in results]
    for i, result in enumerate(results):
        out_ref[i] = result
    if next_refs:
        coeff_ref, inner_ref, outer_ref, values_ref = next_refs
        for i, result in enumerate(results):
            values_ref[i] = result
        emit_edges(out_ref, inner_ref, outer_ref)
        emit_coeffs(results, basis_ref, transfer_ref, ranks_ref, coeff_ref)


def params(mebibytes):
    return pltpu.CompilerParams(vmem_limit_bytes=mebibytes << 20)


def local(charges, basis, transfer, near_field, coupling, ranks, block_source, block_target):
    leaves, rank_top, width = basis.shape
    rhs = charges.shape[1]
    clusters = ranks.shape[0]
    blocks = coupling.shape[0]
    devices = lax.axis_size("clu")
    mains = clusters * 3 // 4
    shape = jax.ShapeDtypeStruct

    cores, chips = CORES, CHIPS
    cube = cores * chips
    far = devices // cube
    x, y, z = 1, 2, 4

    def swap_far(part, shift):
        return lax.ppermute(part, "clu", [(d, (d + shift * cube) % devices) for d in range(devices)])

    def swap(part, direction):
        turned = direction << 1 & 7 | direction >> 2
        return lax.ppermute(
            part, "clu", [(d, d ^ (turned if d % cores else direction) * cores) for d in range(devices)]
        )

    def swap_cores(part):
        return lax.ppermute(part, "clu", [(d, d ^ 1) for d in range(devices)])

    barrier = lax.optimization_barrier

    shift = 19
    magic = -(-(1 << shift) // clusters)
    numbers = np.arange(devices * clusters)
    assert (numbers * magic >> shift == numbers // clusters).all() and far & far - 1 == 0
    list_shape = jax.ShapeDtypeStruct((1, blocks), jnp.int32)
    source_rows, target_rows = pl.pallas_call(
        functools.partial(rows_kernel, clusters=clusters, far=far, magic=magic, shift=shift),
        out_shape=[list_shape] * 2,
        in_specs=[VMEM] * 2,
        out_specs=[VMEM] * 2,
        compiler_params=params(1),
    )(block_source.reshape(1, blocks), block_target.reshape(1, blocks))
    source_rows, target_rows = source_rows.reshape(blocks), target_rows.reshape(blocks)

    tile_shape = (mains, rhs, LANES)
    out_shape = shape((leaves, rhs, width), BF)
    tile_out = shape(tile_shape, BF)
    part_shape = shape((far,) + tile_shape, BF)
    edge_shape = shape((1, rhs, width), BF)
    first_coeffs, inner, outer = pl.pallas_call(
        coeff_kernel,
        out_shape=[tile_out, edge_shape, edge_shape],
        in_specs=[SMEM, HBM, HBM, HBM],
        out_specs=[VMEM] * 3,
        scratch_shapes=[
            pltpu.VMEM(charges.shape, BF),
            pltpu.VMEM(basis.shape, BF),
            pltpu.VMEM(transfer.shape, BF),
            pltpu.SemaphoreType.DMA((3,)),
        ],
    )(ranks, charges, basis, transfer)

    order = ((x | y | z, x | y, y | z, z | x), (0, x, y, z))
    def couple(joined, *args):
        return pl.pallas_call(
            functools.partial(couple_kernel, order=order, joined=joined, unroll=blocks),
            out_shape=[shape((4, far) + tile_shape, BF)] * 4,
            in_specs=[SMEM, SMEM] + [VMEM] * (len(args) - 2),
            out_specs=[VMEM] * 4,
            scratch_shapes=[
                pltpu.VMEM((devices * clusters, rhs, LANES), BF),
                pltpu.VMEM((devices * clusters, rhs, LANES), F32),
            ],
            compiler_params=params(24 if devices <= 32 else 60),
            cost_estimate=pl.CostEstimate(
                flops=2 * blocks * rhs * rank_top * rank_top, bytes_accessed=10 << 20, transcendentals=0
            ),
        )(*args)

    near = pl.pallas_call(
        near_kernel,
        out_shape=shape((leaves, rhs, width), F32),
        in_specs=[VMEM, VMEM],
        out_specs=VMEM,
        compiler_params=params(16),
        cost_estimate=pl.CostEstimate(
            flops=2 * leaves * 3 * rhs * width * width, bytes_accessed=4 << 20, transcendentals=0
        ),
    )

    edge = pl.pallas_call(
        edge_kernel,
        out_shape=shape((2, rhs, width), F32),
        grid=(1,),
        in_specs=[
            VMEM,
            VMEM,
            pl.BlockSpec((1, 1, width, width), lambda i: (0, 0, 0, 0)),
            pl.BlockSpec((1, 1, width, width), lambda i: (leaves - 1, 2, 0, 0)),
        ],
        out_specs=VMEM,
        compiler_params=params(16),
    )

    def adder(kernel, inputs, outputs):
        return pl.pallas_call(
            kernel,
            out_shape=outputs,
            in_specs=[VMEM] * inputs,
            out_specs=[VMEM] * len(outputs),
            compiler_params=params(16),
        )

    own_shape = shape((far,) + tile_shape, F32)
    join = adder(join_kernel, far, [part_shape])
    relaid = pl.pallas_call(
        order_kernel,
        out_shape=shape((8, LANES), F32),
        in_specs=[pl.BlockSpec(memory_space=pl.ANY)] * 2,
        out_specs=VMEM,
    )
    first_join = pl.pallas_call(
        lambda _, *refs: join_kernel(*refs),
        out_shape=[part_shape],
        in_specs=[pl.BlockSpec(memory_space=pl.ANY)] + [VMEM] * far,
        out_specs=[VMEM],
        compiler_params=params(16),
    )
    far_add = adder(add_kernel, 2, [part_shape] * 4)
    join_near = adder(join_kernel, 4, [shape((4,) + part_shape.shape, BF)])

    def middle_add(*args):
        kernel = functools.partial(middle_add_kernel, parts=len(args) - 2)
        return adder(kernel, len(args), [own_shape] + [part_shape] * 3)(*args)

    def last_add(*args):
        kernel = functools.partial(last_add_kernel, parts=len(args) - 1)
        return adder(kernel, len(args), [shape(tile_shape, F32)] + [tile_out] * (far - 1))(*args)

    def finish(with_coeffs):
        return pl.pallas_call(
            functools.partial(field_kernel, away=far - 1),
            out_shape=[out_shape, tile_out, edge_shape, edge_shape, out_shape] if with_coeffs else [out_shape],
            in_specs=[SMEM] + [VMEM] * (4 + far),
            out_specs=[VMEM] * 5 if with_coeffs else [VMEM],
            compiler_params=params(16),
        )

    halo_pairs = [(d, d + cores) for d in range(1, devices - cores, cores)]
    halo_pairs += [(d, d - cores) for d in range(cores, devices, cores)]

    def apply_matrix(field_in, coeffs, inner, outer, coupling, with_coeffs):
        away = [swap_far(coeffs, s) for s in range(1, far)]
        (column,) = first_join(relaid(coupling, coeffs), coeffs, *away) if with_coeffs else join(coeffs, *away)
        got = {0: column, x: swap(column, x), y: swap(column, y), z: swap(column, z)}
        near_sum = near(field_in, near_field)
        got, near_sum = barrier((got, near_sum))
        second_round = {x | y: swap(got[x], y), y | z: swap(got[y], z), z | x: swap(got[z], x)}
        if with_coeffs:
            second_round[x | y | z] = swap(got[x], y | z)
            (near_pieces,) = join_near(*[got[chip] for chip in order[1]])
            far_pieces, other_near = barrier(([second_round[chip] for chip in order[0]], swap_cores(near_pieces)))
            other_far = [swap_cores(part) for part in far_pieces]
            args = (near_pieces, *far_pieces, other_near, *other_far)
        else:
            corner = swap(column, x | y | z)
            other = {chip: swap_cores(part) for chip, part in got.items()}
            got |= second_round
            got, corner, outer = barrier((got, corner, lax.ppermute(outer, "clu", halo_pairs)))
            got[x | y | z] = corner
            other |= {chip: swap_cores(got[chip]) for chip in order[0]}
            args = [got[chip] for chip in range(chips)] + [other[chip] for chip in range(chips)]
        keep_long, keep, send_long, send = couple(with_coeffs, source_rows, target_rows, coupling, *args)

        corner, xy, yz, zx = far_add(keep_long, swap_cores(send_long))
        corner, xy, yz, zx, send = barrier((corner, xy, yz, zx, send))
        arrived = [swap(xy, y), swap(yz, z), swap(zx, x)]
        if not with_coeffs:
            arrived.append(swap(corner, y | z))
        arrived, swapped = barrier((arrived, swap_cores(send)))
        (own, *sums), inner, outer = barrier((middle_add(keep, swapped, *arrived), inner, outer))
        ways = (x, y, z)
        if with_coeffs:
            sums, ways = sums + [corner], ways + (x | y | z,)
            outer = lax.ppermute(outer, "clu", halo_pairs)
        parts = [swap(part, way) for part, way in zip(sums, ways)]
        own, parts, inner, outer = barrier((own, parts, inner, outer))
        total, *away = last_add(own, *parts)
        edges = edge(swap_cores(inner), swap_cores(outer), near_field, near_field)
        terms, edges = barrier(([swap_far(part, s + 1) for s, part in enumerate(away)], edges))
        return finish(with_coeffs)(ranks, near_sum, edges, basis, transfer, total, *terms)

    first, *second_args, values = apply_matrix(charges, first_coeffs, inner, outer, coupling, True)
    (second,) = apply_matrix(values, *second_args, coupling, False)
    return (first, second)


def solution(mesh):
    in_specs = (
        P("clu", None, None),
        P("clu", None, None),
        P("clu", None, None),
        P("clu", None, None, None),
        P("clu", None, None),
        P("clu"),
        P("clu"),
        P("clu"),
    )
    out_specs = (P("clu", None, None), P("clu", None, None))
    return jax.shard_map(local, mesh=mesh, in_specs=in_specs, out_specs=out_specs, check_vma=False)
```
